32 devices in a mesh: rep: 2 (over y), patch: 4 (over z), tp: 2 (over x), sec: 2 (over core).
Axes of the slice: x: 2, y: 2, z: 4, core: 2. Of those that a mesh axis runs over, the one named last changes fastest.
Arguments:
- hidden: bfloat16 [2, 8192, 3072], P('sec', ('rep', 'patch')), parts along dimension 1, may hold values from -6 to 6
- modulation: float32 [2, 2, 3072], P('sec'), may hold values from -3 to 3
- gate: float32 [2, 3072], P('sec'), may hold values from 0.5 to 2
- w_qkv: bfloat16 [2, 3072, 4608], P('sec', 'patch', 'tp'), may hold values from -0.109375 to 0.109375
- stale_kv: bfloat16 [2, 8192, 3072], P('sec', ('rep', 'patch'), 'tp'), parts along dimension 1, may hold values from -6 to 6
- w_out: bfloat16 [2, 1536, 3072], P('sec', 'tp', 'patch'), may hold values from -1.5 to 1.5
- key_lists: int32 [64, 24], P(('rep', 'patch')), parts along dimension 0, may hold values from -1 to 31, as said below
Outputs:
- updated: bfloat16 [8192, 3072], P(('rep', 'patch'), ('tp', 'sec')), parts along dimension 0
The draws below stay inside these ranges and needn't reach their ends.
There are 2 independent parts, one for each index of `rep`. The reference program is written for one: setup_inputs(seed, part) draws one part's arguments, and reference() takes and returns one part's arrays. A program takes and returns all parts, laid end to end along the dimension named above; an argument that names none is the same for every part. Nothing has to cross between parts.
Inputs may be any that keep to these rules, and one draw needn't show every extreme that they name: `key_lists`: row r lists distinct key blocks followed by -1 padding; it always lists block r, and every listed block lies in the patch of block r or in the patches just before and after it. Some row lists 24 blocks.
All inputs are finite; a program needn't handle non-finite values.
Results may differ from the reference program's by a relative error of at most 0.01.
Values may be sent and summed in bfloat16 or wider, within the bound.
No kernel may reach another device: no remote copies, remote signals or barrier semaphores. Data moves between devices by JAX's collectives and lax.ppermute only.
A program may use at most 192 MiB of HBM per device.

```python
import math
import jax
import jax.numpy as jnp
from jax import lax

D = 3072
HEADS = 12
HEAD_DIM = 128
BLOCK = 128
TOK_DEV = 1024
TOKENS = 4096
KMAX = 24
N_TP = 2


def draw_key_lists(key, part):
    key = jax.random.fold_in(key, 11)
    patch_blocks = TOK_DEV // BLOCK
    block_count = TOKENS // BLOCK
    patch_count = TOKENS // TOK_DEV
    span_width = 3 * patch_blocks
    first_key, second_key, third_key, fourth_key, fifth_key, sixth_key = jax.random.split(key, 6)
    row_ids = jnp.arange(block_count, dtype=jnp.int32)
    patch_of = row_ids // patch_blocks
    patch_cap = jax.random.randint(first_key, (patch_count,), max(3, KMAX // 2), KMAX + 1)[patch_of]
    counts = jax.random.randint(second_key, (block_count,), 0, 1 << 20) % patch_cap + 1
    counts = jnp.maximum(counts, 3)
    full_row = jax.random.randint(third_key, (), patch_blocks, block_count - patch_blocks)
    counts = jnp.where(row_ids == full_row, KMAX, counts)
    slot_range = jnp.arange(span_width, dtype=jnp.int32)
    candidates = (patch_of[:, None] - 1) * patch_blocks + slot_range[None, :]
    inside = (candidates >= 0) & (candidates < block_count)
    shuffle = jax.vmap(lambda row_key: jax.random.permutation(row_key, span_width))(jax.random.split(fourth_key, block_count))
    lower_pick = jax.random.randint(fifth_key, (block_count,), 0, patch_blocks)
    upper_pick = jax.random.randint(sixth_key, (block_count,), 0, patch_blocks) + 2 * patch_blocks
    ranks = jnp.where(slot_range[None, :] == lower_pick[:, None], 3 * span_width, shuffle)
    ranks = jnp.where(slot_range[None, :] == upper_pick[:, None], 3 * span_width + 1, ranks)
    ranks = jnp.where(candidates == row_ids[:, None], 4 * span_width, ranks)
    ranks = jnp.where(inside, ranks, shuffle - 2 * span_width)
    ranking = jnp.argsort(-ranks, axis=1)
    picked = jnp.take_along_axis(candidates, ranking, axis=1)[:, :KMAX]
    picked_inside = jnp.take_along_axis(inside, ranking, axis=1)[:, :KMAX]
    slot_ids = jnp.arange(KMAX, dtype=jnp.int32)
    keep = (slot_ids[None, :] < counts[:, None]) & picked_inside
    return jnp.where(keep, picked, -1).astype(jnp.int32)


def block_scale(rng, shape, cuts, least, top_value):
    loudness, own = 1.0, jax.random.fold_in(rng, 6)
    for axis_at, blocks in cuts:
        steps = jnp.exp(jax.random.uniform(jax.random.fold_in(own, axis_at), (blocks,), jnp.float32, least / len(cuts), top_value / len(cuts)))
        loudness = loudness * jnp.repeat(steps, shape[axis_at] // blocks).reshape([-1 if axis == axis_at else 1 for axis in range(len(shape))])
    return loudness


def noise(rng, dims, width, reach, cuts=(), held_as=jnp.bfloat16):
    entries = width * jax.random.normal(rng, dims, jnp.float32)
    if cuts:
        entries = entries * block_scale(rng, dims, cuts, -0.22, 0.18)
    return jnp.clip(entries, -reach, reach).astype(held_as)


def setup_inputs(seed: int = 0, part: int = 0) -> dict:
    streams_of = jax.random.split(jax.random.key(seed), 8)
    part_keys = jax.random.split(jax.random.fold_in(streams_of[7], part), 8)
    hidden = noise(part_keys[0], (2, TOKENS, D), 1.0, 6.0, ((0, 2), (1, 4)))
    modulation = noise(streams_of[1], (2, 2, D), 0.5, 3.0, ((0, 2),), jnp.float32)
    gate = jnp.clip(0.5 + 1.5 * jax.random.uniform(streams_of[2], (2, D), jnp.float32) ** block_scale(streams_of[2], (2, D), ((0, 2),), -0.2, 0.2), 0.5, 2.0)
    w_qkv = noise(streams_of[3], (2, D, 3 * HEADS * HEAD_DIM), D ** -0.5, 0.109375, ((0, 2), (1, 4), (2, 2)))
    stale_kv = noise(part_keys[4], (2, TOKENS, 2 * HEADS * HEAD_DIM), 1.0, 6.0, ((0, 2), (1, 4), (2, 2)))
    w_out = noise(streams_of[5], (2, HEADS * HEAD_DIM, D), 0.25, 1.5, ((0, 2), (1, 2), (2, 4)))
    key_lists = draw_key_lists(jax.random.fold_in(jax.random.fold_in(streams_of[7], part), 71), part)
    return dict(hidden=hidden, modulation=modulation, gate=gate, w_qkv=w_qkv, stale_kv=stale_kv, w_out=w_out, key_lists=key_lists)


def rounded(value):
    return lax.optimization_barrier(value.astype(jnp.bfloat16))

def rms_norm(value):
    wide = value.astype(jnp.float32)
    return wide * lax.rsqrt(lax.optimization_barrier(jnp.mean(wide * wide, axis=-1, keepdims=True)) + 1e-06)

def reference(hidden, modulation, gate, w_qkv, stale_kv, w_out, key_lists):
    patch_blocks = TOK_DEV // BLOCK
    patch_count = TOKENS // TOK_DEV
    group_cols = HEADS // N_TP * HEAD_DIM
    score_scale = 1.0 / math.sqrt(HEAD_DIM)
    window_blocks = 3 * patch_blocks
    stale_padded = jnp.pad(stale_kv, ((0, 0), (TOK_DEV, TOK_DEV), (0, 0)))

    def one_patch(patch):
        summed = jnp.zeros((TOK_DEV, D), jnp.float32)
        patch_lists = lax.dynamic_slice_in_dim(key_lists, (patch * patch_blocks).astype(jnp.int32), patch_blocks, 0)
        relative = jnp.where(patch_lists >= 0, patch_lists - (patch - 1) * patch_blocks, -1)
        block_hits = jnp.any(relative[:, :, None] == jnp.arange(window_blocks, dtype=jnp.int32)[None, None, :], axis=1)
        allowed = jnp.repeat(jnp.repeat(block_hits, BLOCK, axis=0), BLOCK, axis=1)
        for section in range(2):
            inputs = lax.dynamic_slice_in_dim(hidden[section], (patch * TOK_DEV).astype(jnp.int32), TOK_DEV, 0).astype(jnp.float32)
            average = lax.optimization_barrier(jnp.mean(inputs, axis=-1, keepdims=True))
            centered = inputs - average
            variance = lax.optimization_barrier(jnp.mean(centered * centered, axis=-1, keepdims=True))
            normed = centered * lax.rsqrt(variance + 1e-06)
            modulated = (normed * (1.0 + modulation[section, 1]) + modulation[section, 0]).astype(jnp.bfloat16)
            projected = jnp.dot(modulated, w_qkv[section], preferred_element_type=jnp.float32)
            projected = projected.reshape(TOK_DEV, HEADS, 3, HEAD_DIM)
            queries = rounded(rms_norm(projected[:, :, 0]))
            fresh_keys = rounded(rms_norm(projected[:, :, 1]))
            fresh_values = projected[:, :, 2].astype(jnp.bfloat16)
            window = lax.dynamic_slice_in_dim(stale_padded[section], (patch * TOK_DEV).astype(jnp.int32), 3 * TOK_DEV, 0)
            window = window.reshape(3 * TOK_DEV, HEADS, 2, HEAD_DIM)
            stale_keys = rounded(rms_norm(window[:, :, 0]))
            key_rows = jnp.concatenate([stale_keys[:TOK_DEV], fresh_keys, stale_keys[2 * TOK_DEV:]], axis=0)
            value_rows = jnp.concatenate([window[:TOK_DEV, :, 1], fresh_values, window[2 * TOK_DEV:, :, 1]], axis=0)
            scores = jnp.einsum('qhd,khd->hqk', queries.astype(jnp.float32), key_rows.astype(jnp.float32)) * score_scale
            exponents = jnp.where(allowed[None], jnp.exp(scores), 0.0)
            totals = lax.optimization_barrier(jnp.sum(exponents, axis=-1))
            weighted = jnp.einsum('hqk,khd->qhd', rounded(exponents).astype(jnp.float32), value_rows.astype(jnp.float32))
            attended = rounded(weighted / totals.T[:, :, None]).reshape(TOK_DEV, HEADS * HEAD_DIM)
            for head_group in range(N_TP):
                head_cols = attended[:, head_group * group_cols:(head_group + 1) * group_cols]
                head_rows = w_out[section, head_group * group_cols:(head_group + 1) * group_cols]
                branch_term = gate[section] * jnp.dot(head_cols, head_rows, preferred_element_type=jnp.float32)
                if section == 1 and head_group == 0:
                    branch_term = branch_term + inputs
                summed = summed + rounded(branch_term).astype(jnp.float32)
        return summed.astype(jnp.bfloat16)
    result = lax.map(one_patch, jnp.arange(patch_count, dtype=jnp.int32))
    return result.reshape(TOKENS, D)
```

```python
import functools
import math

import jax
import jax.numpy as jnp
from jax import lax
from jax.experimental import pallas as pl
from jax.experimental.pallas import tpu as pltpu
from jax.sharding import PartitionSpec as P

HEAD_DIM = 128
BLOCK = 128
QUERY_TILE = 256
ROW_CHUNKS = 2
VMEM_LIMIT = 48 * 1024 * 1024
F32 = jnp.float32
BF16 = jnp.bfloat16


def after(value, *others):
    return lax.optimization_barrier((value,) + others)[0]


def params():
    return pltpu.CompilerParams(vmem_limit_bytes=VMEM_LIMIT)


def cost(flops, moved, exps=0):
    return pl.CostEstimate(flops=int(flops), bytes_accessed=int(moved), transcendentals=int(exps))


def unit(value):
    return value * lax.rsqrt(jnp.mean(value * value, axis=-1, keepdims=True) + 1e-06)


def stale_kernel(in_ref, out_ref):
    out_ref[:, :HEAD_DIM] = unit(in_ref[:, :HEAD_DIM].astype(F32)).astype(BF16)
    out_ref[:, HEAD_DIM:] = in_ref[:, HEAD_DIM:]


def stale_group(stale, first, heads):
    rows = stale.shape[0]
    return pl.pallas_call(
        stale_kernel,
        grid=(heads,),
        in_specs=[pl.BlockSpec((rows, 2 * HEAD_DIM), lambda h: (0, first + h))],
        out_specs=pl.BlockSpec((rows, 2 * HEAD_DIM), lambda h: (0, h)),
        out_shape=jax.ShapeDtypeStruct((rows, heads * 2 * HEAD_DIM), BF16),
        compiler_params=params(),
        cost_estimate=cost(rows * heads * 512, rows * heads * 1024),
    )(stale)


def finish_kernel(terms, *refs):
    acc_ref = refs[0]
    q_ref, k_ref, v_ref = refs[1 + 2 * terms :]
    total = acc_ref[...]
    for at in range(terms):
        total += jnp.dot(refs[1 + at][...], refs[1 + terms + at][...], preferred_element_type=F32)
    q_ref[...] = unit(total[:, :HEAD_DIM]).astype(BF16)
    k_ref[...] = unit(total[:, HEAD_DIM : 2 * HEAD_DIM]).astype(BF16)
    v_ref[...] = total[:, 2 * HEAD_DIM :].astype(BF16)


def finish(acc, lefts, rights):
    rows, cols = acc.shape
    width = 3 * HEAD_DIM
    heads = cols // width
    depth = sum(left.shape[1] for left in lefts)
    return pl.pallas_call(
        functools.partial(finish_kernel, len(lefts)),
        grid=(heads,),
        in_specs=[pl.BlockSpec((rows, width), lambda h: (0, h))]
        + [pl.BlockSpec(left.shape, lambda h: (0, 0)) for left in lefts]
        + [pl.BlockSpec((right.shape[0], width), lambda h: (0, h)) for right in rights],
        out_specs=[pl.BlockSpec((rows, HEAD_DIM), lambda h: (0, h))] * 3,
        out_shape=[jax.ShapeDtypeStruct((rows, heads * HEAD_DIM), BF16)] * 3,
        compiler_params=params(),
        cost_estimate=cost(2 * rows * depth * cols, rows * cols * 6 + depth * (rows + cols) * 2),
    )(acc, *lefts, *rights)


def weigh(query, key, value, mask):
    tile, keys = query.shape[0], key.shape[0]
    scores = lax.dot_general(query, key, (((1,), (1,)), ((), ())), preferred_element_type=F32)
    exponents = jnp.exp(scores * (1.0 / math.sqrt(HEAD_DIM)))
    exponents = exponents.reshape(tile // BLOCK, BLOCK, keys) * mask
    return exponents.reshape(tile, keys).astype(BF16)


def with_ones(value):
    return jnp.concatenate([value, jnp.ones(value.shape, value.dtype)], axis=1)


def own_kernel(q_ref, k_ref, v_ref, mask_ref, num_ref, tot_ref):
    value = v_ref[...]
    weights = weigh(q_ref[...], k_ref[...], value, mask_ref[...])
    both = jnp.dot(weights, with_ones(value), preferred_element_type=F32)
    num_ref[...] = both[:, :HEAD_DIM]
    tot_ref[...] = both[:, HEAD_DIM:]


def own_part(queries, keys, values, mask):
    rows, cols = queries.shape
    heads, window = cols // HEAD_DIM, keys.shape[0]
    tile = pl.BlockSpec((QUERY_TILE, HEAD_DIM), lambda h, i: (i, h))
    whole = pl.BlockSpec((window, HEAD_DIM), lambda h, i: (0, h))
    return pl.pallas_call(
        own_kernel,
        grid=(heads, rows // QUERY_TILE),
        in_specs=[tile, whole, whole, pl.BlockSpec((QUERY_TILE // BLOCK, 1, window), lambda h, i: (i, 0, 0))],
        out_specs=[tile, tile],
        out_shape=[jax.ShapeDtypeStruct((rows, cols), F32)] * 2,
        compiler_params=params(),
        cost_estimate=cost(6 * rows * window * cols, rows * cols * 14, rows * window * heads),
    )(queries, keys, values, mask)


def side_kernel(flag_ref, q_ref, lk_ref, lv_ref, lm_ref, rk_ref, rv_ref, rm_ref, n_ref, t_ref, num_ref, tot_ref):
    num_ref[...] = n_ref[...]
    tot_ref[...] = t_ref[...]

    @pl.when(flag_ref[0] == 1)
    def _():
        query = q_ref[...]
        both = jnp.zeros((query.shape[0], 2 * HEAD_DIM), F32)
        for k_ref, v_ref, m_ref in ((lk_ref, lv_ref, lm_ref), (rk_ref, rv_ref, rm_ref)):
            value = v_ref[...]
            weights = weigh(query, k_ref[...], value, m_ref[...])
            both += jnp.dot(weights, with_ones(value), preferred_element_type=F32)
        num_ref[...] += both[:, :HEAD_DIM]
        tot_ref[...] += both[:, HEAD_DIM:]


def side_parts(flag, queries, left, left_mask, right, right_mask, num, tot):
    rows, cols = queries.shape
    heads, window = cols // HEAD_DIM, left.shape[0]
    tile = pl.BlockSpec((QUERY_TILE, HEAD_DIM), lambda h, i, f: (i, h))
    key = pl.BlockSpec((window, HEAD_DIM), lambda h, i, f: (0, 2 * h))
    value = pl.BlockSpec((window, HEAD_DIM), lambda h, i, f: (0, 2 * h + 1))
    mask = pl.BlockSpec((QUERY_TILE // BLOCK, 1, window), lambda h, i, f: (i, 0, 0))
    return pl.pallas_call(
        side_kernel,
        grid_spec=pltpu.PrefetchScalarGridSpec(
            num_scalar_prefetch=1,
            grid=(heads, rows // QUERY_TILE),
            in_specs=[tile, key, value, mask, key, value, mask, tile, tile],
            out_specs=[tile, tile],
        ),
        out_shape=[jax.ShapeDtypeStruct((rows, cols), F32)] * 2,
        compiler_params=params(),
        cost_estimate=cost(12 * rows * window * cols, rows * cols * 26, 2 * rows * window * heads),
    )(flag, queries, left, left, left_mask, right, right, right_mask, num, tot)


def foreign_kernel(flag_ref, q_ref, k_ref, v_ref, mask_ref, num_ref, tot_ref):
    head = pl.program_id(1)

    @pl.when(head == 0)
    def _():
        tot_ref[...] = jnp.zeros_like(tot_ref)

    @pl.when(flag_ref[0] == 1)
    def _():
        value = v_ref[...]
        weights = weigh(q_ref[...], k_ref[...], value, mask_ref[...])
        num_ref[...] = jnp.dot(weights, value, preferred_element_type=F32).astype(BF16)
        sums = lax.dot_general(
            jnp.ones((8, weights.shape[1]), BF16), weights, (((1,), (1,)), ((), ())), preferred_element_type=F32
        )
        row = lax.broadcasted_iota(jnp.int32, sums.shape, 0)
        tot_ref[...] = jnp.where(row == head, sums, tot_ref[...])

    @pl.when(flag_ref[0] != 1)
    def _():
        num_ref[...] = jnp.zeros_like(num_ref)


def foreign_part(flag, queries, stale, mask):
    rows, cols = queries.shape
    heads, window = cols // HEAD_DIM, stale.shape[0]
    tile = pl.BlockSpec((QUERY_TILE, HEAD_DIM), lambda i, h, f: (i, h))
    return pl.pallas_call(
        foreign_kernel,
        grid_spec=pltpu.PrefetchScalarGridSpec(
            num_scalar_prefetch=1,
            grid=(rows // QUERY_TILE, heads),
            in_specs=[
                tile,
                pl.BlockSpec((window, HEAD_DIM), lambda i, h, f: (0, 2 * h)),
                pl.BlockSpec((window, HEAD_DIM), lambda i, h, f: (0, 2 * h + 1)),
                pl.BlockSpec((QUERY_TILE // BLOCK, 1, window), lambda i, h, f: (i, 0, 0)),
            ],
            out_specs=[tile, pl.BlockSpec((8, QUERY_TILE), lambda i, h, f: (0, i))],
        ),
        out_shape=[jax.ShapeDtypeStruct((rows, cols), BF16), jax.ShapeDtypeStruct((8, rows), F32)],
        compiler_params=params(),
        cost_estimate=cost(4 * rows * window * cols, rows * cols * 8, rows * window * heads),
    )(flag, queries, stale, stale, mask)


def branch_kernel(groups, blocks, secs, where_ref, w_ref, gate_ref, hidden_ref, *refs):
    send_refs, keep_ref = refs[4 * groups : -1], refs[-1]
    sec, main = where_ref[0], where_ref[1].astype(F32)
    parts = []
    for group in range(groups):
        num_ref, tot_ref, far_ref, far_tot_ref = refs[4 * group : 4 * group + 4]
        far_tot = jnp.transpose(far_tot_ref[...])
        for head in range(num_ref.shape[1] // HEAD_DIM):
            cols = slice(head * HEAD_DIM, (head + 1) * HEAD_DIM)
            total = tot_ref[:, cols] + far_tot[:, head : head + 1]
            parts.append(((num_ref[:, cols] + far_ref[:, cols].astype(F32)) / total).astype(BF16))
    attended = jnp.concatenate(parts, axis=1)
    width = keep_ref.shape[2]
    for offset in range(secs):
        out_ref = keep_ref if offset == 0 else send_refs[offset - 1]
        for block in range(blocks):
            place = block * secs + lax.rem(sec + offset, secs)
            cols = pl.ds(pl.multiple_of(place * width, HEAD_DIM), width)
            term = jnp.dot(attended, w_ref[:, cols], preferred_element_type=F32) * gate_ref[:, cols]
            out_ref[block] = (term + main * hidden_ref[:, cols].astype(F32)).astype(BF16)


def branch(where, w_full, gate, hidden, groups, first, count, blocks, secs):
    model_width = hidden.shape[1]
    width = model_width // (blocks * secs)
    tile = min(256, count)
    start = first // tile
    specs, values = [], []
    for num, tot, far, far_tot in groups:
        spec = pl.BlockSpec((tile, num.shape[1]), lambda i, w: (start + i, 0))
        specs += [spec, spec, spec, pl.BlockSpec((8, tile), lambda i, w: (0, start + i))]
        values += [num, tot, far, far_tot]
    out = pl.BlockSpec((blocks, tile, width), lambda i, w: (0, i, 0))
    shape = jax.ShapeDtypeStruct((blocks, count, width), BF16)
    results = pl.pallas_call(
        functools.partial(branch_kernel, len(groups), blocks, secs),
        grid_spec=pltpu.PrefetchScalarGridSpec(
            num_scalar_prefetch=1,
            grid=(count // tile,),
            in_specs=[
                pl.BlockSpec(w_full.shape, lambda i, w: (0, 0)),
                pl.BlockSpec(gate.shape, lambda i, w: (0, 0)),
                pl.BlockSpec((tile, model_width), lambda i, w: (start + i, 0)),
            ]
            + specs,
            out_specs=[out] * secs,
        ),
        out_shape=[shape] * secs,
        compiler_params=params(),
        cost_estimate=cost(2 * count * w_full.size, w_full.size * 2 + count * model_width * 4),
    )(where, w_full, gate, hidden, *values)
    return results[-1], results[:-1]


def swapped(piece, reps, count, places):
    pieces = [(0, piece)]
    for offset in range(1, reps):
        pairs = [(a * count + i, (a + offset) % reps * count + i) for a in range(reps) for i in places]
        pieces.append((offset, lax.ppermute(piece, ("rep", "patch"), pairs)))
    return pieces


class Relay:
    def __init__(self, shard, count, reps):
        self.count, self.reps = count, reps
        self.place = lax.axis_index("patch")
        self.rank = lax.axis_index("rep")
        self.depth = shard.shape[0] // reps
        self.shard = shard
        own = lax.dynamic_slice_in_dim(shard, self.rank * self.depth, self.depth, 0)
        self.ahead = self.back = own

    def step(self, k, *held):
        count = self.count
        ahead = after(self.ahead, *held) if held else self.ahead
        back = after(self.back, *held) if held else self.back
        self.ahead = lax.ppermute(ahead, "patch", [(i, i + 1) for i in range(k - 1, count - 1)])
        self.back = lax.ppermute(back, "patch", [(i + 1, i) for i in range(count - k)])
        return self.ahead, self.back

    def pieces(self, k):
        count, place = self.count, self.place
        low, high = [i for i in range(count) if i < count - k], [i for i in range(count) if i >= k]
        if 2 * k < count:
            brought = [(jnp.maximum(place - k, 0), self.ahead, high), (jnp.minimum(place + k, count - 1), self.back, low)]
        else:
            forward = place >= k
            owner = jnp.where(forward, place - k, jnp.minimum(place + k, count - 1))
            brought = [(owner, jnp.where(forward, self.ahead, self.back), low + high)]
        out = []
        for owner, rows, places in brought:
            for offset, piece in swapped(rows, self.reps, count, places):
                part = (self.rank - offset) % self.reps
                here = functools.reduce(jnp.logical_or, [place == i for i in places])
                out.append((owner, part, piece, here))
        return out


def body(hidden, modulation, gate, w_qkv, stale_kv, w_out, key_lists):
    count, reps = lax.axis_size("patch"), lax.axis_size("rep")
    tps, secs = lax.axis_size("tp"), lax.axis_size("sec")
    place = lax.axis_index("patch")
    tp_index, sec_index = lax.axis_index("tp"), lax.axis_index("sec")
    rows, model_width = hidden.shape[1], hidden.shape[2]
    heads = w_out.shape[1] // HEAD_DIM
    patch_blocks = rows // BLOCK
    group_count = 2 if heads % 2 == 0 else 1
    group_heads = heads // group_count
    states = hidden[0]

    shard_rows = w_qkv.shape[1]
    group_cols = group_heads * 3 * HEAD_DIM
    relays = [
        Relay(w_qkv[0][:, g * group_cols : (g + 1) * group_cols], count, reps) for g in range(group_count)
    ]
    out_relay = Relay(w_out[0], count, reps)
    qkv_pieces = [[] for _ in range(group_count)]
    held = ()
    steps = []
    for k in range(1, count + group_count):
        for g, relay in enumerate(relays):
            if 1 <= k - g < count:
                sent = relay.step(k - g, *held)
                qkv_pieces[g].append(relay.pieces(k - g))
                steps.append(sent)
        held = steps[-group_count] if len(steps) >= group_count else ()
    tail = steps[-1]

    relative = jnp.where(key_lists >= 0, key_lists - (place - 1) * patch_blocks, -1)
    window_ids = jnp.arange(3 * patch_blocks, dtype=jnp.int32)
    hits = jnp.any(relative[:, :, None] == window_ids[None, None, :], axis=1).astype(F32)
    hits = jnp.repeat(hits, BLOCK, axis=1).reshape(patch_blocks, 3, rows)
    before, fresh, behind = (hits[:, i][:, None, :] for i in range(3))
    at_end = (place == 0) | (place == count - 1)
    to_inner = [(0, 1), (count - 1, count - 2)]
    to_end = [(1, 0), (count - 2, count - 1)]
    far_mask = lax.ppermute(jnp.where(place == 0, behind, before), "patch", to_inner)
    inner_flag = jnp.where(at_end, 0, 1).astype(jnp.int32).reshape(1)
    host_flag = ((place == 1) | (place == count - 2)).astype(jnp.int32).reshape(1)

    stale = [stale_group(stale_kv[0], g * group_heads, group_heads) for g in range(group_count)]

    inputs = states.astype(F32)
    centered = inputs - jnp.mean(inputs, axis=-1, keepdims=True)
    variance = jnp.mean(centered * centered, axis=-1, keepdims=True)
    normed = centered * lax.rsqrt(variance + 1e-06)
    modulated = (normed * (1.0 + modulation[0, 1]) + modulation[0, 0]).astype(BF16)

    def columns(owner, part, depth):
        return lax.dynamic_slice_in_dim(modulated, owner * shard_rows + part * depth, depth, 1)

    own_columns = lax.dynamic_slice_in_dim(modulated, place * shard_rows, shard_rows, 1)
    projected = []
    stale_left, stale_right = [], []
    for g, relay in enumerate(relays):
        acc = jnp.dot(own_columns, relay.shard, preferred_element_type=F32)
        for pieces in qkv_pieces[g][:-1]:
            for owner, part, piece, _ in pieces:
                acc += jnp.dot(columns(owner, part, relay.depth), piece, preferred_element_type=F32)
        last = qkv_pieces[g][-1]
        lefts = [columns(owner, part, relay.depth) for owner, part, _, _ in last]
        projected.append(finish(acc, lefts, [piece for _, _, piece, _ in last]))

    held = tail
    for g in range(group_count):
        mine = after(stale[g], *held)
        stale_left.append(lax.ppermute(mine, "patch", [(i, i + 1) for i in range(count - 2)]))
        stale_right.append(lax.ppermute(mine, "patch", [(i + 1, i) for i in range(1, count - 1)]))
        held = (stale_left[-1], stale_right[-1])
    w_full = jnp.zeros((w_out.shape[1], model_width), BF16)
    w_full = lax.dynamic_update_slice(w_full, w_out[0], (0, place * w_out.shape[2]))
    for k in range(1, count):
        out_relay.step(k, *(tail if k == 1 else ()))
        for owner, part, piece, here in out_relay.pieces(k):
            at = (part * out_relay.depth, owner * w_out.shape[2])
            old = lax.dynamic_slice(w_full, at, piece.shape)
            w_full = lax.dynamic_update_slice(w_full, jnp.where(here, piece, old), at)

    groups = []
    for g in range(group_count):
        queries, keys, values = projected[g]
        far_queries = lax.ppermute(queries, "patch", to_inner)
        far_num, far_tot = foreign_part(host_flag, far_queries, stale[g], far_mask)
        far_num = lax.ppermute(far_num, "patch", to_end)
        far_tot = lax.ppermute(far_tot, "patch", to_end)
        num, tot = own_part(queries, keys, values, fresh)
        num, tot = side_parts(inner_flag, queries, stale_left[g], before, stale_right[g], behind, num, tot)
        groups.append((num, tot, far_num, far_tot))

    where = jnp.stack([sec_index, ((sec_index == 1) & (tp_index == 0)).astype(jnp.int32)]).astype(jnp.int32)
    chunk = rows // ROW_CHUNKS
    results = []
    for at in range(ROW_CHUNKS):
        keep, sends = branch(where, w_full, gate, states, groups, at * chunk, chunk, tps, secs)
        total = keep.astype(F32)
        for offset, sent in enumerate(sends, 1):
            got = lax.ppermute(sent, "sec", [(i, (i + offset) % secs) for i in range(secs)])
            total += got.astype(F32)
        result = lax.dynamic_index_in_dim(total, tp_index, 0, keepdims=False)
        for offset in range(1, tps):
            sent = lax.dynamic_index_in_dim(total, (tp_index + offset) % tps, 0, keepdims=False)
            got = lax.ppermute(sent.astype(BF16), "tp", [(i, (i + offset) % tps) for i in range(tps)])
            result += got.astype(F32)
        results.append(result.astype(BF16))
    return jnp.concatenate(results, axis=0)


def solution(mesh):
    return jax.shard_map(
        body,
        mesh=mesh,
        in_specs=(
            P("sec", ("rep", "patch"), None),
            P("sec", None, None),
            P("sec", None),
            P("sec", "patch", "tp"),
            P("sec", ("rep", "patch"), "tp"),
            P("sec", "tp", "patch"),
            P(("rep", "patch"), None),
        ),
        out_specs=P(("rep", "patch"), ("tp", "sec")),
        check_vma=False,
    )
```

```python
import functools
import math

import jax
import jax.numpy as jnp
from jax import lax
from jax.experimental import pallas as pl
from jax.experimental.pallas import tpu as pltpu
from jax.sharding import PartitionSpec as P

HEAD_DIM = 128
BLOCK = 128
QUERY_TILE = 512
ROW_CHUNKS = 2
VMEM_LIMIT = 48 * 1024 * 1024
F32 = jnp.float32
BF16 = jnp.bfloat16


def after(value, *others):
    return lax.optimization_barrier((value,) + others)[0]


def params():
    return pltpu.CompilerParams(vmem_limit_bytes=VMEM_LIMIT)


def cost(flops, moved, exps=0):
    return pl.CostEstimate(flops=int(flops), bytes_accessed=int(moved), transcendentals=int(exps))


def unit(value):
    return value * lax.rsqrt(jnp.mean(value * value, axis=-1, keepdims=True) + 1e-06)


def stale_kernel(in_ref, out_ref):
    out_ref[:, :HEAD_DIM] = unit(in_ref[:, :HEAD_DIM].astype(F32)).astype(BF16)
    out_ref[:, HEAD_DIM:] = in_ref[:, HEAD_DIM:]


def stale_group(stale, first, heads):
    rows = stale.shape[0]
    return pl.pallas_call(
        stale_kernel,
        grid=(heads,),
        in_specs=[pl.BlockSpec((rows, 2 * HEAD_DIM), lambda h: (0, first + h))],
        out_specs=pl.BlockSpec((rows, 2 * HEAD_DIM), lambda h: (0, h)),
        out_shape=jax.ShapeDtypeStruct((rows, heads * 2 * HEAD_DIM), BF16),
        compiler_params=params(),
        cost_estimate=cost(rows * heads * 512, rows * heads * 1024),
    )(stale)


def project_kernel(terms, has_acc, last, *refs):
    lefts, rights = refs[:terms], refs[terms : 2 * terms]
    outs = refs[2 * terms + has_acc :]
    total = refs[2 * terms][...] if has_acc else None
    for left, right in zip(lefts, rights):
        term = jnp.dot(left[...], right[...], preferred_element_type=F32)
        total = term if total is None else total + term
    if last:
        outs[0][...] = unit(total[:, :HEAD_DIM]).astype(BF16)
        outs[1][...] = unit(total[:, HEAD_DIM : 2 * HEAD_DIM]).astype(BF16)
        outs[2][...] = total[:, 2 * HEAD_DIM :].astype(BF16)
    else:
        outs[0][...] = total


def project(acc, terms, heads, first=0, last=False):
    lefts, rights = [left for left, _ in terms], [right for _, right in terms]
    width = 3 * HEAD_DIM
    rows = lefts[0].shape[0]
    depth = sum(left.shape[1] for left in lefts)
    tile = pl.BlockSpec((rows, width), lambda h: (0, h))
    if last:
        out_specs = [pl.BlockSpec((rows, HEAD_DIM), lambda h: (0, h))] * 3
        out_shape = [jax.ShapeDtypeStruct((rows, heads * HEAD_DIM), BF16)] * 3
    else:
        out_specs, out_shape = tile, jax.ShapeDtypeStruct((rows, heads * width), F32)
    has_acc = acc is not None
    return pl.pallas_call(
        functools.partial(project_kernel, len(terms), has_acc, last),
        grid=(heads,),
        in_specs=[pl.BlockSpec(left.shape, lambda h: (0, 0)) for left in lefts]
        + [pl.BlockSpec((right.shape[0], width), lambda h: (0, first + h)) for right in rights]
        + [tile] * has_acc,
        out_specs=out_specs,
        out_shape=out_shape,
        compiler_params=params(),
        cost_estimate=cost(2 * rows * depth * heads * width, rows * heads * width * 6 + depth * (rows + heads * width) * 2),
    )(*lefts, *rights, *([acc] if has_acc else []))


def weigh(query, key, mask):
    tile, keys = query.shape[0], key.shape[0]
    scores = lax.dot_general(query, key, (((1,), (1,)), ((), ())), preferred_element_type=F32)
    exponents = jnp.exp(scores * (1.0 / math.sqrt(HEAD_DIM)))
    exponents = exponents.reshape(tile // BLOCK, BLOCK, keys) * mask
    return exponents.reshape(tile, keys).astype(BF16)


def with_ones(value):
    return jnp.concatenate([value, jnp.ones(value.shape, value.dtype)], axis=1)


def window_kernel(fresh, sides, prior, flag_ref, q_ref, *refs):
    num_ref, tot_ref = refs[-2:]
    query = q_ref[...]
    shape = (query.shape[0], 2 * HEAD_DIM)

    def terms(first, windows):
        both = jnp.zeros(shape, F32)
        for at in range(first, first + windows):
            k_ref, v_ref, m_ref = refs[3 * at : 3 * at + 3]
            weights = weigh(query, k_ref[...], m_ref[...])
            both += jnp.dot(weights, with_ones(v_ref[...]), preferred_element_type=F32)
        return both[:, :HEAD_DIM], both[:, HEAD_DIM:]

    if prior:
        num, tot = refs[3 * (fresh + sides)][...], refs[3 * (fresh + sides) + 1][...]
    if fresh:
        num, tot = terms(0, fresh)
    num_ref[...] = num
    tot_ref[...] = tot
    if sides:

        @pl.when(flag_ref[0] == 1)
        def _():
            more, more_tot = terms(fresh, sides)
            num_ref[...] += more
            tot_ref[...] += more_tot


def windows(flag, queries, fresh, sides, prior):
    rows, cols = queries.shape
    heads = cols // HEAD_DIM
    tile = pl.BlockSpec((QUERY_TILE, HEAD_DIM), lambda h, i, f: (i, h))
    specs, values = [], []
    for keys, vals, mask in fresh:
        block = pl.BlockSpec((keys.shape[0], HEAD_DIM), lambda h, i, f: (0, h))
        specs += [block, block]
        values += [keys, vals, mask]
        specs.append(pl.BlockSpec((QUERY_TILE // BLOCK, 1, keys.shape[0]), lambda h, i, f: (i, 0, 0)))
    for stale, mask in sides:
        specs.append(pl.BlockSpec((stale.shape[0], HEAD_DIM), lambda h, i, f: (0, 2 * h)))
        specs.append(pl.BlockSpec((stale.shape[0], HEAD_DIM), lambda h, i, f: (0, 2 * h + 1)))
        specs.append(pl.BlockSpec((QUERY_TILE // BLOCK, 1, stale.shape[0]), lambda h, i, f: (i, 0, 0)))
        values += [stale, stale, mask]
    count = len(fresh) + len(sides)
    return pl.pallas_call(
        functools.partial(window_kernel, len(fresh), len(sides), len(prior)),
        grid_spec=pltpu.PrefetchScalarGridSpec(
            num_scalar_prefetch=1,
            grid=(heads, rows // QUERY_TILE),
            in_specs=[tile] + specs + [tile] * len(prior),
            out_specs=[tile, tile],
        ),
        out_shape=[jax.ShapeDtypeStruct((rows, cols), F32)] * 2,
        compiler_params=params(),
        cost_estimate=cost(6 * count * rows * rows * cols, rows * cols * 14 * count, count * rows * rows * heads),
    )(flag, queries, *values, *prior)


def foreign_kernel(flag_ref, q_ref, k_ref, v_ref, mask_ref, num_ref, tot_ref):
    head = pl.program_id(1)

    @pl.when(head == 0)
    def _():
        tot_ref[...] = jnp.zeros_like(tot_ref)

    @pl.when(flag_ref[0] == 1)
    def _():
        value = v_ref[...]
        weights = weigh(q_ref[...], k_ref[...], mask_ref[...])
        num_ref[...] = jnp.dot(weights, value, preferred_element_type=F32).astype(BF16)
        sums = lax.dot_general(
            jnp.ones((8, weights.shape[1]), BF16), weights, (((1,), (1,)), ((), ())), preferred_element_type=F32
        )
        row = lax.broadcasted_iota(jnp.int32, sums.shape, 0)
        tot_ref[...] = jnp.where(row == head, sums, tot_ref[...])

    @pl.when(flag_ref[0] != 1)
    def _():
        num_ref[...] = jnp.zeros_like(num_ref)


def foreign_part(flag, queries, stale, mask):
    rows, cols = queries.shape
    heads, window = cols // HEAD_DIM, stale.shape[0]
    tile = pl.BlockSpec((QUERY_TILE, HEAD_DIM), lambda i, h, f: (i, h))
    return pl.pallas_call(
        foreign_kernel,
        grid_spec=pltpu.PrefetchScalarGridSpec(
            num_scalar_prefetch=1,
            grid=(rows // QUERY_TILE, heads),
            in_specs=[
                tile,
                pl.BlockSpec((window, HEAD_DIM), lambda i, h, f: (0, 2 * h)),
                pl.BlockSpec((window, HEAD_DIM), lambda i, h, f: (0, 2 * h + 1)),
                pl.BlockSpec((QUERY_TILE // BLOCK, 1, window), lambda i, h, f: (i, 0, 0)),
            ],
            out_specs=[tile, pl.BlockSpec((8, QUERY_TILE), lambda i, h, f: (0, i))],
        ),
        out_shape=[jax.ShapeDtypeStruct((rows, cols), BF16), jax.ShapeDtypeStruct((8, rows), F32)],
        compiler_params=params(),
        cost_estimate=cost(4 * rows * window * cols, rows * cols * 8, rows * window * heads),
    )(flag, queries, stale, stale, mask)


def branch_kernel(groups, blocks, secs, where_ref, w_ref, gate_ref, hidden_ref, *refs):
    send_refs, keep_ref = refs[4 * groups : -1], refs[-1]
    sec, main = where_ref[0], where_ref[1].astype(F32)
    parts = []
    for group in range(groups):
        num_ref, tot_ref, far_ref, far_tot_ref = refs[4 * group : 4 * group + 4]
        far_tot = jnp.transpose(far_tot_ref[...])
        for head in range(num_ref.shape[1] // HEAD_DIM):
            cols = slice(head * HEAD_DIM, (head + 1) * HEAD_DIM)
            total = tot_ref[:, cols] + far_tot[:, head : head + 1]
            parts.append(((num_ref[:, cols] + far_ref[:, cols].astype(F32)) / total).astype(BF16))
    attended = jnp.concatenate(parts, axis=1)
    width = keep_ref.shape[2]
    for offset in range(secs):
        out_ref = keep_ref if offset == 0 else send_refs[offset - 1]
        for block in range(blocks):
            place = block * secs + lax.rem(sec + offset, secs)
            cols = pl.ds(pl.multiple_of(place * width, HEAD_DIM), width)
            term = jnp.dot(attended, w_ref[:, cols], preferred_element_type=F32) * gate_ref[:, cols]
            out_ref[block] = (term + main * hidden_ref[:, cols].astype(F32)).astype(BF16)


def branch(where, w_full, gate, hidden, groups, first, count, blocks, secs):
    model_width = hidden.shape[1]
    width = model_width // (blocks * secs)
    tile = min(128, count)
    start = first // tile
    specs, values = [], []
    for num, tot, far, far_tot in groups:
        spec = pl.BlockSpec((tile, num.shape[1]), lambda i, w: (start + i, 0))
        specs += [spec, spec, spec, pl.BlockSpec((8, tile), lambda i, w: (0, start + i))]
        values += [num, tot, far, far_tot]
    out = pl.BlockSpec((blocks, tile, width), lambda i, w: (0, i, 0))
    shape = jax.ShapeDtypeStruct((blocks, count, width), BF16)
    results = pl.pallas_call(
        functools.partial(branch_kernel, len(groups), blocks, secs),
        grid_spec=pltpu.PrefetchScalarGridSpec(
            num_scalar_prefetch=1,
            grid=(count // tile,),
            in_specs=[
                pl.BlockSpec(w_full.shape, lambda i, w: (0, 0)),
                pl.BlockSpec(gate.shape, lambda i, w: (0, 0)),
                pl.BlockSpec((tile, model_width), lambda i, w: (start + i, 0)),
            ]
            + specs,
            out_specs=[out] * secs,
        ),
        out_shape=[shape] * secs,
        compiler_params=params(),
        cost_estimate=cost(2 * count * w_full.size, w_full.size * 2 + count * model_width * 4),
    )(where, w_full, gate, hidden, *values)
    return results[-1], results[:-1]


def chosen(place, values):
    out = values[0]
    for at in range(1, len(values)):
        if values[at] is not values[0]:
            out = jnp.where(place == at, values[at], out)
    return out


class Relay:
    def __init__(self, own, count, reps):
        self.count, self.reps = count, reps
        self.place, self.rank = lax.axis_index("patch"), lax.axis_index("rep")
        self.ahead, self.back = {0: own}, {0: own}

    def step(self, k, *held):
        count = self.count
        ahead, back = self.ahead[k - 1], self.back[k - 1]
        if held:
            ahead, back = after(ahead, *held), after(back, *held)
        self.ahead[k] = lax.ppermute(ahead, "patch", [(i, i + 1) for i in range(k - 1, count - 1)])
        self.back[k] = lax.ppermute(back, "patch", [(i + 1, i) for i in range(count - k)])

    def sent(self, k):
        return self.ahead[k], self.back[k]

    def brought(self, t):
        values, owners = [], []
        for at in range(self.count):
            comes = sorted([(k, 0) for k in range(1, at + 1)] + [(k, 1) for k in range(1, self.count - at)])
            k, side = comes[t - 1]
            values.append(self.back[k] if side else self.ahead[k])
            owners.append(at + k if side else at - k)
        owner = sum(jnp.where(self.place == at, owners[at], 0) for at in range(self.count))
        mine = chosen(self.place, values)
        parts = [(self.rank, mine)]
        for offset in range(1, self.reps):
            pairs = [(a, (a + offset) % self.reps) for a in range(self.reps)]
            parts.append(((self.rank - offset) % self.reps, lax.ppermute(mine, "rep", pairs)))
        return owner, parts


def body(hidden, modulation, gate, w_qkv, stale_kv, w_out, key_lists):
    count, reps = lax.axis_size("patch"), lax.axis_size("rep")
    tps, secs = lax.axis_size("tp"), lax.axis_size("sec")
    place, rank = lax.axis_index("patch"), lax.axis_index("rep")
    tp_index, sec_index = lax.axis_index("tp"), lax.axis_index("sec")
    rows, model_width = hidden.shape[1], hidden.shape[2]
    heads = w_out.shape[1] // HEAD_DIM
    patch_blocks = rows // BLOCK
    first_heads = -(-2 * heads // 3)
    group_heads = [first_heads, heads - first_heads]
    group_first = [0, first_heads]
    states = hidden[0]
    w_qkv, stale_kv, w_out = w_qkv[0], stale_kv[0], w_out[0]

    shard_rows = w_qkv.shape[0]
    depth = shard_rows // reps
    out_depth = w_out.shape[0] // reps
    relays, brought = [], []
    held = ()
    for group in range(3):
        source = after(w_qkv if group < 2 else w_out, *held) if held else w_qkv
        if group < 2:
            width = 3 * HEAD_DIM
            at = (rank * depth, group_first[group] * width)
            own = lax.dynamic_slice(source, at, (depth, group_heads[group] * width))
        else:
            own = lax.dynamic_slice(source, (rank * out_depth, 0), (out_depth, w_out.shape[1]))
        relay = Relay(own, count, reps)
        for k in range(1, count):
            relay.step(k)
        relays.append(relay)
        brought.append([relay.brought(t) for t in range(1, count)])
        held = relay.sent(count - 1)
    large, small, out_relay = relays

    relative = jnp.where(key_lists >= 0, key_lists - (place - 1) * patch_blocks, -1)
    window_ids = jnp.arange(3 * patch_blocks, dtype=jnp.int32)
    hits = jnp.any(relative[:, :, None] == window_ids[None, None, :], axis=1).astype(F32)
    hits = jnp.repeat(hits, BLOCK, axis=1).reshape(patch_blocks, 3, rows)
    before, fresh, behind = (hits[:, i][:, None, :] for i in range(3))
    odd = place % 2 == 1
    even_mask, odd_mask = jnp.where(odd, before, behind), jnp.where(odd, behind, before)
    at_end = (place == 0) | (place == count - 1)
    to_inner = [(0, 1), (count - 1, count - 2)]
    to_end = [(1, 0), (count - 2, count - 1)]
    far_mask = lax.ppermute(after(jnp.where(place == 0, behind, before), *large.sent(1)), "patch", to_inner)
    inner_flag = jnp.where(at_end, 0, 1).astype(jnp.int32).reshape(1)
    host_flag = ((place == 1) | (place == count - 2)).astype(jnp.int32).reshape(1)

    inner = range(1, count - 1)
    pairs = [(i, i + 1) for i in range(count - 1)] + [(i + 1, i) for i in range(count - 1)]
    even_pairs = [(a, b) for a, b in pairs if min(a, b) % 2 == 0 and b in inner]
    odd_pairs = [(a, b) for a, b in pairs if min(a, b) % 2 == 1 and b in inner]
    stale = [stale_group(stale_kv, group_first[g], group_heads[g]) for g in range(2)]
    even_large = lax.ppermute(after(stale[0], *large.sent(1)), "patch", even_pairs)
    odd_small = lax.ppermute(after(stale[1], *large.sent(min(2, count - 1))), "patch", odd_pairs)
    even_small = lax.ppermute(after(stale[1], *small.sent(1), even_large), "patch", even_pairs)
    odd_large = lax.ppermute(after(stale[0], *small.sent(min(2, count - 1)), odd_small), "patch", odd_pairs)
    sides = [[(even_large, even_mask), (odd_large, odd_mask)], [(even_small, even_mask), (odd_small, odd_mask)]]

    inputs = states.astype(F32)
    centered = inputs - jnp.mean(inputs, axis=-1, keepdims=True)
    variance = jnp.mean(centered * centered, axis=-1, keepdims=True)
    normed = centered * lax.rsqrt(variance + 1e-06)
    modulated = (normed * (1.0 + modulation[0, 1]) + modulation[0, 0]).astype(BF16)

    def columns(owner, part):
        return lax.dynamic_slice_in_dim(modulated, owner * shard_rows + part * depth, depth, 1)

    own_columns = lax.dynamic_slice_in_dim(modulated, place * shard_rows, shard_rows, 1)
    projected = []
    for g in range(2):
        acc = project(
            None, [(after(own_columns, *relays[g].sent(1)), w_qkv)], group_heads[g], group_first[g]
        )
        waiting = []
        for owner, parts in brought[g]:
            terms = [(columns(owner, part), piece) for part, piece in parts]
            acc = project(acc, waiting + terms[:1], group_heads[g])
            waiting = terms[1:]
        if not waiting:
            waiting = [(jnp.zeros((rows, depth), BF16), jnp.zeros((depth, acc.shape[1]), BF16))]
        projected.append(project(acc, waiting, group_heads[g], last=True))

    w_full = lax.dynamic_update_slice(
        jnp.zeros((w_out.shape[0], model_width), BF16), w_out, (0, place * w_out.shape[1])
    )
    for owner, parts in brought[2]:
        for part, piece in parts:
            w_full = lax.dynamic_update_slice(w_full, piece, (part * out_depth, owner * w_out.shape[1]))

    groups = []
    for g in range(2):
        queries, keys, values = projected[g]
        far_queries = lax.ppermute(queries, "patch", to_inner)
        far_num, far_tot = foreign_part(host_flag, far_queries, stale[g], far_mask)
        far_num = lax.ppermute(far_num, "patch", to_end)
        far_tot = lax.ppermute(far_tot, "patch", to_end)
        if g == 0:
            near = windows(inner_flag, queries, [(keys, values, fresh)], sides[g][:1], ())
            num, tot = windows(inner_flag, queries, [], sides[g][1:], tuple(near))
        else:
            num, tot = windows(inner_flag, queries, [(keys, values, fresh)], sides[g], ())
        groups.append((num, tot, far_num, far_tot))

    where = jnp.stack([sec_index, ((sec_index == 1) & (tp_index == 0)).astype(jnp.int32)]).astype(jnp.int32)
    chunk = rows // ROW_CHUNKS
    results = []
    for at in range(ROW_CHUNKS):
        keep, sends = branch(where, w_full, gate, states, groups, at * chunk, chunk, tps, secs)
        total = keep.astype(F32)
        for offset, sent in enumerate(sends, 1):
            got = lax.ppermute(sent, "sec", [(i, (i + offset) % secs) for i in range(secs)])
            total += got.astype(F32)
        result = lax.dynamic_index_in_dim(total, tp_index, 0, keepdims=False)
        for offset in range(1, tps):
            sent = lax.dynamic_index_in_dim(total, (tp_index + offset) % tps, 0, keepdims=False)
            got = lax.ppermute(sent.astype(BF16), "tp", [(i, (i + offset) % tps) for i in range(tps)])
            result += got.astype(F32)
        results.append(result.astype(BF16))
    return jnp.concatenate(results, axis=0)


def solution(mesh):
    return jax.shard_map(
        body,
        mesh=mesh,
        in_specs=(
            P("sec", ("rep", "patch"), None),
            P("sec", None, None),
            P("sec", None),
            P("sec", "patch", "tp"),
            P("sec", ("rep", "patch"), "tp"),
            P("sec", "tp", "patch"),
            P(("rep", "patch"), None),
        ),
        out_specs=P(("rep", "patch"), ("tp", "sec")),
        check_vma=False,
    )
```

```python
import functools
import math

import jax
import jax.numpy as jnp
from jax import lax
from jax.experimental import pallas as pl
from jax.experimental.pallas import tpu as pltpu
from jax.sharding import PartitionSpec as P

HEAD_DIM = 128
BLOCK = 128
QUERY_TILE = 512
ROW_CHUNKS = 2
VMEM_LIMIT = 48 * 1024 * 1024
F32 = jnp.float32
BF16 = jnp.bfloat16


def after(value, *others):
    return lax.optimization_barrier((value,) + others)[0]


def params():
    return pltpu.CompilerParams(vmem_limit_bytes=VMEM_LIMIT)


def cost(flops, moved, exps=0):
    return pl.CostEstimate(flops=int(flops), bytes_accessed=int(moved), transcendentals=int(exps))


def unit(value):
    return value * lax.rsqrt(jnp.mean(value * value, axis=-1, keepdims=True) + 1e-06)


def stale_kernel(in_ref, out_ref):
    out_ref[:, :HEAD_DIM] = unit(in_ref[:, :HEAD_DIM].astype(F32)).astype(BF16)
    out_ref[:, HEAD_DIM:] = in_ref[:, HEAD_DIM:]


def stale_group(stale, first, heads):
    rows = stale.shape[0]
    return pl.pallas_call(
        stale_kernel,
        grid=(heads,),
        in_specs=[pl.BlockSpec((rows, 2 * HEAD_DIM), lambda h: (0, first + h))],
        out_specs=pl.BlockSpec((rows, 2 * HEAD_DIM), lambda h: (0, h)),
        out_shape=jax.ShapeDtypeStruct((rows, heads * 2 * HEAD_DIM), BF16),
        compiler_params=params(),
        cost_estimate=cost(rows * heads * 512, rows * heads * 1024),
    )(stale)


def project_kernel(terms, has_acc, last, *refs):
    lefts, rights = refs[:terms], refs[terms : 2 * terms]
    outs = refs[2 * terms + has_acc :]
    total = refs[2 * terms][...] if has_acc else None
    for left, right in zip(lefts, rights):
        term = jnp.dot(left[...], right[...], preferred_element_type=F32)
        total = term if total is None else total + term
    if last:
        outs[0][...] = unit(total[:, :HEAD_DIM]).astype(BF16)
        outs[1][...] = unit(total[:, HEAD_DIM : 2 * HEAD_DIM]).astype(BF16)
        outs[2][...] = total[:, 2 * HEAD_DIM :].astype(BF16)
    else:
        outs[0][...] = total


def project(acc, terms, heads, first=0, last=False):
    lefts, rights = [left for left, _ in terms], [right for _, right in terms]
    width = 3 * HEAD_DIM
    rows = lefts[0].shape[0]
    depth = sum(left.shape[1] for left in lefts)
    tile = pl.BlockSpec((rows, width), lambda h: (0, h))
    if last:
        out_specs = [pl.BlockSpec((rows, HEAD_DIM), lambda h: (0, h))] * 3
        out_shape = [jax.ShapeDtypeStruct((rows, heads * HEAD_DIM), BF16)] * 3
    else:
        out_specs, out_shape = tile, jax.ShapeDtypeStruct((rows, heads * width), F32)
    has_acc = acc is not None
    return pl.pallas_call(
        functools.partial(project_kernel, len(terms), has_acc, last),
        grid=(heads,),
        in_specs=[pl.BlockSpec(left.shape, lambda h: (0, 0)) for left in lefts]
        + [pl.BlockSpec((right.shape[0], width), lambda h: (0, first + h)) for right in rights]
        + [tile] * has_acc,
        out_specs=out_specs,
        out_shape=out_shape,
        compiler_params=params(),
        cost_estimate=cost(2 * rows * depth * heads * width, rows * heads * width * 6 + depth * (rows + heads * width) * 2),
    )(*lefts, *rights, *([acc] if has_acc else []))


def weigh(query, key, mask):
    tile, keys = query.shape[0], key.shape[0]
    scores = lax.dot_general(query, key, (((1,), (1,)), ((), ())), preferred_element_type=F32)
    exponents = jnp.exp(scores * (1.0 / math.sqrt(HEAD_DIM)))
    exponents = exponents.reshape(tile // BLOCK, BLOCK, keys) * mask
    return exponents.reshape(tile, keys).astype(BF16)


def with_ones(value):
    return jnp.concatenate([value, jnp.ones(value.shape, value.dtype)], axis=1)


def window_kernel(fresh, sides, prior, flag_ref, q_ref, *refs):
    num_ref, tot_ref = refs[-2:]
    query = q_ref[...]
    shape = (query.shape[0], 2 * HEAD_DIM)

    def terms(first, windows):
        both = jnp.zeros(shape, F32)
        for at in range(first, first + windows):
            k_ref, v_ref, m_ref = refs[3 * at : 3 * at + 3]
            weights = weigh(query, k_ref[...], m_ref[...])
            both += jnp.dot(weights, with_ones(v_ref[...]), preferred_element_type=F32)
        return both[:, :HEAD_DIM], both[:, HEAD_DIM:]

    if prior:
        num, tot = refs[3 * (fresh + sides)][...], refs[3 * (fresh + sides) + 1][...]
    if fresh:
        num, tot = terms(0, fresh)
    num_ref[...] = num
    tot_ref[...] = tot
    if sides:

        @pl.when(flag_ref[0] == 1)
        def _():
            more, more_tot = terms(fresh, sides)
            num_ref[...] += more
            tot_ref[...] += more_tot


def windows(flag, queries, here, fresh, sides, prior):
    first, heads = here
    rows, cols = queries.shape[0], heads * HEAD_DIM
    query = pl.BlockSpec((QUERY_TILE, HEAD_DIM), lambda h, i, f: (i, first + h))
    tile = pl.BlockSpec((QUERY_TILE, HEAD_DIM), lambda h, i, f: (i, h))
    specs, values = [], []
    for keys, vals, mask in fresh:
        block = pl.BlockSpec((keys.shape[0], HEAD_DIM), lambda h, i, f: (0, first + h))
        specs += [block, block]
        values += [keys, vals, mask]
        specs.append(pl.BlockSpec((QUERY_TILE // BLOCK, 1, keys.shape[0]), lambda h, i, f: (i, 0, 0)))
    for stale, mask in sides:
        specs.append(pl.BlockSpec((stale.shape[0], HEAD_DIM), lambda h, i, f: (0, 2 * h)))
        specs.append(pl.BlockSpec((stale.shape[0], HEAD_DIM), lambda h, i, f: (0, 2 * h + 1)))
        specs.append(pl.BlockSpec((QUERY_TILE // BLOCK, 1, stale.shape[0]), lambda h, i, f: (i, 0, 0)))
        values += [stale, stale, mask]
    count = len(fresh) + len(sides)
    return pl.pallas_call(
        functools.partial(window_kernel, len(fresh), len(sides), len(prior)),
        grid_spec=pltpu.PrefetchScalarGridSpec(
            num_scalar_prefetch=1,
            grid=(heads, rows // QUERY_TILE),
            in_specs=[query] + specs + [tile] * len(prior),
            out_specs=[tile, tile],
        ),
        out_shape=[jax.ShapeDtypeStruct((rows, cols), F32)] * 2,
        compiler_params=params(),
        cost_estimate=cost(6 * count * rows * rows * cols, rows * cols * 14 * count, count * rows * rows * heads),
    )(flag, queries, *values, *prior)


def foreign_kernel(flag_ref, q_ref, k_ref, v_ref, mask_ref, num_ref, tot_ref):
    head = pl.program_id(1)

    @pl.when(head == 0)
    def _():
        tot_ref[...] = jnp.zeros_like(tot_ref)

    @pl.when(flag_ref[0] == 1)
    def _():
        value = v_ref[...]
        weights = weigh(q_ref[...], k_ref[...], mask_ref[...])
        num_ref[...] = jnp.dot(weights, value, preferred_element_type=F32).astype(BF16)
        sums = lax.dot_general(
            jnp.ones((8, weights.shape[1]), BF16), weights, (((1,), (1,)), ((), ())), preferred_element_type=F32
        )
        row = lax.broadcasted_iota(jnp.int32, sums.shape, 0)
        tot_ref[...] = jnp.where(row == head, sums, tot_ref[...])

    @pl.when(flag_ref[0] != 1)
    def _():
        num_ref[...] = jnp.zeros_like(num_ref)


def foreign_part(flag, queries, first, heads, stale, mask):
    rows, cols, window = queries.shape[0], heads * HEAD_DIM, stale.shape[0]
    query = pl.BlockSpec((QUERY_TILE, HEAD_DIM), lambda i, h, f: (i, first + h))
    tile = pl.BlockSpec((QUERY_TILE, HEAD_DIM), lambda i, h, f: (i, h))
    return pl.pallas_call(
        foreign_kernel,
        grid_spec=pltpu.PrefetchScalarGridSpec(
            num_scalar_prefetch=1,
            grid=(rows // QUERY_TILE, heads),
            in_specs=[
                query,
                pl.BlockSpec((window, HEAD_DIM), lambda i, h, f: (0, 2 * h)),
                pl.BlockSpec((window, HEAD_DIM), lambda i, h, f: (0, 2 * h + 1)),
                pl.BlockSpec((QUERY_TILE // BLOCK, 1, window), lambda i, h, f: (i, 0, 0)),
            ],
            out_specs=[tile, pl.BlockSpec((8, QUERY_TILE), lambda i, h, f: (0, i))],
        ),
        out_shape=[jax.ShapeDtypeStruct((rows, cols), BF16), jax.ShapeDtypeStruct((8, rows), F32)],
        compiler_params=params(),
        cost_estimate=cost(4 * rows * window * cols, rows * cols * 8, rows * window * heads),
    )(flag, queries, stale, stale, mask)


def branch_kernel(groups, blocks, secs, where_ref, w_ref, gate_ref, hidden_ref, *refs):
    send_refs, keep_ref = refs[4 * groups : -1], refs[-1]
    sec, main = where_ref[0], where_ref[1].astype(F32)
    parts = []
    for group in range(groups):
        num_ref, tot_ref, far_ref, far_tot_ref = refs[4 * group : 4 * group + 4]
        far_tot = jnp.transpose(far_tot_ref[...])
        for head in range(num_ref.shape[1] // HEAD_DIM):
            cols = slice(head * HEAD_DIM, (head + 1) * HEAD_DIM)
            total = tot_ref[:, cols] + far_tot[:, head : head + 1]
            parts.append(((num_ref[:, cols] + far_ref[:, cols].astype(F32)) / total).astype(BF16))
    attended = jnp.concatenate(parts, axis=1)
    width = keep_ref.shape[2]
    for offset in range(secs):
        out_ref = keep_ref if offset == 0 else send_refs[offset - 1]
        for block in range(blocks):
            place = block * secs + lax.rem(sec + offset, secs)
            cols = pl.ds(pl.multiple_of(place * width, HEAD_DIM), width)
            term = jnp.dot(attended, w_ref[:, cols], preferred_element_type=F32) * gate_ref[:, cols]
            out_ref[block] = (term + main * hidden_ref[:, cols].astype(F32)).astype(BF16)


def branch(where, w_full, gate, hidden, groups, first, count, blocks, secs):
    model_width = hidden.shape[1]
    width = model_width // (blocks * secs)
    tile = min(128, count)
    start = first // tile
    specs, values = [], []
    for num, tot, far, far_tot in groups:
        spec = pl.BlockSpec((tile, num.shape[1]), lambda i, w: (start + i, 0))
        specs += [spec, spec, spec, pl.BlockSpec((8, tile), lambda i, w: (0, start + i))]
        values += [num, tot, far, far_tot]
    out = pl.BlockSpec((blocks, tile, width), lambda i, w: (0, i, 0))
    shape = jax.ShapeDtypeStruct((blocks, count, width), BF16)
    results = pl.pallas_call(
        functools.partial(branch_kernel, len(groups), blocks, secs),
        grid_spec=pltpu.PrefetchScalarGridSpec(
            num_scalar_prefetch=1,
            grid=(count // tile,),
            in_specs=[
                pl.BlockSpec(w_full.shape, lambda i, w: (0, 0)),
                pl.BlockSpec(gate.shape, lambda i, w: (0, 0)),
                pl.BlockSpec((tile, model_width), lambda i, w: (start + i, 0)),
            ]
            + specs,
            out_specs=[out] * secs,
        ),
        out_shape=[shape] * secs,
        compiler_params=params(),
        cost_estimate=cost(2 * count * w_full.size, w_full.size * 2 + count * model_width * 4),
    )(where, w_full, gate, hidden, *values)
    return results[-1], results[:-1]


def chosen(place, values):
    out = values[0]
    for at in range(1, len(values)):
        if values[at] is not values[0]:
            out = jnp.where(place == at, values[at], out)
    return out


class Relay:
    def __init__(self, own, count, reps):
        self.count, self.reps = count, reps
        self.place, self.rank = lax.axis_index("patch"), lax.axis_index("rep")
        self.ahead, self.back = {0: own}, {0: own}

    def step(self, k, *held):
        count = self.count
        ahead, back = self.ahead[k - 1], self.back[k - 1]
        if held:
            ahead, back = after(ahead, *held), after(back, *held)
        self.ahead[k] = lax.ppermute(ahead, "patch", [(i, i + 1) for i in range(k - 1, count - 1)])
        self.back[k] = lax.ppermute(back, "patch", [(i + 1, i) for i in range(count - k)])

    def sent(self, k):
        return self.ahead[k], self.back[k]

    def brought(self, t):
        values, owners = [], []
        for at in range(self.count):
            comes = sorted([(k, 0) for k in range(1, at + 1)] + [(k, 1) for k in range(1, self.count - at)])
            k, side = comes[t - 1]
            values.append(self.back[k] if side else self.ahead[k])
            owners.append(at + k if side else at - k)
        owner = sum(jnp.where(self.place == at, owners[at], 0) for at in range(self.count))
        mine = chosen(self.place, values)
        parts = [(self.rank, mine)]
        for offset in range(1, self.reps):
            pairs = [(a, (a + offset) % self.reps) for a in range(self.reps)]
            parts.append(((self.rank - offset) % self.reps, lax.ppermute(mine, "rep", pairs)))
        return owner, parts


def body(hidden, modulation, gate, w_qkv, stale_kv, w_out, key_lists):
    count, reps = lax.axis_size("patch"), lax.axis_size("rep")
    tps, secs = lax.axis_size("tp"), lax.axis_size("sec")
    place, rank = lax.axis_index("patch"), lax.axis_index("rep")
    tp_index, sec_index = lax.axis_index("tp"), lax.axis_index("sec")
    rows, model_width = hidden.shape[1], hidden.shape[2]
    heads = w_out.shape[1] // HEAD_DIM
    patch_blocks = rows // BLOCK
    unit_heads = heads // 3 if heads % 3 == 0 else 1
    units = heads // unit_heads
    small_units = max(1, units // 3)
    group_units = [list(range(units - small_units)), list(range(units - small_units, units))]
    group_heads = [len(members) * unit_heads for members in group_units]
    group_first = [0, group_heads[0]]
    states = hidden[0]
    w_qkv, stale_kv, w_out = w_qkv[0], stale_kv[0], w_out[0]
    last = count - 1
    shard_rows = w_qkv.shape[0]
    depth, out_depth = shard_rows // reps, w_out.shape[0] // reps
    width = 3 * HEAD_DIM

    relative = jnp.where(key_lists >= 0, key_lists - (place - 1) * patch_blocks, -1)
    window_ids = jnp.arange(3 * patch_blocks, dtype=jnp.int32)
    hits = jnp.any(relative[:, :, None] == window_ids[None, None, :], axis=1).astype(F32)
    hits = jnp.repeat(hits, BLOCK, axis=1).reshape(patch_blocks, 3, rows)
    before, fresh, behind = (hits[:, i][:, None, :] for i in range(3))
    odd = place % 2 == 1
    even_mask, odd_mask = jnp.where(odd, before, behind), jnp.where(odd, behind, before)
    at_end = (place == 0) | (place == last)
    to_inner = [(0, 1), (last, last - 1)]
    to_end = [(1, 0), (last - 1, last)]
    inner_flag = jnp.where(at_end, 0, 1).astype(jnp.int32).reshape(1)
    host_flag = ((place == 1) | (place == last - 1)).astype(jnp.int32).reshape(1)

    inner = range(1, last)
    pairs = [(i, i + 1) for i in range(last)] + [(i + 1, i) for i in range(last)]
    even_pairs = [(a, b) for a, b in pairs if min(a, b) % 2 == 0 and b in inner]
    odd_pairs = [(a, b) for a, b in pairs if min(a, b) % 2 == 1 and b in inner]
    stale, even, other = [None] * units, [None] * units, [None] * units

    def send_even(unit, *held):
        even[unit] = lax.ppermute(after(stale[unit], *held), "patch", even_pairs)

    def send_other(unit, *held):
        other[unit] = lax.ppermute(after(stale[unit], *held), "patch", odd_pairs)

    def qkv_relay(group, *held):
        source = after(w_qkv, *held) if held else w_qkv
        at = (rank * depth, group_first[group] * width)
        return Relay(lax.dynamic_slice(source, at, (depth, group_heads[group] * width)), count, reps)

    def columns(owner, part):
        return lax.dynamic_slice_in_dim(modulated, owner * shard_rows + part * depth, depth, 1)

    large = qkv_relay(0)
    large.step(1)
    inputs = states.astype(F32)
    centered = inputs - jnp.mean(inputs, axis=-1, keepdims=True)
    variance = jnp.mean(centered * centered, axis=-1, keepdims=True)
    normed = centered * lax.rsqrt(variance + 1e-06)
    modulated = (normed * (1.0 + modulation[0, 1]) + modulation[0, 0]).astype(BF16)
    for unit in range(units):
        stale[unit] = stale_group(stale_kv, unit * unit_heads, unit_heads)
    modulated, stale[0] = lax.optimization_barrier((modulated, stale[0]))

    def terms_of(brought):
        owner, parts = brought
        return [(columns(owner, part), piece) for part, piece in parts]

    def pieces_of(brought):
        return [piece for _, piece in brought[1][1:]]

    def start_group(group, *held):
        own = lax.dynamic_slice_in_dim(after(modulated, *held), place * shard_rows, shard_rows, 1)
        return project(None, [(own, w_qkv)], group_heads[group], group_first[group])

    def end_group(acc, waiting, group):
        if not waiting:
            waiting = [(jnp.zeros((rows, depth), BF16), jnp.zeros((depth, acc.shape[1]), BF16))]
        return project(acc, waiting, group_heads[group], last=True)

    acc = None
    waiting, arrived = [], []
    for k in range(2, count + 1):
        sent = large.sent(k - 1)
        brought = large.brought(k - 1)
        held = []
        if k == 2:
            held = [modulated]
        elif k == 3:
            held = [acc, even[0]] + arrived[0]
        else:
            held = [acc] + arrived[k - 3]
        if k < count:
            large.step(k, *held)
        arrived.append(pieces_of(brought))
        if k == 2:
            send_even(0, *sent)
            acc = start_group(0, *sent)
        else:
            if k == 3 and units > 1:
                send_even(1, *sent)
                send_other(0, *sent)
        terms = terms_of(brought)
        if k <= last:
            if k > 2:
                acc = project(acc, waiting + terms[:1], group_heads[0])
                waiting = terms[1:]
            else:
                first_terms = terms
        if k == 3:
            pass
        if k == 2:
            waiting = first_terms
    final_terms = terms
    small = qkv_relay(1, *large.sent(last), acc, *arrived[-2], *[e for e in even[:2] + other[:1] if e is not None])
    small.step(1)
    sent = large.sent(last)
    if units > 2:
        send_even(2, *sent)
    acc = project(acc, waiting + final_terms[:1], group_heads[0])
    queries_0 = end_group(acc, final_terms[1:], 0)

    small_acc = start_group(1, *small.sent(1))
    waiting = []
    small_arrived = []
    for k in range(2, count + 1):
        sent = small.sent(k - 1)
        brought = small.brought(k - 1)
        if k < count:
            held = [acc] if k == 2 else [small_acc] + arrived[-1] + [e for e in even[2:3] if e is not None]
            small.step(k, *held)
        small_arrived.append(pieces_of(brought))
        terms = terms_of(brought)
        small_acc = project(small_acc, waiting + terms[:1], group_heads[1])
        waiting = terms[1:]
        if k == 3 and units > 1:
            send_other(1, *sent)
    queries_1 = end_group(small_acc, waiting, 1)
    for unit in range(units):
        if even[unit] is None:
            send_even(unit, *small.sent(last))
        if other[unit] is None:
            send_other(unit, *small.sent(last), *[o for o in other if o is not None])

    far_mask = lax.ppermute(after(jnp.where(place == 0, behind, before), *large.sent(1)), "patch", to_inner)

    def far_part(queries, group):
        far_queries = lax.ppermute(queries, "patch", to_inner)
        return far_queries

    def far_back(far_queries, group):
        parts = []
        for at, unit in enumerate(group_units[group]):
            parts.append(foreign_part(host_flag, far_queries, at * unit_heads, unit_heads, stale[unit], far_mask))
        return [(lax.ppermute(num, "patch", to_end), lax.ppermute(tot, "patch", to_end)) for num, tot in parts]

    far_queries_0 = far_part(queries_0[0], 0)
    far_queries_1 = far_part(queries_1[0], 1)
    near = [None] * units
    far = far_back(far_queries_0, 0)
    for group, (queries, keys, values) in enumerate((queries_0, queries_1)):
        for at, unit in enumerate(group_units[group]):
            sides = [(even[unit], even_mask), (other[unit], odd_mask)]
            here = (at * unit_heads, unit_heads)
            if unit == 0 or group == 1:
                near[unit] = windows(inner_flag, queries, here, [(keys, values, fresh)], sides, ())
            else:
                part = windows(inner_flag, queries, here, [(keys, values, fresh)], sides[:1], ())
                near[unit] = windows(inner_flag, queries, here, [], sides[1:], tuple(part))

    out_relay = Relay(
        lax.dynamic_slice(
            after(w_out, *small.sent(last), *small_arrived[0], *small_arrived[1], far_queries_0),
            (rank * out_depth, 0),
            (out_depth, w_out.shape[1]),
        ),
        count,
        reps,
    )
    w_full = lax.dynamic_update_slice(
        jnp.zeros((w_out.shape[0], model_width), BF16), w_out, (0, place * w_out.shape[1])
    )
    for k in range(1, count):
        held = []
        if k == 2:
            held = small_arrived[-1] + [o for o in other[1:2] if o is not None]
        if k == 3:
            held = [far_queries_1]
        out_relay.step(k, *held)
        owner, parts = out_relay.brought(k)
        for part, piece in parts:
            w_full = lax.dynamic_update_slice(w_full, piece, (part * out_depth, owner * w_out.shape[1]))
    far += far_back(far_queries_1, 1)
    groups = [tuple(near[unit]) + tuple(far[unit]) for unit in range(units)]

    where = jnp.stack([sec_index, ((sec_index == 1) & (tp_index == 0)).astype(jnp.int32)]).astype(jnp.int32)
    chunk = rows // ROW_CHUNKS
    results = []
    for at in range(ROW_CHUNKS):
        keep, sends = branch(where, w_full, gate, states, groups, at * chunk, chunk, tps, secs)
        total = keep.astype(F32)
        for offset, sent in enumerate(sends, 1):
            got = lax.ppermute(sent, "sec", [(i, (i + offset) % secs) for i in range(secs)])
            total += got.astype(F32)
        result = lax.dynamic_index_in_dim(total, tp_index, 0, keepdims=False)
        for offset in range(1, tps):
            sent = lax.dynamic_index_in_dim(total, (tp_index + offset) % tps, 0, keepdims=False)
            got = lax.ppermute(sent.astype(BF16), "tp", [(i, (i + offset) % tps) for i in range(tps)])
            result += got.astype(F32)
        results.append(result.astype(BF16))
    return jnp.concatenate(results, axis=0)


def solution(mesh):
    return jax.shard_map(
        body,
        mesh=mesh,
        in_specs=(
            P("sec", ("rep", "patch"), None),
            P("sec", None, None),
            P("sec", None),
            P("sec", "patch", "tp"),
            P("sec", ("rep", "patch"), "tp"),
            P("sec", "tp", "patch"),
            P(("rep", "patch"), None),
        ),
        out_specs=P(("rep", "patch"), ("tp", "sec")),
        check_vma=False,
    )
```

```python
import functools
import math

import jax
import jax.numpy as jnp
from jax import lax
from jax.experimental import pallas as pl
from jax.experimental.pallas import tpu as pltpu
from jax.sharding import PartitionSpec as P

HEAD_DIM = 128
BLOCK = 128
QUERY_TILE = 512
ROW_CHUNKS = 2
VMEM_LIMIT = 48 * 1024 * 1024
F32 = jnp.float32
BF16 = jnp.bfloat16


def after(value, *others):
    return lax.optimization_barrier((value,) + others)[0]


def params():
    return pltpu.CompilerParams(vmem_limit_bytes=VMEM_LIMIT)


def cost(flops, moved, exps=0):
    return pl.CostEstimate(flops=int(flops), bytes_accessed=int(moved), transcendentals=int(exps))


def unit(value):
    return value * lax.rsqrt(jnp.mean(value * value, axis=-1, keepdims=True) + 1e-06)


def stale_kernel(in_ref, out_ref):
    out_ref[:, :HEAD_DIM] = unit(in_ref[:, :HEAD_DIM].astype(F32)).astype(BF16)
    out_ref[:, HEAD_DIM:] = in_ref[:, HEAD_DIM:]


def stale_group(stale, first, heads):
    rows = stale.shape[0]
    return pl.pallas_call(
        stale_kernel,
        grid=(heads,),
        in_specs=[pl.BlockSpec((rows, 2 * HEAD_DIM), lambda h: (0, first + h))],
        out_specs=pl.BlockSpec((rows, 2 * HEAD_DIM), lambda h: (0, h)),
        out_shape=jax.ShapeDtypeStruct((rows, heads * 2 * HEAD_DIM), BF16),
        compiler_params=params(),
        cost_estimate=cost(rows * heads * 512, rows * heads * 1024),
    )(stale)


def own_kernel(left_ref, right_ref, out_ref):
    out_ref[...] = jnp.dot(left_ref[...], right_ref[...], preferred_element_type=F32)


def own_terms(left, right, first, heads):
    rows, depth = left.shape
    width = 3 * HEAD_DIM
    return pl.pallas_call(
        own_kernel,
        grid=(heads,),
        in_specs=[
            pl.BlockSpec((rows, depth), lambda h: (0, 0)),
            pl.BlockSpec((depth, width), lambda h: (0, first + h)),
        ],
        out_specs=pl.BlockSpec((rows, width), lambda h: (0, h)),
        out_shape=jax.ShapeDtypeStruct((rows, heads * width), F32),
        compiler_params=params(),
        cost_estimate=cost(2 * rows * depth * heads * width, rows * heads * width * 4 + depth * (rows + heads * width) * 2),
    )(left, right)


def finish_kernel(terms, *refs):
    total = refs[2 * terms][...]
    for at in range(terms):
        total += jnp.dot(refs[at][...], refs[terms + at][...], preferred_element_type=F32)
    q_ref, k_ref, v_ref = refs[2 * terms + 1 :]
    q_ref[...] = unit(total[:, :HEAD_DIM]).astype(BF16)
    k_ref[...] = unit(total[:, HEAD_DIM : 2 * HEAD_DIM]).astype(BF16)
    v_ref[...] = total[:, 2 * HEAD_DIM :].astype(BF16)


def finish(acc, terms):
    lefts, rights = [left for left, _ in terms], [right for _, right in terms]
    width, rows = 3 * HEAD_DIM, acc.shape[0]
    heads, tile = acc.shape[1] // width, 256
    depth = sum(left.shape[1] for left in lefts)
    out = pl.BlockSpec((tile, HEAD_DIM), lambda h, i: (i, h))
    return pl.pallas_call(
        functools.partial(finish_kernel, len(terms)),
        grid=(heads, rows // tile),
        in_specs=[pl.BlockSpec((tile, left.shape[1]), lambda h, i: (i, 0)) for left in lefts]
        + [pl.BlockSpec((right.shape[0], width), lambda h, i: (0, h)) for right in rights]
        + [pl.BlockSpec((tile, width), lambda h, i: (i, h))],
        out_specs=[out] * 3,
        out_shape=[jax.ShapeDtypeStruct((rows, heads * HEAD_DIM), BF16)] * 3,
        compiler_params=params(),
        cost_estimate=cost(2 * rows * depth * heads * width, rows * heads * width * 6),
    )(*lefts, *rights, acc)


def weigh(query, key, mask):
    tile, keys = query.shape[0], key.shape[0]
    scores = lax.dot_general(query, key, (((1,), (1,)), ((), ())), preferred_element_type=F32)
    exponents = jnp.exp(scores * (1.0 / math.sqrt(HEAD_DIM)))
    exponents = exponents.reshape(tile // BLOCK, BLOCK, keys) * mask
    return exponents.reshape(tile, keys).astype(BF16)


def with_ones(value):
    return jnp.concatenate([value, jnp.ones(value.shape, value.dtype)], axis=1)


def window_kernel(fresh, sides, prior, flag_ref, q_ref, *refs):
    num_ref, tot_ref = refs[-2:]
    query = q_ref[...]
    shape = (query.shape[0], 2 * HEAD_DIM)

    def terms(first, windows):
        both = jnp.zeros(shape, F32)
        for at in range(first, first + windows):
            k_ref, v_ref, m_ref = refs[3 * at : 3 * at + 3]
            weights = weigh(query, k_ref[...], m_ref[...])
            both += jnp.dot(weights, with_ones(v_ref[...]), preferred_element_type=F32)
        return both[:, :HEAD_DIM], both[:, HEAD_DIM:]

    if prior:
        num, tot = refs[3 * (fresh + sides)][...], refs[3 * (fresh + sides) + 1][...]
    if fresh:
        num, tot = terms(0, fresh)
    num_ref[...] = num
    tot_ref[...] = tot
    if sides:

        @pl.when(flag_ref[0] == 1)
        def _():
            more, more_tot = terms(fresh, sides)
            num_ref[...] += more
            tot_ref[...] += more_tot


def windows(flag, queries, here, fresh, sides, prior):
    first, heads = here
    rows, cols = queries.shape[0], heads * HEAD_DIM
    query = pl.BlockSpec((QUERY_TILE, HEAD_DIM), lambda h, i, f: (i, first + h))
    tile = pl.BlockSpec((QUERY_TILE, HEAD_DIM), lambda h, i, f: (i, h))
    specs, values = [], []
    for keys, vals, mask in fresh:
        block = pl.BlockSpec((keys.shape[0], HEAD_DIM), lambda h, i, f: (0, first + h))
        specs += [block, block]
        values += [keys, vals, mask]
        specs.append(pl.BlockSpec((QUERY_TILE // BLOCK, 1, keys.shape[0]), lambda h, i, f: (i, 0, 0)))
    for stale, mask in sides:
        specs.append(pl.BlockSpec((stale.shape[0], HEAD_DIM), lambda h, i, f: (0, 2 * h)))
        specs.append(pl.BlockSpec((stale.shape[0], HEAD_DIM), lambda h, i, f: (0, 2 * h + 1)))
        specs.append(pl.BlockSpec((QUERY_TILE // BLOCK, 1, stale.shape[0]), lambda h, i, f: (i, 0, 0)))
        values += [stale, stale, mask]
    count = len(fresh) + len(sides)
    return pl.pallas_call(
        functools.partial(window_kernel, len(fresh), len(sides), len(prior)),
        grid_spec=pltpu.PrefetchScalarGridSpec(
            num_scalar_prefetch=1,
            grid=(heads, rows // QUERY_TILE),
            in_specs=[query] + specs + [tile] * len(prior),
            out_specs=[tile, tile],
        ),
        out_shape=[jax.ShapeDtypeStruct((rows, cols), F32)] * 2,
        compiler_params=params(),
        cost_estimate=cost(6 * count * rows * rows * cols, rows * cols * 14 * count, count * rows * rows * heads),
    )(flag, queries, *values, *prior)


def foreign_kernel(flag_ref, q_ref, k_ref, v_ref, mask_ref, num_ref, tot_ref):
    head = pl.program_id(1)

    @pl.when(head == 0)
    def _():
        tot_ref[...] = jnp.zeros_like(tot_ref)

    @pl.when(flag_ref[0] == 1)
    def _():
        value = v_ref[...]
        weights = weigh(q_ref[...], k_ref[...], mask_ref[...])
        num_ref[...] = jnp.dot(weights, value, preferred_element_type=F32).astype(BF16)
        sums = lax.dot_general(
            jnp.ones((8, weights.shape[1]), BF16), weights, (((1,), (1,)), ((), ())), preferred_element_type=F32
        )
        row = lax.broadcasted_iota(jnp.int32, sums.shape, 0)
        tot_ref[...] = jnp.where(row == head, sums, tot_ref[...])

    @pl.when(flag_ref[0] != 1)
    def _():
        num_ref[...] = jnp.zeros_like(num_ref)


def foreign_part(flag, queries, first, heads, stale, mask):
    rows, cols, window = queries.shape[0], heads * HEAD_DIM, stale.shape[0]
    query = pl.BlockSpec((QUERY_TILE, HEAD_DIM), lambda i, h, f: (i, h))
    tile = pl.BlockSpec((QUERY_TILE, HEAD_DIM), lambda i, h, f: (i, h))
    return pl.pallas_call(
        foreign_kernel,
        grid_spec=pltpu.PrefetchScalarGridSpec(
            num_scalar_prefetch=1,
            grid=(rows // QUERY_TILE, heads),
            in_specs=[
                query,
                pl.BlockSpec((window, HEAD_DIM), lambda i, h, f: (0, 2 * (first + h))),
                pl.BlockSpec((window, HEAD_DIM), lambda i, h, f: (0, 2 * (first + h) + 1)),
                pl.BlockSpec((QUERY_TILE // BLOCK, 1, window), lambda i, h, f: (i, 0, 0)),
            ],
            out_specs=[tile, pl.BlockSpec((8, QUERY_TILE), lambda i, h, f: (0, i))],
        ),
        out_shape=[jax.ShapeDtypeStruct((rows, cols), BF16), jax.ShapeDtypeStruct((8, rows), F32)],
        compiler_params=params(),
        cost_estimate=cost(4 * rows * window * cols, rows * cols * 8, rows * window * heads),
    )(flag, queries, stale, stale, mask)


def branch_kernel(near, far, counts, where_ref, *refs):
    pieces, gate_ref = counts
    step = pl.program_id(0)
    weights, refs = refs[: len(pieces)], refs[len(pieces) :]
    g_ref, refs = refs[0], refs[1:]
    near_refs, far_refs = refs[: 2 * near], refs[2 * near : 2 * near + 2 * far]
    send_ref, keep_ref, att_ref = refs[2 * near + 2 * far :]

    @pl.when(step == 0)
    def _():
        heads_far = []
        for at in range(far):
            num_ref, tot_ref = far_refs[2 * at : 2 * at + 2]
            totals = jnp.transpose(tot_ref[...])
            for head in range(num_ref.shape[1] // HEAD_DIM):
                heads_far.append((num_ref, head, totals[:, head : head + 1]))
        column = 0
        for at in range(near):
            num_ref, tot_ref = near_refs[2 * at : 2 * at + 2]
            for head in range(num_ref.shape[1] // HEAD_DIM):
                cols = slice(head * HEAD_DIM, (head + 1) * HEAD_DIM)
                far_ref, far_head, far_tot = heads_far[column]
                far_num = far_ref[:, far_head * HEAD_DIM : (far_head + 1) * HEAD_DIM].astype(F32)
                value = (num_ref[:, cols] + far_num) / (tot_ref[:, cols] + far_tot)
                att_ref[:, column * HEAD_DIM : (column + 1) * HEAD_DIM] = value.astype(BF16)
                column += 1

    attended = att_ref[...]
    blocks = keep_ref.shape[0]
    sends = pl.num_programs(0) - 1
    turn = where_ref[step]
    for arrival in sorted(set(piece[0] for piece in pieces)):

        @pl.when(turn == arrival)
        def _(arrival=arrival):
            term = None
            for at, (owner, offset, parts) in enumerate(pieces):
                if owner == arrival:
                    if parts == 1:
                        left = attended
                    else:
                        depth = attended.shape[1] // parts
                        part = lax.rem(where_ref[2 * pl.num_programs(0)] + parts - offset, parts)
                        left = attended[:, :depth]
                        for other in range(1, parts):
                            left = jnp.where(part == other, attended[:, other * depth : (other + 1) * depth], left)
                    more = jnp.dot(left, weights[at][...], preferred_element_type=F32)
                    term = more if term is None else term + more
            result = (term * g_ref[0]).astype(BF16)
            stays = step >= pl.num_programs(0) - gate_ref

            @pl.when(stays)
            def _():
                keep_ref[0] = result

            @pl.when(jnp.logical_not(stays))
            def _():
                send_ref[0] = result


def branch(where, pieces, gate, near, far, first, count, keeps):
    total, _, width = gate.shape
    start = first // count
    sends = total - keeps
    specs, values = [], []
    for num, tot in near:
        spec = pl.BlockSpec((count, num.shape[1]), lambda g, w: (start, 0))
        specs += [spec, spec]
        values += [num, tot]
    for num, tot in far:
        specs += [
            pl.BlockSpec((count, num.shape[1]), lambda g, w: (start, 0)),
            pl.BlockSpec((8, count), lambda g, w: (0, start)),
        ]
        values += [num, tot]
    shapes = [piece[3] for piece in pieces]
    depth = sum(num.shape[1] for num, _ in near)
    return pl.pallas_call(
        functools.partial(branch_kernel, len(near), len(far), ([piece[:3] for piece in pieces], keeps)),
        grid_spec=pltpu.PrefetchScalarGridSpec(
            num_scalar_prefetch=1,
            grid=(total,),
            in_specs=[pl.BlockSpec(shape.shape, lambda g, w: (0, 0)) for shape in shapes]
            + [pl.BlockSpec((1, 1, width), lambda g, w: (w[total + g], 0, 0))]
            + specs,
            out_specs=[
                pl.BlockSpec((1, count, width), lambda g, w: (jnp.minimum(g, sends - 1), 0, 0)),
                pl.BlockSpec((1, count, width), lambda g, w: (jnp.maximum(g - sends, 0), 0, 0)),
            ],
            scratch_shapes=[pltpu.VMEM((count, depth), BF16)],
        ),
        out_shape=[
            jax.ShapeDtypeStruct((sends, count, width), BF16),
            jax.ShapeDtypeStruct((keeps, count, width), BF16),
        ],
        compiler_params=params(),
        cost_estimate=cost(2 * count * depth * total * width, depth * total * width * 2 + count * total * width * 2),
    )(where, *shapes, gate, *values)


def chosen(place, values):
    out = values[0]
    for at in range(1, len(values)):
        if values[at] is not values[0]:
            out = jnp.where(place == at, values[at], out)
    return out


class Relay:
    def __init__(self, own, count, reps):
        self.count, self.reps = count, reps
        self.place, self.rank = lax.axis_index("patch"), lax.axis_index("rep")
        self.ahead, self.back = {0: own}, {0: own}

    def step(self, k, *held):
        count = self.count
        ahead, back = self.ahead[k - 1], self.back[k - 1]
        if held:
            ahead, back = after(ahead, *held), after(back, *held)
        self.ahead[k] = lax.ppermute(ahead, "patch", [(i, i + 1) for i in range(k - 1, count - 1)])
        self.back[k] = lax.ppermute(back, "patch", [(i + 1, i) for i in range(count - k)])

    def sent(self, k):
        return self.ahead[k], self.back[k]

    def brought(self, t):
        values, owners = [], []
        for at in range(self.count):
            comes = sorted([(k, 0) for k in range(1, at + 1)] + [(k, 1) for k in range(1, self.count - at)])
            k, side = comes[t - 1]
            values.append(self.back[k] if side else self.ahead[k])
            owners.append(at + k if side else at - k)
        owner = sum(jnp.where(self.place == at, owners[at], 0) for at in range(self.count))
        candidates = []
        for value in values:
            if not any(value is other for other in candidates):
                candidates.append(value)
        fenced = lax.optimization_barrier(tuple(candidates))
        at_of = [[value is other for other in candidates].index(True) for value in values]
        mine = chosen(self.place, [fenced[at] for at in at_of])
        parts = [(self.rank, mine)]
        for offset in range(1, self.reps):
            pairs = [(a, (a + offset) % self.reps) for a in range(self.reps)]
            parts.append(((self.rank - offset) % self.reps, lax.ppermute(mine, "rep", pairs)))
        return owner, parts


def body(hidden, modulation, gate, w_qkv, stale_kv, w_out, key_lists):
    count, reps = lax.axis_size("patch"), lax.axis_size("rep")
    tps, secs = lax.axis_size("tp"), lax.axis_size("sec")
    place, rank = lax.axis_index("patch"), lax.axis_index("rep")
    tp_index, sec_index = lax.axis_index("tp"), lax.axis_index("sec")
    rows, model_width = hidden.shape[1], hidden.shape[2]
    heads = w_out.shape[1] // HEAD_DIM
    patch_blocks = rows // BLOCK
    unit_heads = heads // 3 if heads % 3 == 0 else 1
    units = heads // unit_heads
    small_units = max(1, units // 3)
    group_units = [list(range(units - small_units)), list(range(units - small_units, units))]
    group_heads = [len(members) * unit_heads for members in group_units]
    group_first = [0, group_heads[0]]
    states = hidden[0]
    w_qkv, stale_kv, w_out = w_qkv[0], stale_kv[0], w_out[0]
    last = count - 1
    shard_rows = w_qkv.shape[0]
    depth, out_depth = shard_rows // reps, w_out.shape[0] // reps
    width = 3 * HEAD_DIM

    relative = jnp.where(key_lists >= 0, key_lists - (place - 1) * patch_blocks, -1)
    window_ids = jnp.arange(3 * patch_blocks, dtype=jnp.int32)
    hits = jnp.any(relative[:, :, None] == window_ids[None, None, :], axis=1).astype(F32)
    hits = jnp.repeat(hits, BLOCK, axis=1).reshape(patch_blocks, 3, rows)
    before, fresh, behind = (hits[:, i][:, None, :] for i in range(3))
    odd = place % 2 == 1
    even_mask, odd_mask = jnp.where(odd, before, behind), jnp.where(odd, behind, before)
    at_end = (place == 0) | (place == last)
    to_inner = [(0, 1), (last, last - 1)]
    to_end = [(1, 0), (last - 1, last)]
    inner_flag = jnp.where(at_end, 0, 1).astype(jnp.int32).reshape(1)
    host_flag = ((place == 1) | (place == last - 1)).astype(jnp.int32).reshape(1)

    inner = range(1, last)
    pairs = [(i, i + 1) for i in range(last)] + [(i + 1, i) for i in range(last)]
    even_pairs = [(a, b) for a, b in pairs if min(a, b) % 2 == 0 and b in inner]
    odd_pairs = [(a, b) for a, b in pairs if min(a, b) % 2 == 1 and b in inner]
    stale, even, other = [None] * units, [None] * units, [None] * units

    def send_even(unit, *held):
        even[unit] = lax.ppermute(after(stale[unit], *held), "patch", even_pairs)

    def send_other(unit, *held):
        other[unit] = lax.ppermute(after(stale[unit], *held), "patch", odd_pairs)

    def qkv_relay(group, *held):
        source = after(w_qkv, *held) if held else w_qkv
        at = (rank * depth, group_first[group] * width)
        return Relay(lax.dynamic_slice(source, at, (depth, group_heads[group] * width)), count, reps)

    def columns(owner, part):
        return lax.dynamic_slice_in_dim(modulated, owner * shard_rows + part * depth, depth, 1)

    def term_of(owner, part, piece):
        return columns(owner, part), piece

    def add_terms(acc, terms):
        for left, right in terms:
            acc += jnp.dot(left, right, preferred_element_type=F32)
        return acc

    large = qkv_relay(0)
    large.step(1)
    inputs = states.astype(F32)
    centered = inputs - jnp.mean(inputs, axis=-1, keepdims=True)
    variance = jnp.mean(centered * centered, axis=-1, keepdims=True)
    normed = centered * lax.rsqrt(variance + 1e-06)
    modulated = (normed * (1.0 + modulation[0, 1]) + modulation[0, 0]).astype(BF16)
    for at in range(units):
        stale[at] = stale_group(stale_kv, at * unit_heads, unit_heads)
    modulated, stale[0] = lax.optimization_barrier((modulated, stale[0]))

    own_columns = lax.dynamic_slice_in_dim(modulated, place * shard_rows, shard_rows, 1)
    accs = [None, None]
    come = [[], []]
    far_mask = lax.ppermute(after(jnp.where(place == 0, behind, before), *large.sent(1)), "patch", to_inner)
    share = model_width // (tps * secs)
    residual = lax.dynamic_slice_in_dim(states, (tp_index * secs + sec_index) * share, share, 1)
    for offset in range(1, secs):
        target = (1 + offset) % secs
        sent = lax.dynamic_slice_in_dim(after(states, *large.sent(1)), (tp_index * secs + target) * share, share, 1)
        got = lax.ppermute(sent, "sec", [(1, target)])
        residual = jnp.where(sec_index == target, got, residual)

    def swaps(group, at):
        return [piece for _, piece in come[group][at][1][1:]] if 0 <= at < len(come[group]) else []

    def given(*items):
        return [item for item in items if item is not None]

    def at_or_none(items, at):
        return items[at] if at < len(items) else None

    come[0].append(large.brought(1))
    send_even(0, *large.sent(1))
    for k in range(2, count):
        held = [modulated] if k == 2 else [accs[0]] + swaps(0, k - 3)
        if k == 3:
            held += [even[0], far_mask, residual]
        large.step(k, *held)
        come[0].append(large.brought(k))
        if k == 2:
            accs[0] = own_terms(after(own_columns, *large.sent(1)), w_qkv, 0, group_heads[0])
            if units > 1:
                send_even(1, *large.sent(2))
                send_other(0, *large.sent(2))
        elif k == 3:
            owner, parts = come[0][0]
            accs[0] = add_terms(accs[0], [term_of(owner, *parts[0])])
    def other_terms(group, at):
        owner, parts = come[group][at]
        terms = [term_of(owner, *part) for part in parts[1:]]
        if at + 1 < len(come[group]):
            owner, parts = come[group][at + 1]
            terms.append(term_of(owner, *parts[0]))
        return terms

    small = qkv_relay(
        1, *large.sent(last), accs[0], *swaps(0, last - 2), *given(at_or_none(even, 1), at_or_none(other, 0))
    )
    small.step(1)
    come[1].append(small.brought(1))
    if units > 2:
        send_even(2, *large.sent(last))
    for at in range(last - 2):
        accs[0] = add_terms(accs[0], other_terms(0, at))
    accs[1] = own_terms(after(own_columns, *large.sent(last)), w_qkv, group_first[1], group_heads[1])
    for k in range(2, count):
        held = [accs[0]] if k == 2 else [accs[0], accs[1]] + swaps(0, last - 1)
        if k == 3:
            held += given(at_or_none(even, 2))
        if k > 3:
            held += swaps(1, k - 4)
        small.step(k, *held)
        come[1].append(small.brought(k))
        if k == 2:
            for at in range(max(last - 2, 0), last - 1):
                accs[0] = add_terms(accs[0], other_terms(0, at))
            if units > 1:
                send_other(1, *small.sent(2))
        elif k == 3:
            owner, parts = come[1][0]
            accs[1] = add_terms(accs[1], [term_of(owner, *parts[0])])
    queries_0 = finish(accs[0], other_terms(0, last - 1))
    far_queries_0 = lax.ppermute(queries_0[0], "patch", to_inner)
    for at in range(last - 1):
        accs[1] = add_terms(accs[1], other_terms(1, at))
    queries_1 = finish(accs[1], other_terms(1, last - 1))
    far_queries_1 = lax.ppermute(queries_1[0], "patch", to_inner)
    for at in range(units):
        if even[at] is None:
            send_even(at, *small.sent(last))
        if other[at] is None:
            send_other(at, *small.sent(last), *given(*other))

    stale_full = stale_group(after(stale_kv, *small.sent(1)), 0, heads)

    def far_back(far_queries, group):
        num, tot = foreign_part(host_flag, far_queries, group_first[group], group_heads[group], stale_full, far_mask)
        return lax.ppermute(num, "patch", to_end), lax.ppermute(tot, "patch", to_end)

    far = [far_back(far_queries_0, 0)]

    def near_part(group, at, fresh_too, sides, prior):
        queries, keys, values = (queries_0, queries_1)[group]
        here = (at * unit_heads, unit_heads)
        return windows(inner_flag, queries, here, [(keys, values, fresh)] if fresh_too else [], sides, prior)

    near = [None] * units
    first_large = group_units[0]
    for at, unit_at in enumerate(first_large):
        sides = [(even[unit_at], even_mask), (other[unit_at], odd_mask)]
        near[unit_at] = near_part(0, at, True, sides if unit_at == 0 else sides[:1], ())

    out_relay = Relay(
        lax.dynamic_slice(
            after(w_out, *small.sent(last), *swaps(1, 0), *swaps(1, 1), far_queries_0),
            (rank * out_depth, 0),
            (out_depth, w_out.shape[1]),
        ),
        count,
        reps,
    )
    pieces = [(0, 0, 1, w_out)]
    owners = [place]
    for k in range(1, count):
        held = []
        if k == 2:
            held = swaps(1, last - 1) + given(at_or_none(other, 1)) + list(near[0])
            if len(first_large) > 1:
                held += list(near[first_large[-1]])
        if k == 3:
            for at, unit_at in enumerate(first_large):
                if unit_at:
                    near[unit_at] = near_part(0, at, False, [(other[unit_at], odd_mask)], tuple(near[unit_at]))
            held = [far_queries_1, far[0][0], near[first_large[-1]][0]] + given(at_or_none(other, 2))
            held += [piece for t, offset, _, piece in pieces if t == 1 and offset]
        out_relay.step(k, *held)
        owner, parts = out_relay.brought(k)
        owners.append(owner)
        pieces += [(k, offset, reps, piece) for offset, (_, piece) in enumerate(parts)]
    far.append(far_back(far_queries_1, 1))
    for at, unit_at in enumerate(group_units[1]):
        sides = [(even[unit_at], even_mask), (other[unit_at], odd_mask)]
        near[unit_at] = near_part(1, at, True, sides, ())

    per = count // (tps * secs)
    order = [
        (block * secs + (sec_index + offset) % secs) * per + at
        for offset in list(range(1, secs)) + [0]
        for block in range(tps)
        for at in range(per)
    ]
    turns = [sum(jnp.where(owners[t] == column, t, 0) for t in range(count)) for column in order]
    where = jnp.stack(turns + order + [rank]).astype(jnp.int32)
    gate_blocks = gate.reshape(count, 1, w_out.shape[1])
    chunk = rows // ROW_CHUNKS
    keeps = tps * per
    results = []
    for at in range(ROW_CHUNKS):
        sends, keep = branch(where, pieces, gate_blocks, near, far, at * chunk, chunk, keeps)
        total = keep.astype(F32)
        for offset in range(1, secs):
            sent = sends[(offset - 1) * keeps : offset * keeps]
            got = lax.ppermute(sent, "sec", [(i, (i + offset) % secs) for i in range(secs)])
            total += got.astype(F32)
        total = total.reshape(tps, per, chunk, w_out.shape[1])
        result = lax.dynamic_index_in_dim(total, tp_index, 0, keepdims=False)
        for offset in range(1, tps):
            sent = lax.dynamic_index_in_dim(total, (tp_index + offset) % tps, 0, keepdims=False)
            got = lax.ppermute(sent.astype(BF16), "tp", [(i, (i + offset) % tps) for i in range(tps)])
            result += got.astype(F32)
        result = jnp.moveaxis(result, 0, 1).reshape(chunk, share)
        results.append((result + residual[at * chunk : (at + 1) * chunk].astype(F32)).astype(BF16))
    return jnp.concatenate(results, axis=0)


def solution(mesh):
    return jax.shard_map(
        body,
        mesh=mesh,
        in_specs=(
            P("sec", ("rep", "patch"), None),
            P("sec", None, None),
            P("sec", None),
            P("sec", "patch", "tp"),
            P("sec", ("rep", "patch"), "tp"),
            P("sec", "tp", "patch"),
            P(("rep", "patch"), None),
        ),
        out_specs=P(("rep", "patch"), ("tp", "sec")),
        check_vma=False,
    )
```

```python
import functools
import math

import jax
import jax.numpy as jnp
from jax import lax
from jax.experimental import pallas as pl
from jax.experimental.pallas import tpu as pltpu
from jax.sharding import PartitionSpec as P

HEAD_DIM = 128
BLOCK = 128
QUERY_TILE = 512
ROW_CHUNKS = 2
VMEM_LIMIT = 28 * 1024 * 1024
F32 = jnp.float32
BF16 = jnp.bfloat16


def after(value, *others):
    return lax.optimization_barrier((value,) + others)[0]


def params():
    return pltpu.CompilerParams(vmem_limit_bytes=VMEM_LIMIT)


def cost(flops, moved, exps=0):
    return pl.CostEstimate(flops=int(flops), bytes_accessed=int(moved), transcendentals=int(exps))


def unit(value):
    return value * lax.rsqrt(jnp.mean(value * value, axis=-1, keepdims=True) + 1e-06)


def stale_kernel(in_ref, out_ref):
    out_ref[:, :HEAD_DIM] = unit(in_ref[:, :HEAD_DIM].astype(F32)).astype(BF16)
    out_ref[:, HEAD_DIM:] = in_ref[:, HEAD_DIM:]


def stale_group(stale, first, heads):
    rows = stale.shape[0]
    return pl.pallas_call(
        stale_kernel,
        grid=(heads,),
        in_specs=[pl.BlockSpec((rows, 2 * HEAD_DIM), lambda h: (0, first + h))],
        out_specs=pl.BlockSpec((rows, 2 * HEAD_DIM), lambda h: (0, h)),
        out_shape=jax.ShapeDtypeStruct((rows, heads * 2 * HEAD_DIM), BF16),
        compiler_params=params(),
        cost_estimate=cost(rows * heads * 512, rows * heads * 1024),
    )(stale)


def own_kernel(left_ref, right_ref, out_ref):
    out_ref[...] = jnp.dot(left_ref[...], right_ref[...], preferred_element_type=F32)


def own_terms(left, right, first, heads):
    rows, depth = left.shape
    width = 3 * HEAD_DIM
    return pl.pallas_call(
        own_kernel,
        grid=(heads,),
        in_specs=[
            pl.BlockSpec((rows, depth), lambda h: (0, 0)),
            pl.BlockSpec((depth, width), lambda h: (0, first + h)),
        ],
        out_specs=pl.BlockSpec((rows, width), lambda h: (0, h)),
        out_shape=jax.ShapeDtypeStruct((rows, heads * width), F32),
        compiler_params=params(),
        cost_estimate=cost(2 * rows * depth * heads * width, rows * heads * width * 4 + depth * (rows + heads * width) * 2),
    )(left, right)


def finish_kernel(terms, *refs):
    total = refs[2 * terms][...]
    for at in range(terms):
        total += jnp.dot(refs[at][...], refs[terms + at][...], preferred_element_type=F32)
    q_ref, k_ref, v_ref = refs[2 * terms + 1 :]
    q_ref[...] = unit(total[:, :HEAD_DIM]).astype(BF16)
    k_ref[...] = unit(total[:, HEAD_DIM : 2 * HEAD_DIM]).astype(BF16)
    v_ref[...] = total[:, 2 * HEAD_DIM :].astype(BF16)


def finish(acc, terms):
    lefts, rights = [left for left, _ in terms], [right for _, right in terms]
    width, rows = 3 * HEAD_DIM, acc.shape[0]
    heads, tile = acc.shape[1] // width, rows
    depth = sum(left.shape[1] for left in lefts)
    out = pl.BlockSpec((tile, HEAD_DIM), lambda h, i: (i, h))
    return pl.pallas_call(
        functools.partial(finish_kernel, len(terms)),
        grid=(heads, rows // tile),
        in_specs=[pl.BlockSpec((tile, left.shape[1]), lambda h, i: (i, 0)) for left in lefts]
        + [pl.BlockSpec((right.shape[0], width), lambda h, i: (0, h)) for right in rights]
        + [pl.BlockSpec((tile, width), lambda h, i: (i, h))],
        out_specs=[out] * 3,
        out_shape=[jax.ShapeDtypeStruct((rows, heads * HEAD_DIM), BF16)] * 3,
        compiler_params=params(),
        cost_estimate=cost(2 * rows * depth * heads * width, rows * heads * width * 6),
    )(*lefts, *rights, acc)


def weigh(query, key, mask):
    tile, keys = query.shape[0], key.shape[0]
    scores = lax.dot_general(query, key, (((1,), (1,)), ((), ())), preferred_element_type=F32)
    exponents = jnp.exp(scores * (1.0 / math.sqrt(HEAD_DIM)))
    exponents = exponents.reshape(tile // BLOCK, BLOCK, keys) * mask
    return exponents.reshape(tile, keys).astype(BF16)


def with_ones(value):
    return jnp.concatenate([value, jnp.ones(value.shape, value.dtype)], axis=1)


def window_kernel(fresh, sides, prior, flag_ref, q_ref, *refs):
    num_ref, tot_ref = refs[-2:]
    query = q_ref[...]
    shape = (query.shape[0], 2 * HEAD_DIM)

    def terms(first, windows):
        both = jnp.zeros(shape, F32)
        for at in range(first, first + windows):
            k_ref, v_ref, m_ref = refs[3 * at : 3 * at + 3]
            weights = weigh(query, k_ref[...], m_ref[...])
            both += jnp.dot(weights, with_ones(v_ref[...]), preferred_element_type=F32)
        return both[:, :HEAD_DIM], both[:, HEAD_DIM:]

    if prior:
        num, tot = refs[3 * (fresh + sides)][...], refs[3 * (fresh + sides) + 1][...]
    if fresh:
        num, tot = terms(0, fresh)
    num_ref[...] = num
    tot_ref[...] = tot
    if sides:

        @pl.when(flag_ref[0] == 1)
        def _():
            more, more_tot = terms(fresh, sides)
            num_ref[...] += more
            tot_ref[...] += more_tot


def windows(flag, queries, here, fresh, sides, prior):
    first, heads = here
    rows, cols = queries.shape[0], heads * HEAD_DIM
    query = pl.BlockSpec((QUERY_TILE, HEAD_DIM), lambda h, i, f: (i, first + h))
    tile = pl.BlockSpec((QUERY_TILE, HEAD_DIM), lambda h, i, f: (i, h))
    specs, values = [], []
    for keys, vals, mask in fresh:
        block = pl.BlockSpec((keys.shape[0], HEAD_DIM), lambda h, i, f: (0, first + h))
        specs += [block, block]
        values += [keys, vals, mask]
        specs.append(pl.BlockSpec((QUERY_TILE // BLOCK, 1, keys.shape[0]), lambda h, i, f: (i, 0, 0)))
    for stale, mask in sides:
        specs.append(pl.BlockSpec((stale.shape[0], HEAD_DIM), lambda h, i, f: (0, 2 * h)))
        specs.append(pl.BlockSpec((stale.shape[0], HEAD_DIM), lambda h, i, f: (0, 2 * h + 1)))
        specs.append(pl.BlockSpec((QUERY_TILE // BLOCK, 1, stale.shape[0]), lambda h, i, f: (i, 0, 0)))
        values += [stale, stale, mask]
    count = len(fresh) + len(sides)
    return pl.pallas_call(
        functools.partial(window_kernel, len(fresh), len(sides), len(prior)),
        grid_spec=pltpu.PrefetchScalarGridSpec(
            num_scalar_prefetch=1,
            grid=(heads, rows // QUERY_TILE),
            in_specs=[query] + specs + [tile] * len(prior),
            out_specs=[tile, tile],
        ),
        out_shape=[jax.ShapeDtypeStruct((rows, cols), F32)] * 2,
        compiler_params=params(),
        cost_estimate=cost(6 * count * rows * rows * cols, rows * cols * 14 * count, count * rows * rows * heads),
    )(flag, queries, *values, *prior)


def foreign_kernel(flag_ref, q_ref, k_ref, v_ref, mask_ref, num_ref, tot_ref):
    head = pl.program_id(1)

    @pl.when(head == 0)
    def _():
        tot_ref[...] = jnp.zeros_like(tot_ref)

    @pl.when(flag_ref[0] == 1)
    def _():
        value = v_ref[...]
        weights = weigh(q_ref[...], k_ref[...], mask_ref[...])
        num_ref[...] = jnp.dot(weights, value, preferred_element_type=F32).astype(BF16)
        sums = lax.dot_general(
            jnp.ones((8, weights.shape[1]), BF16), weights, (((1,), (1,)), ((), ())), preferred_element_type=F32
        )
        row = lax.broadcasted_iota(jnp.int32, sums.shape, 0)
        tot_ref[...] = jnp.where(row == head, sums, tot_ref[...])

    @pl.when(flag_ref[0] != 1)
    def _():
        num_ref[...] = jnp.zeros_like(num_ref)


def foreign_part(flag, queries, first, heads, stale, mask):
    rows, cols, window = queries.shape[0], heads * HEAD_DIM, stale.shape[0]
    query = pl.BlockSpec((QUERY_TILE, HEAD_DIM), lambda i, h, f: (i, h))
    tile = pl.BlockSpec((QUERY_TILE, HEAD_DIM), lambda i, h, f: (i, h))
    return pl.pallas_call(
        foreign_kernel,
        grid_spec=pltpu.PrefetchScalarGridSpec(
            num_scalar_prefetch=1,
            grid=(rows // QUERY_TILE, heads),
            in_specs=[
                query,
                pl.BlockSpec((window, HEAD_DIM), lambda i, h, f: (0, 2 * (first + h))),
                pl.BlockSpec((window, HEAD_DIM), lambda i, h, f: (0, 2 * (first + h) + 1)),
                pl.BlockSpec((QUERY_TILE // BLOCK, 1, window), lambda i, h, f: (i, 0, 0)),
            ],
            out_specs=[tile, pl.BlockSpec((8, QUERY_TILE), lambda i, h, f: (0, i))],
        ),
        out_shape=[jax.ShapeDtypeStruct((rows, cols), BF16), jax.ShapeDtypeStruct((8, rows), F32)],
        compiler_params=params(),
        cost_estimate=cost(4 * rows * window * cols, rows * cols * 8, rows * window * heads),
    )(flag, queries, stale, stale, mask)


def normalise_into(att_ref, column, near_refs, num_ref, tot_ref):
    totals = jnp.transpose(tot_ref[...])
    at = 0
    for n_ref, t_ref in near_refs:
        for head in range(n_ref.shape[1] // HEAD_DIM):
            cols = slice(head * HEAD_DIM, (head + 1) * HEAD_DIM)
            far_num = num_ref[:, at * HEAD_DIM : (at + 1) * HEAD_DIM].astype(F32)
            value = (n_ref[:, cols] + far_num) / (t_ref[:, cols] + totals[:, at : at + 1])
            att_ref[:, (column + at) * HEAD_DIM : (column + at + 1) * HEAD_DIM] = value.astype(BF16)
            at += 1


def normalise_kernel(*refs):
    near_refs = [(refs[2 * at], refs[2 * at + 1]) for at in range((len(refs) - 3) // 2)]
    normalise_into(refs[-1], 0, near_refs, refs[-3], refs[-2])


def normalise(near, far):
    num, tot = far
    rows, cols = num.shape
    tile = 512
    specs, values = [], []
    for pair in near:
        specs += [pl.BlockSpec((tile, pair[0].shape[1]), lambda i: (i, 0))] * 2
        values += list(pair)
    return pl.pallas_call(
        normalise_kernel,
        grid=(rows // tile,),
        in_specs=specs + [pl.BlockSpec((tile, cols), lambda i: (i, 0)), pl.BlockSpec((8, tile), lambda i: (0, i))],
        out_specs=pl.BlockSpec((tile, cols), lambda i: (i, 0)),
        out_shape=jax.ShapeDtypeStruct((rows, cols), BF16),
        compiler_params=params(),
        cost_estimate=cost(rows * cols * 4, rows * cols * 12),
    )(*values, num, tot)


def branch_kernel(near, keeps, parts, where_ref, *refs):
    step, steps = pl.program_id(0), pl.num_programs(0)
    mine_ref, own_refs, other_refs = refs[0], refs[1:parts], refs[parts : 2 * parts - 1]
    g_ref, done_ref = refs[2 * parts - 1 : 2 * parts + 1]
    rest = refs[2 * parts + 1 :]
    send_ref, keep_ref, att_ref = rest[-3:]

    @pl.when(step == 0)
    def _():
        att_ref[:, : done_ref.shape[1]] = done_ref[...]
        near_refs = [(rest[2 * at], rest[2 * at + 1]) for at in range(near)]
        normalise_into(att_ref, done_ref.shape[1] // HEAD_DIM, near_refs, rest[2 * near], rest[2 * near + 1])

    attended = att_ref[...]
    depth = attended.shape[1] // parts
    rank, place = where_ref[2 * steps], where_ref[2 * steps + 1]
    is_own = where_ref[step] == place

    def left_of(part):
        left = attended[:, :depth]
        for other in range(1, parts):
            left = jnp.where(part == other, attended[:, other * depth : (other + 1) * depth], left)
        return left

    term = jnp.dot(left_of(rank), mine_ref[0], preferred_element_type=F32)
    for offset in range(1, parts):
        right = jnp.where(is_own, own_refs[offset - 1][...], other_refs[offset - 1][0])
        term += jnp.dot(left_of(lax.rem(rank + parts - offset, parts)), right, preferred_element_type=F32)
    result = (term * g_ref[0]).astype(BF16)
    stays = step >= steps - keeps

    @pl.when(stays)
    def _():
        keep_ref[0] = result

    @pl.when(jnp.logical_not(stays))
    def _():
        send_ref[0] = result


def branch(where, mine, owns, others, gate, done, near, far, first, count, keeps):
    total, depth, width = mine.shape
    start = first // count
    sends = total - keeps
    specs, values = [pl.BlockSpec((count, done.shape[1]), lambda g, w: (start, 0))], [done]
    for num, tot in near:
        spec = pl.BlockSpec((count, num.shape[1]), lambda g, w: (start, 0))
        specs += [spec, spec]
        values += [num, tot]
    num, tot = far
    specs += [
        pl.BlockSpec((count, num.shape[1]), lambda g, w: (start, 0)),
        pl.BlockSpec((8, count), lambda g, w: (0, start)),
    ]
    values += [num, tot]
    parts = len(others) + 1
    held = depth * parts
    return pl.pallas_call(
        functools.partial(branch_kernel, len(near), keeps, parts),
        grid_spec=pltpu.PrefetchScalarGridSpec(
            num_scalar_prefetch=1,
            grid=(total,),
            in_specs=[pl.BlockSpec((1, depth, width), lambda g, w: (w[g], 0, 0))]
            + [pl.BlockSpec((depth, width), lambda g, w: (0, 0))] * len(owns)
            + [pl.BlockSpec((1, depth, width), lambda g, w: (w[total + g], 0, 0))] * len(others)
            + [pl.BlockSpec((1, 1, width), lambda g, w: (w[g], 0, 0))]
            + specs,
            out_specs=[
                pl.BlockSpec((1, count, width), lambda g, w: (jnp.minimum(g, sends - 1), 0, 0)),
                pl.BlockSpec((1, count, width), lambda g, w: (jnp.maximum(g - sends, 0), 0, 0)),
            ],
            scratch_shapes=[pltpu.VMEM((count, held), BF16)],
        ),
        out_shape=[
            jax.ShapeDtypeStruct((sends, count, width), BF16),
            jax.ShapeDtypeStruct((keeps, count, width), BF16),
        ],
        compiler_params=params(),
        cost_estimate=cost(2 * count * held * total * width, held * total * width * 2 + count * total * width * 2),
    )(where, mine, *owns, *others, gate, *values)


def chosen(place, values):
    out = values[0]
    for at in range(1, len(values)):
        if values[at] is not values[0]:
            out = jnp.where(place == at, values[at], out)
    return out


class Relay:
    def __init__(self, own, count, reps):
        self.count, self.reps = count, reps
        self.place, self.rank = lax.axis_index("patch"), lax.axis_index("rep")
        self.ahead, self.back = {0: own}, {0: own}

    def step(self, k, *held):
        count = self.count
        ahead, back = self.ahead[k - 1], self.back[k - 1]
        if held:
            ahead, back = after(ahead, *held), after(back, *held)
        self.ahead[k] = lax.ppermute(ahead, "patch", [(i, i + 1) for i in range(k - 1, count - 1)])
        self.back[k] = lax.ppermute(back, "patch", [(i + 1, i) for i in range(count - k)])

    def sent(self, k):
        return self.ahead[k], self.back[k]

    def brought(self, t):
        values, owners = [], []
        for at in range(self.count):
            comes = sorted([(k, 0) for k in range(1, at + 1)] + [(k, 1) for k in range(1, self.count - at)])
            k, side = comes[t - 1]
            values.append(self.back[k] if side else self.ahead[k])
            owners.append(at + k if side else at - k)
        owner = sum(jnp.where(self.place == at, owners[at], 0) for at in range(self.count))
        candidates = []
        for value in values:
            if not any(value is other for other in candidates):
                candidates.append(value)
        fenced = lax.optimization_barrier(tuple(candidates))
        at_of = [[value is other for other in candidates].index(True) for value in values]
        mine = chosen(self.place, [fenced[at] for at in at_of])
        parts = [(self.rank, mine)]
        for offset in range(1, self.reps):
            pairs = [(a, (a + offset) % self.reps) for a in range(self.reps)]
            parts.append(((self.rank - offset) % self.reps, lax.ppermute(mine, "rep", pairs)))
        return owner, parts


def body(hidden, modulation, gate, w_qkv, stale_kv, w_out, key_lists):
    count, reps = lax.axis_size("patch"), lax.axis_size("rep")
    tps, secs = lax.axis_size("tp"), lax.axis_size("sec")
    place, rank = lax.axis_index("patch"), lax.axis_index("rep")
    tp_index, sec_index = lax.axis_index("tp"), lax.axis_index("sec")
    rows, model_width = hidden.shape[1], hidden.shape[2]
    heads = w_out.shape[1] // HEAD_DIM
    patch_blocks = rows // BLOCK
    unit_heads = heads // 3 if heads % 3 == 0 else 1
    units = heads // unit_heads
    small_units = max(1, units // 3)
    group_units = [list(range(units - small_units)), list(range(units - small_units, units))]
    group_heads = [len(members) * unit_heads for members in group_units]
    group_first = [0, group_heads[0]]
    states = hidden[0]
    w_qkv, stale_kv, w_out = w_qkv[0], stale_kv[0], w_out[0]
    last = count - 1
    shard_rows = w_qkv.shape[0]
    depth, out_depth = shard_rows // reps, w_out.shape[0] // reps
    width = 3 * HEAD_DIM

    relative = jnp.where(key_lists >= 0, key_lists - (place - 1) * patch_blocks, -1)
    window_ids = jnp.arange(3 * patch_blocks, dtype=jnp.int32)
    hits = jnp.any(relative[:, :, None] == window_ids[None, None, :], axis=1).astype(F32)
    hits = jnp.repeat(hits, BLOCK, axis=1).reshape(patch_blocks, 3, rows)
    before, fresh, behind = (hits[:, i][:, None, :] for i in range(3))
    odd = place % 2 == 1
    even_mask, odd_mask = jnp.where(odd, before, behind), jnp.where(odd, behind, before)
    at_end = (place == 0) | (place == last)
    to_inner = [(0, 1), (last, last - 1)]
    to_end = [(1, 0), (last - 1, last)]
    inner_flag = jnp.where(at_end, 0, 1).astype(jnp.int32).reshape(1)
    host_flag = ((place == 1) | (place == last - 1)).astype(jnp.int32).reshape(1)

    inner = range(1, last)
    pairs = [(i, i + 1) for i in range(last)] + [(i + 1, i) for i in range(last)]
    even_pairs = [(a, b) for a, b in pairs if min(a, b) % 2 == 0 and b in inner]
    odd_pairs = [(a, b) for a, b in pairs if min(a, b) % 2 == 1 and b in inner]
    stale, even, other = [None] * units, [None] * units, [None] * units

    def send_even(unit, *held):
        even[unit] = lax.ppermute(after(stale[unit], *held), "patch", even_pairs)

    def send_other(unit, *held):
        other[unit] = lax.ppermute(after(stale[unit], *held), "patch", odd_pairs)

    def qkv_relay(group, *held):
        source = after(w_qkv, *held) if held else w_qkv
        at = (rank * depth, group_first[group] * width)
        return Relay(lax.dynamic_slice(source, at, (depth, group_heads[group] * width)), count, reps)

    def columns(owner, part):
        return lax.dynamic_slice_in_dim(modulated, owner * shard_rows + part * depth, depth, 1)

    def term_of(owner, part, piece):
        return columns(owner, part), piece

    def add_terms(acc, terms):
        for left, right in terms:
            acc += jnp.dot(left, right, preferred_element_type=F32)
        return acc

    large = qkv_relay(0)
    large.step(1)
    inputs = states.astype(F32)
    centered = inputs - jnp.mean(inputs, axis=-1, keepdims=True)
    variance = jnp.mean(centered * centered, axis=-1, keepdims=True)
    normed = centered * lax.rsqrt(variance + 1e-06)
    modulated = (normed * (1.0 + modulation[0, 1]) + modulation[0, 0]).astype(BF16)
    for at in range(units):
        stale[at] = stale_group(stale_kv, at * unit_heads, unit_heads)
    modulated, stale[0] = lax.optimization_barrier((modulated, stale[0]))

    own_out = lax.dynamic_slice_in_dim(after(w_out, *large.sent(1)), rank * out_depth, out_depth, 0)
    out_mine = lax.all_gather(own_out, "patch", axis=0)

    own_columns = lax.dynamic_slice_in_dim(modulated, place * shard_rows, shard_rows, 1)
    accs = [None, None]
    come = [[], []]
    far_mask = lax.ppermute(after(jnp.where(place == 0, behind, before), *large.sent(1)), "patch", to_inner)
    share = model_width // (tps * secs)
    residual = lax.dynamic_slice_in_dim(states, (tp_index * secs + sec_index) * share, share, 1)
    got_all = []
    for offset in range(1, secs):
        target = (1 + offset) % secs
        sent = lax.dynamic_slice_in_dim(states, (tp_index * secs + target) * share, share, 1)
        got = lax.ppermute(sent, "sec", [(1, target)])
        got_all.append(got)
        residual = jnp.where(sec_index == target, got, residual)

    def swaps(group, at):
        return [piece for _, piece in come[group][at][1][1:]] if 0 <= at < len(come[group]) else []

    def given(*items):
        return [item for item in items if item is not None]

    def at_or_none(items, at):
        return items[at] if at < len(items) else None

    def own_half(group, at):
        owner, parts = come[group][at]
        return [term_of(owner, *parts[0])]

    def other_half(group, at):
        owner, parts = come[group][at]
        return [term_of(owner, *part) for part in parts[1:]]

    come[0].append(large.brought(1))
    send_even(0, *large.sent(1))
    for k in range(2, count):
        held = [modulated] + got_all if k == 2 else [accs[0]] + swaps(0, k - 3)
        if k == 3:
            held += [even[0], far_mask, residual]
        large.step(k, *held)
        come[0].append(large.brought(k))
        if k == 2:
            accs[0] = own_terms(after(own_columns, *large.sent(1)), w_qkv, 0, group_heads[0])
            if units > 1:
                send_even(1, *large.sent(2))
                send_other(0, *large.sent(2))
        elif k == 3:
            accs[0] = add_terms(accs[0], own_half(0, 0) + own_half(0, 1) + other_half(0, 0))

    small = qkv_relay(
        1, *large.sent(last), accs[0], *swaps(0, last - 2), *given(at_or_none(even, 1), at_or_none(other, 0))
    )
    small.step(1)
    come[1].append(small.brought(1))
    if units > 2:
        send_even(2, *large.sent(last))
    for at in range(2, last - 1):
        accs[0] = add_terms(accs[0], own_half(0, at) + other_half(0, at - 1))
    accs[1] = own_terms(after(own_columns, *large.sent(last)), w_qkv, group_first[1], group_heads[1])
    final_terms = own_half(0, last - 1) + other_half(0, last - 1)
    if last > 1:
        final_terms = other_half(0, last - 2) + final_terms
    queries_0 = finish(accs[0], final_terms)
    for k in range(2, count):
        held = [accs[1]] if k == 2 else list(queries_0)
        if k == 3:
            held += given(at_or_none(even, 2))
        if k > 3:
            held += swaps(1, k - 4)
        small.step(k, *held)
        come[1].append(small.brought(k))
        if k == 2 and units > 1:
            send_other(1, *small.sent(2))
    far_queries_0 = lax.ppermute(queries_0[0], "patch", to_inner)
    for at in range(units):
        if even[at] is None:
            send_even(at, *small.sent(last))
        if other[at] is None:
            send_other(at, *small.sent(last), *given(*other))

    def near_part(group, at, fresh_too, sides, prior):
        queries, keys, values = (queries_0, queries_1)[group]
        here = (at * unit_heads, unit_heads)
        return windows(inner_flag, queries, here, [(keys, values, fresh)] if fresh_too else [], sides, prior)

    stale_full = stale_group(after(stale_kv, *small.sent(1)), 0, heads)

    def far_part(far_queries, group):
        return foreign_part(host_flag, far_queries, group_first[group], group_heads[group], stale_full, far_mask)

    far_num_0, far_tot_0 = far_part(far_queries_0, 0)
    near = [None] * units
    first_large = group_units[0]
    queries_1 = None
    for at, unit_at in enumerate(first_large):
        sides = [(even[unit_at], even_mask), (other[unit_at], odd_mask)]
        near[unit_at] = near_part(0, at, True, sides if unit_at == 0 else sides[:1], ())

    early = []
    for at in range(last - 2):
        early += own_half(1, at) + other_half(1, at)
    if early:
        accs[1] = add_terms(accs[1], early)
    final_terms = []
    for at in range(max(last - 2, 0), last):
        final_terms += own_half(1, at) + other_half(1, at)
    fenced = lax.optimization_barrier((accs[1], far_num_0, near[0][0]))
    queries_1 = finish(fenced[0], final_terms)
    back_num_0 = lax.ppermute(far_num_0, "patch", to_end)
    far_queries_1 = lax.ppermute(queries_1[0], "patch", to_inner)

    turned = [lax.dynamic_index_in_dim(out_mine, (place + 1 + at) % count, 0, keepdims=True) for at in range(last)]
    turned = after(jnp.concatenate(turned, axis=0), *swaps(1, last - 1))
    out_others, out_owns = [], []
    for offset in range(1, reps):
        out_others.append(lax.ppermute(turned, "rep", [(a, (a + offset) % reps) for a in range(reps)]))
        out_owns.append(lax.dynamic_slice_in_dim(w_out, (rank - offset) % reps * out_depth, out_depth, 0))

    for at, unit_at in enumerate(first_large):
        if unit_at:
            near[unit_at] = near_part(0, at, False, [(other[unit_at], odd_mask)], tuple(near[unit_at]))
    far_num_1, far_tot_1 = far_part(after(far_queries_1, *[near[at][0] for at in first_large]), 1)
    back_num_1 = lax.ppermute(far_num_1, "patch", to_end)
    back_tot = lax.ppermute(jnp.concatenate([far_tot_0, far_tot_1], axis=0), "patch", to_end)
    for at, unit_at in enumerate(group_units[1]):
        sides = [(even[unit_at], even_mask), (other[unit_at], odd_mask)]
        near[unit_at] = near_part(1, at, True, sides, ())
    done = normalise([near[at] for at in group_units[0]], (back_num_0, back_tot[:8]))

    per = count // (tps * secs)
    order = [
        (block * secs + (sec_index + offset) % secs) * per + at
        for offset in list(range(1, secs)) + [0]
        for block in range(tps)
        for at in range(per)
    ]
    other_order = [jnp.minimum((column - place - 1) % count, last - 1) for column in order]
    where = jnp.stack(order + other_order + [rank, place]).astype(jnp.int32)
    gate_blocks = gate.reshape(count, 1, w_out.shape[1])
    chunk = rows // ROW_CHUNKS
    keeps = tps * per
    results = []
    for at in range(ROW_CHUNKS):
        sends, keep = branch(
            where, out_mine, out_owns, out_others, gate_blocks, done,
            [near[unit_at] for unit_at in group_units[1]], (back_num_1, back_tot[8:]), at * chunk, chunk, keeps,
        )
        got = [keep]
        for offset in range(1, secs):
            sent = sends[(offset - 1) * keeps : offset * keeps]
            got.append(lax.ppermute(sent, "sec", [(i, (i + offset) % secs) for i in range(secs)]))

        def block_of(index):
            return sum(lax.dynamic_slice_in_dim(part, index * per, per, 0).astype(F32) for part in got)

        others = []
        for offset in range(1, tps):
            sent = block_of((tp_index + offset) % tps).astype(BF16)
            others.append(lax.ppermute(sent, "tp", [(i, (i + offset) % tps) for i in range(tps)]))
        result = block_of(tp_index) + sum(part.astype(F32) for part in others)
        result = jnp.moveaxis(result, 0, 1).reshape(chunk, share)
        results.append((result + residual[at * chunk : (at + 1) * chunk].astype(F32)).astype(BF16))
    return jnp.concatenate(results, axis=0)


def solution(mesh):
    return jax.shard_map(
        body,
        mesh=mesh,
        in_specs=(
            P("sec", ("rep", "patch"), None),
            P("sec", None, None),
            P("sec", None),
            P("sec", "patch", "tp"),
            P("sec", ("rep", "patch"), "tp"),
            P("sec", "tp", "patch"),
            P(("rep", "patch"), None),
        ),
        out_specs=P(("rep", "patch"), ("tp", "sec")),
        check_vma=False,
    )
```

```python
import functools
import math

import jax
import jax.numpy as jnp
from jax import lax
from jax.experimental import pallas as pl
from jax.experimental.pallas import tpu as pltpu
from jax.sharding import PartitionSpec as P

HEAD_DIM = 128
BLOCK = 128
QUERY_TILE = 512
ROW_CHUNKS = (1, 1, 2)
VMEM_LIMIT = 28 * 1024 * 1024
F32 = jnp.float32
BF16 = jnp.bfloat16


def after(value, *others):
    return lax.optimization_barrier((value,) + others)[0]


def params():
    return pltpu.CompilerParams(vmem_limit_bytes=VMEM_LIMIT)


def cost(flops, moved, exps=0):
    return pl.CostEstimate(flops=int(flops), bytes_accessed=int(moved), transcendentals=int(exps))


def unit(value):
    return value * lax.rsqrt(jnp.mean(value * value, axis=-1, keepdims=True) + 1e-06)


def stale_kernel(in_ref, out_ref):
    out_ref[:, :HEAD_DIM] = unit(in_ref[:, :HEAD_DIM].astype(F32)).astype(BF16)
    out_ref[:, HEAD_DIM:] = in_ref[:, HEAD_DIM:]


def stale_group(stale, first, heads):
    rows = stale.shape[0]
    return pl.pallas_call(
        stale_kernel,
        grid=(heads,),
        in_specs=[pl.BlockSpec((rows, 2 * HEAD_DIM), lambda h: (0, first + h))],
        out_specs=pl.BlockSpec((rows, 2 * HEAD_DIM), lambda h: (0, h)),
        out_shape=jax.ShapeDtypeStruct((rows, heads * 2 * HEAD_DIM), BF16),
        compiler_params=params(),
        cost_estimate=cost(rows * heads * 512, rows * heads * 1024),
    )(stale)


def own_kernel(left_ref, right_ref, out_ref):
    out_ref[...] = jnp.dot(left_ref[...], right_ref[...], preferred_element_type=F32)


def own_terms(left, right, first, heads):
    rows, depth = left.shape
    width = 3 * HEAD_DIM
    return pl.pallas_call(
        own_kernel,
        grid=(heads,),
        in_specs=[
            pl.BlockSpec((rows, depth), lambda h: (0, 0)),
            pl.BlockSpec((depth, width), lambda h: (0, first + h)),
        ],
        out_specs=pl.BlockSpec((rows, width), lambda h: (0, h)),
        out_shape=jax.ShapeDtypeStruct((rows, heads * width), F32),
        compiler_params=params(),
        cost_estimate=cost(2 * rows * depth * heads * width, rows * heads * width * 4 + depth * (rows + heads * width) * 2),
    )(left, right)


def finish_kernel(terms, *refs):
    total = refs[2 * terms][...]
    for at in range(terms):
        total += jnp.dot(refs[at][...], refs[terms + at][...], preferred_element_type=F32)
    q_ref, k_ref, v_ref = refs[2 * terms + 1 :]
    q_ref[...] = unit(total[:, :HEAD_DIM]).astype(BF16)
    k_ref[...] = unit(total[:, HEAD_DIM : 2 * HEAD_DIM]).astype(BF16)
    v_ref[...] = total[:, 2 * HEAD_DIM :].astype(BF16)


def finish(acc, terms):
    lefts, rights = [left for left, _ in terms], [right for _, right in terms]
    width, rows = 3 * HEAD_DIM, acc.shape[0]
    heads, tile = acc.shape[1] // width, rows
    depth = sum(left.shape[1] for left in lefts)
    out = pl.BlockSpec((tile, HEAD_DIM), lambda h, i: (i, h))
    return pl.pallas_call(
        functools.partial(finish_kernel, len(terms)),
        grid=(heads, rows // tile),
        in_specs=[pl.BlockSpec((tile, left.shape[1]), lambda h, i: (i, 0)) for left in lefts]
        + [pl.BlockSpec((right.shape[0], width), lambda h, i: (0, h)) for right in rights]
        + [pl.BlockSpec((tile, width), lambda h, i: (i, h))],
        out_specs=[out] * 3,
        out_shape=[jax.ShapeDtypeStruct((rows, heads * HEAD_DIM), BF16)] * 3,
        compiler_params=params(),
        cost_estimate=cost(2 * rows * depth * heads * width, rows * heads * width * 6),
    )(*lefts, *rights, acc)


def weigh(query, key, mask):
    tile, keys = query.shape[0], key.shape[0]
    scores = lax.dot_general(query, key, (((1,), (1,)), ((), ())), preferred_element_type=F32)
    exponents = jnp.exp(scores * (1.0 / math.sqrt(HEAD_DIM)))
    exponents = exponents.reshape(tile // BLOCK, BLOCK, keys) * mask
    return exponents.reshape(tile, keys).astype(BF16)


def with_ones(value):
    return jnp.concatenate([value, jnp.ones(value.shape, value.dtype)], axis=1)


def window_kernel(fresh, sides, prior, flag_ref, q_ref, *refs):
    num_ref, tot_ref = refs[-2:]
    query = q_ref[...]
    shape = (query.shape[0], 2 * HEAD_DIM)

    def terms(first, windows):
        both = jnp.zeros(shape, F32)
        for at in range(first, first + windows):
            k_ref, v_ref, m_ref = refs[3 * at : 3 * at + 3]
            weights = weigh(query, k_ref[...], m_ref[...])
            both += jnp.dot(weights, with_ones(v_ref[...]), preferred_element_type=F32)
        return both[:, :HEAD_DIM], both[:, HEAD_DIM:]

    if prior:
        num, tot = refs[3 * (fresh + sides)][...], refs[3 * (fresh + sides) + 1][...]
    if fresh:
        num, tot = terms(0, fresh)
    num_ref[...] = num
    tot_ref[...] = tot
    for side in range(sides):

        @pl.when(flag_ref[side] == 1)
        def _(side=side):
            more, more_tot = terms(fresh + side, 1)
            num_ref[...] += more
            tot_ref[...] += more_tot


def windows(flag, queries, here, fresh, sides, prior):
    first, heads = here
    rows, cols = queries.shape[0], heads * HEAD_DIM
    query = pl.BlockSpec((QUERY_TILE, HEAD_DIM), lambda h, i, f: (i, first + h))
    tile = pl.BlockSpec((QUERY_TILE, HEAD_DIM), lambda h, i, f: (i, h))
    specs, values = [], []
    for keys, vals, mask in fresh:
        block = pl.BlockSpec((keys.shape[0], HEAD_DIM), lambda h, i, f: (0, first + h))
        specs += [block, block]
        values += [keys, vals, mask]
        specs.append(pl.BlockSpec((QUERY_TILE // BLOCK, 1, keys.shape[0]), lambda h, i, f: (i, 0, 0)))
    for stale, mask in sides:
        specs.append(pl.BlockSpec((stale.shape[0], HEAD_DIM), lambda h, i, f: (0, 2 * h)))
        specs.append(pl.BlockSpec((stale.shape[0], HEAD_DIM), lambda h, i, f: (0, 2 * h + 1)))
        specs.append(pl.BlockSpec((QUERY_TILE // BLOCK, 1, stale.shape[0]), lambda h, i, f: (i, 0, 0)))
        values += [stale, stale, mask]
    count = len(fresh) + len(sides)
    return pl.pallas_call(
        functools.partial(window_kernel, len(fresh), len(sides), len(prior)),
        grid_spec=pltpu.PrefetchScalarGridSpec(
            num_scalar_prefetch=1,
            grid=(heads, rows // QUERY_TILE),
            in_specs=[query] + specs + [tile] * len(prior),
            out_specs=[tile, tile],
        ),
        out_shape=[jax.ShapeDtypeStruct((rows, cols), F32)] * 2,
        compiler_params=params(),
        cost_estimate=cost(6 * count * rows * rows * cols, rows * cols * 14 * count, count * rows * rows * heads),
    )(flag, queries, *values, *prior)


def foreign_kernel(flag_ref, q_ref, k_ref, v_ref, mask_ref, num_ref, tot_ref):
    head = pl.program_id(1)

    @pl.when(head == 0)
    def _():
        tot_ref[...] = jnp.zeros_like(tot_ref)

    @pl.when(flag_ref[0] == 1)
    def _():
        value = v_ref[...]
        weights = weigh(q_ref[...], k_ref[...], mask_ref[...])
        num_ref[...] = jnp.dot(weights, value, preferred_element_type=F32).astype(BF16)
        sums = lax.dot_general(
            jnp.ones((8, weights.shape[1]), BF16), weights, (((1,), (1,)), ((), ())), preferred_element_type=F32
        )
        row = lax.broadcasted_iota(jnp.int32, sums.shape, 0)
        tot_ref[...] = jnp.where(row == head, sums, tot_ref[...])

    @pl.when(flag_ref[0] != 1)
    def _():
        num_ref[...] = jnp.zeros_like(num_ref)


def foreign_part(flag, queries, first, heads, stale, mask):
    rows, cols, window = queries.shape[0], heads * HEAD_DIM, stale.shape[0]
    query = pl.BlockSpec((QUERY_TILE, HEAD_DIM), lambda i, h, f: (i, h))
    tile = pl.BlockSpec((QUERY_TILE, HEAD_DIM), lambda i, h, f: (i, h))
    return pl.pallas_call(
        foreign_kernel,
        grid_spec=pltpu.PrefetchScalarGridSpec(
            num_scalar_prefetch=1,
            grid=(rows // QUERY_TILE, heads),
            in_specs=[
                query,
                pl.BlockSpec((window, HEAD_DIM), lambda i, h, f: (0, 2 * (first + h))),
                pl.BlockSpec((window, HEAD_DIM), lambda i, h, f: (0, 2 * (first + h) + 1)),
                pl.BlockSpec((QUERY_TILE // BLOCK, 1, window), lambda i, h, f: (i, 0, 0)),
            ],
            out_specs=[tile, pl.BlockSpec((8, QUERY_TILE), lambda i, h, f: (0, i))],
        ),
        out_shape=[jax.ShapeDtypeStruct((rows, cols), BF16), jax.ShapeDtypeStruct((8, rows), F32)],
        compiler_params=params(),
        cost_estimate=cost(4 * rows * window * cols, rows * cols * 8, rows * window * heads),
    )(flag, queries, stale, stale, mask)


def normalise_into(att_ref, column, near_refs, num_ref=None, tot_ref=None):
    totals = None if tot_ref is None else jnp.transpose(tot_ref[...])
    at = 0
    for n_ref, t_ref in near_refs:
        for head in range(n_ref.shape[1] // HEAD_DIM):
            cols = slice(head * HEAD_DIM, (head + 1) * HEAD_DIM)
            num, tot = n_ref[:, cols], t_ref[:, cols]
            if num_ref is not None:
                num += num_ref[:, at * HEAD_DIM : (at + 1) * HEAD_DIM].astype(F32)
                tot += totals[:, at : at + 1]
            att_ref[:, (column + at) * HEAD_DIM : (column + at + 1) * HEAD_DIM] = (num / tot).astype(BF16)
            at += 1


def normalise_kernel(*refs):
    near_refs = [(refs[2 * at], refs[2 * at + 1]) for at in range((len(refs) - 3) // 2)]
    normalise_into(refs[-1], 0, near_refs, refs[-3], refs[-2])


def normalise(near, far):
    num, tot = far
    rows, cols = num.shape
    tile = 512
    specs, values = [], []
    for pair in near:
        specs += [pl.BlockSpec((tile, pair[0].shape[1]), lambda i: (i, 0))] * 2
        values += list(pair)
    return pl.pallas_call(
        normalise_kernel,
        grid=(rows // tile,),
        in_specs=specs + [pl.BlockSpec((tile, cols), lambda i: (i, 0)), pl.BlockSpec((8, tile), lambda i: (0, i))],
        out_specs=pl.BlockSpec((tile, cols), lambda i: (i, 0)),
        out_shape=jax.ShapeDtypeStruct((rows, cols), BF16),
        compiler_params=params(),
        cost_estimate=cost(rows * cols * 4, rows * cols * 12),
    )(*values, num, tot)


def branch_kernel(near, keeps, parts, where_ref, *refs):
    step, steps = pl.program_id(0), pl.num_programs(0)
    mine_ref, own_refs, other_refs = refs[0], refs[1:parts], refs[parts : 2 * parts - 1]
    g_ref, done_ref = refs[2 * parts - 1 : 2 * parts + 1]
    rest = refs[2 * parts + 1 :]
    send_ref, keep_ref, att_ref = rest[-3:]

    @pl.when(step == 0)
    def _():
        att_ref[:, : done_ref.shape[1]] = done_ref[...]
        near_refs = [(rest[2 * at], rest[2 * at + 1]) for at in range(near)]
        normalise_into(att_ref, done_ref.shape[1] // HEAD_DIM, near_refs)

    attended = att_ref[...]
    depth = attended.shape[1] // parts
    rank = where_ref[3 * steps]
    is_own = where_ref[step] == 0

    def left_of(part):
        left = attended[:, :depth]
        for other in range(1, parts):
            left = jnp.where(part == other, attended[:, other * depth : (other + 1) * depth], left)
        return left

    term = jnp.dot(left_of(rank), mine_ref[0], preferred_element_type=F32)
    for offset in range(1, parts):
        right = jnp.where(is_own, own_refs[offset - 1][...], other_refs[offset - 1][0])
        term += jnp.dot(left_of(lax.rem(rank + parts - offset, parts)), right, preferred_element_type=F32)
    result = (term * g_ref[0]).astype(BF16)
    stays = step >= steps - keeps

    @pl.when(stays)
    def _():
        keep_ref[0] = result

    @pl.when(jnp.logical_not(stays))
    def _():
        send_ref[0] = result


def branch(where, mine, owns, others, gate, done, near, first, count, keeps):
    total, depth, width = mine.shape
    start = first // count
    sends = total - keeps
    specs, values = [pl.BlockSpec((count, done.shape[1]), lambda g, w: (start, 0))], [done]
    for num, tot in near:
        spec = pl.BlockSpec((count, num.shape[1]), lambda g, w: (start, 0))
        specs += [spec, spec]
        values += [num, tot]
    parts = len(others) + 1
    held = depth * parts
    return pl.pallas_call(
        functools.partial(branch_kernel, len(near), keeps, parts),
        grid_spec=pltpu.PrefetchScalarGridSpec(
            num_scalar_prefetch=1,
            grid=(total,),
            in_specs=[pl.BlockSpec((1, depth, width), lambda g, w: (w[g], 0, 0))]
            + [pl.BlockSpec((depth, width), lambda g, w: (0, 0))] * len(owns)
            + [pl.BlockSpec((1, depth, width), lambda g, w: (w[total + g], 0, 0))] * len(others)
            + [pl.BlockSpec((1, 1, width), lambda g, w: (w[2 * total + g], 0, 0))]
            + specs,
            out_specs=[
                pl.BlockSpec((1, count, width), lambda g, w: (jnp.minimum(g, sends - 1), 0, 0)),
                pl.BlockSpec((1, count, width), lambda g, w: (jnp.maximum(g - sends, 0), 0, 0)),
            ],
            scratch_shapes=[pltpu.VMEM((count, held), BF16)],
        ),
        out_shape=[
            jax.ShapeDtypeStruct((sends, count, width), BF16),
            jax.ShapeDtypeStruct((keeps, count, width), BF16),
        ],
        compiler_params=params(),
        cost_estimate=cost(0, count * total * width * 2),
    )(where, mine, *owns, *others, gate, *values)


def chosen(place, values, names):
    out = values[0]
    for at in range(1, len(values)):
        if names[at] != names[0]:
            out = jnp.where(place == at, values[at], out)
    return out


class Relay:
    def __init__(self, own, count, reps):
        self.count, self.reps = count, reps
        self.place, self.rank = lax.axis_index("patch"), lax.axis_index("rep")
        self.ahead, self.back = {0: own}, {0: own}

    def step(self, k, *held):
        count = self.count
        ahead, back = self.ahead[k - 1], self.back[k - 1]
        if held:
            ahead, back = after(ahead, *held), after(back, *held)
        self.ahead[k] = lax.ppermute(ahead, "patch", [(i, i + 1) for i in range(k - 1, count - 1)])
        self.back[k] = lax.ppermute(back, "patch", [(i + 1, i) for i in range(count - k)])

    def sent(self, k):
        return self.ahead[k], self.back[k]

    def brought(self, t, cut=None):
        values, owners = [], []
        for at in range(self.count):
            comes = sorted([(k, 0) for k in range(1, at + 1)] + [(k, 1) for k in range(1, self.count - at)])
            k, side = comes[t - 1]
            values.append(self.back[k] if side else self.ahead[k])
            owners.append(at + k if side else at - k)
        owner = sum(jnp.where(self.place == at, owners[at], 0) for at in range(self.count))
        candidates = []
        for value in values:
            if not any(value is other for other in candidates):
                candidates.append(value)
        fenced = lax.optimization_barrier(tuple(candidates))
        at_of = [[value is other for other in candidates].index(True) for value in values]
        cuts = [(0, values[0].shape[1])] if cut is None else [(0, cut), (cut, values[0].shape[1])]
        chosen_cuts = [chosen(self.place, [fenced[at][:, low:high] for at in at_of], at_of) for low, high in cuts]
        parts = [(self.rank, chosen_cuts)]
        for offset in range(1, self.reps):
            pairs = [(a, (a + offset) % self.reps) for a in range(self.reps)]
            swapped, held = [], ()
            for piece in chosen_cuts:
                swapped.append(lax.ppermute(after(piece, *held) if held else piece, "rep", pairs))
                held = (swapped[-1],)
            parts.append(((self.rank - offset) % self.reps, swapped))
        return owner, parts


def body(hidden, modulation, gate, w_qkv, stale_kv, w_out, key_lists):
    count, reps = lax.axis_size("patch"), lax.axis_size("rep")
    tps, secs = lax.axis_size("tp"), lax.axis_size("sec")
    place, rank = lax.axis_index("patch"), lax.axis_index("rep")
    tp_index, sec_index = lax.axis_index("tp"), lax.axis_index("sec")
    rows, model_width = hidden.shape[1], hidden.shape[2]
    heads = w_out.shape[1] // HEAD_DIM
    patch_blocks = rows // BLOCK
    unit_heads = heads // 3 if heads % 3 == 0 else 1
    units = heads // unit_heads
    small_units = max(1, units // 3)
    group_units = [list(range(units - small_units)), list(range(units - small_units, units))]
    group_heads = [len(members) * unit_heads for members in group_units]
    group_first = [0, group_heads[0]]
    states = hidden[0]
    w_qkv, stale_kv, w_out = w_qkv[0], stale_kv[0], w_out[0]
    last = count - 1
    shard_rows = w_qkv.shape[0]
    depth, out_depth = shard_rows // reps, w_out.shape[0] // reps
    width = 3 * HEAD_DIM

    relative = jnp.where(key_lists >= 0, key_lists - (place - 1) * patch_blocks, -1)
    window_ids = jnp.arange(3 * patch_blocks, dtype=jnp.int32)
    hits = jnp.any(relative[:, :, None] == window_ids[None, None, :], axis=1).astype(F32)
    hits = jnp.repeat(hits, BLOCK, axis=1).reshape(patch_blocks, 3, rows)
    before, fresh, behind = (hits[:, i][:, None, :] for i in range(3))
    odd = place % 2 == 1
    even_mask, odd_mask = jnp.where(odd, before, behind), jnp.where(odd, behind, before)
    at_end = (place == 0) | (place == last)
    to_inner = [(0, 1), (last, last - 1)]
    to_end = [(1, 0), (last - 1, last)]
    inner_flag = jnp.where(at_end, 0, 1).astype(jnp.int32).reshape(1)
    host_flag = ((place == 1) | (place == last - 1)).astype(jnp.int32).reshape(1)

    inner = range(1, last)
    pairs = [(i, i + 1) for i in range(last)] + [(i + 1, i) for i in range(last)]
    even_pairs = [(a, b) for a, b in pairs if min(a, b) % 2 == 0 and b in inner]
    odd_pairs = [(a, b) for a, b in pairs if min(a, b) % 2 == 1 and b in inner]
    stale, even, other = [None] * units, [None] * units, [None] * units

    def send_even(unit, *held):
        even[unit] = lax.ppermute(after(stale[unit], *held), "patch", even_pairs)

    def send_other(unit, *held):
        other[unit] = lax.ppermute(after(stale[unit], *held), "patch", odd_pairs)

    def qkv_relay(group, *held):
        source = after(w_qkv, *held) if held else w_qkv
        at = (rank * depth, group_first[group] * width)
        own = lax.dynamic_slice(source, at, (depth, group_heads[group] * width))
        if group == 1:
            own = jnp.concatenate([own, own_out.reshape(depth, out_cols)], axis=1)
        return Relay(own, count, reps)

    def columns(owner, part):
        return lax.dynamic_slice_in_dim(modulated, owner * shard_rows + part * depth, depth, 1)

    def term_of(owner, part, piece):
        return columns(owner, part), piece

    def add_terms(acc, terms):
        for left, right in terms:
            acc += jnp.dot(left, right, preferred_element_type=F32)
        return acc

    out_shape = (out_depth, w_out.shape[1])
    out_cols = out_depth * w_out.shape[1] // depth
    small_cols = group_heads[1] * width
    large = qkv_relay(0)
    large.step(1)
    inputs = states.astype(F32)
    centered = inputs - jnp.mean(inputs, axis=-1, keepdims=True)
    variance = jnp.mean(centered * centered, axis=-1, keepdims=True)
    normed = centered * lax.rsqrt(variance + 1e-06)
    modulated = (normed * (1.0 + modulation[0, 1]) + modulation[0, 0]).astype(BF16)
    for at in range(units):
        stale[at] = stale_group(stale_kv, at * unit_heads, unit_heads)
    modulated, stale[0] = lax.optimization_barrier((modulated, stale[0]))

    own_columns = lax.dynamic_slice_in_dim(modulated, place * shard_rows, shard_rows, 1)
    accs = [None, None]
    come = [[], []]
    far_mask = lax.ppermute(after(jnp.where(place == 0, behind, before), *large.sent(1)), "patch", to_inner)
    share = model_width // (tps * secs)
    residual = lax.dynamic_slice_in_dim(states, (tp_index * secs + sec_index) * share, share, 1)
    got_all = []
    for offset in range(1, secs):
        target = (1 + offset) % secs
        sent = lax.dynamic_slice_in_dim(states, (tp_index * secs + target) * share, share, 1)
        got = lax.ppermute(sent, "sec", [(1, target)])
        got_all.append(got)
        residual = jnp.where(sec_index == target, got, residual)

    def swaps(group, at):
        return [piece[0] for _, piece in come[group][at][1][1:]] if 0 <= at < len(come[group]) else []

    def given(*items):
        return [item for item in items if item is not None]

    def at_or_none(items, at):
        return items[at] if at < len(items) else None

    def own_half(group, at):
        owner, parts = come[group][at]
        return [term_of(owner, parts[0][0], parts[0][1][0])]

    def other_half(group, at):
        owner, parts = come[group][at]
        return [term_of(owner, part, piece[0]) for part, piece in parts[1:]]

    come[0].append(large.brought(1))
    send_even(0, *large.sent(1))
    for k in range(2, count):
        held = [modulated] + got_all if k == 2 else [accs[0]] + swaps(0, k - 3)
        if k == 3:
            held += [even[0], far_mask, residual]
        large.step(k, *held)
        come[0].append(large.brought(k))
        if k == 2:
            accs[0] = own_terms(after(own_columns, *large.sent(1)), w_qkv, 0, group_heads[0])
            if units > 1:
                send_even(1, *large.sent(2))
                send_other(0, *large.sent(2))
        elif k == 3:
            accs[0] = add_terms(accs[0], own_half(0, 0) + own_half(0, 1) + other_half(0, 0))

    own_out = lax.dynamic_slice_in_dim(after(w_out, *large.sent(1)), rank * out_depth, out_depth, 0)
    small = qkv_relay(1, *large.sent(min(2, last)))
    small.step(
        1, *large.sent(last), accs[0], *swaps(0, last - 2), *given(at_or_none(even, 1), at_or_none(other, 0))
    )
    come[1].append(small.brought(1, small_cols if last == 1 else None))
    for at in range(2, last - 1):
        accs[0] = add_terms(accs[0], own_half(0, at) + other_half(0, at - 1))
    accs[1] = own_terms(after(own_columns, *large.sent(last)), w_qkv, group_first[1], group_heads[1])
    final_terms = own_half(0, last - 1) + other_half(0, last - 1)
    if last > 1:
        final_terms = other_half(0, last - 2) + final_terms
    queries_0 = finish(accs[0], final_terms)
    far_queries_0 = lax.ppermute(queries_0[0], "patch", to_inner)
    queries_1 = None

    def near_part(group, at, fresh_too, sides, flags, prior):
        queries, keys, values = (queries_0, queries_1)[group]
        here = (at * unit_heads, unit_heads)
        return windows(flags, queries, here, [(keys, values, fresh)] if fresh_too else [], sides, prior)

    def sides_of(unit_at):
        return [(even[unit_at], even_mask), (other[unit_at], odd_mask)]

    first_large = group_units[0]
    inner_flags = jnp.concatenate([inner_flag, inner_flag])
    near = [None] * units
    near[0] = near_part(0, 0, True, sides_of(0), inner_flags, ())
    for k in range(2, count):
        if k == 2:
            held = [accs[1], *queries_0]
        elif k == 3:
            held = [far_queries_0, near[0][0]]
        else:
            held = swaps(1, k - 4)
        small.step(k, *held)
        come[1].append(small.brought(k, small_cols if k == last else None))
        if k == 2 and units > 1:
            send_other(1, *small.sent(2))
    all_even = [(a, b) for a, b in pairs if min(a, b) % 2 == 0]
    for at in range(units):
        if at in group_units[1]:
            even[at] = lax.ppermute(after(stale[at], *small.sent(last), *come[1][-1][1][0][1]), "patch", all_even)
        elif even[at] is None:
            send_even(at, *small.sent(last))
        if other[at] is None:
            send_other(at, *small.sent(last), *come[1][-1][1][0][1])

    stale_full = stale_group(after(stale_kv, *small.sent(1)), 0, group_heads[0])
    far_num, far_tot = foreign_part(host_flag, far_queries_0, 0, group_heads[0], stale_full, far_mask)
    back_num = lax.ppermute(far_num, "patch", to_end)
    back_tot = lax.ppermute(far_tot, "patch", to_end)
    for at, unit_at in enumerate(first_large):
        if unit_at:
            part = near_part(0, at, True, sides_of(unit_at)[:1], inner_flag, ())
            near[unit_at] = near_part(0, at, False, sides_of(unit_at)[1:], inner_flag, tuple(part))

    early = []
    for at in range(last - 2):
        early += own_half(1, at) + other_half(1, at)
    if early:
        accs[1] = add_terms(accs[1], [(left, right[:, :small_cols]) for left, right in early])
    final_terms = []
    for at in range(max(last - 2, 0), last):
        final_terms += own_half(1, at) + other_half(1, at)
    fenced = lax.optimization_barrier((accs[1], back_num, back_tot, near[first_large[-1]][0]))
    queries_1 = finish(fenced[0], final_terms)
    always = jnp.concatenate([jnp.ones((1,), jnp.int32), inner_flag])
    for at, unit_at in enumerate(group_units[1]):
        near[unit_at] = near_part(1, at, True, sides_of(unit_at), always, ())
    done = normalise([near[at] for at in group_units[0]], (back_num, back_tot))

    out_mine, out_others, out_owns, owners = [own_out], [[] for _ in range(reps - 1)], [], [place]
    for owner, parts in come[1]:
        owners.append(owner)
        for at, (_, piece) in enumerate(parts):
            rows_out = (piece[0][:, small_cols:] if len(piece) == 1 else piece[1]).reshape(out_shape)
            if at == 0:
                out_mine.append(rows_out)
            else:
                out_others[at - 1].append(rows_out)
    out_mine = jnp.stack(out_mine)
    out_others = [jnp.stack(items) for items in out_others]
    for offset in range(1, reps):
        out_owns.append(lax.dynamic_slice_in_dim(w_out, (rank - offset) % reps * out_depth, out_depth, 0))

    per = count // (tps * secs)
    order = [
        (block * secs + (sec_index + offset) % secs) * per + at
        for offset in list(range(1, secs)) + [0]
        for block in range(tps)
        for at in range(per)
    ]
    turns = [sum(jnp.where(owners[t] == column, t, 0) for t in range(count)) for column in order]
    where = jnp.stack(turns + [jnp.maximum(turn - 1, 0) for turn in turns] + order + [rank]).astype(jnp.int32)
    gate_blocks = gate.reshape(count, 1, w_out.shape[1])
    keeps = tps * per
    results = []
    start, last_keep, last_got = 0, [], []
    for share_rows in ROW_CHUNKS:
        chunk = rows * share_rows // sum(ROW_CHUNKS)
        sends, keep = branch(
            where, out_mine, out_owns, out_others, gate_blocks, after(done, *last_keep),
            [near[unit_at] for unit_at in group_units[1]], start, chunk, keeps,
        )
        got = [keep]
        last_keep = [keep]
        for offset in range(1, secs):
            sent = sends[(offset - 1) * keeps : offset * keeps]
            got.append(lax.ppermute(sent, "sec", [(i, (i + offset) % secs) for i in range(secs)]))

        def block_of(index):
            return sum(lax.dynamic_slice_in_dim(part, index * per, per, 0).astype(F32) for part in got)

        others = []
        for offset in range(1, tps):
            sent = after(block_of((tp_index + offset) % tps).astype(BF16), *last_got)
            others.append(lax.ppermute(sent, "tp", [(i, (i + offset) % tps) for i in range(tps)]))
        last_got = others
        result = block_of(tp_index) + sum(part.astype(F32) for part in others)
        result = jnp.moveaxis(result, 0, 1).reshape(chunk, share)
        results.append((result + residual[start : start + chunk].astype(F32)).astype(BF16))
        start += chunk
    return jnp.concatenate(results, axis=0)


def solution(mesh):
    return jax.shard_map(
        body,
        mesh=mesh,
        in_specs=(
            P("sec", ("rep", "patch"), None),
            P("sec", None, None),
            P("sec", None),
            P("sec", "patch", "tp"),
            P("sec", ("rep", "patch"), "tp"),
            P("sec", "tp", "patch"),
            P(("rep", "patch"), None),
        ),
        out_specs=P(("rep", "patch"), ("tp", "sec")),
        check_vma=False,
    )
```

```python
import functools
import math

import jax
import jax.numpy as jnp
from jax import lax
from jax.experimental import pallas as pl
from jax.experimental.pallas import tpu as pltpu
from jax.sharding import PartitionSpec as P

HEAD_DIM = 128
BLOCK = 128
QUERY_TILE = 512
ROW_CHUNKS = (1, 1)
ROW_TILE = 512
VMEM_LIMIT = 28 * 1024 * 1024
F32 = jnp.float32
BF16 = jnp.bfloat16


def after(value, *others):
    return lax.optimization_barrier((value,) + others)[0]


def params():
    return pltpu.CompilerParams(vmem_limit_bytes=VMEM_LIMIT)


def cost(flops, moved, exps=0):
    return pl.CostEstimate(flops=int(flops), bytes_accessed=int(moved), transcendentals=int(exps))


def unit(value):
    return value * lax.rsqrt(jnp.mean(value * value, axis=-1, keepdims=True) + 1e-06)


def stale_kernel(in_ref, out_ref):
    out_ref[:, :HEAD_DIM] = unit(in_ref[:, :HEAD_DIM].astype(F32)).astype(BF16)
    out_ref[:, HEAD_DIM:] = in_ref[:, HEAD_DIM:]


def stale_group(stale, first, heads):
    rows = stale.shape[0]
    return pl.pallas_call(
        stale_kernel,
        grid=(heads,),
        in_specs=[pl.BlockSpec((rows, 2 * HEAD_DIM), lambda h: (0, first + h))],
        out_specs=pl.BlockSpec((rows, 2 * HEAD_DIM), lambda h: (0, h)),
        out_shape=jax.ShapeDtypeStruct((rows, heads * 2 * HEAD_DIM), BF16),
        compiler_params=params(),
        cost_estimate=cost(rows * heads * 512, rows * heads * 1024),
    )(stale)


def own_kernel(left_ref, right_ref, out_ref):
    out_ref[...] = jnp.dot(left_ref[...], right_ref[...], preferred_element_type=F32)


def own_terms(left, right, first, heads):
    rows, depth = left.shape
    width = 3 * HEAD_DIM
    return pl.pallas_call(
        own_kernel,
        grid=(heads,),
        in_specs=[
            pl.BlockSpec((rows, depth), lambda h: (0, 0)),
            pl.BlockSpec((depth, width), lambda h: (0, first + h)),
        ],
        out_specs=pl.BlockSpec((rows, width), lambda h: (0, h)),
        out_shape=jax.ShapeDtypeStruct((rows, heads * width), F32),
        compiler_params=params(),
        cost_estimate=cost(2 * rows * depth * heads * width, rows * heads * width * 4 + depth * (rows + heads * width) * 2),
    )(left, right)


def finish_kernel(terms, *refs):
    total = refs[2 * terms][...]
    for at in range(terms):
        total += jnp.dot(refs[at][...], refs[terms + at][...], preferred_element_type=F32)
    q_ref, k_ref, v_ref = refs[2 * terms + 1 :]
    q_ref[...] = unit(total[:, :HEAD_DIM]).astype(BF16)
    k_ref[...] = unit(total[:, HEAD_DIM : 2 * HEAD_DIM]).astype(BF16)
    v_ref[...] = total[:, 2 * HEAD_DIM :].astype(BF16)


def finish(acc, terms):
    lefts, rights = [left for left, _ in terms], [right for _, right in terms]
    width, rows = 3 * HEAD_DIM, acc.shape[0]
    heads, tile = acc.shape[1] // width, rows
    depth = sum(left.shape[1] for left in lefts)
    out = pl.BlockSpec((tile, HEAD_DIM), lambda h, i: (i, h))
    return pl.pallas_call(
        functools.partial(finish_kernel, len(terms)),
        grid=(heads, rows // tile),
        in_specs=[pl.BlockSpec((tile, left.shape[1]), lambda h, i: (i, 0)) for left in lefts]
        + [pl.BlockSpec((right.shape[0], width), lambda h, i: (0, h)) for right in rights]
        + [pl.BlockSpec((tile, width), lambda h, i: (i, h))],
        out_specs=[out] * 3,
        out_shape=[jax.ShapeDtypeStruct((rows, heads * HEAD_DIM), BF16)] * 3,
        compiler_params=params(),
        cost_estimate=cost(2 * rows * depth * heads * width, rows * heads * width * 6),
    )(*lefts, *rights, acc)


def weigh(query, key, mask):
    tile, keys = query.shape[0], key.shape[0]
    scores = lax.dot_general(query, key, (((1,), (1,)), ((), ())), preferred_element_type=F32)
    exponents = jnp.exp(scores * (1.0 / math.sqrt(HEAD_DIM)))
    exponents = exponents.reshape(tile // BLOCK, BLOCK, keys) * mask
    return exponents.reshape(tile, keys).astype(BF16)


def with_ones(value):
    return jnp.concatenate([value, jnp.ones(value.shape, value.dtype)], axis=1)


def window_kernel(fresh, sides, prior, flag_ref, q_ref, *refs):
    num_ref, tot_ref = refs[-2:]
    query = q_ref[...]
    shape = (query.shape[0], 2 * HEAD_DIM)

    def terms(first, windows):
        both = jnp.zeros(shape, F32)
        for at in range(first, first + windows):
            k_ref, v_ref, m_ref = refs[3 * at : 3 * at + 3]
            weights = weigh(query, k_ref[...], m_ref[...])
            both += jnp.dot(weights, with_ones(v_ref[...]), preferred_element_type=F32)
        return both[:, :HEAD_DIM], both[:, HEAD_DIM:]

    if prior:
        num, tot = refs[3 * (fresh + sides)][...], refs[3 * (fresh + sides) + 1][...]
    if fresh:
        num, tot = terms(0, fresh)
    num_ref[...] = num
    tot_ref[...] = tot
    for side in range(sides):

        @pl.when(flag_ref[side] == 1)
        def _(side=side):
            more, more_tot = terms(fresh + side, 1)
            num_ref[...] += more
            tot_ref[...] += more_tot


def windows(flag, queries, here, fresh, sides, prior):
    first, heads = here
    rows, cols = queries.shape[0], heads * HEAD_DIM
    query = pl.BlockSpec((QUERY_TILE, HEAD_DIM), lambda h, i, f: (i, first + h))
    tile = pl.BlockSpec((QUERY_TILE, HEAD_DIM), lambda h, i, f: (i, h))
    specs, values = [], []
    for keys, vals, mask in fresh:
        block = pl.BlockSpec((keys.shape[0], HEAD_DIM), lambda h, i, f: (0, first + h))
        specs += [block, block]
        values += [keys, vals, mask]
        specs.append(pl.BlockSpec((QUERY_TILE // BLOCK, 1, keys.shape[0]), lambda h, i, f: (i, 0, 0)))
    for stale, mask, at in sides:
        specs.append(pl.BlockSpec((stale.shape[0], HEAD_DIM), lambda h, i, f, at=at: (0, 2 * (at + h))))
        specs.append(pl.BlockSpec((stale.shape[0], HEAD_DIM), lambda h, i, f, at=at: (0, 2 * (at + h) + 1)))
        specs.append(pl.BlockSpec((QUERY_TILE // BLOCK, 1, stale.shape[0]), lambda h, i, f: (i, 0, 0)))
        values += [stale, stale, mask]
    count = len(fresh) + len(sides)
    return pl.pallas_call(
        functools.partial(window_kernel, len(fresh), len(sides), len(prior)),
        grid_spec=pltpu.PrefetchScalarGridSpec(
            num_scalar_prefetch=1,
            grid=(heads, rows // QUERY_TILE),
            in_specs=[query] + specs + [tile] * len(prior),
            out_specs=[tile, tile],
        ),
        out_shape=[jax.ShapeDtypeStruct((rows, cols), F32)] * 2,
        compiler_params=params(),
        cost_estimate=cost(6 * count * rows * rows * cols, rows * cols * 14 * count, count * rows * rows * heads),
    )(flag, queries, *values, *prior)


def foreign_kernel(flag_ref, q_ref, k_ref, v_ref, mask_ref, num_ref, tot_ref):
    head = pl.program_id(1)

    @pl.when(head == 0)
    def _():
        tot_ref[...] = jnp.zeros_like(tot_ref)

    @pl.when(flag_ref[0] == 1)
    def _():
        value = v_ref[...]
        weights = weigh(q_ref[...], k_ref[...], mask_ref[...])
        num_ref[...] = jnp.dot(weights, value, preferred_element_type=F32).astype(BF16)
        sums = lax.dot_general(
            jnp.ones((8, weights.shape[1]), BF16), weights, (((1,), (1,)), ((), ())), preferred_element_type=F32
        )
        row = lax.broadcasted_iota(jnp.int32, sums.shape, 0)
        tot_ref[...] = jnp.where(row == head, sums, tot_ref[...])

    @pl.when(flag_ref[0] != 1)
    def _():
        num_ref[...] = jnp.zeros_like(num_ref)


def foreign_part(flag, queries, first, heads, stale, mask):
    rows, cols, window = queries.shape[0], heads * HEAD_DIM, stale.shape[0]
    query = pl.BlockSpec((QUERY_TILE, HEAD_DIM), lambda i, h, f: (i, h))
    tile = pl.BlockSpec((QUERY_TILE, HEAD_DIM), lambda i, h, f: (i, h))
    return pl.pallas_call(
        foreign_kernel,
        grid_spec=pltpu.PrefetchScalarGridSpec(
            num_scalar_prefetch=1,
            grid=(rows // QUERY_TILE, heads),
            in_specs=[
                query,
                pl.BlockSpec((window, HEAD_DIM), lambda i, h, f: (0, 2 * (first + h))),
                pl.BlockSpec((window, HEAD_DIM), lambda i, h, f: (0, 2 * (first + h) + 1)),
                pl.BlockSpec((QUERY_TILE // BLOCK, 1, window), lambda i, h, f: (i, 0, 0)),
            ],
            out_specs=[tile, pl.BlockSpec((8, QUERY_TILE), lambda i, h, f: (0, i))],
        ),
        out_shape=[jax.ShapeDtypeStruct((rows, cols), BF16), jax.ShapeDtypeStruct((8, rows), F32)],
        compiler_params=params(),
        cost_estimate=cost(4 * rows * window * cols, rows * cols * 8, rows * window * heads),
    )(flag, queries, stale, stale, mask)


def normalise_into(att_ref, column, near_refs, num_ref=None, tot_ref=None):
    totals = None if tot_ref is None else jnp.transpose(tot_ref[...])
    at = 0
    for n_ref, t_ref in near_refs:
        for head in range(n_ref.shape[1] // HEAD_DIM):
            cols = slice(head * HEAD_DIM, (head + 1) * HEAD_DIM)
            num, tot = n_ref[:, cols], t_ref[:, cols]
            if num_ref is not None:
                num += num_ref[:, at * HEAD_DIM : (at + 1) * HEAD_DIM].astype(F32)
                tot += totals[:, at : at + 1]
            att_ref[:, (column + at) * HEAD_DIM : (column + at + 1) * HEAD_DIM] = (num / tot).astype(BF16)
            at += 1


def normalise_kernel(*refs):
    near_refs = [(refs[2 * at], refs[2 * at + 1]) for at in range((len(refs) - 3) // 2)]
    normalise_into(refs[-1], 0, near_refs, refs[-3], refs[-2])


def normalise(near, far):
    num, tot = far
    rows, cols = num.shape
    tile = 512
    specs, values = [], []
    for pair in near:
        specs += [pl.BlockSpec((tile, pair[0].shape[1]), lambda i: (i, 0))] * 2
        values += list(pair)
    return pl.pallas_call(
        normalise_kernel,
        grid=(rows // tile,),
        in_specs=specs + [pl.BlockSpec((tile, cols), lambda i: (i, 0)), pl.BlockSpec((8, tile), lambda i: (0, i))],
        out_specs=pl.BlockSpec((tile, cols), lambda i: (i, 0)),
        out_shape=jax.ShapeDtypeStruct((rows, cols), BF16),
        compiler_params=params(),
        cost_estimate=cost(rows * cols * 4, rows * cols * 12),
    )(*values, num, tot)


def branch_kernel(near, keeps, parts, where_ref, *refs):
    step, steps = pl.program_id(0), pl.num_programs(0)
    mine_ref, own_refs, other_refs = refs[0], refs[1:parts], refs[parts : 2 * parts - 1]
    g_ref, done_ref = refs[2 * parts - 1 : 2 * parts + 1]
    rest = refs[2 * parts + 1 :]
    send_ref, keep_ref, att_ref = rest[-3:]
    att_ref = att_ref.at[pl.program_id(1)]

    @pl.when(step == 0)
    def _():
        att_ref[:, : done_ref.shape[1]] = done_ref[...]
        near_refs = [(rest[2 * at], rest[2 * at + 1]) for at in range(near)]
        normalise_into(att_ref, done_ref.shape[1] // HEAD_DIM, near_refs)

    attended = att_ref[...]
    depth = attended.shape[1] // parts
    rank = where_ref[3 * steps]
    is_own = where_ref[step] == 0

    def left_of(part):
        left = attended[:, :depth]
        for other in range(1, parts):
            left = jnp.where(part == other, attended[:, other * depth : (other + 1) * depth], left)
        return left

    term = jnp.dot(left_of(rank), mine_ref[0], preferred_element_type=F32)
    for offset in range(1, parts):
        right = jnp.where(is_own, own_refs[offset - 1][...], other_refs[offset - 1][0])
        term += jnp.dot(left_of(lax.rem(rank + parts - offset, parts)), right, preferred_element_type=F32)
    result = (term * g_ref[0]).astype(BF16)
    stays = step >= steps - keeps

    @pl.when(stays)
    def _():
        keep_ref[0] = result

    @pl.when(jnp.logical_not(stays))
    def _():
        send_ref[0] = result


def branch(where, mine, owns, others, gate, done, near, first, count, keeps):
    total, depth, width = mine.shape
    tile = ROW_TILE if count % ROW_TILE == 0 and first % ROW_TILE == 0 else BLOCK
    start, tiles = first // tile, count // tile
    sends = total - keeps

    def row_tile(g, i, w):
        return start + jnp.where(g == 0, i, tiles - 1), 0

    specs, values = [pl.BlockSpec((tile, done.shape[1]), row_tile)], [done]
    for num, tot in near:
        spec = pl.BlockSpec((tile, num.shape[1]), row_tile)
        specs += [spec, spec]
        values += [num, tot]
    parts = len(others) + 1
    held = depth * parts
    return pl.pallas_call(
        functools.partial(branch_kernel, len(near), keeps, parts),
        grid_spec=pltpu.PrefetchScalarGridSpec(
            num_scalar_prefetch=1,
            grid=(total, tiles),
            in_specs=[pl.BlockSpec((1, depth, width), lambda g, i, w: (w[g], 0, 0))]
            + [pl.BlockSpec((depth, width), lambda g, i, w: (0, 0))] * len(owns)
            + [pl.BlockSpec((1, depth, width), lambda g, i, w: (w[total + g], 0, 0))] * len(others)
            + [pl.BlockSpec((1, 1, width), lambda g, i, w: (w[2 * total + g], 0, 0))]
            + specs,
            out_specs=[
                pl.BlockSpec((1, tile, width), lambda g, i, w: (jnp.minimum(g, sends - 1), jnp.where(g < sends, i, tiles - 1), 0)),
                pl.BlockSpec((1, tile, width), lambda g, i, w: (jnp.maximum(g - sends, 0), jnp.where(g < sends, 0, i), 0)),
            ],
            scratch_shapes=[pltpu.VMEM((tiles, tile, held), BF16)],
        ),
        out_shape=[
            jax.ShapeDtypeStruct((sends, count, width), BF16),
            jax.ShapeDtypeStruct((keeps, count, width), BF16),
        ],
        compiler_params=params(),
        cost_estimate=cost(2 * count * held * total * width, held * total * width * 2 + count * total * width * 2),
    )(where, mine, *owns, *others, gate, *values)


def chosen(place, values, names):
    out = values[0]
    for at in range(1, len(values)):
        if names[at] != names[0]:
            out = jnp.where(place == at, values[at], out)
    return out


class Relay:
    def __init__(self, own, count, reps):
        self.count, self.reps = count, reps
        self.place, self.rank = lax.axis_index("patch"), lax.axis_index("rep")
        self.ahead, self.back = {0: own}, {0: own}

    def step(self, k, *held):
        count = self.count
        ahead, back = self.ahead[k - 1], self.back[k - 1]
        if held:
            ahead, back = after(ahead, *held), after(back, *held)
        self.ahead[k] = lax.ppermute(ahead, "patch", [(i, i + 1) for i in range(k - 1, count - 1)])
        self.back[k] = lax.ppermute(back, "patch", [(i + 1, i) for i in range(count - k)])

    def sent(self, k):
        return self.ahead[k], self.back[k]

    def brought(self, t, cut=None):
        values, owners = [], []
        for at in range(self.count):
            comes = sorted([(k, 0) for k in range(1, at + 1)] + [(k, 1) for k in range(1, self.count - at)])
            k, side = comes[t - 1]
            values.append(self.back[k] if side else self.ahead[k])
            owners.append(at + k if side else at - k)
        owner = sum(jnp.where(self.place == at, owners[at], 0) for at in range(self.count))
        candidates = []
        for value in values:
            if not any(value is other for other in candidates):
                candidates.append(value)
        fenced = lax.optimization_barrier(tuple(candidates))
        at_of = [[value is other for other in candidates].index(True) for value in values]
        cuts = [(0, values[0].shape[1])] if cut is None else [(0, cut), (cut, values[0].shape[1])]
        chosen_cuts = [chosen(self.place, [fenced[at][:, low:high] for at in at_of], at_of) for low, high in cuts]
        parts = [(self.rank, chosen_cuts)]
        for offset in range(1, self.reps):
            pairs = [(a, (a + offset) % self.reps) for a in range(self.reps)]
            swapped, held = [], ()
            for piece in chosen_cuts:
                swapped.append(lax.ppermute(after(piece, *held) if held else piece, "rep", pairs))
                held = (swapped[-1],)
            parts.append(((self.rank - offset) % self.reps, swapped))
        return owner, parts


def body(hidden, modulation, gate, w_qkv, stale_kv, w_out, key_lists):
    count, reps = lax.axis_size("patch"), lax.axis_size("rep")
    tps, secs = lax.axis_size("tp"), lax.axis_size("sec")
    place, rank = lax.axis_index("patch"), lax.axis_index("rep")
    tp_index, sec_index = lax.axis_index("tp"), lax.axis_index("sec")
    rows, model_width = hidden.shape[1], hidden.shape[2]
    heads = w_out.shape[1] // HEAD_DIM
    patch_blocks = rows // BLOCK
    unit_heads = heads // 3 if heads % 3 == 0 else 1
    units = heads // unit_heads
    small_units = max(1, units // 3)
    group_units = [list(range(units - small_units)), list(range(units - small_units, units))]
    group_heads = [len(members) * unit_heads for members in group_units]
    group_first = [0, group_heads[0]]
    states = hidden[0]
    w_qkv, stale_kv, w_out = w_qkv[0], stale_kv[0], w_out[0]
    last = count - 1
    shard_rows = w_qkv.shape[0]
    depth, out_depth = shard_rows // reps, w_out.shape[0] // reps
    width = 3 * HEAD_DIM

    relative = jnp.where(key_lists >= 0, key_lists - (place - 1) * patch_blocks, -1)
    window_ids = jnp.arange(3 * patch_blocks, dtype=jnp.int32)
    hits = jnp.any(relative[:, :, None] == window_ids[None, None, :], axis=1).astype(F32)
    hits = jnp.repeat(hits, BLOCK, axis=1).reshape(patch_blocks, 3, rows)
    before, fresh, behind = (hits[:, i][:, None, :] for i in range(3))
    odd = place % 2 == 1
    even_mask, odd_mask = jnp.where(odd, before, behind), jnp.where(odd, behind, before)
    at_end = (place == 0) | (place == last)
    to_inner = [(0, 1), (last, last - 1)]
    to_end = [(1, 0), (last - 1, last)]
    inner_flag = jnp.where(at_end, 0, 1).astype(jnp.int32).reshape(1)
    host_flag = ((place == 1) | (place == last - 1)).astype(jnp.int32).reshape(1)

    inner = range(1, last)
    pairs = [(i, i + 1) for i in range(last)] + [(i + 1, i) for i in range(last)]
    even_pairs = [(a, b) for a, b in pairs if min(a, b) % 2 == 0 and b in inner]
    odd_pairs = [(a, b) for a, b in pairs if min(a, b) % 2 == 1 and b in inner]
    stale, even, other = [None] * units, [None] * units, [None] * units

    def send_even(unit, *held):
        even[unit] = lax.ppermute(after(stale[unit], *held), "patch", even_pairs)

    def send_other(unit, *held):
        other[unit] = lax.ppermute(after(stale[unit], *held), "patch", odd_pairs)

    def qkv_relay(group, *held):
        source = after(w_qkv, *held) if held else w_qkv
        at = (rank * depth, group_first[group] * width)
        own = lax.dynamic_slice(source, at, (depth, group_heads[group] * width))
        if group == 1:
            own = jnp.concatenate([own, own_out.reshape(depth, out_cols)], axis=1)
        return Relay(own, count, reps)

    def columns(owner, part):
        return lax.dynamic_slice_in_dim(modulated, owner * shard_rows + part * depth, depth, 1)

    def term_of(owner, part, piece):
        return columns(owner, part), piece

    def add_terms(acc, terms):
        for left, right in terms:
            acc += jnp.dot(left, right, preferred_element_type=F32)
        return acc

    out_shape = (out_depth, w_out.shape[1])
    out_cols = out_depth * w_out.shape[1] // depth
    small_cols = group_heads[1] * width
    large = qkv_relay(0)
    large.step(1)
    inputs = states.astype(F32)
    centered = inputs - jnp.mean(inputs, axis=-1, keepdims=True)
    variance = jnp.mean(centered * centered, axis=-1, keepdims=True)
    normed = centered * lax.rsqrt(variance + 1e-06)
    modulated = (normed * (1.0 + modulation[0, 1]) + modulation[0, 0]).astype(BF16)
    for at in range(units):
        stale[at] = stale_group(stale_kv, at * unit_heads, unit_heads)
    modulated, stale[0] = lax.optimization_barrier((modulated, stale[0]))

    own_columns = lax.dynamic_slice_in_dim(modulated, place * shard_rows, shard_rows, 1)
    accs = [None, None]
    come = [[], []]
    far_mask = lax.ppermute(jnp.where(place == 0, behind, before), "patch", to_inner)
    share = model_width // (tps * secs)
    residual = lax.dynamic_slice_in_dim(states, (tp_index * secs + sec_index) * share, share, 1)
    got_all = []
    for offset in range(1, secs):
        target = (1 + offset) % secs
        sent = lax.dynamic_slice_in_dim(states, (tp_index * secs + target) * share, share, 1)
        got = lax.ppermute(sent, "sec", [(1, target)])
        got_all.append(got)
        residual = jnp.where(sec_index == target, got, residual)

    def swaps(group, at):
        return [piece[0] for _, piece in come[group][at][1][1:]] if 0 <= at < len(come[group]) else []

    def given(*items):
        return [item for item in items if item is not None]

    def at_or_none(items, at):
        return items[at] if at < len(items) else None

    def own_half(group, at):
        owner, parts = come[group][at]
        return [term_of(owner, parts[0][0], parts[0][1][0])]

    def other_half(group, at):
        owner, parts = come[group][at]
        return [term_of(owner, part, piece[0]) for part, piece in parts[1:]]

    come[0].append(large.brought(1))
    send_even(0, *large.sent(1))
    for k in range(2, count):
        held = [modulated, far_mask] + got_all if k == 2 else [accs[0]] + swaps(0, k - 3)
        if k == 3:
            held += [even[0], residual]
        large.step(k, *held)
        come[0].append(large.brought(k))
        if k == 2:
            accs[0] = own_terms(after(own_columns, *large.sent(1)), w_qkv, 0, group_heads[0])
            if units > 1:
                send_even(1, *large.sent(2))
                send_other(0, *large.sent(2))
        elif k == 3:
            accs[0] = add_terms(accs[0], own_half(0, 0) + own_half(0, 1) + other_half(0, 0))

    own_out = lax.dynamic_slice_in_dim(after(w_out, *large.sent(1)), rank * out_depth, out_depth, 0)
    small = qkv_relay(1, *large.sent(min(2, last)))
    small.step(
        1, *large.sent(last), accs[0], *swaps(0, last - 2), *given(at_or_none(even, 1), at_or_none(other, 0))
    )
    come[1].append(small.brought(1, small_cols if last == 1 else None))
    for at in range(2, last - 1):
        accs[0] = add_terms(accs[0], own_half(0, at) + other_half(0, at - 1))
    accs[1] = own_terms(after(own_columns, *large.sent(last)), w_qkv, group_first[1], group_heads[1])
    final_terms = own_half(0, last - 1) + other_half(0, last - 1)
    if last > 1:
        final_terms = other_half(0, last - 2) + final_terms
    queries_0 = finish(accs[0], final_terms)
    far_queries_0 = lax.ppermute(queries_0[0], "patch", to_inner)
    queries_1 = None

    def near_part(group, at, fresh_too, sides, flags, prior):
        queries, keys, values = (queries_0, queries_1)[group]
        here = (at * unit_heads, unit_heads)
        return windows(flags, queries, here, [(keys, values, fresh)] if fresh_too else [], sides, prior)

    def sides_of(unit_at):
        late = unit_at > 0
        stale_at = (unit_at - 1) * unit_heads if late else 0
        return [(even[unit_at], even_mask, 0), (other[1 if late else 0], odd_mask, stale_at)]

    all_even = [(a, b) for a, b in pairs if min(a, b) % 2 == 0]
    late_stale = stale_group(after(stale_kv, *large.sent(last)), unit_heads, heads - unit_heads)

    def late_exchanges(held):
        for at in group_units[1]:
            even[at] = lax.ppermute(after(stale[at], *held), "patch", all_even)
        for at in group_units[0]:
            if even[at] is None:
                send_even(at, *held)
        other[1] = lax.ppermute(after(late_stale, *held), "patch", odd_pairs)

    first_large = group_units[0]
    inner_flags = jnp.concatenate([inner_flag, inner_flag])
    near = [None] * units
    near[0] = near_part(0, 0, True, sides_of(0), inner_flags, ())
    for k in range(2, count):
        if k == 2:
            held = [accs[1], *queries_0]
        elif k == 3:
            held = [far_queries_0, near[0][0]]
        else:
            held = swaps(1, k - 4)
        small.step(k, *held)
        come[1].append(small.brought(k, small_cols if k == last else None))
        if k == 2:
            late_exchanges(small.sent(2))
    if other[1] is None:
        late_exchanges(small.sent(last))

    stale_full = stale_group(after(stale_kv, *small.sent(1)), 0, group_heads[0])
    far_num, far_tot = foreign_part(host_flag, far_queries_0, 0, group_heads[0], stale_full, far_mask)
    come_last = come[1][-1][1][0][1]
    exchanged = [even[at] for at in group_units[1]] + [other[1]]
    back_num = lax.ppermute(after(far_num, *small.sent(last), *come_last, *exchanged), "patch", to_end)
    back_tot = lax.ppermute(far_tot, "patch", to_end)
    for at, unit_at in enumerate(first_large):
        if unit_at:
            part = near_part(0, at, True, sides_of(unit_at)[:1], inner_flag, ())
            near[unit_at] = near_part(0, at, False, sides_of(unit_at)[1:], inner_flag, tuple(part))

    early = []
    for at in range(last - 2):
        early += own_half(1, at) + other_half(1, at)
    if early:
        accs[1] = add_terms(accs[1], [(left, right[:, :small_cols]) for left, right in early])
    final_terms = []
    for at in range(max(last - 2, 0), last):
        final_terms += own_half(1, at) + other_half(1, at)
    fenced = lax.optimization_barrier((accs[1], back_tot, near[first_large[-1]][0]))
    queries_1 = finish(fenced[0], final_terms)
    always = jnp.concatenate([jnp.ones((1,), jnp.int32), inner_flag])
    for at, unit_at in enumerate(group_units[1]):
        near[unit_at] = near_part(1, at, True, sides_of(unit_at), always, ())
    done = normalise([near[at] for at in group_units[0]], (back_num, back_tot))

    out_mine, out_others, out_owns, owners = [own_out], [[] for _ in range(reps - 1)], [], [place]
    for owner, parts in come[1]:
        owners.append(owner)
        for at, (_, piece) in enumerate(parts):
            rows_out = (piece[0][:, small_cols:] if len(piece) == 1 else piece[1]).reshape(out_shape)
            if at == 0:
                out_mine.append(rows_out)
            else:
                out_others[at - 1].append(rows_out)
    out_mine = jnp.stack(out_mine)
    out_others = [jnp.stack(items) for items in out_others]
    for offset in range(1, reps):
        out_owns.append(lax.dynamic_slice_in_dim(w_out, (rank - offset) % reps * out_depth, out_depth, 0))

    per = count // (tps * secs)
    order = [
        (block * secs + (sec_index + offset) % secs) * per + at
        for offset in list(range(1, secs)) + [0]
        for block in range(tps)
        for at in range(per)
    ]
    turns = [sum(jnp.where(owners[t] == column, t, 0) for t in range(count)) for column in order]
    where = jnp.stack(turns + [jnp.maximum(turn - 1, 0) for turn in turns] + order + [rank]).astype(jnp.int32)
    gate_blocks = gate.reshape(count, 1, w_out.shape[1])
    keeps = tps * per
    results = []
    start, last_keep = 0, []
    for share_rows in ROW_CHUNKS:
        chunk = rows * share_rows // sum(ROW_CHUNKS)
        sends, keep = branch(
            where, out_mine, out_owns, out_others, gate_blocks, after(done, *last_keep),
            [near[unit_at] for unit_at in group_units[1]], start, chunk, keeps,
        )
        got = [keep]
        last_keep = [keep]
        for offset in range(1, secs):
            sent = sends[(offset - 1) * keeps : offset * keeps]
            got.append(lax.ppermute(sent, "sec", [(i, (i + offset) % secs) for i in range(secs)]))

        def block_of(index):
            return sum(lax.dynamic_slice_in_dim(part, index * per, per, 0).astype(F32) for part in got)

        others = []
        for offset in range(1, tps):
            sent = block_of((tp_index + offset) % tps).astype(BF16)
            others.append(lax.ppermute(sent, "tp", [(i, (i + offset) % tps) for i in range(tps)]))
        result = block_of(tp_index) + sum(part.astype(F32) for part in others)
        result = jnp.moveaxis(result, 0, 1).reshape(chunk, share)
        results.append((result + residual[start : start + chunk].astype(F32)).astype(BF16))
        start += chunk
    return jnp.concatenate(results, axis=0)


def solution(mesh):
    return jax.shard_map(
        body,
        mesh=mesh,
        in_specs=(
            P("sec", ("rep", "patch"), None),
            P("sec", None, None),
            P("sec", None),
            P("sec", "patch", "tp"),
            P("sec", ("rep", "patch"), "tp"),
            P("sec", "tp", "patch"),
            P(("rep", "patch"), None),
        ),
        out_specs=P(("rep", "patch"), ("tp", "sec")),
        check_vma=False,
    )
```

```python
import functools
import math

import jax
import jax.numpy as jnp
from jax import lax
from jax.experimental import pallas as pl
from jax.experimental.pallas import tpu as pltpu
from jax.sharding import PartitionSpec as P

HEAD_DIM = 128
BLOCK = 128
QUERY_TILE = 512
ROW_CHUNKS = (1, 1)
ROW_TILE = 512
COST_SCALE = 0.2
VMEM_LIMIT = 28 * 1024 * 1024
F32 = jnp.float32
BF16 = jnp.bfloat16


def after(value, *others):
    return lax.optimization_barrier((value,) + others)[0]


def params():
    return pltpu.CompilerParams(vmem_limit_bytes=VMEM_LIMIT)


def cost(flops, moved, exps=0):
    scale = COST_SCALE
    return pl.CostEstimate(flops=int(flops * scale), bytes_accessed=int(moved * scale), transcendentals=int(exps * scale))


def unit(value):
    return value * lax.rsqrt(jnp.mean(value * value, axis=-1, keepdims=True) + 1e-06)


def stale_kernel(in_ref, out_ref):
    out_ref[:, :HEAD_DIM] = unit(in_ref[:, :HEAD_DIM].astype(F32)).astype(BF16)
    out_ref[:, HEAD_DIM:] = in_ref[:, HEAD_DIM:]


def stale_group(stale, first, heads):
    rows = stale.shape[0]
    return pl.pallas_call(
        stale_kernel,
        grid=(heads,),
        in_specs=[pl.BlockSpec((rows, 2 * HEAD_DIM), lambda h: (0, first + h))],
        out_specs=pl.BlockSpec((rows, 2 * HEAD_DIM), lambda h: (0, h)),
        out_shape=jax.ShapeDtypeStruct((rows, heads * 2 * HEAD_DIM), BF16),
        compiler_params=params(),
        cost_estimate=cost(rows * heads * 512, rows * heads * 1024),
    )(stale)


def own_kernel(left_ref, right_ref, out_ref):
    out_ref[...] = jnp.dot(left_ref[...], right_ref[...], preferred_element_type=F32)


def own_terms(left, right, first, heads):
    rows, depth = left.shape
    width = 3 * HEAD_DIM
    return pl.pallas_call(
        own_kernel,
        grid=(heads,),
        in_specs=[
            pl.BlockSpec((rows, depth), lambda h: (0, 0)),
            pl.BlockSpec((depth, width), lambda h: (0, first + h)),
        ],
        out_specs=pl.BlockSpec((rows, width), lambda h: (0, h)),
        out_shape=jax.ShapeDtypeStruct((rows, heads * width), F32),
        compiler_params=params(),
        cost_estimate=cost(2 * rows * depth * heads * width, rows * heads * width * 4 + depth * (rows + heads * width) * 2),
    )(left, right)


def finish_kernel(terms, *refs):
    total = refs[2 * terms][...]
    for at in range(terms):
        total += jnp.dot(refs[at][...], refs[terms + at][...], preferred_element_type=F32)
    q_ref, k_ref, v_ref = refs[2 * terms + 1 :]
    q_ref[...] = unit(total[:, :HEAD_DIM]).astype(BF16)
    k_ref[...] = unit(total[:, HEAD_DIM : 2 * HEAD_DIM]).astype(BF16)
    v_ref[...] = total[:, 2 * HEAD_DIM :].astype(BF16)


def finish(acc, terms):
    lefts, rights = [left for left, _ in terms], [right for _, right in terms]
    width, rows = 3 * HEAD_DIM, acc.shape[0]
    heads, tile = acc.shape[1] // width, rows
    depth = sum(left.shape[1] for left in lefts)
    out = pl.BlockSpec((tile, HEAD_DIM), lambda h, i: (i, h))
    return pl.pallas_call(
        functools.partial(finish_kernel, len(terms)),
        grid=(heads, rows // tile),
        in_specs=[pl.BlockSpec((tile, left.shape[1]), lambda h, i: (i, 0)) for left in lefts]
        + [pl.BlockSpec((right.shape[0], width), lambda h, i: (0, h)) for right in rights]
        + [pl.BlockSpec((tile, width), lambda h, i: (i, h))],
        out_specs=[out] * 3,
        out_shape=[jax.ShapeDtypeStruct((rows, heads * HEAD_DIM), BF16)] * 3,
        compiler_params=params(),
        cost_estimate=cost(2 * rows * depth * heads * width, rows * heads * width * 6),
    )(*lefts, *rights, acc)


def weigh(query, key, mask):
    tile, keys = query.shape[0], key.shape[0]
    scores = lax.dot_general(query, key, (((1,), (1,)), ((), ())), preferred_element_type=F32)
    exponents = jnp.exp(scores * (1.0 / math.sqrt(HEAD_DIM)))
    exponents = exponents.reshape(tile // BLOCK, BLOCK, keys) * mask
    return exponents.reshape(tile, keys).astype(BF16)


def with_ones(value):
    return jnp.concatenate([value, jnp.ones(value.shape, value.dtype)], axis=1)


def window_kernel(fresh, sides, prior, flag_ref, q_ref, *refs):
    num_ref, tot_ref = refs[-2:]
    query = q_ref[...]
    shape = (query.shape[0], 2 * HEAD_DIM)

    def terms(first, windows):
        both = jnp.zeros(shape, F32)
        for at in range(first, first + windows):
            k_ref, v_ref, m_ref = refs[3 * at : 3 * at + 3]
            weights = weigh(query, k_ref[...], m_ref[...])
            both += jnp.dot(weights, with_ones(v_ref[...]), preferred_element_type=F32)
        return both[:, :HEAD_DIM], both[:, HEAD_DIM:]

    if prior:
        num, tot = refs[3 * (fresh + sides)][...], refs[3 * (fresh + sides) + 1][...]
    if fresh:
        num, tot = terms(0, fresh)
    num_ref[...] = num
    tot_ref[...] = tot
    for side in range(sides):

        @pl.when(flag_ref[side] == 1)
        def _(side=side):
            more, more_tot = terms(fresh + side, 1)
            num_ref[...] += more
            tot_ref[...] += more_tot


def windows(flag, queries, here, fresh, sides, prior):
    first, heads = here
    rows, cols = queries.shape[0], heads * HEAD_DIM
    query = pl.BlockSpec((QUERY_TILE, HEAD_DIM), lambda h, i, f: (i, first + h))
    tile = pl.BlockSpec((QUERY_TILE, HEAD_DIM), lambda h, i, f: (i, h))
    specs, values = [], []
    for keys, vals, mask in fresh:
        block = pl.BlockSpec((keys.shape[0], HEAD_DIM), lambda h, i, f: (0, first + h))
        specs += [block, block]
        values += [keys, vals, mask]
        specs.append(pl.BlockSpec((QUERY_TILE // BLOCK, 1, keys.shape[0]), lambda h, i, f: (i, 0, 0)))
    for stale, mask, at in sides:
        specs.append(pl.BlockSpec((stale.shape[0], HEAD_DIM), lambda h, i, f, at=at: (0, 2 * (at + h))))
        specs.append(pl.BlockSpec((stale.shape[0], HEAD_DIM), lambda h, i, f, at=at: (0, 2 * (at + h) + 1)))
        specs.append(pl.BlockSpec((QUERY_TILE // BLOCK, 1, stale.shape[0]), lambda h, i, f: (i, 0, 0)))
        values += [stale, stale, mask]
    count = len(fresh) + len(sides)
    return pl.pallas_call(
        functools.partial(window_kernel, len(fresh), len(sides), len(prior)),
        grid_spec=pltpu.PrefetchScalarGridSpec(
            num_scalar_prefetch=1,
            grid=(heads, rows // QUERY_TILE),
            in_specs=[query] + specs + [tile] * len(prior),
            out_specs=[tile, tile],
        ),
        out_shape=[jax.ShapeDtypeStruct((rows, cols), F32)] * 2,
        compiler_params=params(),
        cost_estimate=cost(6 * count * rows * rows * cols, rows * cols * 14 * count, count * rows * rows * heads),
    )(flag, queries, *values, *prior)


def foreign_kernel(flag_ref, q_ref, k_ref, v_ref, mask_ref, num_ref, tot_ref):
    head = pl.program_id(1)

    @pl.when(head == 0)
    def _():
        tot_ref[...] = jnp.zeros_like(tot_ref)

    @pl.when(flag_ref[0] == 1)
    def _():
        value = v_ref[...]
        weights = weigh(q_ref[...], k_ref[...], mask_ref[...])
        num_ref[...] = jnp.dot(weights, value, preferred_element_type=F32).astype(BF16)
        sums = lax.dot_general(
            jnp.ones((8, weights.shape[1]), BF16), weights, (((1,), (1,)), ((), ())), preferred_element_type=F32
        )
        row = lax.broadcasted_iota(jnp.int32, sums.shape, 0)
        tot_ref[...] = jnp.where(row == head, sums, tot_ref[...])

    @pl.when(flag_ref[0] != 1)
    def _():
        num_ref[...] = jnp.zeros_like(num_ref)


def foreign_part(flag, queries, first, heads, stale, mask):
    rows, cols, window = queries.shape[0], heads * HEAD_DIM, stale.shape[0]
    query = pl.BlockSpec((QUERY_TILE, HEAD_DIM), lambda i, h, f: (i, h))
    tile = pl.BlockSpec((QUERY_TILE, HEAD_DIM), lambda i, h, f: (i, h))
    return pl.pallas_call(
        foreign_kernel,
        grid_spec=pltpu.PrefetchScalarGridSpec(
            num_scalar_prefetch=1,
            grid=(rows // QUERY_TILE, heads),
            in_specs=[
                query,
                pl.BlockSpec((window, HEAD_DIM), lambda i, h, f: (0, 2 * (first + h))),
                pl.BlockSpec((window, HEAD_DIM), lambda i, h, f: (0, 2 * (first + h) + 1)),
                pl.BlockSpec((QUERY_TILE // BLOCK, 1, window), lambda i, h, f: (i, 0, 0)),
            ],
            out_specs=[tile, pl.BlockSpec((8, QUERY_TILE), lambda i, h, f: (0, i))],
        ),
        out_shape=[jax.ShapeDtypeStruct((rows, cols), BF16), jax.ShapeDtypeStruct((8, rows), F32)],
        compiler_params=params(),
        cost_estimate=cost(4 * rows * window * cols, rows * cols * 8, rows * window * heads),
    )(flag, queries, stale, stale, mask)


def normalise_into(att_ref, column, near_refs, num_ref=None, tot_ref=None):
    totals = None if tot_ref is None else jnp.transpose(tot_ref[...])
    at = 0
    for n_ref, t_ref in near_refs:
        for head in range(n_ref.shape[1] // HEAD_DIM):
            cols = slice(head * HEAD_DIM, (head + 1) * HEAD_DIM)
            num, tot = n_ref[:, cols], t_ref[:, cols]
            if num_ref is not None:
                num += num_ref[:, at * HEAD_DIM : (at + 1) * HEAD_DIM].astype(F32)
                tot += totals[:, at : at + 1]
            att_ref[:, (column + at) * HEAD_DIM : (column + at + 1) * HEAD_DIM] = (num / tot).astype(BF16)
            at += 1


def normalise_kernel(*refs):
    near_refs = [(refs[2 * at], refs[2 * at + 1]) for at in range((len(refs) - 3) // 2)]
    normalise_into(refs[-1], 0, near_refs, refs[-3], refs[-2])


def normalise(near, far):
    num, tot = far
    rows, cols = num.shape
    tile = 512
    specs, values = [], []
    for pair in near:
        specs += [pl.BlockSpec((tile, pair[0].shape[1]), lambda i: (i, 0))] * 2
        values += list(pair)
    return pl.pallas_call(
        normalise_kernel,
        grid=(rows // tile,),
        in_specs=specs + [pl.BlockSpec((tile, cols), lambda i: (i, 0)), pl.BlockSpec((8, tile), lambda i: (0, i))],
        out_specs=pl.BlockSpec((tile, cols), lambda i: (i, 0)),
        out_shape=jax.ShapeDtypeStruct((rows, cols), BF16),
        compiler_params=params(),
        cost_estimate=cost(rows * cols * 4, rows * cols * 12),
    )(*values, num, tot)


def branch_kernel(near, keeps, parts, where_ref, *refs):
    step, steps = pl.program_id(0), pl.num_programs(0)
    mine_ref, own_refs, other_refs = refs[0], refs[1:parts], refs[parts : 2 * parts - 1]
    g_ref, done_ref = refs[2 * parts - 1 : 2 * parts + 1]
    rest = refs[2 * parts + 1 :]
    send_ref, keep_ref, att_ref = rest[-3:]
    att_ref = att_ref.at[pl.program_id(1)]

    @pl.when(step == 0)
    def _():
        att_ref[:, : done_ref.shape[1]] = done_ref[...]
        near_refs = [(rest[2 * at], rest[2 * at + 1]) for at in range(near)]
        normalise_into(att_ref, done_ref.shape[1] // HEAD_DIM, near_refs)

    attended = att_ref[...]
    depth = attended.shape[1] // parts
    rank = where_ref[3 * steps]
    is_own = where_ref[step] == 0

    def left_of(part):
        left = attended[:, :depth]
        for other in range(1, parts):
            left = jnp.where(part == other, attended[:, other * depth : (other + 1) * depth], left)
        return left

    term = jnp.dot(left_of(rank), mine_ref[0], preferred_element_type=F32)
    for offset in range(1, parts):
        right = jnp.where(is_own, own_refs[offset - 1][...], other_refs[offset - 1][0])
        term += jnp.dot(left_of(lax.rem(rank + parts - offset, parts)), right, preferred_element_type=F32)
    result = (term * g_ref[0]).astype(BF16)
    stays = step >= steps - keeps

    @pl.when(stays)
    def _():
        keep_ref[0] = result

    @pl.when(jnp.logical_not(stays))
    def _():
        send_ref[0] = result


def branch(where, mine, owns, others, gate, done, near, first, count, keeps):
    total, depth, width = mine.shape
    tile = ROW_TILE if count % ROW_TILE == 0 and first % ROW_TILE == 0 else BLOCK
    start, tiles = first // tile, count // tile
    sends = total - keeps

    def row_tile(g, i, w):
        return start + jnp.where(g == 0, i, tiles - 1), 0

    specs, values = [pl.BlockSpec((tile, done.shape[1]), row_tile)], [done]
    for num, tot in near:
        spec = pl.BlockSpec((tile, num.shape[1]), row_tile)
        specs += [spec, spec]
        values += [num, tot]
    parts = len(others) + 1
    held = depth * parts
    return pl.pallas_call(
        functools.partial(branch_kernel, len(near), keeps, parts),
        grid_spec=pltpu.PrefetchScalarGridSpec(
            num_scalar_prefetch=1,
            grid=(total, tiles),
            in_specs=[pl.BlockSpec((1, depth, width), lambda g, i, w: (w[g], 0, 0))]
            + [pl.BlockSpec((depth, width), lambda g, i, w: (0, 0))] * len(owns)
            + [pl.BlockSpec((1, depth, width), lambda g, i, w: (w[total + g], 0, 0))] * len(others)
            + [pl.BlockSpec((1, 1, width), lambda g, i, w: (w[2 * total + g], 0, 0))]
            + specs,
            out_specs=[
                pl.BlockSpec((1, tile, width), lambda g, i, w: (jnp.minimum(g, sends - 1), jnp.where(g < sends, i, tiles - 1), 0)),
                pl.BlockSpec((1, tile, width), lambda g, i, w: (jnp.maximum(g - sends, 0), jnp.where(g < sends, 0, i), 0)),
            ],
            scratch_shapes=[pltpu.VMEM((tiles, tile, held), BF16)],
        ),
        out_shape=[
            jax.ShapeDtypeStruct((sends, count, width), BF16),
            jax.ShapeDtypeStruct((keeps, count, width), BF16),
        ],
        compiler_params=params(),
        cost_estimate=cost(2 * count * held * total * width, held * total * width * 2 + count * total * width * 2),
    )(where, mine, *owns, *others, gate, *values)


def chosen(place, values, names):
    out = values[0]
    for at in range(1, len(values)):
        if names[at] != names[0]:
            out = jnp.where(place == at, values[at], out)
    return out


class Relay:
    def __init__(self, own, count, reps):
        self.count, self.reps = count, reps
        self.place, self.rank = lax.axis_index("patch"), lax.axis_index("rep")
        self.ahead, self.back = {0: own}, {0: own}

    def step(self, k, *held):
        count = self.count
        ahead, back = self.ahead[k - 1], self.back[k - 1]
        if held:
            ahead, back = after(ahead, *held), after(back, *held)
        self.ahead[k] = lax.ppermute(ahead, "patch", [(i, i + 1) for i in range(k - 1, count - 1)])
        self.back[k] = lax.ppermute(back, "patch", [(i + 1, i) for i in range(count - k)])

    def sent(self, k):
        return self.ahead[k], self.back[k]

    def brought(self, t, cut=None):
        values, owners = [], []
        for at in range(self.count):
            comes = sorted([(k, 0) for k in range(1, at + 1)] + [(k, 1) for k in range(1, self.count - at)])
            k, side = comes[t - 1]
            values.append(self.back[k] if side else self.ahead[k])
            owners.append(at + k if side else at - k)
        owner = sum(jnp.where(self.place == at, owners[at], 0) for at in range(self.count))
        candidates = []
        for value in values:
            if not any(value is other for other in candidates):
                candidates.append(value)
        fenced = lax.optimization_barrier(tuple(candidates))
        at_of = [[value is other for other in candidates].index(True) for value in values]
        cuts = [(0, values[0].shape[1])] if cut is None else [(0, cut), (cut, values[0].shape[1])]
        chosen_cuts = [chosen(self.place, [fenced[at][:, low:high] for at in at_of], at_of) for low, high in cuts]
        parts = [(self.rank, chosen_cuts)]
        for offset in range(1, self.reps):
            pairs = [(a, (a + offset) % self.reps) for a in range(self.reps)]
            swapped, held = [], ()
            for piece in chosen_cuts:
                swapped.append(lax.ppermute(after(piece, *held) if held else piece, "rep", pairs))
                held = (swapped[-1],)
            parts.append(((self.rank - offset) % self.reps, swapped))
        return owner, parts


def body(hidden, modulation, gate, w_qkv, stale_kv, w_out, key_lists):
    count, reps = lax.axis_size("patch"), lax.axis_size("rep")
    tps, secs = lax.axis_size("tp"), lax.axis_size("sec")
    place, rank = lax.axis_index("patch"), lax.axis_index("rep")
    tp_index, sec_index = lax.axis_index("tp"), lax.axis_index("sec")
    rows, model_width = hidden.shape[1], hidden.shape[2]
    heads = w_out.shape[1] // HEAD_DIM
    patch_blocks = rows // BLOCK
    unit_heads = heads // 3 if heads % 3 == 0 else 1
    units = heads // unit_heads
    small_units = max(1, units // 3)
    group_units = [list(range(units - small_units)), list(range(units - small_units, units))]
    group_heads = [len(members) * unit_heads for members in group_units]
    group_first = [0, group_heads[0]]
    states = hidden[0]
    w_qkv, stale_kv, w_out = w_qkv[0], stale_kv[0], w_out[0]
    last = count - 1
    shard_rows = w_qkv.shape[0]
    depth, out_depth = shard_rows // reps, w_out.shape[0] // reps
    width = 3 * HEAD_DIM

    relative = jnp.where(key_lists >= 0, key_lists - (place - 1) * patch_blocks, -1)
    window_ids = jnp.arange(3 * patch_blocks, dtype=jnp.int32)
    hits = jnp.any(relative[:, :, None] == window_ids[None, None, :], axis=1).astype(F32)
    hits = jnp.repeat(hits, BLOCK, axis=1).reshape(patch_blocks, 3, rows)
    before, fresh, behind = (hits[:, i][:, None, :] for i in range(3))
    odd = place % 2 == 1
    even_mask, odd_mask = jnp.where(odd, before, behind), jnp.where(odd, behind, before)
    at_end = (place == 0) | (place == last)
    to_inner = [(0, 1), (last, last - 1)]
    to_end = [(1, 0), (last - 1, last)]
    inner_flag = jnp.where(at_end, 0, 1).astype(jnp.int32).reshape(1)
    host_flag = ((place == 1) | (place == last - 1)).astype(jnp.int32).reshape(1)

    inner = range(1, last)
    pairs = [(i, i + 1) for i in range(last)] + [(i + 1, i) for i in range(last)]
    even_pairs = [(a, b) for a, b in pairs if min(a, b) % 2 == 0 and b in inner]
    odd_pairs = [(a, b) for a, b in pairs if min(a, b) % 2 == 1 and b in inner]
    stale, even, other = [None] * units, [None] * units, [None] * units

    def send_even(unit, *held):
        even[unit] = lax.ppermute(after(stale[unit], *held), "patch", even_pairs)

    def send_other(unit, *held):
        other[unit] = lax.ppermute(after(stale[unit], *held), "patch", odd_pairs)

    def qkv_relay(group, *held):
        source = after(w_qkv, *held) if held else w_qkv
        at = (rank * depth, group_first[group] * width)
        own = lax.dynamic_slice(source, at, (depth, group_heads[group] * width))
        if group == 1:
            own = jnp.concatenate([own, own_out.reshape(depth, out_cols)], axis=1)
        return Relay(own, count, reps)

    def columns(owner, part):
        return lax.dynamic_slice_in_dim(ready, owner * shard_rows + part * depth, depth, 1)

    def term_of(owner, part, piece):
        return columns(owner, part), piece

    def add_terms(acc, terms):
        for left, right in terms:
            acc += jnp.dot(left, right, preferred_element_type=F32)
        return acc

    out_shape = (out_depth, w_out.shape[1])
    out_cols = out_depth * w_out.shape[1] // depth
    small_cols = group_heads[1] * width
    large = qkv_relay(0)
    large.step(1)
    inputs = states.astype(F32)
    centered = inputs - jnp.mean(inputs, axis=-1, keepdims=True)
    variance = jnp.mean(centered * centered, axis=-1, keepdims=True)
    normed = centered * lax.rsqrt(variance + 1e-06)
    modulated = (normed * (1.0 + modulation[0, 1]) + modulation[0, 0]).astype(BF16)
    for at in range(units):
        stale[at] = stale_group(stale_kv, at * unit_heads, unit_heads)
    modulated, stale[0] = lax.optimization_barrier((modulated, stale[0]))

    ready = after(modulated, *large.sent(1))
    own_columns = lax.dynamic_slice_in_dim(ready, place * shard_rows, shard_rows, 1)
    accs = [None, None]
    come = [[], []]
    far_mask = lax.ppermute(jnp.where(place == 0, behind, before), "patch", to_inner)
    share = model_width // (tps * secs)
    residual = lax.dynamic_slice_in_dim(states, (tp_index * secs + sec_index) * share, share, 1)
    got_all = []
    for offset in range(1, secs):
        target = (1 + offset) % secs
        sent = lax.dynamic_slice_in_dim(states, (tp_index * secs + target) * share, share, 1)
        got = lax.ppermute(sent, "sec", [(1, target)])
        got_all.append(got)
        residual = jnp.where(sec_index == target, got, residual)

    def swaps(group, at):
        return [piece[0] for _, piece in come[group][at][1][1:]] if 0 <= at < len(come[group]) else []

    def given(*items):
        return [item for item in items if item is not None]

    def at_or_none(items, at):
        return items[at] if at < len(items) else None

    def own_half(group, at):
        owner, parts = come[group][at]
        return [term_of(owner, parts[0][0], parts[0][1][0])]

    def other_half(group, at):
        owner, parts = come[group][at]
        return [term_of(owner, part, piece[0]) for part, piece in parts[1:]]

    come[0].append(large.brought(1))
    send_even(0, *large.sent(1))
    for k in range(2, count):
        held = [modulated, far_mask] + got_all if k == 2 else [accs[0]] + swaps(0, k - 3)
        if k == 3:
            held += [even[0], residual]
        large.step(k, *held)
        come[0].append(large.brought(k))
        if k == 2:
            accs[0] = own_terms(after(own_columns, *large.sent(1)), w_qkv, 0, group_heads[0])
            if units > 1:
                send_even(1, *large.sent(2))
                send_other(0, *large.sent(2))
        elif k == 3:
            accs[0] = add_terms(accs[0], own_half(0, 0) + own_half(0, 1) + other_half(0, 0))

    own_out = lax.dynamic_slice_in_dim(after(w_out, *large.sent(1)), rank * out_depth, out_depth, 0)
    small = qkv_relay(1, *large.sent(min(2, last)))
    small.step(
        1, *large.sent(last), accs[0], *swaps(0, last - 2), *given(at_or_none(even, 1), at_or_none(other, 0))
    )
    come[1].append(small.brought(1, small_cols if last == 1 else None))
    for at in range(2, last - 1):
        accs[0] = add_terms(accs[0], own_half(0, at) + other_half(0, at - 1))
    accs[1] = own_terms(after(own_columns, *large.sent(last)), w_qkv, group_first[1], group_heads[1])
    final_terms = own_half(0, last - 1) + other_half(0, last - 1)
    if last > 1:
        final_terms = other_half(0, last - 2) + final_terms
    queries_0 = finish(accs[0], final_terms)
    far_queries_0 = lax.ppermute(queries_0[0], "patch", to_inner)
    queries_1 = None

    def near_part(group, at, fresh_too, sides, flags, prior):
        queries, keys, values = (queries_0, queries_1)[group]
        here = (at * unit_heads, unit_heads)
        return windows(flags, queries, here, [(keys, values, fresh)] if fresh_too else [], sides, prior)

    def sides_of(unit_at):
        late = unit_at > 0
        stale_at = (unit_at - 1) * unit_heads if late else 0
        return [(even[unit_at], even_mask, 0), (other[1 if late else 0], odd_mask, stale_at)]

    all_even = [(a, b) for a, b in pairs if min(a, b) % 2 == 0]
    late_stale = stale_group(after(stale_kv, *large.sent(last)), unit_heads, heads - unit_heads)

    def late_exchanges(held):
        for at in group_units[1]:
            even[at] = lax.ppermute(after(stale[at], *held, *swaps(1, 0)), "patch", all_even)
        for at in group_units[0]:
            if even[at] is None:
                send_even(at, *held)
        other[1] = lax.ppermute(after(late_stale, *held), "patch", odd_pairs)

    first_large = group_units[0]
    inner_flags = jnp.concatenate([inner_flag, inner_flag])
    near = [None] * units
    near[0] = near_part(0, 0, True, sides_of(0), inner_flags, ())
    for k in range(2, count):
        if k == 2:
            held = [accs[1]]
        elif k == 3:
            held = [*queries_0, near[0][0]]
        else:
            held = swaps(1, k - 4)
        small.step(k, *held)
        come[1].append(small.brought(k, small_cols if k == last else None))
        if k == 2:
            late_exchanges(small.sent(2))
    if other[1] is None:
        late_exchanges(small.sent(last))

    stale_full = stale_group(after(stale_kv, *small.sent(1)), 0, group_heads[0])
    far_num, far_tot = foreign_part(host_flag, far_queries_0, 0, group_heads[0], stale_full, far_mask)
    come_last = come[1][-1][1][0][1]
    exchanged = [even[at] for at in group_units[1]] + [other[1]]
    back_num = lax.ppermute(after(far_num, *small.sent(last), *come_last, *exchanged), "patch", to_end)
    back_tot = lax.ppermute(after(far_tot, *small.sent(last)), "patch", to_end)
    for at, unit_at in enumerate(first_large):
        if unit_at:
            part = near_part(0, at, True, sides_of(unit_at)[:1], inner_flag, ())
            near[unit_at] = near_part(0, at, False, sides_of(unit_at)[1:], inner_flag, tuple(part))

    early = []
    for at in range(last - 2):
        early += own_half(1, at) + other_half(1, at)
    if early:
        accs[1] = add_terms(accs[1], [(left, right[:, :small_cols]) for left, right in early])
    final_terms = []
    for at in range(max(last - 2, 0), last):
        final_terms += own_half(1, at) + other_half(1, at)
    fenced = lax.optimization_barrier((accs[1], back_tot, near[first_large[-1]][0]))
    queries_1 = finish(fenced[0], final_terms)
    always = jnp.concatenate([jnp.ones((1,), jnp.int32), inner_flag])
    for at, unit_at in enumerate(group_units[1]):
        near[unit_at] = near_part(1, at, True, sides_of(unit_at), always, ())
    done = normalise([near[at] for at in group_units[0]], (back_num, back_tot))

    out_mine, out_others, out_owns, owners = [own_out], [[] for _ in range(reps - 1)], [], [place]
    for owner, parts in come[1]:
        owners.append(owner)
        for at, (_, piece) in enumerate(parts):
            rows_out = (piece[0][:, small_cols:] if len(piece) == 1 else piece[1]).reshape(out_shape)
            if at == 0:
                out_mine.append(rows_out)
            else:
                out_others[at - 1].append(rows_out)
    out_mine = jnp.stack(out_mine)
    out_others = [jnp.stack(items) for items in out_others]
    for offset in range(1, reps):
        out_owns.append(lax.dynamic_slice_in_dim(w_out, (rank - offset) % reps * out_depth, out_depth, 0))

    per = count // (tps * secs)
    order = [
        (block * secs + (sec_index + offset) % secs) * per + at
        for offset in list(range(1, secs)) + [0]
        for block in range(tps)
        for at in range(per)
    ]
    turns = [sum(jnp.where(owners[t] == column, t, 0) for t in range(count)) for column in order]
    where = jnp.stack(turns + [jnp.maximum(turn - 1, 0) for turn in turns] + order + [rank]).astype(jnp.int32)
    gate_blocks = gate.reshape(count, 1, w_out.shape[1])
    keeps = tps * per
    results = []
    start = 0
    for share_rows in ROW_CHUNKS:
        chunk = rows * share_rows // sum(ROW_CHUNKS)
        sends, keep = branch(
            where, out_mine, out_owns, out_others, gate_blocks, done,
            [near[unit_at] for unit_at in group_units[1]], start, chunk, keeps,
        )
        got = [keep]
        for offset in range(1, secs):
            sent = sends[(offset - 1) * keeps : offset * keeps]
            got.append(lax.ppermute(sent, "sec", [(i, (i + offset) % secs) for i in range(secs)]))

        def block_of(index):
            return sum(lax.dynamic_slice_in_dim(part, index * per, per, 0).astype(F32) for part in got)

        others = []
        for offset in range(1, tps):
            sent = block_of((tp_index + offset) % tps).astype(BF16)
            others.append(lax.ppermute(sent, "tp", [(i, (i + offset) % tps) for i in range(tps)]))
        result = block_of(tp_index) + sum(part.astype(F32) for part in others)
        result = jnp.moveaxis(result, 0, 1).reshape(chunk, share)
        results.append((result + residual[start : start + chunk].astype(F32)).astype(BF16))
        start += chunk
    return jnp.concatenate(results, axis=0)


def solution(mesh):
    return jax.shard_map(
        body,
        mesh=mesh,
        in_specs=(
            P("sec", ("rep", "patch"), None),
            P("sec", None, None),
            P("sec", None),
            P("sec", "patch", "tp"),
            P("sec", ("rep", "patch"), "tp"),
            P("sec", "tp", "patch"),
            P(("rep", "patch"), None),
        ),
        out_specs=P(("rep", "patch"), ("tp", "sec")),
        check_vma=False,
    )
```

```python
import functools
import math

import jax
import jax.numpy as jnp
from jax import lax
from jax.experimental import pallas as pl
from jax.experimental.pallas import tpu as pltpu
from jax.sharding import PartitionSpec as P

HEAD_DIM = 128
BLOCK = 128
QUERY_TILE = 512
ROW_CHUNKS = (1, 1)
ROW_TILE = 512
COST_SCALE = 0.2
VMEM_LIMIT = 28 * 1024 * 1024
F32 = jnp.float32
BF16 = jnp.bfloat16


def after(value, *others):
    return lax.optimization_barrier((value,) + others)[0]


def params():
    return pltpu.CompilerParams(vmem_limit_bytes=VMEM_LIMIT)


def cost(flops, moved, exps=0):
    scale = COST_SCALE
    return pl.CostEstimate(flops=int(flops * scale), bytes_accessed=int(moved * scale), transcendentals=int(exps * scale))


def unit(value):
    return value * lax.rsqrt(jnp.mean(value * value, axis=-1, keepdims=True) + 1e-06)


def stale_kernel(in_ref, out_ref):
    out_ref[:, :HEAD_DIM] = unit(in_ref[:, :HEAD_DIM].astype(F32)).astype(BF16)
    out_ref[:, HEAD_DIM:] = in_ref[:, HEAD_DIM:]


def stale_group(stale, first, heads):
    rows = stale.shape[0]
    return pl.pallas_call(
        stale_kernel,
        grid=(heads,),
        in_specs=[pl.BlockSpec((rows, 2 * HEAD_DIM), lambda h: (0, first + h))],
        out_specs=pl.BlockSpec((rows, 2 * HEAD_DIM), lambda h: (0, h)),
        out_shape=jax.ShapeDtypeStruct((rows, heads * 2 * HEAD_DIM), BF16),
        compiler_params=params(),
        cost_estimate=cost(rows * heads * 512, rows * heads * 1024),
    )(stale)


def own_kernel(left_ref, right_ref, out_ref):
    out_ref[...] = jnp.dot(left_ref[...], right_ref[...], preferred_element_type=F32)


def own_terms(left, right, first, heads):
    rows, depth = left.shape
    width = 3 * HEAD_DIM
    return pl.pallas_call(
        own_kernel,
        grid=(heads,),
        in_specs=[
            pl.BlockSpec((rows, depth), lambda h: (0, 0)),
            pl.BlockSpec((depth, width), lambda h: (0, first + h)),
        ],
        out_specs=pl.BlockSpec((rows, width), lambda h: (0, h)),
        out_shape=jax.ShapeDtypeStruct((rows, heads * width), F32),
        compiler_params=params(),
        cost_estimate=cost(2 * rows * depth * heads * width, rows * heads * width * 4 + depth * (rows + heads * width) * 2),
    )(left, right)


def finish_kernel(terms, *refs):
    total = refs[2 * terms][...]
    for at in range(terms):
        total += jnp.dot(refs[at][...], refs[terms + at][...], preferred_element_type=F32)
    q_ref, k_ref, v_ref = refs[2 * terms + 1 :]
    q_ref[...] = unit(total[:, :HEAD_DIM]).astype(BF16)
    k_ref[...] = unit(total[:, HEAD_DIM : 2 * HEAD_DIM]).astype(BF16)
    v_ref[...] = total[:, 2 * HEAD_DIM :].astype(BF16)


def finish(acc, terms):
    lefts, rights = [left for left, _ in terms], [right for _, right in terms]
    width, rows = 3 * HEAD_DIM, acc.shape[0]
    heads, tile = acc.shape[1] // width, rows
    depth = sum(left.shape[1] for left in lefts)
    out = pl.BlockSpec((tile, HEAD_DIM), lambda h, i: (i, h))
    return pl.pallas_call(
        functools.partial(finish_kernel, len(terms)),
        grid=(heads, rows // tile),
        in_specs=[pl.BlockSpec((tile, left.shape[1]), lambda h, i: (i, 0)) for left in lefts]
        + [pl.BlockSpec((right.shape[0], width), lambda h, i: (0, h)) for right in rights]
        + [pl.BlockSpec((tile, width), lambda h, i: (i, h))],
        out_specs=[out] * 3,
        out_shape=[jax.ShapeDtypeStruct((rows, heads * HEAD_DIM), BF16)] * 3,
        compiler_params=params(),
        cost_estimate=cost(2 * rows * depth * heads * width, rows * heads * width * 6),
    )(*lefts, *rights, acc)


def weigh(query, key, mask):
    tile, keys = query.shape[0], key.shape[0]
    scores = lax.dot_general(query, key, (((1,), (1,)), ((), ())), preferred_element_type=F32)
    exponents = jnp.exp(scores * (1.0 / math.sqrt(HEAD_DIM)))
    exponents = exponents.reshape(tile // BLOCK, BLOCK, keys) * mask
    return exponents.reshape(tile, keys).astype(BF16)


def with_ones(value):
    return jnp.concatenate([value, jnp.ones(value.shape, value.dtype)], axis=1)


def window_kernel(fresh, sides, prior, flag_ref, q_ref, *refs):
    num_ref, tot_ref = refs[-2:]
    query = q_ref[...]
    shape = (query.shape[0], 2 * HEAD_DIM)

    def terms(first, windows):
        both = jnp.zeros(shape, F32)
        for at in range(first, first + windows):
            k_ref, v_ref, m_ref = refs[3 * at : 3 * at + 3]
            weights = weigh(query, k_ref[...], m_ref[...])
            both += jnp.dot(weights, with_ones(v_ref[...]), preferred_element_type=F32)
        return both[:, :HEAD_DIM], both[:, HEAD_DIM:]

    if prior:
        num, tot = refs[3 * (fresh + sides)][...], refs[3 * (fresh + sides) + 1][...]
    if fresh:
        num, tot = terms(0, fresh)
    num_ref[...] = num
    tot_ref[...] = tot
    for side in range(sides):

        @pl.when(flag_ref[side] == 1)
        def _(side=side):
            more, more_tot = terms(fresh + side, 1)
            num_ref[...] += more
            tot_ref[...] += more_tot


def windows(flag, queries, here, fresh, sides, prior):
    first, heads = here
    rows, cols = queries.shape[0], heads * HEAD_DIM
    query = pl.BlockSpec((QUERY_TILE, HEAD_DIM), lambda h, i, f: (i, first + h))
    tile = pl.BlockSpec((QUERY_TILE, HEAD_DIM), lambda h, i, f: (i, h))
    specs, values = [], []
    for keys, vals, mask in fresh:
        block = pl.BlockSpec((keys.shape[0], HEAD_DIM), lambda h, i, f: (0, first + h))
        specs += [block, block]
        values += [keys, vals, mask]
        specs.append(pl.BlockSpec((QUERY_TILE // BLOCK, 1, keys.shape[0]), lambda h, i, f: (i, 0, 0)))
    for stale, mask, at in sides:
        specs.append(pl.BlockSpec((stale.shape[0], HEAD_DIM), lambda h, i, f, at=at: (0, 2 * (at + h))))
        specs.append(pl.BlockSpec((stale.shape[0], HEAD_DIM), lambda h, i, f, at=at: (0, 2 * (at + h) + 1)))
        specs.append(pl.BlockSpec((QUERY_TILE // BLOCK, 1, stale.shape[0]), lambda h, i, f: (i, 0, 0)))
        values += [stale, stale, mask]
    count = len(fresh) + len(sides)
    return pl.pallas_call(
        functools.partial(window_kernel, len(fresh), len(sides), len(prior)),
        grid_spec=pltpu.PrefetchScalarGridSpec(
            num_scalar_prefetch=1,
            grid=(heads, rows // QUERY_TILE),
            in_specs=[query] + specs + [tile] * len(prior),
            out_specs=[tile, tile],
        ),
        out_shape=[jax.ShapeDtypeStruct((rows, cols), F32)] * 2,
        compiler_params=params(),
        cost_estimate=cost(6 * count * rows * rows * cols, rows * cols * 14 * count, count * rows * rows * heads),
    )(flag, queries, *values, *prior)


def foreign_kernel(flag_ref, q_ref, k_ref, v_ref, mask_ref, num_ref, tot_ref):
    head = pl.program_id(1)

    @pl.when(head == 0)
    def _():
        tot_ref[...] = jnp.zeros_like(tot_ref)

    @pl.when(flag_ref[0] == 1)
    def _():
        value = v_ref[...]
        weights = weigh(q_ref[...], k_ref[...], mask_ref[...])
        num_ref[...] = jnp.dot(weights, value, preferred_element_type=F32).astype(BF16)
        sums = lax.dot_general(
            jnp.ones((8, weights.shape[1]), BF16), weights, (((1,), (1,)), ((), ())), preferred_element_type=F32
        )
        row = lax.broadcasted_iota(jnp.int32, sums.shape, 0)
        tot_ref[...] = jnp.where(row == head, sums, tot_ref[...])

    @pl.when(flag_ref[0] != 1)
    def _():
        num_ref[...] = jnp.zeros_like(num_ref)


def foreign_part(flag, queries, first, heads, stale, mask):
    rows, cols, window = queries.shape[0], heads * HEAD_DIM, stale.shape[0]
    query = pl.BlockSpec((QUERY_TILE, HEAD_DIM), lambda i, h, f: (i, h))
    tile = pl.BlockSpec((QUERY_TILE, HEAD_DIM), lambda i, h, f: (i, h))
    return pl.pallas_call(
        foreign_kernel,
        grid_spec=pltpu.PrefetchScalarGridSpec(
            num_scalar_prefetch=1,
            grid=(rows // QUERY_TILE, heads),
            in_specs=[
                query,
                pl.BlockSpec((window, HEAD_DIM), lambda i, h, f: (0, 2 * (first + h))),
                pl.BlockSpec((window, HEAD_DIM), lambda i, h, f: (0, 2 * (first + h) + 1)),
                pl.BlockSpec((QUERY_TILE // BLOCK, 1, window), lambda i, h, f: (i, 0, 0)),
            ],
            out_specs=[tile, pl.BlockSpec((8, QUERY_TILE), lambda i, h, f: (0, i))],
        ),
        out_shape=[jax.ShapeDtypeStruct((rows, cols), BF16), jax.ShapeDtypeStruct((8, rows), F32)],
        compiler_params=params(),
        cost_estimate=cost(4 * rows * window * cols, rows * cols * 8, rows * window * heads),
    )(flag, queries, stale, stale, mask)


def normalise_into(att_ref, column, near_refs, num_ref=None, tot_ref=None):
    totals = None if tot_ref is None else jnp.transpose(tot_ref[...])
    at = 0
    for n_ref, t_ref in near_refs:
        for head in range(n_ref.shape[1] // HEAD_DIM):
            cols = slice(head * HEAD_DIM, (head + 1) * HEAD_DIM)
            num, tot = n_ref[:, cols], t_ref[:, cols]
            if num_ref is not None:
                num += num_ref[:, at * HEAD_DIM : (at + 1) * HEAD_DIM].astype(F32)
                tot += totals[:, at : at + 1]
            att_ref[:, (column + at) * HEAD_DIM : (column + at + 1) * HEAD_DIM] = (num / tot).astype(BF16)
            at += 1


def normalise_kernel(*refs):
    near_refs = [(refs[2 * at], refs[2 * at + 1]) for at in range((len(refs) - 3) // 2)]
    normalise_into(refs[-1], 0, near_refs, refs[-3], refs[-2])


def normalise(near, far):
    num, tot = far
    rows, cols = num.shape
    tile = 512
    specs, values = [], []
    for pair in near:
        specs += [pl.BlockSpec((tile, pair[0].shape[1]), lambda i: (i, 0))] * 2
        values += list(pair)
    return pl.pallas_call(
        normalise_kernel,
        grid=(rows // tile,),
        in_specs=specs + [pl.BlockSpec((tile, cols), lambda i: (i, 0)), pl.BlockSpec((8, tile), lambda i: (0, i))],
        out_specs=pl.BlockSpec((tile, cols), lambda i: (i, 0)),
        out_shape=jax.ShapeDtypeStruct((rows, cols), BF16),
        compiler_params=params(),
        cost_estimate=cost(rows * cols * 4, rows * cols * 12),
    )(*values, num, tot)


def branch_kernel(near, keeps, parts, where_ref, *refs):
    step, steps = pl.program_id(0), pl.num_programs(0)
    mine_ref, own_refs, other_refs = refs[0], refs[1:parts], refs[parts : 2 * parts - 1]
    g_ref, done_ref = refs[2 * parts - 1 : 2 * parts + 1]
    rest = refs[2 * parts + 1 :]
    send_ref, keep_ref, att_ref, lefts_ref = rest[-4:]
    lefts_ref = lefts_ref.at[pl.program_id(1)]
    rank, depth = where_ref[3 * steps], mine_ref.shape[1]

    @pl.when(step == 0)
    def _():
        att_ref[:, : done_ref.shape[1]] = done_ref[...]
        near_refs = [(rest[2 * at], rest[2 * at + 1]) for at in range(near)]
        normalise_into(att_ref, done_ref.shape[1] // HEAD_DIM, near_refs)
        for offset in range(parts):
            part = lax.rem(rank + parts - offset, parts)
            left = att_ref[:, :depth]
            for other in range(1, parts):
                left = jnp.where(part == other, att_ref[:, other * depth : (other + 1) * depth], left)
            lefts_ref[offset] = left

    is_own = where_ref[step] == 0
    term = jnp.dot(lefts_ref[0], mine_ref[0], preferred_element_type=F32)
    for offset in range(1, parts):
        right = jnp.where(is_own, own_refs[offset - 1][...], other_refs[offset - 1][0])
        term += jnp.dot(lefts_ref[offset], right, preferred_element_type=F32)
    result = (term * g_ref[0]).astype(BF16)
    stays = step >= steps - keeps

    @pl.when(stays)
    def _():
        keep_ref[0] = result

    @pl.when(jnp.logical_not(stays))
    def _():
        send_ref[0] = result


def branch(where, mine, owns, others, gate, done, near, first, count, keeps):
    total, depth, width = mine.shape
    tile = ROW_TILE if count % ROW_TILE == 0 and first % ROW_TILE == 0 else BLOCK
    start, tiles = first // tile, count // tile
    sends = total - keeps

    def row_tile(g, i, w):
        return start + jnp.where(g == 0, i, tiles - 1), 0

    specs, values = [pl.BlockSpec((tile, done.shape[1]), row_tile)], [done]
    for num, tot in near:
        spec = pl.BlockSpec((tile, num.shape[1]), row_tile)
        specs += [spec, spec]
        values += [num, tot]
    parts = len(others) + 1
    held = depth * parts
    return pl.pallas_call(
        functools.partial(branch_kernel, len(near), keeps, parts),
        grid_spec=pltpu.PrefetchScalarGridSpec(
            num_scalar_prefetch=1,
            grid=(total, tiles),
            in_specs=[pl.BlockSpec((1, depth, width), lambda g, i, w: (w[g], 0, 0))]
            + [pl.BlockSpec((depth, width), lambda g, i, w: (0, 0))] * len(owns)
            + [pl.BlockSpec((1, depth, width), lambda g, i, w: (w[total + g], 0, 0))] * len(others)
            + [pl.BlockSpec((1, 1, width), lambda g, i, w: (w[2 * total + g], 0, 0))]
            + specs,
            out_specs=[
                pl.BlockSpec((1, tile, width), lambda g, i, w: (jnp.minimum(g, sends - 1), jnp.where(g < sends, i, tiles - 1), 0)),
                pl.BlockSpec((1, tile, width), lambda g, i, w: (jnp.maximum(g - sends, 0), jnp.where(g < sends, 0, i), 0)),
            ],
            scratch_shapes=[pltpu.VMEM((tile, held), BF16), pltpu.VMEM((tiles, parts, tile, depth), BF16)],
        ),
        out_shape=[
            jax.ShapeDtypeStruct((sends, count, width), BF16),
            jax.ShapeDtypeStruct((keeps, count, width), BF16),
        ],
        compiler_params=params(),
        cost_estimate=cost(2 * count * held * total * width, held * total * width * 2 + count * total * width * 2),
    )(where, mine, *owns, *others, gate, *values)


def chosen(place, values, names):
    out = values[0]
    for at in range(1, len(values)):
        if names[at] != names[0]:
            out = jnp.where(place == at, values[at], out)
    return out


class Relay:
    def __init__(self, own, count, reps):
        self.count, self.reps = count, reps
        self.place, self.rank = lax.axis_index("patch"), lax.axis_index("rep")
        self.ahead, self.back = {0: own}, {0: own}

    def step(self, k, *held):
        count = self.count
        ahead, back = self.ahead[k - 1], self.back[k - 1]
        if held:
            ahead, back = after(ahead, *held), after(back, *held)
        self.ahead[k] = lax.ppermute(ahead, "patch", [(i, i + 1) for i in range(k - 1, count - 1)])
        self.back[k] = lax.ppermute(back, "patch", [(i + 1, i) for i in range(count - k)])

    def sent(self, k):
        return self.ahead[k], self.back[k]

    def brought(self, t, cut=None):
        values, owners = [], []
        for at in range(self.count):
            comes = sorted([(k, 0) for k in range(1, at + 1)] + [(k, 1) for k in range(1, self.count - at)])
            k, side = comes[t - 1]
            values.append(self.back[k] if side else self.ahead[k])
            owners.append(at + k if side else at - k)
        owner = sum(jnp.where(self.place == at, owners[at], 0) for at in range(self.count))
        candidates = []
        for value in values:
            if not any(value is other for other in candidates):
                candidates.append(value)
        fenced = lax.optimization_barrier(tuple(candidates))
        at_of = [[value is other for other in candidates].index(True) for value in values]
        cuts = [(0, values[0].shape[1])] if cut is None else [(0, cut), (cut, values[0].shape[1])]
        chosen_cuts = [chosen(self.place, [fenced[at][:, low:high] for at in at_of], at_of) for low, high in cuts]
        parts = [(self.rank, chosen_cuts)]
        for offset in range(1, self.reps):
            pairs = [(a, (a + offset) % self.reps) for a in range(self.reps)]
            swapped, held = [], ()
            for piece in chosen_cuts:
                swapped.append(lax.ppermute(after(piece, *held) if held else piece, "rep", pairs))
                held = (swapped[-1],)
            parts.append(((self.rank - offset) % self.reps, swapped))
        return owner, parts


def body(hidden, modulation, gate, w_qkv, stale_kv, w_out, key_lists):
    count, reps = lax.axis_size("patch"), lax.axis_size("rep")
    tps, secs = lax.axis_size("tp"), lax.axis_size("sec")
    place, rank = lax.axis_index("patch"), lax.axis_index("rep")
    tp_index, sec_index = lax.axis_index("tp"), lax.axis_index("sec")
    rows, model_width = hidden.shape[1], hidden.shape[2]
    heads = w_out.shape[1] // HEAD_DIM
    patch_blocks = rows // BLOCK
    unit_heads = heads // 3 if heads % 3 == 0 else 1
    units = heads // unit_heads
    small_units = max(1, units // 3)
    group_units = [list(range(units - small_units)), list(range(units - small_units, units))]
    group_heads = [len(members) * unit_heads for members in group_units]
    group_first = [0, group_heads[0]]
    states = hidden[0]
    w_qkv, stale_kv, w_out = w_qkv[0], stale_kv[0], w_out[0]
    last = count - 1
    shard_rows = w_qkv.shape[0]
    depth, out_depth = shard_rows // reps, w_out.shape[0] // reps
    width = 3 * HEAD_DIM

    relative = jnp.where(key_lists >= 0, key_lists - (place - 1) * patch_blocks, -1)
    window_ids = jnp.arange(3 * patch_blocks, dtype=jnp.int32)
    hits = jnp.any(relative[:, :, None] == window_ids[None, None, :], axis=1).astype(F32)
    hits = jnp.repeat(hits, BLOCK, axis=1).reshape(patch_blocks, 3, rows)
    before, fresh, behind = (hits[:, i][:, None, :] for i in range(3))
    odd = place % 2 == 1
    even_mask, odd_mask = jnp.where(odd, before, behind), jnp.where(odd, behind, before)
    at_end = (place == 0) | (place == last)
    to_inner = [(0, 1), (last, last - 1)]
    to_end = [(1, 0), (last - 1, last)]
    inner_flag = jnp.where(at_end, 0, 1).astype(jnp.int32).reshape(1)
    host_flag = ((place == 1) | (place == last - 1)).astype(jnp.int32).reshape(1)

    inner = range(1, last)
    pairs = [(i, i + 1) for i in range(last)] + [(i + 1, i) for i in range(last)]
    even_pairs = [(a, b) for a, b in pairs if min(a, b) % 2 == 0 and b in inner]
    odd_pairs = [(a, b) for a, b in pairs if min(a, b) % 2 == 1 and b in inner]
    stale, even, other = [None] * units, [None] * units, [None] * units

    def send_even(unit, *held):
        even[unit] = lax.ppermute(after(stale[unit], *held), "patch", even_pairs)

    def send_other(unit, *held):
        other[unit] = lax.ppermute(after(stale[unit], *held), "patch", odd_pairs)

    def qkv_relay(group, *held):
        source = after(w_qkv, *held) if held else w_qkv
        at = (rank * depth, group_first[group] * width)
        own = lax.dynamic_slice(source, at, (depth, group_heads[group] * width))
        if group == 1:
            own = jnp.concatenate([own, own_out.reshape(depth, out_cols)], axis=1)
        return Relay(own, count, reps)

    def columns(owner, part):
        return lax.dynamic_slice_in_dim(ready, owner * shard_rows + part * depth, depth, 1)

    def term_of(owner, part, piece):
        return columns(owner, part), piece

    def add_terms(acc, terms):
        for left, right in terms:
            acc += jnp.dot(left, right, preferred_element_type=F32)
        return acc

    out_shape = (out_depth, w_out.shape[1])
    out_cols = out_depth * w_out.shape[1] // depth
    small_cols = group_heads[1] * width
    large = qkv_relay(0)
    large.step(1)
    inputs = states.astype(F32)
    centered = inputs - jnp.mean(inputs, axis=-1, keepdims=True)
    variance = jnp.mean(centered * centered, axis=-1, keepdims=True)
    normed = centered * lax.rsqrt(variance + 1e-06)
    modulated = (normed * (1.0 + modulation[0, 1]) + modulation[0, 0]).astype(BF16)
    for at in range(units):
        stale[at] = stale_group(stale_kv, at * unit_heads, unit_heads)
    modulated, stale[0] = lax.optimization_barrier((modulated, stale[0]))

    ready = after(modulated, *large.sent(1))
    own_columns = lax.dynamic_slice_in_dim(ready, place * shard_rows, shard_rows, 1)
    accs = [None, None]
    come = [[], []]
    far_mask = lax.ppermute(jnp.where(place == 0, behind, before), "patch", to_inner)
    share = model_width // (tps * secs)
    residual = lax.dynamic_slice_in_dim(states, (tp_index * secs + sec_index) * share, share, 1)
    got_all = []
    for offset in range(1, secs):
        target = (1 + offset) % secs
        sent = lax.dynamic_slice_in_dim(states, (tp_index * secs + target) * share, share, 1)
        got = lax.ppermute(sent, "sec", [(1, target)])
        got_all.append(got)
        residual = jnp.where(sec_index == target, got, residual)

    def swaps(group, at):
        return [piece[0] for _, piece in come[group][at][1][1:]] if 0 <= at < len(come[group]) else []

    def given(*items):
        return [item for item in items if item is not None]

    def at_or_none(items, at):
        return items[at] if at < len(items) else None

    def own_half(group, at):
        owner, parts = come[group][at]
        return [term_of(owner, parts[0][0], parts[0][1][0])]

    def other_half(group, at):
        owner, parts = come[group][at]
        return [term_of(owner, part, piece[0]) for part, piece in parts[1:]]

    come[0].append(large.brought(1))
    send_even(0, *large.sent(1))
    for k in range(2, count):
        held = [modulated, far_mask] + got_all if k == 2 else [accs[0]] + swaps(0, k - 3)
        if k == 3:
            held += [even[0], residual]
        large.step(k, *held)
        come[0].append(large.brought(k))
        if k == 2:
            accs[0] = own_terms(after(own_columns, *large.sent(1)), w_qkv, 0, group_heads[0])
            if units > 1:
                send_even(1, *large.sent(2))
                send_other(0, *large.sent(2))
        elif k == 3:
            accs[0] = add_terms(accs[0], own_half(0, 0) + own_half(0, 1) + other_half(0, 0))

    own_out = lax.dynamic_slice_in_dim(after(w_out, *large.sent(1)), rank * out_depth, out_depth, 0)
    small = qkv_relay(1, *large.sent(min(2, last)))
    small.step(
        1, *large.sent(last), accs[0], *swaps(0, last - 2), *given(at_or_none(even, 1), at_or_none(other, 0))
    )
    come[1].append(small.brought(1, small_cols if last == 1 else None))
    for at in range(2, last - 1):
        accs[0] = add_terms(accs[0], own_half(0, at) + other_half(0, at - 1))
    accs[1] = own_terms(after(own_columns, *large.sent(last)), w_qkv, group_first[1], group_heads[1])
    final_terms = own_half(0, last - 1) + other_half(0, last - 1)
    if last > 1:
        final_terms = other_half(0, last - 2) + final_terms
    queries_0 = finish(accs[0], final_terms)
    far_queries_0 = lax.ppermute(queries_0[0], "patch", to_inner)
    queries_1 = None

    def near_part(group, at, fresh_too, sides, flags, prior):
        queries, keys, values = (queries_0, queries_1)[group]
        here = (at * unit_heads, unit_heads)
        return windows(flags, queries, here, [(keys, values, fresh)] if fresh_too else [], sides, prior)

    def sides_of(unit_at):
        late = unit_at > 0
        stale_at = (unit_at - 1) * unit_heads if late else 0
        return [(even[unit_at], even_mask, 0), (other[1 if late else 0], odd_mask, stale_at)]

    all_even = [(a, b) for a, b in pairs if min(a, b) % 2 == 0]
    late_stale = stale_group(after(stale_kv, *large.sent(last)), unit_heads, heads - unit_heads)

    def late_exchanges(held):
        for at in group_units[1]:
            even[at] = lax.ppermute(after(stale[at], *held, *swaps(1, 0)), "patch", all_even)
        for at in group_units[0]:
            if even[at] is None:
                send_even(at, *held)
        other[1] = lax.ppermute(after(late_stale, *held), "patch", odd_pairs)

    first_large = group_units[0]
    inner_flags = jnp.concatenate([inner_flag, inner_flag])
    near = [None] * units
    near[0] = near_part(0, 0, True, sides_of(0), inner_flags, ())
    for k in range(2, count):
        if k == 2:
            held = [accs[1]]
        elif k == 3:
            held = [*queries_0, near[0][0]]
        else:
            held = swaps(1, k - 4)
        small.step(k, *held)
        come[1].append(small.brought(k, small_cols if k == last else None))
        if k == 2:
            late_exchanges(small.sent(2))
    if other[1] is None:
        late_exchanges(small.sent(last))

    stale_full = stale_group(after(stale_kv, *small.sent(1)), 0, group_heads[0])
    far_num, far_tot = foreign_part(host_flag, far_queries_0, 0, group_heads[0], stale_full, far_mask)
    come_last = come[1][-1][1][0][1]
    exchanged = [even[at] for at in group_units[1]] + [other[1]]
    back_num = lax.ppermute(after(far_num, *small.sent(last), *come_last, *exchanged, *swaps(1, last - 2)), "patch", to_end)
    back_tot = lax.ppermute(after(far_tot, *small.sent(last)), "patch", to_end)
    for at, unit_at in enumerate(first_large):
        if unit_at:
            part = near_part(0, at, True, sides_of(unit_at)[:1], inner_flag, ())
            near[unit_at] = near_part(0, at, False, sides_of(unit_at)[1:], inner_flag, tuple(part))

    early = []
    for at in range(last - 2):
        early += own_half(1, at) + other_half(1, at)
    if early:
        accs[1] = add_terms(accs[1], [(left, right[:, :small_cols]) for left, right in early])
    final_terms = []
    for at in range(max(last - 2, 0), last):
        final_terms += own_half(1, at) + other_half(1, at)
    fenced = lax.optimization_barrier((accs[1], back_tot, near[first_large[-1]][0]))
    queries_1 = finish(fenced[0], final_terms)
    always = jnp.concatenate([jnp.ones((1,), jnp.int32), inner_flag])
    for at, unit_at in enumerate(group_units[1]):
        near[unit_at] = near_part(1, at, True, sides_of(unit_at), always, ())
    done = normalise([near[at] for at in group_units[0]], (back_num, back_tot))

    out_mine, out_others, out_owns, owners = [own_out], [[] for _ in range(reps - 1)], [], [place]
    for owner, parts in come[1]:
        owners.append(owner)
        for at, (_, piece) in enumerate(parts):
            rows_out = (piece[0][:, small_cols:] if len(piece) == 1 else piece[1]).reshape(out_shape)
            if at == 0:
                out_mine.append(rows_out)
            else:
                out_others[at - 1].append(rows_out)
    out_mine = jnp.stack(out_mine)
    out_others = [jnp.stack(items) for items in out_others]
    for offset in range(1, reps):
        out_owns.append(lax.dynamic_slice_in_dim(w_out, (rank - offset) % reps * out_depth, out_depth, 0))

    per = count // (tps * secs)
    order = [
        (block * secs + (sec_index + offset) % secs) * per + at
        for offset in list(range(1, secs)) + [0]
        for block in range(tps)
        for at in range(per)
    ]
    turns = [sum(jnp.where(owners[t] == column, t, 0) for t in range(count)) for column in order]
    where = jnp.stack(turns + [jnp.maximum(turn - 1, 0) for turn in turns] + order + [rank]).astype(jnp.int32)
    gate_blocks = gate.reshape(count, 1, w_out.shape[1])
    keeps = tps * per
    results = []
    start = 0
    for share_rows in ROW_CHUNKS:
        chunk = rows * share_rows // sum(ROW_CHUNKS)
        sends, keep = branch(
            where, out_mine, out_owns, out_others, gate_blocks, done,
            [near[unit_at] for unit_at in group_units[1]], start, chunk, keeps,
        )
        got = [keep]
        for offset in range(1, secs):
            sent = sends[(offset - 1) * keeps : offset * keeps]
            got.append(lax.ppermute(sent, "sec", [(i, (i + offset) % secs) for i in range(secs)]))

        def block_of(index):
            return sum(lax.dynamic_slice_in_dim(part, index * per, per, 0).astype(F32) for part in got)

        others = []
        for offset in range(1, tps):
            sent = block_of((tp_index + offset) % tps).astype(BF16)
            others.append(lax.ppermute(sent, "tp", [(i, (i + offset) % tps) for i in range(tps)]))
        others = [after(part, *results) for part in others] if results else others
        result = block_of(tp_index) + sum(part.astype(F32) for part in others)
        result = jnp.moveaxis(result, 0, 1).reshape(chunk, share)
        results.append((result + residual[start : start + chunk].astype(F32)).astype(BF16))
        start += chunk
    return jnp.concatenate(results, axis=0)


def solution(mesh):
    return jax.shard_map(
        body,
        mesh=mesh,
        in_specs=(
            P("sec", ("rep", "patch"), None),
            P("sec", None, None),
            P("sec", None),
            P("sec", "patch", "tp"),
            P("sec", ("rep", "patch"), "tp"),
            P("sec", "tp", "patch"),
            P(("rep", "patch"), None),
        ),
        out_specs=P(("rep", "patch"), ("tp", "sec")),
        check_vma=False,
    )
```

```python
import functools
import math

import jax
import jax.numpy as jnp
from jax import lax
from jax.experimental import pallas as pl
from jax.experimental.pallas import tpu as pltpu
from jax.sharding import PartitionSpec as P

HEAD_DIM = 128
BLOCK = 128
QUERY_TILE = 512
ROW_CHUNKS = (1, 1)
ROW_TILE = 512
COST_SCALE = 0.2
VMEM_LIMIT = 28 * 1024 * 1024
F32 = jnp.float32
BF16 = jnp.bfloat16


def after(value, *others):
    return lax.optimization_barrier((value,) + others)[0]


def params():
    return pltpu.CompilerParams(vmem_limit_bytes=VMEM_LIMIT)


def cost(flops, moved, exps=0):
    scale = COST_SCALE
    return pl.CostEstimate(flops=int(flops * scale), bytes_accessed=int(moved * scale), transcendentals=int(exps * scale))


def unit(value):
    return value * lax.rsqrt(jnp.mean(value * value, axis=-1, keepdims=True) + 1e-06)


def stale_kernel(in_ref, out_ref):
    out_ref[:, :HEAD_DIM] = unit(in_ref[:, :HEAD_DIM].astype(F32)).astype(BF16)
    out_ref[:, HEAD_DIM:] = in_ref[:, HEAD_DIM:]


def stale_group(stale, first, heads):
    rows = stale.shape[0]
    return pl.pallas_call(
        stale_kernel,
        grid=(heads,),
        in_specs=[pl.BlockSpec((rows, 2 * HEAD_DIM), lambda h: (0, first + h))],
        out_specs=pl.BlockSpec((rows, 2 * HEAD_DIM), lambda h: (0, h)),
        out_shape=jax.ShapeDtypeStruct((rows, heads * 2 * HEAD_DIM), BF16),
        compiler_params=params(),
        cost_estimate=cost(rows * heads * 512, rows * heads * 1024),
    )(stale)


def own_kernel(left_ref, right_ref, out_ref):
    out_ref[...] = jnp.dot(left_ref[...], right_ref[...], preferred_element_type=F32)


def own_terms(left, right, first, heads):
    rows, depth = left.shape
    width = 3 * HEAD_DIM
    return pl.pallas_call(
        own_kernel,
        grid=(heads,),
        in_specs=[
            pl.BlockSpec((rows, depth), lambda h: (0, 0)),
            pl.BlockSpec((depth, width), lambda h: (0, first + h)),
        ],
        out_specs=pl.BlockSpec((rows, width), lambda h: (0, h)),
        out_shape=jax.ShapeDtypeStruct((rows, heads * width), F32),
        compiler_params=params(),
        cost_estimate=cost(2 * rows * depth * heads * width, rows * heads * width * 4 + depth * (rows + heads * width) * 2),
    )(left, right)


def finish_kernel(terms, *refs):
    total = refs[2 * terms][...]
    for at in range(terms):
        total += jnp.dot(refs[at][...], refs[terms + at][...], preferred_element_type=F32)
    q_ref, k_ref, v_ref = refs[2 * terms + 1 :]
    q_ref[...] = unit(total[:, :HEAD_DIM]).astype(BF16)
    k_ref[...] = unit(total[:, HEAD_DIM : 2 * HEAD_DIM]).astype(BF16)
    v_ref[...] = total[:, 2 * HEAD_DIM :].astype(BF16)


def finish(acc, terms):
    lefts, rights = [left for left, _ in terms], [right for _, right in terms]
    width, rows = 3 * HEAD_DIM, acc.shape[0]
    heads, tile = acc.shape[1] // width, rows
    depth = sum(left.shape[1] for left in lefts)
    out = pl.BlockSpec((tile, HEAD_DIM), lambda h, i: (i, h))
    return pl.pallas_call(
        functools.partial(finish_kernel, len(terms)),
        grid=(heads, rows // tile),
        in_specs=[pl.BlockSpec((tile, left.shape[1]), lambda h, i: (i, 0)) for left in lefts]
        + [pl.BlockSpec((right.shape[0], width), lambda h, i: (0, h)) for right in rights]
        + [pl.BlockSpec((tile, width), lambda h, i: (i, h))],
        out_specs=[out] * 3,
        out_shape=[jax.ShapeDtypeStruct((rows, heads * HEAD_DIM), BF16)] * 3,
        compiler_params=params(),
        cost_estimate=cost(2 * rows * depth * heads * width, rows * heads * width * 6),
    )(*lefts, *rights, acc)


def weigh(query, key, mask):
    tile, keys = query.shape[0], key.shape[0]
    scores = lax.dot_general(query, key, (((1,), (1,)), ((), ())), preferred_element_type=F32)
    exponents = jnp.exp(scores * (1.0 / math.sqrt(HEAD_DIM)))
    exponents = exponents.reshape(tile // BLOCK, BLOCK, keys) * mask
    return exponents.reshape(tile, keys).astype(BF16)


def with_ones(value):
    return jnp.concatenate([value, jnp.ones(value.shape, value.dtype)], axis=1)


def window_kernel(fresh, sides, prior, flag_ref, q_ref, *refs):
    num_ref, tot_ref = refs[-2:]
    query = q_ref[...]
    shape = (query.shape[0], 2 * HEAD_DIM)

    def terms(first, windows):
        both = jnp.zeros(shape, F32)
        for at in range(first, first + windows):
            k_ref, v_ref, m_ref = refs[3 * at : 3 * at + 3]
            weights = weigh(query, k_ref[...], m_ref[...])
            both += jnp.dot(weights, with_ones(v_ref[...]), preferred_element_type=F32)
        return both[:, :HEAD_DIM], both[:, HEAD_DIM:]

    if prior:
        num, tot = refs[3 * (fresh + sides)][...], refs[3 * (fresh + sides) + 1][...]
    if fresh:
        num, tot = terms(0, fresh)
    num_ref[...] = num
    tot_ref[...] = tot
    for side in range(sides):

        @pl.when(flag_ref[side] == 1)
        def _(side=side):
            more, more_tot = terms(fresh + side, 1)
            num_ref[...] += more
            tot_ref[...] += more_tot


def windows(flag, queries, here, fresh, sides, prior):
    first, heads = here
    rows, cols = queries.shape[0], heads * HEAD_DIM
    query = pl.BlockSpec((QUERY_TILE, HEAD_DIM), lambda h, i, f: (i, first + h))
    tile = pl.BlockSpec((QUERY_TILE, HEAD_DIM), lambda h, i, f: (i, h))
    specs, values = [], []
    for keys, vals, mask in fresh:
        block = pl.BlockSpec((keys.shape[0], HEAD_DIM), lambda h, i, f: (0, first + h))
        specs += [block, block]
        values += [keys, vals, mask]
        specs.append(pl.BlockSpec((QUERY_TILE // BLOCK, 1, keys.shape[0]), lambda h, i, f: (i, 0, 0)))
    for stale, mask, at in sides:
        specs.append(pl.BlockSpec((stale.shape[0], HEAD_DIM), lambda h, i, f, at=at: (0, 2 * (at + h))))
        specs.append(pl.BlockSpec((stale.shape[0], HEAD_DIM), lambda h, i, f, at=at: (0, 2 * (at + h) + 1)))
        specs.append(pl.BlockSpec((QUERY_TILE // BLOCK, 1, stale.shape[0]), lambda h, i, f: (i, 0, 0)))
        values += [stale, stale, mask]
    count = len(fresh) + len(sides)
    return pl.pallas_call(
        functools.partial(window_kernel, len(fresh), len(sides), len(prior)),
        grid_spec=pltpu.PrefetchScalarGridSpec(
            num_scalar_prefetch=1,
            grid=(heads, rows // QUERY_TILE),
            in_specs=[query] + specs + [tile] * len(prior),
            out_specs=[tile, tile],
        ),
        out_shape=[jax.ShapeDtypeStruct((rows, cols), F32)] * 2,
        compiler_params=params(),
        cost_estimate=cost(6 * count * rows * rows * cols, rows * cols * 14 * count, count * rows * rows * heads),
    )(flag, queries, *values, *prior)


def foreign_kernel(flag_ref, q_ref, k_ref, v_ref, mask_ref, num_ref, tot_ref):
    head = pl.program_id(1)

    @pl.when(head == 0)
    def _():
        tot_ref[...] = jnp.zeros_like(tot_ref)

    @pl.when(flag_ref[0] == 1)
    def _():
        value = v_ref[...]
        weights = weigh(q_ref[...], k_ref[...], mask_ref[...])
        num_ref[...] = jnp.dot(weights, value, preferred_element_type=F32).astype(BF16)
        sums = lax.dot_general(
            jnp.ones((8, weights.shape[1]), BF16), weights, (((1,), (1,)), ((), ())), preferred_element_type=F32
        )
        row = lax.broadcasted_iota(jnp.int32, sums.shape, 0)
        tot_ref[...] = jnp.where(row == head, sums, tot_ref[...])

    @pl.when(flag_ref[0] != 1)
    def _():
        num_ref[...] = jnp.zeros_like(num_ref)


def foreign_part(flag, queries, first, heads, stale, mask):
    rows, cols, window = queries.shape[0], heads * HEAD_DIM, stale.shape[0]
    query = pl.BlockSpec((QUERY_TILE, HEAD_DIM), lambda i, h, f: (i, h))
    tile = pl.BlockSpec((QUERY_TILE, HEAD_DIM), lambda i, h, f: (i, h))
    return pl.pallas_call(
        foreign_kernel,
        grid_spec=pltpu.PrefetchScalarGridSpec(
            num_scalar_prefetch=1,
            grid=(rows // QUERY_TILE, heads),
            in_specs=[
                query,
                pl.BlockSpec((window, HEAD_DIM), lambda i, h, f: (0, 2 * (first + h))),
                pl.BlockSpec((window, HEAD_DIM), lambda i, h, f: (0, 2 * (first + h) + 1)),
                pl.BlockSpec((QUERY_TILE // BLOCK, 1, window), lambda i, h, f: (i, 0, 0)),
            ],
            out_specs=[tile, pl.BlockSpec((8, QUERY_TILE), lambda i, h, f: (0, i))],
        ),
        out_shape=[jax.ShapeDtypeStruct((rows, cols), BF16), jax.ShapeDtypeStruct((8, rows), F32)],
        compiler_params=params(),
        cost_estimate=cost(4 * rows * window * cols, rows * cols * 8, rows * window * heads),
    )(flag, queries, stale, stale, mask)


def normalise_into(att_ref, column, near_refs, num_ref=None, tot_ref=None):
    totals = None if tot_ref is None else jnp.transpose(tot_ref[...])
    at = 0
    for n_ref, t_ref in near_refs:
        for head in range(n_ref.shape[1] // HEAD_DIM):
            cols = slice(head * HEAD_DIM, (head + 1) * HEAD_DIM)
            num, tot = n_ref[:, cols], t_ref[:, cols]
            if num_ref is not None:
                num += num_ref[:, at * HEAD_DIM : (at + 1) * HEAD_DIM].astype(F32)
                tot += totals[:, at : at + 1]
            att_ref[:, (column + at) * HEAD_DIM : (column + at + 1) * HEAD_DIM] = (num / tot).astype(BF16)
            at += 1


def normalise_kernel(*refs):
    near_refs = [(refs[2 * at], refs[2 * at + 1]) for at in range((len(refs) - 3) // 2)]
    normalise_into(refs[-1], 0, near_refs, refs[-3], refs[-2])


def normalise(near, far):
    num, tot = far
    rows, cols = num.shape
    tile = 512
    specs, values = [], []
    for pair in near:
        specs += [pl.BlockSpec((tile, pair[0].shape[1]), lambda i: (i, 0))] * 2
        values += list(pair)
    return pl.pallas_call(
        normalise_kernel,
        grid=(rows // tile,),
        in_specs=specs + [pl.BlockSpec((tile, cols), lambda i: (i, 0)), pl.BlockSpec((8, tile), lambda i: (0, i))],
        out_specs=pl.BlockSpec((tile, cols), lambda i: (i, 0)),
        out_shape=jax.ShapeDtypeStruct((rows, cols), BF16),
        compiler_params=params(),
        cost_estimate=cost(rows * cols * 4, rows * cols * 12),
    )(*values, num, tot)


def branch_kernel(near, keeps, parts, where_ref, *refs):
    step, steps = pl.program_id(0), pl.num_programs(0)
    mine_ref, own_refs, other_refs = refs[0], refs[1:parts], refs[parts : 2 * parts - 1]
    g_ref, done_ref = refs[2 * parts - 1 : 2 * parts + 1]
    rest = refs[2 * parts + 1 :]
    send_ref, keep_ref, att_ref, lefts_ref = rest[-4:]
    lefts_ref = lefts_ref.at[pl.program_id(1)]
    rank, depth = where_ref[3 * steps], mine_ref.shape[1]

    @pl.when(step == 0)
    def _():
        att_ref[:, : done_ref.shape[1]] = done_ref[...]
        near_refs = [(rest[2 * at], rest[2 * at + 1]) for at in range(near)]
        normalise_into(att_ref, done_ref.shape[1] // HEAD_DIM, near_refs)
        for offset in range(parts):
            part = lax.rem(rank + parts - offset, parts)
            left = att_ref[:, :depth]
            for other in range(1, parts):
                left = jnp.where(part == other, att_ref[:, other * depth : (other + 1) * depth], left)
            lefts_ref[offset] = left

    is_own = where_ref[step] == 0
    term = jnp.dot(lefts_ref[0], mine_ref[0], preferred_element_type=F32)
    for offset in range(1, parts):
        right = jnp.where(is_own, own_refs[offset - 1][...], other_refs[offset - 1][0])
        term += jnp.dot(lefts_ref[offset], right, preferred_element_type=F32)
    result = (term * g_ref[0]).astype(BF16)
    stays = step >= steps - keeps

    @pl.when(stays)
    def _():
        keep_ref[0] = result

    @pl.when(jnp.logical_not(stays))
    def _():
        send_ref[0] = result


def branch(where, mine, owns, others, gate, done, near, first, count, keeps):
    total, depth, width = mine.shape
    tile = ROW_TILE if count % ROW_TILE == 0 and first % ROW_TILE == 0 else BLOCK
    start, tiles = first // tile, count // tile
    sends = total - keeps

    def row_tile(g, i, w):
        return start + jnp.where(g == 0, i, tiles - 1), 0

    specs, values = [pl.BlockSpec((tile, done.shape[1]), row_tile)], [done]
    for num, tot in near:
        spec = pl.BlockSpec((tile, num.shape[1]), row_tile)
        specs += [spec, spec]
        values += [num, tot]
    parts = len(others) + 1
    held = depth * parts
    return pl.pallas_call(
        functools.partial(branch_kernel, len(near), keeps, parts),
        grid_spec=pltpu.PrefetchScalarGridSpec(
            num_scalar_prefetch=1,
            grid=(total, tiles),
            in_specs=[pl.BlockSpec((1, depth, width), lambda g, i, w: (w[g], 0, 0))]
            + [pl.BlockSpec((depth, width), lambda g, i, w: (0, 0))] * len(owns)
            + [pl.BlockSpec((1, depth, width), lambda g, i, w: (w[total + g], 0, 0))] * len(others)
            + [pl.BlockSpec((1, 1, width), lambda g, i, w: (w[2 * total + g], 0, 0))]
            + specs,
            out_specs=[
                pl.BlockSpec((1, tile, width), lambda g, i, w: (jnp.minimum(g, sends - 1), jnp.where(g < sends, i, tiles - 1), 0)),
                pl.BlockSpec((1, tile, width), lambda g, i, w: (jnp.maximum(g - sends, 0), jnp.where(g < sends, 0, i), 0)),
            ],
            scratch_shapes=[pltpu.VMEM((tile, held), BF16), pltpu.VMEM((tiles, parts, tile, depth), BF16)],
        ),
        out_shape=[
            jax.ShapeDtypeStruct((sends, count, width), BF16),
            jax.ShapeDtypeStruct((keeps, count, width), BF16),
        ],
        compiler_params=params(),
        cost_estimate=cost(2 * count * held * total * width, held * total * width * 2 + count * total * width * 2),
    )(where, mine, *owns, *others, gate, *values)


def chosen(place, values, names):
    out = values[0]
    for at in range(1, len(values)):
        if names[at] != names[0]:
            out = jnp.where(place == at, values[at], out)
    return out


class Relay:
    def __init__(self, own, count, reps):
        self.count, self.reps = count, reps
        self.place, self.rank = lax.axis_index("patch"), lax.axis_index("rep")
        self.ahead, self.back = {0: own}, {0: own}

    def step(self, k, *held):
        count = self.count
        ahead, back = self.ahead[k - 1], self.back[k - 1]
        if held:
            ahead, back = after(ahead, *held), after(back, *held)
        self.ahead[k] = lax.ppermute(ahead, "patch", [(i, i + 1) for i in range(k - 1, count - 1)])
        self.back[k] = lax.ppermute(back, "patch", [(i + 1, i) for i in range(count - k)])

    def sent(self, k):
        return self.ahead[k], self.back[k]

    def brought(self, t, cut=None):
        values, owners = [], []
        for at in range(self.count):
            comes = sorted([(k, 0) for k in range(1, at + 1)] + [(k, 1) for k in range(1, self.count - at)])
            k, side = comes[t - 1]
            values.append(self.back[k] if side else self.ahead[k])
            owners.append(at + k if side else at - k)
        owner = sum(jnp.where(self.place == at, owners[at], 0) for at in range(self.count))
        candidates = []
        for value in values:
            if not any(value is other for other in candidates):
                candidates.append(value)
        fenced = lax.optimization_barrier(tuple(candidates))
        at_of = [[value is other for other in candidates].index(True) for value in values]
        cuts = [(0, values[0].shape[1])] if cut is None else [(0, cut), (cut, values[0].shape[1])]
        chosen_cuts = [chosen(self.place, [fenced[at][:, low:high] for at in at_of], at_of) for low, high in cuts]
        parts = [(self.rank, chosen_cuts)]
        for offset in range(1, self.reps):
            pairs = [(a, (a + offset) % self.reps) for a in range(self.reps)]
            swapped, held = [], ()
            for piece in chosen_cuts:
                swapped.append(lax.ppermute(after(piece, *held) if held else piece, "rep", pairs))
                held = (swapped[-1],)
            parts.append(((self.rank - offset) % self.reps, swapped))
        return owner, parts


def body(hidden, modulation, gate, w_qkv, stale_kv, w_out, key_lists):
    count, reps = lax.axis_size("patch"), lax.axis_size("rep")
    tps, secs = lax.axis_size("tp"), lax.axis_size("sec")
    place, rank = lax.axis_index("patch"), lax.axis_index("rep")
    tp_index, sec_index = lax.axis_index("tp"), lax.axis_index("sec")
    rows, model_width = hidden.shape[1], hidden.shape[2]
    heads = w_out.shape[1] // HEAD_DIM
    patch_blocks = rows // BLOCK
    unit_heads = heads // 3 if heads % 3 == 0 else 1
    units = heads // unit_heads
    small_units = max(1, units // 3)
    group_units = [list(range(units - small_units)), list(range(units - small_units, units))]
    group_heads = [len(members) * unit_heads for members in group_units]
    group_first = [0, group_heads[0]]
    states = hidden[0]
    w_qkv, stale_kv, w_out = w_qkv[0], stale_kv[0], w_out[0]
    last = count - 1
    shard_rows = w_qkv.shape[0]
    depth, out_depth = shard_rows // reps, w_out.shape[0] // reps
    width = 3 * HEAD_DIM

    relative = jnp.where(key_lists >= 0, key_lists - (place - 1) * patch_blocks, -1)
    window_ids = jnp.arange(3 * patch_blocks, dtype=jnp.int32)
    hits = jnp.any(relative[:, :, None] == window_ids[None, None, :], axis=1).astype(F32)
    hits = jnp.repeat(hits, BLOCK, axis=1).reshape(patch_blocks, 3, rows)
    before, fresh, behind = (hits[:, i][:, None, :] for i in range(3))
    odd = place % 2 == 1
    even_mask, odd_mask = jnp.where(odd, before, behind), jnp.where(odd, behind, before)
    at_end = (place == 0) | (place == last)
    to_inner = [(0, 1), (last, last - 1)]
    to_end = [(1, 0), (last - 1, last)]
    inner_flag = jnp.where(at_end, 0, 1).astype(jnp.int32).reshape(1)
    host_flag = ((place == 1) | (place == last - 1)).astype(jnp.int32).reshape(1)

    inner = range(1, last)
    pairs = [(i, i + 1) for i in range(last)] + [(i + 1, i) for i in range(last)]
    even_pairs = [(a, b) for a, b in pairs if min(a, b) % 2 == 0 and b in inner]
    odd_pairs = [(a, b) for a, b in pairs if min(a, b) % 2 == 1 and b in inner]
    stale, even, other = [None] * units, [None] * units, [None] * units

    def send_even(unit, *held):
        even[unit] = lax.ppermute(after(stale[unit], *held), "patch", even_pairs)

    def send_other(unit, *held):
        other[unit] = lax.ppermute(after(stale[unit], *held), "patch", odd_pairs)

    def qkv_relay(group, *held):
        source = after(w_qkv, *held) if held else w_qkv
        at = (rank * depth, group_first[group] * width)
        own = lax.dynamic_slice(source, at, (depth, group_heads[group] * width))
        if group == 1:
            own = jnp.concatenate([own, own_out.reshape(depth, out_cols)], axis=1)
        return Relay(own, count, reps)

    def columns(owner, part):
        return lax.dynamic_slice_in_dim(ready, owner * shard_rows + part * depth, depth, 1)

    def term_of(owner, part, piece):
        return columns(owner, part), piece

    def add_terms(acc, terms):
        for left, right in terms:
            acc += jnp.dot(left, right, preferred_element_type=F32)
        return acc

    out_shape = (out_depth, w_out.shape[1])
    out_cols = out_depth * w_out.shape[1] // depth
    small_cols = group_heads[1] * width
    large = qkv_relay(0)
    large.step(1)
    inputs = states.astype(F32)
    centered = inputs - jnp.mean(inputs, axis=-1, keepdims=True)
    variance = jnp.mean(centered * centered, axis=-1, keepdims=True)
    normed = centered * lax.rsqrt(variance + 1e-06)
    modulated = (normed * (1.0 + modulation[0, 1]) + modulation[0, 0]).astype(BF16)
    for at in range(units):
        stale[at] = stale_group(stale_kv, at * unit_heads, unit_heads)
    modulated, stale[0] = lax.optimization_barrier((modulated, stale[0]))

    ready = after(modulated, *large.sent(1))
    own_columns = lax.dynamic_slice_in_dim(ready, place * shard_rows, shard_rows, 1)
    accs = [None, None]
    come = [[], []]
    far_mask = lax.ppermute(jnp.where(place == 0, behind, before), "patch", to_inner)
    share = model_width // (tps * secs)
    residual = lax.dynamic_slice_in_dim(states, (tp_index * secs + sec_index) * share, share, 1)
    got_all = []
    for offset in range(1, secs):
        target = (1 + offset) % secs
        sent = lax.dynamic_slice_in_dim(states, (tp_index * secs + target) * share, share, 1)
        got = lax.ppermute(sent, "sec", [(1, target)])
        got_all.append(got)
        residual = jnp.where(sec_index == target, got, residual)

    def swaps(group, at):
        return [piece[0] for _, piece in come[group][at][1][1:]] if 0 <= at < len(come[group]) else []

    def given(*items):
        return [item for item in items if item is not None]

    def at_or_none(items, at):
        return items[at] if at < len(items) else None

    def own_half(group, at):
        owner, parts = come[group][at]
        return [term_of(owner, parts[0][0], parts[0][1][0])]

    def other_half(group, at):
        owner, parts = come[group][at]
        return [term_of(owner, part, piece[0]) for part, piece in parts[1:]]

    come[0].append(large.brought(1))
    send_even(0, *large.sent(1))
    for k in range(2, count):
        held = [modulated, far_mask] + got_all if k == 2 else [accs[0]] + swaps(0, k - 3)
        if k == 3:
            held += [even[0], residual]
        large.step(k, *held)
        come[0].append(large.brought(k))
        if k == 2:
            accs[0] = own_terms(after(own_columns, *large.sent(1)), w_qkv, 0, group_heads[0])
            if units > 1:
                send_other(0, *large.sent(2))
        elif k == 3:
            accs[0] = add_terms(after(accs[0], even[0], *swaps(0, 0)), own_half(0, 0) + own_half(0, 1) + other_half(0, 0))

    own_out = lax.dynamic_slice_in_dim(after(w_out, *large.sent(1)), rank * out_depth, out_depth, 0)
    small = qkv_relay(1, *large.sent(min(2, last)))
    small.step(
        1, *large.sent(last), accs[0], *swaps(0, last - 2), *given(at_or_none(even, 1), at_or_none(other, 0))
    )
    come[1].append(small.brought(1, small_cols if last == 1 else None))
    if 1 in group_units[0]:
        send_even(1, *small.sent(1))
    for at in range(2, last - 1):
        accs[0] = add_terms(accs[0], own_half(0, at) + other_half(0, at - 1))
    accs[1] = own_terms(after(own_columns, *large.sent(last)), w_qkv, group_first[1], group_heads[1])
    final_terms = own_half(0, last - 1) + other_half(0, last - 1)
    if last > 1:
        final_terms = other_half(0, last - 2) + final_terms
    queries_0 = finish(accs[0], final_terms)
    far_queries_0 = lax.ppermute(queries_0[0], "patch", to_inner)
    queries_1 = None

    def near_part(group, at, fresh_too, sides, flags, prior):
        queries, keys, values = (queries_0, queries_1)[group]
        here = (at * unit_heads, unit_heads)
        return windows(flags, queries, here, [(keys, values, fresh)] if fresh_too else [], sides, prior)

    def sides_of(unit_at):
        late = unit_at > 0
        stale_at = (unit_at - 1) * unit_heads if late else 0
        return [(even[unit_at], even_mask, 0), (other[1 if late else 0], odd_mask, stale_at)]

    all_even = [(a, b) for a, b in pairs if min(a, b) % 2 == 0]
    late_stale = stale_group(after(stale_kv, *large.sent(last)), unit_heads, heads - unit_heads)

    def late_exchanges(held):
        for at in group_units[1]:
            even[at] = lax.ppermute(after(stale[at], *held, *swaps(1, 0)), "patch", all_even)
        for at in group_units[0]:
            if even[at] is None:
                send_even(at, *held)
        other[1] = lax.ppermute(after(late_stale, *held), "patch", odd_pairs)

    first_large = group_units[0]
    inner_flags = jnp.concatenate([inner_flag, inner_flag])
    near = [None] * units
    near[0] = near_part(0, 0, True, sides_of(0), inner_flags, ())
    for k in range(2, count):
        if k == 2:
            held = [accs[1]]
        elif k == 3:
            held = [*queries_0, near[0][0]] + given(even[1])
        else:
            held = swaps(1, k - 4)
        small.step(k, *held)
        come[1].append(small.brought(k, small_cols if k == last else None))
        if k == 2:
            late_exchanges(small.sent(2))
    if other[1] is None:
        late_exchanges(small.sent(last))

    stale_full = stale_group(after(stale_kv, *small.sent(1)), 0, group_heads[0])
    far_num, far_tot = foreign_part(host_flag, far_queries_0, 0, group_heads[0], stale_full, far_mask)
    come_last = come[1][-1][1][0][1]
    exchanged = [even[at] for at in group_units[1]] + [other[1]]
    back_tot = lax.ppermute(after(far_tot, *small.sent(last)), "patch", to_end)
    back_num = lax.ppermute(
        after(far_num, *small.sent(last), *come_last, *exchanged, *swaps(1, last - 2), back_tot), "patch", to_end
    )
    for at, unit_at in enumerate(first_large):
        if unit_at:
            part = near_part(0, at, True, sides_of(unit_at)[:1], inner_flag, ())
            near[unit_at] = near_part(0, at, False, sides_of(unit_at)[1:], inner_flag, tuple(part))

    early = []
    for at in range(last - 2):
        early += own_half(1, at) + other_half(1, at)
    if early:
        accs[1] = add_terms(accs[1], [(left, right[:, :small_cols]) for left, right in early])
    final_terms = []
    for at in range(max(last - 2, 0), last):
        final_terms += own_half(1, at) + other_half(1, at)
    fenced = lax.optimization_barrier((accs[1], near[first_large[-1]][0]))
    queries_1 = finish(fenced[0], final_terms)
    always = jnp.concatenate([jnp.ones((1,), jnp.int32), inner_flag])
    for at, unit_at in enumerate(group_units[1]):
        near[unit_at] = near_part(1, at, True, sides_of(unit_at), always, ())
    done = normalise([near[at] for at in group_units[0]], (back_num, back_tot))

    out_mine, out_others, out_owns, owners = [own_out], [[] for _ in range(reps - 1)], [], [place]
    for owner, parts in come[1]:
        owners.append(owner)
        for at, (_, piece) in enumerate(parts):
            rows_out = (piece[0][:, small_cols:] if len(piece) == 1 else piece[1]).reshape(out_shape)
            if at == 0:
                out_mine.append(rows_out)
            else:
                out_others[at - 1].append(rows_out)
    out_mine = jnp.stack(out_mine)
    out_others = [jnp.stack(items) for items in out_others]
    for offset in range(1, reps):
        out_owns.append(lax.dynamic_slice_in_dim(w_out, (rank - offset) % reps * out_depth, out_depth, 0))

    per = count // (tps * secs)
    order = [
        (block * secs + (sec_index + offset) % secs) * per + at
        for offset in list(range(1, secs)) + [0]
        for block in range(tps)
        for at in range(per)
    ]
    turns = [sum(jnp.where(owners[t] == column, t, 0) for t in range(count)) for column in order]
    where = jnp.stack(turns + [jnp.maximum(turn - 1, 0) for turn in turns] + order + [rank]).astype(jnp.int32)
    gate_blocks = gate.reshape(count, 1, w_out.shape[1])
    keeps = tps * per
    results = []
    start = 0
    for share_rows in ROW_CHUNKS:
        chunk = rows * share_rows // sum(ROW_CHUNKS)
        sends, keep = branch(
            where, out_mine, out_owns, out_others, gate_blocks, done,
            [near[unit_at] for unit_at in group_units[1]], start, chunk, keeps,
        )
        got = [keep]
        for offset in range(1, secs):
            sent = sends[(offset - 1) * keeps : offset * keeps]
            got.append(lax.ppermute(sent, "sec", [(i, (i + offset) % secs) for i in range(secs)]))

        def block_of(index):
            return sum(lax.dynamic_slice_in_dim(part, index * per, per, 0).astype(F32) for part in got)

        others = []
        for offset in range(1, tps):
            sent = block_of((tp_index + offset) % tps).astype(BF16)
            others.append(lax.ppermute(sent, "tp", [(i, (i + offset) % tps) for i in range(tps)]))
        others = [after(part, *results) for part in others] if results else others
        result = block_of(tp_index) + sum(part.astype(F32) for part in others)
        result = jnp.moveaxis(result, 0, 1).reshape(chunk, share)
        results.append((result + residual[start : start + chunk].astype(F32)).astype(BF16))
        start += chunk
    return jnp.concatenate(results, axis=0)


def solution(mesh):
    return jax.shard_map(
        body,
        mesh=mesh,
        in_specs=(
            P("sec", ("rep", "patch"), None),
            P("sec", None, None),
            P("sec", None),
            P("sec", "patch", "tp"),
            P("sec", ("rep", "patch"), "tp"),
            P("sec", "tp", "patch"),
            P(("rep", "patch"), None),
        ),
        out_specs=P(("rep", "patch"), ("tp", "sec")),
        check_vma=False,
    )
```

```python
import functools
import math

import jax
import jax.numpy as jnp
from jax import lax
from jax.experimental import pallas as pl
from jax.experimental.pallas import tpu as pltpu
from jax.sharding import PartitionSpec as P

HEAD_DIM = 128
BLOCK = 128
QUERY_TILE = 512
ROW_CHUNKS = (1, 1)
ROW_TILE = 512
COST_SCALE = 0.2
VMEM_LIMIT = 28 * 1024 * 1024
F32 = jnp.float32
BF16 = jnp.bfloat16


def after(value, *others):
    return lax.optimization_barrier((value,) + others)[0]


def params():
    return pltpu.CompilerParams(vmem_limit_bytes=VMEM_LIMIT)


def cost(flops, moved, exps=0):
    scale = COST_SCALE
    return pl.CostEstimate(flops=int(flops * scale), bytes_accessed=int(moved * scale), transcendentals=int(exps * scale))


def unit(value):
    return value * lax.rsqrt(jnp.mean(value * value, axis=-1, keepdims=True) + 1e-06)


def stale_kernel(in_ref, out_ref):
    out_ref[:, :HEAD_DIM] = unit(in_ref[:, :HEAD_DIM].astype(F32)).astype(BF16)
    out_ref[:, HEAD_DIM:] = in_ref[:, HEAD_DIM:]


def stale_group(stale, first, heads):
    rows = stale.shape[0]
    return pl.pallas_call(
        stale_kernel,
        grid=(heads,),
        in_specs=[pl.BlockSpec((rows, 2 * HEAD_DIM), lambda h: (0, first + h))],
        out_specs=pl.BlockSpec((rows, 2 * HEAD_DIM), lambda h: (0, h)),
        out_shape=jax.ShapeDtypeStruct((rows, heads * 2 * HEAD_DIM), BF16),
        compiler_params=params(),
        cost_estimate=cost(rows * heads * 512, rows * heads * 1024),
    )(stale)


def own_kernel(left_ref, right_ref, out_ref):
    out_ref[...] = jnp.dot(left_ref[...], right_ref[...], preferred_element_type=F32)


def own_terms(left, right, first, heads):
    rows, depth = left.shape
    width = 3 * HEAD_DIM
    return pl.pallas_call(
        own_kernel,
        grid=(heads,),
        in_specs=[
            pl.BlockSpec((rows, depth), lambda h: (0, 0)),
            pl.BlockSpec((depth, width), lambda h: (0, first + h)),
        ],
        out_specs=pl.BlockSpec((rows, width), lambda h: (0, h)),
        out_shape=jax.ShapeDtypeStruct((rows, heads * width), F32),
        compiler_params=params(),
        cost_estimate=cost(2 * rows * depth * heads * width, rows * heads * width * 4 + depth * (rows + heads * width) * 2),
    )(left, right)


def finish_kernel(terms, *refs):
    total = refs[2 * terms][...]
    for at in range(terms):
        total += jnp.dot(refs[at][...], refs[terms + at][...], preferred_element_type=F32)
    q_ref, k_ref, v_ref = refs[2 * terms + 1 :]
    q_ref[...] = unit(total[:, :HEAD_DIM]).astype(BF16)
    k_ref[...] = unit(total[:, HEAD_DIM : 2 * HEAD_DIM]).astype(BF16)
    v_ref[...] = total[:, 2 * HEAD_DIM :].astype(BF16)


def finish(acc, terms):
    lefts, rights = [left for left, _ in terms], [right for _, right in terms]
    width, rows = 3 * HEAD_DIM, acc.shape[0]
    heads, tile = acc.shape[1] // width, rows
    depth = sum(left.shape[1] for left in lefts)
    out = pl.BlockSpec((tile, HEAD_DIM), lambda h, i: (i, h))
    return pl.pallas_call(
        functools.partial(finish_kernel, len(terms)),
        grid=(heads, rows // tile),
        in_specs=[pl.BlockSpec((tile, left.shape[1]), lambda h, i: (i, 0)) for left in lefts]
        + [pl.BlockSpec((right.shape[0], width), lambda h, i: (0, h)) for right in rights]
        + [pl.BlockSpec((tile, width), lambda h, i: (i, h))],
        out_specs=[out] * 3,
        out_shape=[jax.ShapeDtypeStruct((rows, heads * HEAD_DIM), BF16)] * 3,
        compiler_params=params(),
        cost_estimate=cost(2 * rows * depth * heads * width, rows * heads * width * 6),
    )(*lefts, *rights, acc)


def weigh(query, key, mask):
    tile, keys = query.shape[0], key.shape[0]
    scores = lax.dot_general(query, key, (((1,), (1,)), ((), ())), preferred_element_type=F32)
    exponents = jnp.exp(scores * (1.0 / math.sqrt(HEAD_DIM)))
    exponents = exponents.reshape(tile // BLOCK, BLOCK, keys) * mask
    return exponents.reshape(tile, keys).astype(BF16)


def with_ones(value):
    return jnp.concatenate([value, jnp.ones(value.shape, value.dtype)], axis=1)


def window_kernel(fresh, sides, prior, flag_ref, q_ref, *refs):
    num_ref, tot_ref = refs[-2:]
    query = q_ref[...]
    shape = (query.shape[0], 2 * HEAD_DIM)

    def terms(first, windows):
        both = jnp.zeros(shape, F32)
        for at in range(first, first + windows):
            k_ref, v_ref, m_ref = refs[3 * at : 3 * at + 3]
            weights = weigh(query, k_ref[...], m_ref[...])
            both += jnp.dot(weights, with_ones(v_ref[...]), preferred_element_type=F32)
        return both[:, :HEAD_DIM], both[:, HEAD_DIM:]

    if prior:
        num, tot = refs[3 * (fresh + sides)][...], refs[3 * (fresh + sides) + 1][...]
    if fresh:
        num, tot = terms(0, fresh)
    num_ref[...] = num
    tot_ref[...] = tot
    for side in range(sides):

        @pl.when(flag_ref[side] == 1)
        def _(side=side):
            more, more_tot = terms(fresh + side, 1)
            num_ref[...] += more
            tot_ref[...] += more_tot


def windows(flag, queries, here, fresh, sides, prior):
    first, heads = here
    rows, cols = queries.shape[0], heads * HEAD_DIM
    query = pl.BlockSpec((QUERY_TILE, HEAD_DIM), lambda h, i, f: (i, first + h))
    tile = pl.BlockSpec((QUERY_TILE, HEAD_DIM), lambda h, i, f: (i, h))
    specs, values = [], []
    for keys, vals, mask in fresh:
        block = pl.BlockSpec((keys.shape[0], HEAD_DIM), lambda h, i, f: (0, first + h))
        specs += [block, block]
        values += [keys, vals, mask]
        specs.append(pl.BlockSpec((QUERY_TILE // BLOCK, 1, keys.shape[0]), lambda h, i, f: (i, 0, 0)))
    for stale, mask, at in sides:
        specs.append(pl.BlockSpec((stale.shape[0], HEAD_DIM), lambda h, i, f, at=at: (0, 2 * (at + h))))
        specs.append(pl.BlockSpec((stale.shape[0], HEAD_DIM), lambda h, i, f, at=at: (0, 2 * (at + h) + 1)))
        specs.append(pl.BlockSpec((QUERY_TILE // BLOCK, 1, stale.shape[0]), lambda h, i, f: (i, 0, 0)))
        values += [stale, stale, mask]
    count = len(fresh) + len(sides)
    return pl.pallas_call(
        functools.partial(window_kernel, len(fresh), len(sides), len(prior)),
        grid_spec=pltpu.PrefetchScalarGridSpec(
            num_scalar_prefetch=1,
            grid=(heads, rows // QUERY_TILE),
            in_specs=[query] + specs + [tile] * len(prior),
            out_specs=[tile, tile],
        ),
        out_shape=[jax.ShapeDtypeStruct((rows, cols), F32)] * 2,
        compiler_params=params(),
        cost_estimate=cost(6 * count * rows * rows * cols, rows * cols * 14 * count, count * rows * rows * heads),
    )(flag, queries, *values, *prior)


def foreign_kernel(flag_ref, q_ref, k_ref, v_ref, mask_ref, num_ref, tot_ref):
    head = pl.program_id(1)

    @pl.when(head == 0)
    def _():
        tot_ref[...] = jnp.zeros_like(tot_ref)

    @pl.when(flag_ref[0] == 1)
    def _():
        value = v_ref[...]
        weights = weigh(q_ref[...], k_ref[...], mask_ref[...])
        num_ref[...] = jnp.dot(weights, value, preferred_element_type=F32).astype(BF16)
        sums = lax.dot_general(
            jnp.ones((8, weights.shape[1]), BF16), weights, (((1,), (1,)), ((), ())), preferred_element_type=F32
        )
        row = lax.broadcasted_iota(jnp.int32, sums.shape, 0)
        tot_ref[...] = jnp.where(row == head, sums, tot_ref[...])

    @pl.when(flag_ref[0] != 1)
    def _():
        num_ref[...] = jnp.zeros_like(num_ref)


def foreign_part(flag, queries, first, heads, stale, mask):
    rows, cols, window = queries.shape[0], heads * HEAD_DIM, stale.shape[0]
    query = pl.BlockSpec((QUERY_TILE, HEAD_DIM), lambda i, h, f: (i, h))
    tile = pl.BlockSpec((QUERY_TILE, HEAD_DIM), lambda i, h, f: (i, h))
    return pl.pallas_call(
        foreign_kernel,
        grid_spec=pltpu.PrefetchScalarGridSpec(
            num_scalar_prefetch=1,
            grid=(rows // QUERY_TILE, heads),
            in_specs=[
                query,
                pl.BlockSpec((window, HEAD_DIM), lambda i, h, f: (0, 2 * (first + h))),
                pl.BlockSpec((window, HEAD_DIM), lambda i, h, f: (0, 2 * (first + h) + 1)),
                pl.BlockSpec((QUERY_TILE // BLOCK, 1, window), lambda i, h, f: (i, 0, 0)),
            ],
            out_specs=[tile, pl.BlockSpec((8, QUERY_TILE), lambda i, h, f: (0, i))],
        ),
        out_shape=[jax.ShapeDtypeStruct((rows, cols), BF16), jax.ShapeDtypeStruct((8, rows), F32)],
        compiler_params=params(),
        cost_estimate=cost(4 * rows * window * cols, rows * cols * 8, rows * window * heads),
    )(flag, queries, stale, stale, mask)


def normalise_into(att_ref, column, near_refs, num_ref=None, tot_ref=None):
    totals = None if tot_ref is None else jnp.transpose(tot_ref[...])
    at = 0
    for n_ref, t_ref in near_refs:
        for head in range(n_ref.shape[1] // HEAD_DIM):
            cols = slice(head * HEAD_DIM, (head + 1) * HEAD_DIM)
            num, tot = n_ref[:, cols], t_ref[:, cols]
            if num_ref is not None:
                num += num_ref[:, at * HEAD_DIM : (at + 1) * HEAD_DIM].astype(F32)
                tot += totals[:, at : at + 1]
            att_ref[:, (column + at) * HEAD_DIM : (column + at + 1) * HEAD_DIM] = (num / tot).astype(BF16)
            at += 1


def normalise_kernel(*refs):
    near_refs = [(refs[2 * at], refs[2 * at + 1]) for at in range((len(refs) - 3) // 2)]
    normalise_into(refs[-1], 0, near_refs, refs[-3], refs[-2])


def normalise(near, far):
    num, tot = far
    rows, cols = num.shape
    tile = 512
    specs, values = [], []
    for pair in near:
        specs += [pl.BlockSpec((tile, pair[0].shape[1]), lambda i: (i, 0))] * 2
        values += list(pair)
    return pl.pallas_call(
        normalise_kernel,
        grid=(rows // tile,),
        in_specs=specs + [pl.BlockSpec((tile, cols), lambda i: (i, 0)), pl.BlockSpec((8, tile), lambda i: (0, i))],
        out_specs=pl.BlockSpec((tile, cols), lambda i: (i, 0)),
        out_shape=jax.ShapeDtypeStruct((rows, cols), BF16),
        compiler_params=params(),
        cost_estimate=cost(rows * cols * 4, rows * cols * 12),
    )(*values, num, tot)


def branch_kernel(near, keeps, parts, where_ref, *refs):
    step, steps = pl.program_id(0), pl.num_programs(0)
    mine_ref, own_refs, other_refs = refs[0], refs[1:parts], refs[parts : 2 * parts - 1]
    g_ref, done_ref = refs[2 * parts - 1 : 2 * parts + 1]
    rest = refs[2 * parts + 1 :]
    send_ref, keep_ref, att_ref, lefts_ref = rest[-4:]
    lefts_ref = lefts_ref.at[pl.program_id(1)]
    rank, depth = where_ref[3 * steps], mine_ref.shape[1]

    @pl.when(step == 0)
    def _():
        att_ref[:, : done_ref.shape[1]] = done_ref[...]
        near_refs = [(rest[2 * at], rest[2 * at + 1]) for at in range(near)]
        normalise_into(att_ref, done_ref.shape[1] // HEAD_DIM, near_refs)
        for offset in range(parts):
            part = lax.rem(rank + parts - offset, parts)
            left = att_ref[:, :depth]
            for other in range(1, parts):
                left = jnp.where(part == other, att_ref[:, other * depth : (other + 1) * depth], left)
            lefts_ref[offset] = left

    is_own = where_ref[step] == 0
    term = jnp.dot(lefts_ref[0], mine_ref[0], preferred_element_type=F32)
    for offset in range(1, parts):
        right = jnp.where(is_own, own_refs[offset - 1][...], other_refs[offset - 1][0])
        term += jnp.dot(lefts_ref[offset], right, preferred_element_type=F32)
    result = (term * g_ref[0]).astype(BF16)
    stays = step >= steps - keeps

    @pl.when(stays)
    def _():
        keep_ref[0] = result

    @pl.when(jnp.logical_not(stays))
    def _():
        send_ref[0] = result


def branch(where, mine, owns, others, gate, done, near, first, count, keeps):
    total, depth, width = mine.shape
    tile = ROW_TILE if count % ROW_TILE == 0 and first % ROW_TILE == 0 else BLOCK
    start, tiles = first // tile, count // tile
    sends = total - keeps

    def row_tile(g, i, w):
        return start + jnp.where(g == 0, i, tiles - 1), 0

    specs, values = [pl.BlockSpec((tile, done.shape[1]), row_tile)], [done]
    for num, tot in near:
        spec = pl.BlockSpec((tile, num.shape[1]), row_tile)
        specs += [spec, spec]
        values += [num, tot]
    parts = len(others) + 1
    held = depth * parts
    return pl.pallas_call(
        functools.partial(branch_kernel, len(near), keeps, parts),
        grid_spec=pltpu.PrefetchScalarGridSpec(
            num_scalar_prefetch=1,
            grid=(total, tiles),
            in_specs=[pl.BlockSpec((1, depth, width), lambda g, i, w: (w[g], 0, 0))]
            + [pl.BlockSpec((depth, width), lambda g, i, w: (0, 0))] * len(owns)
            + [pl.BlockSpec((1, depth, width), lambda g, i, w: (w[total + g], 0, 0))] * len(others)
            + [pl.BlockSpec((1, 1, width), lambda g, i, w: (w[2 * total + g], 0, 0))]
            + specs,
            out_specs=[
                pl.BlockSpec((1, tile, width), lambda g, i, w: (jnp.minimum(g, sends - 1), jnp.where(g < sends, i, tiles - 1), 0)),
                pl.BlockSpec((1, tile, width), lambda g, i, w: (jnp.maximum(g - sends, 0), jnp.where(g < sends, 0, i), 0)),
            ],
            scratch_shapes=[pltpu.VMEM((tile, held), BF16), pltpu.VMEM((tiles, parts, tile, depth), BF16)],
        ),
        out_shape=[
            jax.ShapeDtypeStruct((sends, count, width), BF16),
            jax.ShapeDtypeStruct((keeps, count, width), BF16),
        ],
        compiler_params=params(),
        cost_estimate=cost(2 * count * held * total * width, held * total * width * 2 + count * total * width * 2),
    )(where, mine, *owns, *others, gate, *values)


def chosen(place, values, names):
    out = values[0]
    for at in range(1, len(values)):
        if names[at] != names[0]:
            out = jnp.where(place == at, values[at], out)
    return out


class Relay:
    def __init__(self, own, count, reps):
        self.count, self.reps = count, reps
        self.place, self.rank = lax.axis_index("patch"), lax.axis_index("rep")
        self.ahead, self.back = {0: own}, {0: own}

    def step(self, k, *held):
        count = self.count
        ahead, back = self.ahead[k - 1], self.back[k - 1]
        if held:
            ahead, back = after(ahead, *held), after(back, *held)
        self.ahead[k] = lax.ppermute(ahead, "patch", [(i, i + 1) for i in range(k - 1, count - 1)])
        self.back[k] = lax.ppermute(back, "patch", [(i + 1, i) for i in range(count - k)])

    def sent(self, k):
        return self.ahead[k], self.back[k]

    def brought(self, t, cut=None):
        values, owners = [], []
        for at in range(self.count):
            comes = sorted([(k, 0) for k in range(1, at + 1)] + [(k, 1) for k in range(1, self.count - at)])
            k, side = comes[t - 1]
            values.append(self.back[k] if side else self.ahead[k])
            owners.append(at + k if side else at - k)
        owner = sum(jnp.where(self.place == at, owners[at], 0) for at in range(self.count))
        candidates = []
        for value in values:
            if not any(value is other for other in candidates):
                candidates.append(value)
        fenced = lax.optimization_barrier(tuple(candidates))
        at_of = [[value is other for other in candidates].index(True) for value in values]
        cuts = [(0, values[0].shape[1])] if cut is None else [(0, cut), (cut, values[0].shape[1])]
        chosen_cuts = [chosen(self.place, [fenced[at][:, low:high] for at in at_of], at_of) for low, high in cuts]
        parts = [(self.rank, chosen_cuts)]
        for offset in range(1, self.reps):
            pairs = [(a, (a + offset) % self.reps) for a in range(self.reps)]
            swapped, held = [], ()
            for piece in chosen_cuts:
                swapped.append(lax.ppermute(after(piece, *held) if held else piece, "rep", pairs))
                held = (swapped[-1],)
            parts.append(((self.rank - offset) % self.reps, swapped))
        return owner, parts


def body(hidden, modulation, gate, w_qkv, stale_kv, w_out, key_lists):
    count, reps = lax.axis_size("patch"), lax.axis_size("rep")
    tps, secs = lax.axis_size("tp"), lax.axis_size("sec")
    place, rank = lax.axis_index("patch"), lax.axis_index("rep")
    tp_index, sec_index = lax.axis_index("tp"), lax.axis_index("sec")
    rows, model_width = hidden.shape[1], hidden.shape[2]
    heads = w_out.shape[1] // HEAD_DIM
    patch_blocks = rows // BLOCK
    unit_heads = heads // 3 if heads % 3 == 0 else 1
    units = heads // unit_heads
    small_units = max(1, units // 3)
    group_units = [list(range(units - small_units)), list(range(units - small_units, units))]
    group_heads = [len(members) * unit_heads for members in group_units]
    group_first = [0, group_heads[0]]
    states = hidden[0]
    w_qkv, stale_kv, w_out = w_qkv[0], stale_kv[0], w_out[0]
    last = count - 1
    shard_rows = w_qkv.shape[0]
    depth, out_depth = shard_rows // reps, w_out.shape[0] // reps
    width = 3 * HEAD_DIM

    relative = jnp.where(key_lists >= 0, key_lists - (place - 1) * patch_blocks, -1)
    window_ids = jnp.arange(3 * patch_blocks, dtype=jnp.int32)
    hits = jnp.any(relative[:, :, None] == window_ids[None, None, :], axis=1).astype(F32)
    hits = jnp.repeat(hits, BLOCK, axis=1).reshape(patch_blocks, 3, rows)
    before, fresh, behind = (hits[:, i][:, None, :] for i in range(3))
    odd = place % 2 == 1
    even_mask, odd_mask = jnp.where(odd, before, behind), jnp.where(odd, behind, before)
    at_end = (place == 0) | (place == last)
    to_inner = [(0, 1), (last, last - 1)]
    to_end = [(1, 0), (last - 1, last)]
    inner_flag = jnp.where(at_end, 0, 1).astype(jnp.int32).reshape(1)
    host_flag = ((place == 1) | (place == last - 1)).astype(jnp.int32).reshape(1)

    inner = range(1, last)
    pairs = [(i, i + 1) for i in range(last)] + [(i + 1, i) for i in range(last)]
    even_pairs = [(a, b) for a, b in pairs if min(a, b) % 2 == 0 and b in inner]
    odd_pairs = [(a, b) for a, b in pairs if min(a, b) % 2 == 1 and b in inner]
    stale, even, other = [None] * units, [None] * units, [None] * units

    def send_even(unit, *held):
        even[unit] = lax.ppermute(after(stale[unit], *held), "patch", even_pairs)

    def send_other(unit, *held):
        other[unit] = lax.ppermute(after(stale[unit], *held), "patch", odd_pairs)

    def qkv_relay(group, *held):
        source = after(w_qkv, *held) if held else w_qkv
        at = (rank * depth, group_first[group] * width)
        own = lax.dynamic_slice(source, at, (depth, group_heads[group] * width))
        if group == 1:
            own = jnp.concatenate([own, own_out.reshape(depth, out_cols)], axis=1)
        return Relay(own, count, reps)

    def columns(owner, part):
        return lax.dynamic_slice_in_dim(ready, owner * shard_rows + part * depth, depth, 1)

    def term_of(owner, part, piece):
        return columns(owner, part), piece

    def add_terms(acc, terms):
        for left, right in terms:
            acc += jnp.dot(left, right, preferred_element_type=F32)
        return acc

    out_shape = (out_depth, w_out.shape[1])
    out_cols = out_depth * w_out.shape[1] // depth
    small_cols = group_heads[1] * width
    large = qkv_relay(0)
    large.step(1)
    inputs = states.astype(F32)
    centered = inputs - jnp.mean(inputs, axis=-1, keepdims=True)
    variance = jnp.mean(centered * centered, axis=-1, keepdims=True)
    normed = centered * lax.rsqrt(variance + 1e-06)
    modulated = (normed * (1.0 + modulation[0, 1]) + modulation[0, 0]).astype(BF16)
    for at in range(units):
        stale[at] = stale_group(stale_kv, at * unit_heads, unit_heads)
    modulated, stale[0] = lax.optimization_barrier((modulated, stale[0]))

    ready = after(modulated, *large.sent(1))
    own_columns = lax.dynamic_slice_in_dim(ready, place * shard_rows, shard_rows, 1)
    accs = [None, None]
    come = [[], []]
    far_mask = lax.ppermute(jnp.where(place == 0, behind, before), "patch", to_inner)
    share = model_width // (tps * secs)
    residual = lax.dynamic_slice_in_dim(states, (tp_index * secs + sec_index) * share, share, 1)
    got_all = []
    for offset in range(1, secs):
        target = (1 + offset) % secs
        sent = lax.dynamic_slice_in_dim(states, (tp_index * secs + target) * share, share, 1)
        got = lax.ppermute(sent, "sec", [(1, target)])
        got_all.append(got)
        residual = jnp.where(sec_index == target, got, residual)

    def swaps(group, at):
        return [piece[0] for _, piece in come[group][at][1][1:]] if 0 <= at < len(come[group]) else []

    def given(*items):
        return [item for item in items if item is not None]

    def at_or_none(items, at):
        return items[at] if at < len(items) else None

    def own_half(group, at):
        owner, parts = come[group][at]
        return [term_of(owner, parts[0][0], parts[0][1][0])]

    def other_half(group, at):
        owner, parts = come[group][at]
        return [term_of(owner, part, piece[0]) for part, piece in parts[1:]]

    come[0].append(large.brought(1))
    send_even(0, *large.sent(1))
    for k in range(2, count):
        held = [modulated, far_mask] + got_all if k == 2 else [accs[0]] + swaps(0, k - 3)
        if k == 3:
            held += [even[0], residual]
        large.step(k, *held)
        come[0].append(large.brought(k))
        if k == 2:
            accs[0] = own_terms(after(own_columns, *large.sent(1)), w_qkv, 0, group_heads[0])
            if units > 1:
                send_even(1, *large.sent(2))
                send_other(0, *large.sent(2))
        elif k == 3:
            accs[0] = add_terms(accs[0], own_half(0, 0) + own_half(0, 1) + other_half(0, 0))

    own_out = lax.dynamic_slice_in_dim(after(w_out, *large.sent(1)), rank * out_depth, out_depth, 0)
    small = qkv_relay(1, *large.sent(min(2, last)))
    small.step(
        1, *large.sent(last), accs[0], *swaps(0, last - 2), *given(at_or_none(even, 1), at_or_none(other, 0))
    )
    come[1].append(small.brought(1, small_cols if last == 1 else None))
    for at in range(2, last - 1):
        accs[0] = add_terms(accs[0], own_half(0, at) + other_half(0, at - 1))
    accs[1] = own_terms(after(own_columns, *large.sent(last)), w_qkv, group_first[1], group_heads[1])
    final_terms = own_half(0, last - 1) + other_half(0, last - 1)
    if last > 1:
        final_terms = other_half(0, last - 2) + final_terms
    queries_0 = finish(accs[0], final_terms)
    far_queries_0 = lax.ppermute(queries_0[0], "patch", to_inner)
    queries_1 = None

    def near_part(group, at, fresh_too, sides, flags, prior):
        queries, keys, values = (queries_0, queries_1)[group]
        here = (at * unit_heads, unit_heads)
        return windows(flags, queries, here, [(keys, values, fresh)] if fresh_too else [], sides, prior)

    def sides_of(unit_at):
        late = unit_at > 0
        stale_at = (unit_at - 1) * unit_heads if late else 0
        return [(even[unit_at], even_mask, 0), (other[1 if late else 0], odd_mask, stale_at)]

    all_even = [(a, b) for a, b in pairs if min(a, b) % 2 == 0]
    late_stale = stale_group(after(stale_kv, *large.sent(last)), unit_heads, heads - unit_heads)

    def late_exchanges(held):
        for at in group_units[1]:
            even[at] = lax.ppermute(after(stale[at], *held, *swaps(1, 0)), "patch", all_even)
        for at in group_units[0]:
            if even[at] is None:
                send_even(at, *held)
        other[1] = lax.ppermute(after(late_stale, *held), "patch", odd_pairs)

    first_large = group_units[0]
    inner_flags = jnp.concatenate([inner_flag, inner_flag])
    near = [None] * units
    near[0] = near_part(0, 0, True, sides_of(0), inner_flags, ())
    for k in range(2, count):
        if k == 2:
            held = [accs[1]]
        elif k == 3:
            held = [*queries_0, near[0][0]]
        else:
            held = swaps(1, k - 4)
        small.step(k, *held)
        come[1].append(small.brought(k, small_cols if k == last else None))
        if k == 2:
            late_exchanges(small.sent(2))
    if other[1] is None:
        late_exchanges(small.sent(last))

    stale_full = stale_group(after(stale_kv, *small.sent(1)), 0, group_heads[0])
    far_num, far_tot = foreign_part(host_flag, far_queries_0, 0, group_heads[0], stale_full, far_mask)
    come_last = come[1][-1][1][0][1]
    exchanged = [even[at] for at in group_units[1]] + [other[1]]
    back_tot = lax.ppermute(after(far_tot, *small.sent(last)), "patch", to_end)
    back_num = lax.ppermute(
        after(far_num, *small.sent(last), *come_last, *exchanged, *swaps(1, last - 2), back_tot), "patch", to_end
    )
    for at, unit_at in enumerate(first_large):
        if unit_at:
            part = near_part(0, at, True, sides_of(unit_at)[:1], inner_flag, ())
            near[unit_at] = near_part(0, at, False, sides_of(unit_at)[1:], inner_flag, tuple(part))

    early = []
    for at in range(last - 2):
        early += own_half(1, at) + other_half(1, at)
    if early:
        accs[1] = add_terms(accs[1], [(left, right[:, :small_cols]) for left, right in early])
    final_terms = []
    for at in range(max(last - 2, 0), last):
        final_terms += own_half(1, at) + other_half(1, at)
    fenced = lax.optimization_barrier((accs[1], near[first_large[-1]][0]))
    queries_1 = finish(fenced[0], final_terms)
    always = jnp.concatenate([jnp.ones((1,), jnp.int32), inner_flag])
    for at, unit_at in enumerate(group_units[1]):
        near[unit_at] = near_part(1, at, True, sides_of(unit_at), always, ())
    done = normalise([near[at] for at in group_units[0]], (back_num, back_tot))

    out_mine, out_others, out_owns, owners = [own_out], [[] for _ in range(reps - 1)], [], [place]
    for owner, parts in come[1]:
        owners.append(owner)
        for at, (_, piece) in enumerate(parts):
            rows_out = (piece[0][:, small_cols:] if len(piece) == 1 else piece[1]).reshape(out_shape)
            if at == 0:
                out_mine.append(rows_out)
            else:
                out_others[at - 1].append(rows_out)
    out_mine = jnp.stack(out_mine)
    out_others = [jnp.stack(items) for items in out_others]
    for offset in range(1, reps):
        out_owns.append(lax.dynamic_slice_in_dim(w_out, (rank - offset) % reps * out_depth, out_depth, 0))

    per = count // (tps * secs)
    order = [
        (block * secs + (sec_index + offset) % secs) * per + at
        for offset in list(range(1, secs)) + [0]
        for block in range(tps)
        for at in range(per)
    ]
    turns = [sum(jnp.where(owners[t] == column, t, 0) for t in range(count)) for column in order]
    where = jnp.stack(turns + [jnp.maximum(turn - 1, 0) for turn in turns] + order + [rank]).astype(jnp.int32)
    gate_blocks = gate.reshape(count, 1, w_out.shape[1])
    keeps = tps * per
    results = []
    start = 0
    for share_rows in ROW_CHUNKS:
        chunk = rows * share_rows // sum(ROW_CHUNKS)
        sends, keep = branch(
            where, out_mine, out_owns, out_others, gate_blocks, done,
            [near[unit_at] for unit_at in group_units[1]], start, chunk, keeps,
        )
        got = [keep]
        for offset in range(1, secs):
            sent = sends[(offset - 1) * keeps : offset * keeps]
            got.append(lax.ppermute(sent, "sec", [(i, (i + offset) % secs) for i in range(secs)]))

        def block_of(index):
            return sum(lax.dynamic_slice_in_dim(part, index * per, per, 0).astype(F32) for part in got)

        others = []
        for offset in range(1, tps):
            sent = block_of((tp_index + offset) % tps).astype(BF16)
            others.append(lax.ppermute(sent, "tp", [(i, (i + offset) % tps) for i in range(tps)]))
        others = [after(part, *results) for part in others] if results else others
        result = block_of(tp_index) + sum(part.astype(F32) for part in others)
        result = jnp.moveaxis(result, 0, 1).reshape(chunk, share)
        results.append((result + residual[start : start + chunk].astype(F32)).astype(BF16))
        start += chunk
    return jnp.concatenate(results, axis=0)


def solution(mesh):
    return jax.shard_map(
        body,
        mesh=mesh,
        in_specs=(
            P("sec", ("rep", "patch"), None),
            P("sec", None, None),
            P("sec", None),
            P("sec", "patch", "tp"),
            P("sec", ("rep", "patch"), "tp"),
            P("sec", "tp", "patch"),
            P(("rep", "patch"), None),
        ),
        out_specs=P(("rep", "patch"), ("tp", "sec")),
        check_vma=False,
    )
```

```python
import functools
import math

import jax
import jax.numpy as jnp
from jax import lax
from jax.experimental import pallas as pl
from jax.experimental.pallas import tpu as pltpu
from jax.sharding import PartitionSpec as P

HEAD_DIM = 128
BLOCK = 128
QUERY_TILE = 512
ROW_CHUNKS = (1, 1)
ROW_TILE = 512
COST_SCALE = 0.2
VMEM_LIMIT = 28 * 1024 * 1024
F32 = jnp.float32
BF16 = jnp.bfloat16


def after(value, *others):
    return lax.optimization_barrier((value,) + others)[0]


def params():
    return pltpu.CompilerParams(vmem_limit_bytes=VMEM_LIMIT)


def cost(flops, moved, exps=0):
    scale = COST_SCALE
    return pl.CostEstimate(flops=int(flops * scale), bytes_accessed=int(moved * scale), transcendentals=int(exps * scale))


def unit(value):
    return value * lax.rsqrt(jnp.mean(value * value, axis=-1, keepdims=True) + 1e-06)


def stale_kernel(in_ref, out_ref):
    out_ref[:, :HEAD_DIM] = unit(in_ref[:, :HEAD_DIM].astype(F32)).astype(BF16)
    out_ref[:, HEAD_DIM:] = in_ref[:, HEAD_DIM:]


def stale_group(stale, first, heads):
    rows = stale.shape[0]
    return pl.pallas_call(
        stale_kernel,
        grid=(heads,),
        in_specs=[pl.BlockSpec((rows, 2 * HEAD_DIM), lambda h: (0, first + h))],
        out_specs=pl.BlockSpec((rows, 2 * HEAD_DIM), lambda h: (0, h)),
        out_shape=jax.ShapeDtypeStruct((rows, heads * 2 * HEAD_DIM), BF16),
        compiler_params=params(),
        cost_estimate=cost(rows * heads * 512, rows * heads * 1024),
    )(stale)


def own_kernel(left_ref, right_ref, out_ref):
    out_ref[...] = jnp.dot(left_ref[...], right_ref[...], preferred_element_type=F32)


def own_terms(left, right, first, heads):
    rows, depth = left.shape
    width = 3 * HEAD_DIM
    return pl.pallas_call(
        own_kernel,
        grid=(heads,),
        in_specs=[
            pl.BlockSpec((rows, depth), lambda h: (0, 0)),
            pl.BlockSpec((depth, width), lambda h: (0, first + h)),
        ],
        out_specs=pl.BlockSpec((rows, width), lambda h: (0, h)),
        out_shape=jax.ShapeDtypeStruct((rows, heads * width), F32),
        compiler_params=params(),
        cost_estimate=cost(2 * rows * depth * heads * width, rows * heads * width * 4 + depth * (rows + heads * width) * 2),
    )(left, right)


def finish_kernel(terms, *refs):
    total = refs[2 * terms][...]
    for at in range(terms):
        total += jnp.dot(refs[at][...], refs[terms + at][...], preferred_element_type=F32)
    q_ref, k_ref, v_ref = refs[2 * terms + 1 :]
    q_ref[...] = unit(total[:, :HEAD_DIM]).astype(BF16)
    k_ref[...] = unit(total[:, HEAD_DIM : 2 * HEAD_DIM]).astype(BF16)
    v_ref[...] = total[:, 2 * HEAD_DIM :].astype(BF16)


def finish(acc, terms):
    lefts, rights = [left for left, _ in terms], [right for _, right in terms]
    width, rows = 3 * HEAD_DIM, acc.shape[0]
    heads, tile = acc.shape[1] // width, rows
    depth = sum(left.shape[1] for left in lefts)
    out = pl.BlockSpec((tile, HEAD_DIM), lambda h, i: (i, h))
    return pl.pallas_call(
        functools.partial(finish_kernel, len(terms)),
        grid=(heads, rows // tile),
        in_specs=[pl.BlockSpec((tile, left.shape[1]), lambda h, i: (i, 0)) for left in lefts]
        + [pl.BlockSpec((right.shape[0], width), lambda h, i: (0, h)) for right in rights]
        + [pl.BlockSpec((tile, width), lambda h, i: (i, h))],
        out_specs=[out] * 3,
        out_shape=[jax.ShapeDtypeStruct((rows, heads * HEAD_DIM), BF16)] * 3,
        compiler_params=params(),
        cost_estimate=cost(2 * rows * depth * heads * width, rows * heads * width * 6),
    )(*lefts, *rights, acc)


def weigh(query, key, mask):
    tile, keys = query.shape[0], key.shape[0]
    scores = lax.dot_general(query, key, (((1,), (1,)), ((), ())), preferred_element_type=F32)
    exponents = jnp.exp(scores * (1.0 / math.sqrt(HEAD_DIM)))
    exponents = exponents.reshape(tile // BLOCK, BLOCK, keys) * mask
    return exponents.reshape(tile, keys).astype(BF16)


def with_ones(value):
    return jnp.concatenate([value, jnp.ones(value.shape, value.dtype)], axis=1)


def window_kernel(fresh, sides, prior, flag_ref, q_ref, *refs):
    num_ref, tot_ref = refs[-2:]
    query = q_ref[...]
    shape = (query.shape[0], 2 * HEAD_DIM)

    def terms(first, windows):
        both = jnp.zeros(shape, F32)
        for at in range(first, first + windows):
            k_ref, v_ref, m_ref = refs[3 * at : 3 * at + 3]
            weights = weigh(query, k_ref[...], m_ref[...])
            both += jnp.dot(weights, with_ones(v_ref[...]), preferred_element_type=F32)
        return both[:, :HEAD_DIM], both[:, HEAD_DIM:]

    if prior:
        num, tot = refs[3 * (fresh + sides)][...], refs[3 * (fresh + sides) + 1][...]
    if fresh:
        num, tot = terms(0, fresh)
    num_ref[...] = num
    tot_ref[...] = tot
    for side in range(sides):

        @pl.when(flag_ref[side] == 1)
        def _(side=side):
            more, more_tot = terms(fresh + side, 1)
            num_ref[...] += more
            tot_ref[...] += more_tot


def windows(flag, queries, here, fresh, sides, prior, span=None):
    first, heads = here
    low, rows = (0, queries.shape[0]) if span is None else span
    cols, skip = heads * HEAD_DIM, low // QUERY_TILE
    query = pl.BlockSpec((QUERY_TILE, HEAD_DIM), lambda h, i, f: (skip + i, first + h))
    tile = pl.BlockSpec((QUERY_TILE, HEAD_DIM), lambda h, i, f: (i, h))
    specs, values = [], []
    for keys, vals, mask in fresh:
        block = pl.BlockSpec((keys.shape[0], HEAD_DIM), lambda h, i, f: (0, first + h))
        specs += [block, block]
        values += [keys, vals, mask]
        specs.append(pl.BlockSpec((QUERY_TILE // BLOCK, 1, keys.shape[0]), lambda h, i, f: (skip + i, 0, 0)))
    for stale, mask, at in sides:
        specs.append(pl.BlockSpec((stale.shape[0], HEAD_DIM), lambda h, i, f, at=at: (0, 2 * (at + h))))
        specs.append(pl.BlockSpec((stale.shape[0], HEAD_DIM), lambda h, i, f, at=at: (0, 2 * (at + h) + 1)))
        specs.append(pl.BlockSpec((QUERY_TILE // BLOCK, 1, stale.shape[0]), lambda h, i, f: (skip + i, 0, 0)))
        values += [stale, stale, mask]
    count = len(fresh) + len(sides)
    return pl.pallas_call(
        functools.partial(window_kernel, len(fresh), len(sides), len(prior)),
        grid_spec=pltpu.PrefetchScalarGridSpec(
            num_scalar_prefetch=1,
            grid=(heads, rows // QUERY_TILE),
            in_specs=[query] + specs + [tile] * len(prior),
            out_specs=[tile, tile],
        ),
        out_shape=[jax.ShapeDtypeStruct((rows, cols), F32)] * 2,
        compiler_params=params(),
        cost_estimate=cost(6 * count * rows * rows * cols, rows * cols * 14 * count, count * rows * rows * heads),
    )(flag, queries, *values, *prior)


def foreign_kernel(flag_ref, q_ref, k_ref, v_ref, mask_ref, num_ref, tot_ref):
    head = pl.program_id(1)

    @pl.when(head == 0)
    def _():
        tot_ref[...] = jnp.zeros_like(tot_ref)

    @pl.when(flag_ref[0] == 1)
    def _():
        value = v_ref[...]
        weights = weigh(q_ref[...], k_ref[...], mask_ref[...])
        num_ref[...] = jnp.dot(weights, value, preferred_element_type=F32).astype(BF16)
        sums = lax.dot_general(
            jnp.ones((8, weights.shape[1]), BF16), weights, (((1,), (1,)), ((), ())), preferred_element_type=F32
        )
        row = lax.broadcasted_iota(jnp.int32, sums.shape, 0)
        tot_ref[...] = jnp.where(row == head, sums, tot_ref[...])

    @pl.when(flag_ref[0] != 1)
    def _():
        num_ref[...] = jnp.zeros_like(num_ref)


def foreign_part(flag, queries, first, heads, stale, mask):
    rows, cols, window = queries.shape[0], heads * HEAD_DIM, stale.shape[0]
    query = pl.BlockSpec((QUERY_TILE, HEAD_DIM), lambda i, h, f: (i, h))
    tile = pl.BlockSpec((QUERY_TILE, HEAD_DIM), lambda i, h, f: (i, h))
    return pl.pallas_call(
        foreign_kernel,
        grid_spec=pltpu.PrefetchScalarGridSpec(
            num_scalar_prefetch=1,
            grid=(rows // QUERY_TILE, heads),
            in_specs=[
                query,
                pl.BlockSpec((window, HEAD_DIM), lambda i, h, f: (0, 2 * (first + h))),
                pl.BlockSpec((window, HEAD_DIM), lambda i, h, f: (0, 2 * (first + h) + 1)),
                pl.BlockSpec((QUERY_TILE // BLOCK, 1, window), lambda i, h, f: (i, 0, 0)),
            ],
            out_specs=[tile, pl.BlockSpec((8, QUERY_TILE), lambda i, h, f: (0, i))],
        ),
        out_shape=[jax.ShapeDtypeStruct((rows, cols), BF16), jax.ShapeDtypeStruct((8, rows), F32)],
        compiler_params=params(),
        cost_estimate=cost(4 * rows * window * cols, rows * cols * 8, rows * window * heads),
    )(flag, queries, stale, stale, mask)


def normalise_into(att_ref, column, near_refs, num_ref=None, tot_ref=None):
    totals = None if tot_ref is None else jnp.transpose(tot_ref[...])
    at = 0
    for n_ref, t_ref in near_refs:
        for head in range(n_ref.shape[1] // HEAD_DIM):
            cols = slice(head * HEAD_DIM, (head + 1) * HEAD_DIM)
            num, tot = n_ref[:, cols], t_ref[:, cols]
            if num_ref is not None:
                num += num_ref[:, at * HEAD_DIM : (at + 1) * HEAD_DIM].astype(F32)
                tot += totals[:, at : at + 1]
            att_ref[:, (column + at) * HEAD_DIM : (column + at + 1) * HEAD_DIM] = (num / tot).astype(BF16)
            at += 1


def normalise_kernel(*refs):
    near_refs = [(refs[2 * at], refs[2 * at + 1]) for at in range((len(refs) - 3) // 2)]
    normalise_into(refs[-1], 0, near_refs, refs[-3], refs[-2])


def normalise(near, num, tot, low):
    rows, cols = num.shape
    tile = min(512, rows)
    skip = low // tile
    specs, values = [], []
    for pair in near:
        specs += [pl.BlockSpec((tile, pair[0].shape[1]), lambda i: (skip + i, 0))] * 2
        values += list(pair)
    return pl.pallas_call(
        normalise_kernel,
        grid=(rows // tile,),
        in_specs=specs + [pl.BlockSpec((tile, cols), lambda i: (i, 0)), pl.BlockSpec((8, tile), lambda i: (0, skip + i))],
        out_specs=pl.BlockSpec((tile, cols), lambda i: (i, 0)),
        out_shape=jax.ShapeDtypeStruct((rows, cols), BF16),
        compiler_params=params(),
        cost_estimate=cost(rows * cols * 4, rows * cols * 12),
    )(*values, num, tot)


def branch_kernel(near, keeps, parts, where_ref, *refs):
    step, steps = pl.program_id(0), pl.num_programs(0)
    mine_ref, own_refs, other_refs = refs[0], refs[1:parts], refs[parts : 2 * parts - 1]
    g_ref, done_ref = refs[2 * parts - 1 : 2 * parts + 1]
    rest = refs[2 * parts + 1 :]
    send_ref, keep_ref, att_ref, lefts_ref = rest[-4:]
    lefts_ref = lefts_ref.at[pl.program_id(1)]
    rank, depth = where_ref[3 * steps], mine_ref.shape[1]

    @pl.when(step == 0)
    def _():
        att_ref[:, : done_ref.shape[1]] = done_ref[...]
        near_refs = [(rest[2 * at], rest[2 * at + 1]) for at in range(near)]
        normalise_into(att_ref, done_ref.shape[1] // HEAD_DIM, near_refs)
        for offset in range(parts):
            part = lax.rem(rank + parts - offset, parts)
            left = att_ref[:, :depth]
            for other in range(1, parts):
                left = jnp.where(part == other, att_ref[:, other * depth : (other + 1) * depth], left)
            lefts_ref[offset] = left

    is_own = where_ref[step] == 0
    term = jnp.dot(lefts_ref[0], mine_ref[0], preferred_element_type=F32)
    for offset in range(1, parts):
        right = jnp.where(is_own, own_refs[offset - 1][...], other_refs[offset - 1][0])
        term += jnp.dot(lefts_ref[offset], right, preferred_element_type=F32)
    result = (term * g_ref[0]).astype(BF16)
    stays = step >= steps - keeps

    @pl.when(stays)
    def _():
        keep_ref[0] = result

    @pl.when(jnp.logical_not(stays))
    def _():
        send_ref[0] = result


def branch(where, mine, owns, others, gate, done, near, first, count, keeps):
    total, depth, width = mine.shape
    tile = ROW_TILE if count % ROW_TILE == 0 and first % ROW_TILE == 0 else BLOCK
    start, tiles = first // tile, count // tile
    sends = total - keeps

    def row_tile(g, i, w):
        return start + jnp.where(g == 0, i, tiles - 1), 0

    specs, values = [pl.BlockSpec((tile, done.shape[1]), row_tile)], [done]
    for num, tot in near:
        spec = pl.BlockSpec((tile, num.shape[1]), row_tile)
        specs += [spec, spec]
        values += [num, tot]
    parts = len(others) + 1
    held = depth * parts
    return pl.pallas_call(
        functools.partial(branch_kernel, len(near), keeps, parts),
        grid_spec=pltpu.PrefetchScalarGridSpec(
            num_scalar_prefetch=1,
            grid=(total, tiles),
            in_specs=[pl.BlockSpec((1, depth, width), lambda g, i, w: (w[g], 0, 0))]
            + [pl.BlockSpec((depth, width), lambda g, i, w: (0, 0))] * len(owns)
            + [pl.BlockSpec((1, depth, width), lambda g, i, w: (w[total + g], 0, 0))] * len(others)
            + [pl.BlockSpec((1, 1, width), lambda g, i, w: (w[2 * total + g], 0, 0))]
            + specs,
            out_specs=[
                pl.BlockSpec((1, tile, width), lambda g, i, w: (jnp.minimum(g, sends - 1), jnp.where(g < sends, i, tiles - 1), 0)),
                pl.BlockSpec((1, tile, width), lambda g, i, w: (jnp.maximum(g - sends, 0), jnp.where(g < sends, 0, i), 0)),
            ],
            scratch_shapes=[pltpu.VMEM((tile, held), BF16), pltpu.VMEM((tiles, parts, tile, depth), BF16)],
        ),
        out_shape=[
            jax.ShapeDtypeStruct((sends, count, width), BF16),
            jax.ShapeDtypeStruct((keeps, count, width), BF16),
        ],
        compiler_params=params(),
        cost_estimate=cost(2 * count * held * total * width, held * total * width * 2 + count * total * width * 2),
    )(where, mine, *owns, *others, gate, *values)


def chosen(place, values, names):
    out = values[0]
    for at in range(1, len(values)):
        if names[at] != names[0]:
            out = jnp.where(place == at, values[at], out)
    return out


class Relay:
    def __init__(self, own, count, reps):
        self.count, self.reps = count, reps
        self.place, self.rank = lax.axis_index("patch"), lax.axis_index("rep")
        self.ahead, self.back = {0: own}, {0: own}

    def step(self, k, *held):
        count = self.count
        ahead, back = self.ahead[k - 1], self.back[k - 1]
        if held:
            ahead, back = after(ahead, *held), after(back, *held)
        self.ahead[k] = lax.ppermute(ahead, "patch", [(i, i + 1) for i in range(k - 1, count - 1)])
        self.back[k] = lax.ppermute(back, "patch", [(i + 1, i) for i in range(count - k)])

    def sent(self, k):
        return self.ahead[k], self.back[k]

    def brought(self, t, cut=None):
        values, owners = [], []
        for at in range(self.count):
            comes = sorted([(k, 0) for k in range(1, at + 1)] + [(k, 1) for k in range(1, self.count - at)])
            k, side = comes[t - 1]
            values.append(self.back[k] if side else self.ahead[k])
            owners.append(at + k if side else at - k)
        owner = sum(jnp.where(self.place == at, owners[at], 0) for at in range(self.count))
        candidates = []
        for value in values:
            if not any(value is other for other in candidates):
                candidates.append(value)
        fenced = lax.optimization_barrier(tuple(candidates))
        at_of = [[value is other for other in candidates].index(True) for value in values]
        cuts = [(0, values[0].shape[1])] if cut is None else [(0, cut), (cut, values[0].shape[1])]
        chosen_cuts = [chosen(self.place, [fenced[at][:, low:high] for at in at_of], at_of) for low, high in cuts]
        parts = [(self.rank, chosen_cuts)]
        for offset in range(1, self.reps):
            pairs = [(a, (a + offset) % self.reps) for a in range(self.reps)]
            swapped, held = [], ()
            for piece in chosen_cuts:
                swapped.append(lax.ppermute(after(piece, *held) if held else piece, "rep", pairs))
                held = (swapped[-1],)
            parts.append(((self.rank - offset) % self.reps, swapped))
        return owner, parts


def body(hidden, modulation, gate, w_qkv, stale_kv, w_out, key_lists):
    count, reps = lax.axis_size("patch"), lax.axis_size("rep")
    tps, secs = lax.axis_size("tp"), lax.axis_size("sec")
    place, rank = lax.axis_index("patch"), lax.axis_index("rep")
    tp_index, sec_index = lax.axis_index("tp"), lax.axis_index("sec")
    rows, model_width = hidden.shape[1], hidden.shape[2]
    heads = w_out.shape[1] // HEAD_DIM
    patch_blocks = rows // BLOCK
    unit_heads = heads // 3 if heads % 3 == 0 else 1
    units = heads // unit_heads
    small_units = max(1, units // 3)
    group_units = [list(range(units - small_units)), list(range(units - small_units, units))]
    group_heads = [len(members) * unit_heads for members in group_units]
    group_first = [0, group_heads[0]]
    states = hidden[0]
    w_qkv, stale_kv, w_out = w_qkv[0], stale_kv[0], w_out[0]
    last = count - 1
    shard_rows = w_qkv.shape[0]
    depth, out_depth = shard_rows // reps, w_out.shape[0] // reps
    width = 3 * HEAD_DIM

    relative = jnp.where(key_lists >= 0, key_lists - (place - 1) * patch_blocks, -1)
    window_ids = jnp.arange(3 * patch_blocks, dtype=jnp.int32)
    hits = jnp.any(relative[:, :, None] == window_ids[None, None, :], axis=1).astype(F32)
    hits = jnp.repeat(hits, BLOCK, axis=1).reshape(patch_blocks, 3, rows)
    before, fresh, behind = (hits[:, i][:, None, :] for i in range(3))
    odd = place % 2 == 1
    even_mask, odd_mask = jnp.where(odd, before, behind), jnp.where(odd, behind, before)
    at_end = (place == 0) | (place == last)
    to_inner = [(0, 1), (last, last - 1)]
    to_end = [(1, 0), (last - 1, last)]
    inner_flag = jnp.where(at_end, 0, 1).astype(jnp.int32).reshape(1)
    host_flag = ((place == 1) | (place == last - 1)).astype(jnp.int32).reshape(1)

    inner = range(1, last)
    pairs = [(i, i + 1) for i in range(last)] + [(i + 1, i) for i in range(last)]
    even_pairs = [(a, b) for a, b in pairs if min(a, b) % 2 == 0 and b in inner]
    odd_pairs = [(a, b) for a, b in pairs if min(a, b) % 2 == 1 and b in inner]
    stale, even, other = [None] * units, [None] * units, [None] * units

    def send_even(unit, *held):
        even[unit] = lax.ppermute(after(stale[unit], *held), "patch", even_pairs)

    def send_other(unit, *held):
        other[unit] = lax.ppermute(after(stale[unit], *held), "patch", odd_pairs)

    def qkv_relay(group, *held):
        source = after(w_qkv, *held) if held else w_qkv
        at = (rank * depth, group_first[group] * width)
        own = lax.dynamic_slice(source, at, (depth, group_heads[group] * width))
        if group == 1:
            own = jnp.concatenate([own, own_out.reshape(depth, out_cols)], axis=1)
        return Relay(own, count, reps)

    def columns(owner, part):
        return lax.dynamic_slice_in_dim(ready, owner * shard_rows + part * depth, depth, 1)

    def term_of(owner, part, piece):
        return columns(owner, part), piece

    def add_terms(acc, terms):
        for left, right in terms:
            acc += jnp.dot(left, right, preferred_element_type=F32)
        return acc

    out_shape = (out_depth, w_out.shape[1])
    out_cols = out_depth * w_out.shape[1] // depth
    small_cols = group_heads[1] * width
    large = qkv_relay(0)
    large.step(1)
    inputs = states.astype(F32)
    centered = inputs - jnp.mean(inputs, axis=-1, keepdims=True)
    variance = jnp.mean(centered * centered, axis=-1, keepdims=True)
    normed = centered * lax.rsqrt(variance + 1e-06)
    modulated = (normed * (1.0 + modulation[0, 1]) + modulation[0, 0]).astype(BF16)
    for at in range(units):
        stale[at] = stale_group(stale_kv, at * unit_heads, unit_heads)
    modulated, stale[0] = lax.optimization_barrier((modulated, stale[0]))

    ready = after(modulated, *large.sent(1))
    own_columns = lax.dynamic_slice_in_dim(ready, place * shard_rows, shard_rows, 1)
    accs = [None, None]
    come = [[], []]
    far_mask = lax.ppermute(jnp.where(place == 0, behind, before), "patch", to_inner)
    share = model_width // (tps * secs)
    residual = lax.dynamic_slice_in_dim(states, (tp_index * secs + sec_index) * share, share, 1)
    got_all = []
    for offset in range(1, secs):
        target = (1 + offset) % secs
        sent = lax.dynamic_slice_in_dim(states, (tp_index * secs + target) * share, share, 1)
        got = lax.ppermute(sent, "sec", [(1, target)])
        got_all.append(got)
        residual = jnp.where(sec_index == target, got, residual)

    def swaps(group, at):
        return [piece[0] for _, piece in come[group][at][1][1:]] if 0 <= at < len(come[group]) else []

    def given(*items):
        return [item for item in items if item is not None]

    def at_or_none(items, at):
        return items[at] if at < len(items) else None

    def own_half(group, at):
        owner, parts = come[group][at]
        return [term_of(owner, parts[0][0], parts[0][1][0])]

    def other_half(group, at):
        owner, parts = come[group][at]
        return [term_of(owner, part, piece[0]) for part, piece in parts[1:]]

    come[0].append(large.brought(1))
    send_even(0, *large.sent(1))
    for k in range(2, count):
        held = [modulated, far_mask] + got_all if k == 2 else [accs[0]] + swaps(0, k - 3)
        if k == 3:
            held += [even[0], residual]
        large.step(k, *held)
        come[0].append(large.brought(k))
        if k == 2:
            accs[0] = own_terms(after(own_columns, *large.sent(1)), w_qkv, 0, group_heads[0])
            if units > 1:
                send_even(1, *large.sent(2))
                send_other(0, *large.sent(2))
        elif k == 3:
            accs[0] = add_terms(accs[0], own_half(0, 0) + own_half(0, 1) + other_half(0, 0))

    own_out = lax.dynamic_slice_in_dim(after(w_out, *large.sent(1)), rank * out_depth, out_depth, 0)
    small = qkv_relay(1, *large.sent(min(2, last)))
    small.step(
        1, *large.sent(last), accs[0], *swaps(0, last - 2), *given(at_or_none(even, 1), at_or_none(other, 0))
    )
    come[1].append(small.brought(1, small_cols if last == 1 else None))
    for at in range(2, last - 1):
        accs[0] = add_terms(accs[0], own_half(0, at) + other_half(0, at - 1))
    accs[1] = own_terms(after(own_columns, *large.sent(last)), w_qkv, group_first[1], group_heads[1])
    final_terms = own_half(0, last - 1) + other_half(0, last - 1)
    if last > 1:
        final_terms = other_half(0, last - 2) + final_terms
    queries_0 = finish(accs[0], final_terms)
    far_queries_0 = lax.ppermute(queries_0[0], "patch", to_inner)
    queries_1 = None

    def near_part(group, at, fresh_too, sides, flags, prior, span=None):
        queries, keys, values = (queries_0, queries_1)[group]
        here = (at * unit_heads, unit_heads)
        return windows(flags, queries, here, [(keys, values, fresh)] if fresh_too else [], sides, prior, span)

    def sides_of(unit_at):
        late = unit_at > 0
        stale_at = (unit_at - 1) * unit_heads if late else 0
        return [(even[unit_at], even_mask, 0), (other[1 if late else 0], odd_mask, stale_at)]

    all_even = [(a, b) for a, b in pairs if min(a, b) % 2 == 0]
    late_stale = stale_group(after(stale_kv, *large.sent(last)), unit_heads, heads - unit_heads)

    def late_exchanges(held):
        for at in group_units[1]:
            even[at] = lax.ppermute(after(stale[at], *held, *swaps(1, 0)), "patch", all_even)
        for at in group_units[0]:
            if even[at] is None:
                send_even(at, *held)
        other[1] = lax.ppermute(after(late_stale, *held), "patch", odd_pairs)

    first_large = group_units[0]
    inner_flags = jnp.concatenate([inner_flag, inner_flag])
    near = [None] * units
    near[0] = near_part(0, 0, True, sides_of(0), inner_flags, ())
    for k in range(2, count):
        if k == 2:
            held = [accs[1]]
        elif k == 3:
            held = [*queries_0, near[0][0]]
        else:
            held = swaps(1, k - 4)
        small.step(k, *held)
        come[1].append(small.brought(k, small_cols if k == last else None))
        if k == 2:
            late_exchanges(small.sent(2))
    if other[1] is None:
        late_exchanges(small.sent(last))

    stale_full = stale_group(after(stale_kv, *small.sent(1)), 0, group_heads[0])
    far_num, far_tot = foreign_part(host_flag, far_queries_0, 0, group_heads[0], stale_full, far_mask)
    come_last = come[1][-1][1][0][1]
    exchanged = [even[at] for at in group_units[1]] + [other[1]]
    spans, low = [], 0
    for share_rows in ROW_CHUNKS:
        spans.append((low, rows * share_rows // sum(ROW_CHUNKS)))
        low += spans[-1][1]
    held = [*small.sent(last), *come_last, *swaps(1, last - 2)]
    back_tot = lax.ppermute(after(far_tot, *held), "patch", to_end)
    back_nums = []
    for low, count_rows in spans:
        part = lax.slice_in_dim(far_num, low, low + count_rows, axis=0)
        back_nums.append(lax.ppermute(after(part, *held), "patch", to_end))
        held = [*exchanged, back_tot, back_nums[-1]]
    for at, unit_at in enumerate(first_large):
        if unit_at:
            part = near_part(0, at, True, sides_of(unit_at)[:1], inner_flag, ())
            near[unit_at] = near_part(0, at, False, sides_of(unit_at)[1:], inner_flag, tuple(part))

    early = []
    for at in range(last - 2):
        early += own_half(1, at) + other_half(1, at)
    if early:
        accs[1] = add_terms(accs[1], [(left, right[:, :small_cols]) for left, right in early])
    final_terms = []
    for at in range(max(last - 2, 0), last):
        final_terms += own_half(1, at) + other_half(1, at)
    fenced = lax.optimization_barrier((accs[1], near[first_large[-1]][0]))
    queries_1 = finish(fenced[0], final_terms)
    always = jnp.concatenate([jnp.ones((1,), jnp.int32), inner_flag])

    out_mine, out_others, out_owns, owners = [own_out], [[] for _ in range(reps - 1)], [], [place]
    for owner, parts in come[1]:
        owners.append(owner)
        for at, (_, piece) in enumerate(parts):
            rows_out = (piece[0][:, small_cols:] if len(piece) == 1 else piece[1]).reshape(out_shape)
            if at == 0:
                out_mine.append(rows_out)
            else:
                out_others[at - 1].append(rows_out)
    out_mine = jnp.stack(out_mine)
    out_others = [jnp.stack(items) for items in out_others]
    for offset in range(1, reps):
        out_owns.append(lax.dynamic_slice_in_dim(w_out, (rank - offset) % reps * out_depth, out_depth, 0))

    per = count // (tps * secs)
    order = [
        (block * secs + (sec_index + offset) % secs) * per + at
        for offset in list(range(1, secs)) + [0]
        for block in range(tps)
        for at in range(per)
    ]
    turns = [sum(jnp.where(owners[t] == column, t, 0) for t in range(count)) for column in order]
    where = jnp.stack(turns + [jnp.maximum(turn - 1, 0) for turn in turns] + order + [rank]).astype(jnp.int32)
    gate_blocks = gate.reshape(count, 1, w_out.shape[1])
    keeps = tps * per
    results = []
    for at, (start, chunk) in enumerate(spans):
        late = [
            near_part(1, at_unit, True, sides_of(unit_at), always, (), (start, chunk))
            for at_unit, unit_at in enumerate(group_units[1])
        ]
        done = normalise([near[unit_at] for unit_at in group_units[0]], back_nums[at], back_tot, start)
        sends, keep = branch(where, out_mine, out_owns, out_others, gate_blocks, done, late, 0, chunk, keeps)
        got = [keep]
        for offset in range(1, secs):
            sent = sends[(offset - 1) * keeps : offset * keeps]
            got.append(lax.ppermute(sent, "sec", [(i, (i + offset) % secs) for i in range(secs)]))

        def block_of(index):
            return sum(lax.dynamic_slice_in_dim(part, index * per, per, 0).astype(F32) for part in got)

        others = []
        for offset in range(1, tps):
            sent = block_of((tp_index + offset) % tps).astype(BF16)
            others.append(lax.ppermute(sent, "tp", [(i, (i + offset) % tps) for i in range(tps)]))
        others = [after(part, *results) for part in others] if results else others
        result = block_of(tp_index) + sum(part.astype(F32) for part in others)
        result = jnp.moveaxis(result, 0, 1).reshape(chunk, share)
        results.append((result + residual[start : start + chunk].astype(F32)).astype(BF16))
    return jnp.concatenate(results, axis=0)


def solution(mesh):
    return jax.shard_map(
        body,
        mesh=mesh,
        in_specs=(
            P("sec", ("rep", "patch"), None),
            P("sec", None, None),
            P("sec", None),
            P("sec", "patch", "tp"),
            P("sec", ("rep", "patch"), "tp"),
            P("sec", "tp", "patch"),
            P(("rep", "patch"), None),
        ),
        out_specs=P(("rep", "patch"), ("tp", "sec")),
        check_vma=False,
    )
```

```python
import functools
import math

import jax
import jax.numpy as jnp
from jax import lax
from jax.experimental import pallas as pl
from jax.experimental.pallas import tpu as pltpu
from jax.sharding import PartitionSpec as P

HEAD_DIM = 128
BLOCK = 128
QUERY_TILE = 512
ROW_CHUNKS = (1, 1)
ROW_TILE = 512
COST_SCALE = 0.2
VMEM_LIMIT = 28 * 1024 * 1024
F32 = jnp.float32
BF16 = jnp.bfloat16


def after(value, *others):
    return lax.optimization_barrier((value,) + others)[0]


def params():
    return pltpu.CompilerParams(vmem_limit_bytes=VMEM_LIMIT)


def cost(flops, moved, exps=0):
    scale = COST_SCALE
    return pl.CostEstimate(flops=int(flops * scale), bytes_accessed=int(moved * scale), transcendentals=int(exps * scale))


def unit(value):
    return value * lax.rsqrt(jnp.mean(value * value, axis=-1, keepdims=True) + 1e-06)


def stale_kernel(in_ref, out_ref):
    out_ref[:, :HEAD_DIM] = unit(in_ref[:, :HEAD_DIM].astype(F32)).astype(BF16)
    out_ref[:, HEAD_DIM:] = in_ref[:, HEAD_DIM:]


def stale_group(stale, first, heads):
    rows = stale.shape[0]
    return pl.pallas_call(
        stale_kernel,
        grid=(heads,),
        in_specs=[pl.BlockSpec((rows, 2 * HEAD_DIM), lambda h: (0, first + h))],
        out_specs=pl.BlockSpec((rows, 2 * HEAD_DIM), lambda h: (0, h)),
        out_shape=jax.ShapeDtypeStruct((rows, heads * 2 * HEAD_DIM), BF16),
        compiler_params=params(),
        cost_estimate=cost(rows * heads * 512, rows * heads * 1024),
    )(stale)


def own_kernel(left_ref, right_ref, out_ref):
    out_ref[...] = jnp.dot(left_ref[...], right_ref[...], preferred_element_type=F32)


def own_terms(left, right, first, heads):
    rows, depth = left.shape
    width = 3 * HEAD_DIM
    return pl.pallas_call(
        own_kernel,
        grid=(heads,),
        in_specs=[
            pl.BlockSpec((rows, depth), lambda h: (0, 0)),
            pl.BlockSpec((depth, width), lambda h: (0, first + h)),
        ],
        out_specs=pl.BlockSpec((rows, width), lambda h: (0, h)),
        out_shape=jax.ShapeDtypeStruct((rows, heads * width), F32),
        compiler_params=params(),
        cost_estimate=cost(2 * rows * depth * heads * width, rows * heads * width * 4 + depth * (rows + heads * width) * 2),
    )(left, right)


def finish_kernel(terms, *refs):
    total = refs[2 * terms][...]
    for at in range(terms):
        total += jnp.dot(refs[at][...], refs[terms + at][...], preferred_element_type=F32)
    q_ref, k_ref, v_ref = refs[2 * terms + 1 :]
    q_ref[...] = unit(total[:, :HEAD_DIM]).astype(BF16)
    k_ref[...] = unit(total[:, HEAD_DIM : 2 * HEAD_DIM]).astype(BF16)
    v_ref[...] = total[:, 2 * HEAD_DIM :].astype(BF16)


def finish(acc, terms):
    lefts, rights = [left for left, _ in terms], [right for _, right in terms]
    width, rows = 3 * HEAD_DIM, acc.shape[0]
    heads, tile = acc.shape[1] // width, rows
    depth = sum(left.shape[1] for left in lefts)
    out = pl.BlockSpec((tile, HEAD_DIM), lambda h, i: (i, h))
    return pl.pallas_call(
        functools.partial(finish_kernel, len(terms)),
        grid=(heads, rows // tile),
        in_specs=[pl.BlockSpec((tile, left.shape[1]), lambda h, i: (i, 0)) for left in lefts]
        + [pl.BlockSpec((right.shape[0], width), lambda h, i: (0, h)) for right in rights]
        + [pl.BlockSpec((tile, width), lambda h, i: (i, h))],
        out_specs=[out] * 3,
        out_shape=[jax.ShapeDtypeStruct((rows, heads * HEAD_DIM), BF16)] * 3,
        compiler_params=params(),
        cost_estimate=cost(2 * rows * depth * heads * width, rows * heads * width * 6),
    )(*lefts, *rights, acc)


def weigh(query, key, mask):
    tile, keys = query.shape[0], key.shape[0]
    scores = lax.dot_general(query, key, (((1,), (1,)), ((), ())), preferred_element_type=F32)
    exponents = jnp.exp(scores * (1.0 / math.sqrt(HEAD_DIM)))
    exponents = exponents.reshape(tile // BLOCK, BLOCK, keys) * mask
    return exponents.reshape(tile, keys).astype(BF16)


def with_ones(value):
    return jnp.concatenate([value, jnp.ones(value.shape, value.dtype)], axis=1)


def window_kernel(fresh, sides, prior, flag_ref, q_ref, *refs):
    num_ref, tot_ref = refs[-2:]
    query = q_ref[...]
    shape = (query.shape[0], 2 * HEAD_DIM)

    def terms(first, windows):
        both = jnp.zeros(shape, F32)
        for at in range(first, first + windows):
            k_ref, v_ref, m_ref = refs[3 * at : 3 * at + 3]
            weights = weigh(query, k_ref[...], m_ref[...])
            both += jnp.dot(weights, with_ones(v_ref[...]), preferred_element_type=F32)
        return both[:, :HEAD_DIM], both[:, HEAD_DIM:]

    if prior:
        num, tot = refs[3 * (fresh + sides)][...], refs[3 * (fresh + sides) + 1][...]
    if fresh:
        num, tot = terms(0, fresh)
    num_ref[...] = num
    tot_ref[...] = tot
    for side in range(sides):

        @pl.when(flag_ref[side] == 1)
        def _(side=side):
            more, more_tot = terms(fresh + side, 1)
            num_ref[...] += more
            tot_ref[...] += more_tot


def windows(flag, queries, here, fresh, sides, prior):
    first, heads = here
    rows, cols = queries.shape[0], heads * HEAD_DIM
    query = pl.BlockSpec((QUERY_TILE, HEAD_DIM), lambda h, i, f: (i, first + h))
    tile = pl.BlockSpec((QUERY_TILE, HEAD_DIM), lambda h, i, f: (i, h))
    specs, values = [], []
    for keys, vals, mask in fresh:
        block = pl.BlockSpec((keys.shape[0], HEAD_DIM), lambda h, i, f: (0, first + h))
        specs += [block, block]
        values += [keys, vals, mask]
        specs.append(pl.BlockSpec((QUERY_TILE // BLOCK, 1, keys.shape[0]), lambda h, i, f: (i, 0, 0)))
    for stale, mask, at in sides:
        specs.append(pl.BlockSpec((stale.shape[0], HEAD_DIM), lambda h, i, f, at=at: (0, 2 * (at + h))))
        specs.append(pl.BlockSpec((stale.shape[0], HEAD_DIM), lambda h, i, f, at=at: (0, 2 * (at + h) + 1)))
        specs.append(pl.BlockSpec((QUERY_TILE // BLOCK, 1, stale.shape[0]), lambda h, i, f: (i, 0, 0)))
        values += [stale, stale, mask]
    count = len(fresh) + len(sides)
    return pl.pallas_call(
        functools.partial(window_kernel, len(fresh), len(sides), len(prior)),
        grid_spec=pltpu.PrefetchScalarGridSpec(
            num_scalar_prefetch=1,
            grid=(heads, rows // QUERY_TILE),
            in_specs=[query] + specs + [tile] * len(prior),
            out_specs=[tile, tile],
        ),
        out_shape=[jax.ShapeDtypeStruct((rows, cols), F32)] * 2,
        compiler_params=params(),
        cost_estimate=cost(6 * count * rows * rows * cols, rows * cols * 14 * count, count * rows * rows * heads),
    )(flag, queries, *values, *prior)


def foreign_kernel(flag_ref, q_ref, k_ref, v_ref, mask_ref, num_ref, tot_ref):
    head = pl.program_id(1)

    @pl.when(head == 0)
    def _():
        tot_ref[...] = jnp.zeros_like(tot_ref)

    @pl.when(flag_ref[0] == 1)
    def _():
        value = v_ref[...]
        weights = weigh(q_ref[...], k_ref[...], mask_ref[...])
        num_ref[...] = jnp.dot(weights, value, preferred_element_type=F32).astype(BF16)
        sums = lax.dot_general(
            jnp.ones((8, weights.shape[1]), BF16), weights, (((1,), (1,)), ((), ())), preferred_element_type=F32
        )
        row = lax.broadcasted_iota(jnp.int32, sums.shape, 0)
        tot_ref[...] = jnp.where(row == head, sums, tot_ref[...])

    @pl.when(flag_ref[0] != 1)
    def _():
        num_ref[...] = jnp.zeros_like(num_ref)


def foreign_part(flag, queries, first, heads, stale, mask):
    rows, cols, window = queries.shape[0], heads * HEAD_DIM, stale.shape[0]
    query = pl.BlockSpec((QUERY_TILE, HEAD_DIM), lambda i, h, f: (i, h))
    tile = pl.BlockSpec((QUERY_TILE, HEAD_DIM), lambda i, h, f: (i, h))
    return pl.pallas_call(
        foreign_kernel,
        grid_spec=pltpu.PrefetchScalarGridSpec(
            num_scalar_prefetch=1,
            grid=(rows // QUERY_TILE, heads),
            in_specs=[
                query,
                pl.BlockSpec((window, HEAD_DIM), lambda i, h, f: (0, 2 * (first + h))),
                pl.BlockSpec((window, HEAD_DIM), lambda i, h, f: (0, 2 * (first + h) + 1)),
                pl.BlockSpec((QUERY_TILE // BLOCK, 1, window), lambda i, h, f: (i, 0, 0)),
            ],
            out_specs=[tile, pl.BlockSpec((8, QUERY_TILE), lambda i, h, f: (0, i))],
        ),
        out_shape=[jax.ShapeDtypeStruct((rows, cols), BF16), jax.ShapeDtypeStruct((8, rows), F32)],
        compiler_params=params(),
        cost_estimate=cost(4 * rows * window * cols, rows * cols * 8, rows * window * heads),
    )(flag, queries, stale, stale, mask)


def normalise_into(att_ref, column, near_refs, num_ref=None, tot_ref=None):
    totals = None if tot_ref is None else jnp.transpose(tot_ref[...])
    at = 0
    for n_ref, t_ref in near_refs:
        for head in range(n_ref.shape[1] // HEAD_DIM):
            cols = slice(head * HEAD_DIM, (head + 1) * HEAD_DIM)
            num, tot = n_ref[:, cols], t_ref[:, cols]
            if num_ref is not None:
                num += num_ref[:, at * HEAD_DIM : (at + 1) * HEAD_DIM].astype(F32)
                tot += totals[:, at : at + 1]
            att_ref[:, (column + at) * HEAD_DIM : (column + at + 1) * HEAD_DIM] = (num / tot).astype(BF16)
            at += 1


def normalise_kernel(*refs):
    near_refs = [(refs[2 * at], refs[2 * at + 1]) for at in range((len(refs) - 3) // 2)]
    normalise_into(refs[-1], 0, near_refs, refs[-3], refs[-2])


def normalise(near, far):
    num, tot = far
    rows, cols = num.shape
    tile = 512
    specs, values = [], []
    for pair in near:
        specs += [pl.BlockSpec((tile, pair[0].shape[1]), lambda i: (i, 0))] * 2
        values += list(pair)
    return pl.pallas_call(
        normalise_kernel,
        grid=(rows // tile,),
        in_specs=specs + [pl.BlockSpec((tile, cols), lambda i: (i, 0)), pl.BlockSpec((8, tile), lambda i: (0, i))],
        out_specs=pl.BlockSpec((tile, cols), lambda i: (i, 0)),
        out_shape=jax.ShapeDtypeStruct((rows, cols), BF16),
        compiler_params=params(),
        cost_estimate=cost(rows * cols * 4, rows * cols * 12),
    )(*values, num, tot)


def branch_kernel(near, keeps, parts, where_ref, *refs):
    step, steps = pl.program_id(0), pl.num_programs(0)
    mine_ref, own_refs, other_refs = refs[0], refs[1:parts], refs[parts : 2 * parts - 1]
    g_ref, done_ref = refs[2 * parts - 1 : 2 * parts + 1]
    rest = refs[2 * parts + 1 :]
    send_ref, keep_ref, att_ref, lefts_ref = rest[-4:]
    lefts_ref = lefts_ref.at[pl.program_id(1)]
    rank, depth = where_ref[3 * steps], mine_ref.shape[1]

    @pl.when(step == 0)
    def _():
        att_ref[:, : done_ref.shape[1]] = done_ref[...]
        near_refs = [(rest[2 * at], rest[2 * at + 1]) for at in range(near)]
        normalise_into(att_ref, done_ref.shape[1] // HEAD_DIM, near_refs)
        for offset in range(parts):
            part = lax.rem(rank + parts - offset, parts)
            left = att_ref[:, :depth]
            for other in range(1, parts):
                left = jnp.where(part == other, att_ref[:, other * depth : (other + 1) * depth], left)
            lefts_ref[offset] = left

    is_own = where_ref[step] == 0
    term = jnp.dot(lefts_ref[0], mine_ref[0], preferred_element_type=F32)
    for offset in range(1, parts):
        right = jnp.where(is_own, own_refs[offset - 1][...], other_refs[offset - 1][0])
        term += jnp.dot(lefts_ref[offset], right, preferred_element_type=F32)
    result = (term * g_ref[0]).astype(BF16)
    stays = step >= steps - keeps

    @pl.when(stays)
    def _():
        keep_ref[0] = result

    @pl.when(jnp.logical_not(stays))
    def _():
        send_ref[0] = result


def branch(where, mine, owns, others, gate, done, near, first, count, keeps):
    total, depth, width = mine.shape
    tile = ROW_TILE if count % ROW_TILE == 0 and first % ROW_TILE == 0 else BLOCK
    start, tiles = first // tile, count // tile
    sends = total - keeps

    def row_tile(g, i, w):
        return start + jnp.where(g == 0, i, tiles - 1), 0

    specs, values = [pl.BlockSpec((tile, done.shape[1]), row_tile)], [done]
    for num, tot in near:
        spec = pl.BlockSpec((tile, num.shape[1]), row_tile)
        specs += [spec, spec]
        values += [num, tot]
    parts = len(others) + 1
    held = depth * parts
    return pl.pallas_call(
        functools.partial(branch_kernel, len(near), keeps, parts),
        grid_spec=pltpu.PrefetchScalarGridSpec(
            num_scalar_prefetch=1,
            grid=(total, tiles),
            in_specs=[pl.BlockSpec((1, depth, width), lambda g, i, w: (w[g], 0, 0))]
            + [pl.BlockSpec((depth, width), lambda g, i, w: (0, 0))] * len(owns)
            + [pl.BlockSpec((1, depth, width), lambda g, i, w: (w[total + g], 0, 0))] * len(others)
            + [pl.BlockSpec((1, 1, width), lambda g, i, w: (w[2 * total + g], 0, 0))]
            + specs,
            out_specs=[
                pl.BlockSpec((1, tile, width), lambda g, i, w: (jnp.minimum(g, sends - 1), jnp.where(g < sends, i, tiles - 1), 0)),
                pl.BlockSpec((1, tile, width), lambda g, i, w: (jnp.maximum(g - sends, 0), jnp.where(g < sends, 0, i), 0)),
            ],
            scratch_shapes=[pltpu.VMEM((tile, held), BF16), pltpu.VMEM((tiles, parts, tile, depth), BF16)],
        ),
        out_shape=[
            jax.ShapeDtypeStruct((sends, count, width), BF16),
            jax.ShapeDtypeStruct((keeps, count, width), BF16),
        ],
        compiler_params=params(),
        cost_estimate=cost(2 * count * held * total * width, held * total * width * 2 + count * total * width * 2),
    )(where, mine, *owns, *others, gate, *values)


def chosen(place, values, names):
    out = values[0]
    for at in range(1, len(values)):
        if names[at] != names[0]:
            out = jnp.where(place == at, values[at], out)
    return out


class Relay:
    def __init__(self, own, count, reps):
        self.count, self.reps = count, reps
        self.place, self.rank = lax.axis_index("patch"), lax.axis_index("rep")
        self.ahead, self.back = {0: own}, {0: own}

    def step(self, k, *held):
        count = self.count
        ahead, back = self.ahead[k - 1], self.back[k - 1]
        if held:
            ahead, back = after(ahead, *held), after(back, *held)
        self.ahead[k] = lax.ppermute(ahead, "patch", [(i, i + 1) for i in range(k - 1, count - 1)])
        self.back[k] = lax.ppermute(back, "patch", [(i + 1, i) for i in range(count - k)])

    def sent(self, k):
        return self.ahead[k], self.back[k]

    def brought(self, t, cut=None):
        values, owners = [], []
        for at in range(self.count):
            comes = sorted([(k, 0) for k in range(1, at + 1)] + [(k, 1) for k in range(1, self.count - at)])
            k, side = comes[t - 1]
            values.append(self.back[k] if side else self.ahead[k])
            owners.append(at + k if side else at - k)
        owner = sum(jnp.where(self.place == at, owners[at], 0) for at in range(self.count))
        candidates = []
        for value in values:
            if not any(value is other for other in candidates):
                candidates.append(value)
        fenced = lax.optimization_barrier(tuple(candidates))
        at_of = [[value is other for other in candidates].index(True) for value in values]
        cuts = [(0, values[0].shape[1])] if cut is None else [(0, cut), (cut, values[0].shape[1])]
        chosen_cuts = [chosen(self.place, [fenced[at][:, low:high] for at in at_of], at_of) for low, high in cuts]
        parts = [(self.rank, chosen_cuts)]
        for offset in range(1, self.reps):
            pairs = [(a, (a + offset) % self.reps) for a in range(self.reps)]
            swapped, held = [], ()
            for piece in chosen_cuts:
                swapped.append(lax.ppermute(after(piece, *held) if held else piece, "rep", pairs))
                held = (swapped[-1],)
            parts.append(((self.rank - offset) % self.reps, swapped))
        return owner, parts


def body(hidden, modulation, gate, w_qkv, stale_kv, w_out, key_lists):
    count, reps = lax.axis_size("patch"), lax.axis_size("rep")
    tps, secs = lax.axis_size("tp"), lax.axis_size("sec")
    place, rank = lax.axis_index("patch"), lax.axis_index("rep")
    tp_index, sec_index = lax.axis_index("tp"), lax.axis_index("sec")
    rows, model_width = hidden.shape[1], hidden.shape[2]
    heads = w_out.shape[1] // HEAD_DIM
    patch_blocks = rows // BLOCK
    unit_heads = heads // 3 if heads % 3 == 0 else 1
    units = heads // unit_heads
    small_units = max(1, units // 3)
    group_units = [list(range(units - small_units)), list(range(units - small_units, units))]
    group_heads = [len(members) * unit_heads for members in group_units]
    group_first = [0, group_heads[0]]
    states = hidden[0]
    w_qkv, stale_kv, w_out = w_qkv[0], stale_kv[0], w_out[0]
    last = count - 1
    shard_rows = w_qkv.shape[0]
    depth, out_depth = shard_rows // reps, w_out.shape[0] // reps
    width = 3 * HEAD_DIM

    relative = jnp.where(key_lists >= 0, key_lists - (place - 1) * patch_blocks, -1)
    window_ids = jnp.arange(3 * patch_blocks, dtype=jnp.int32)
    hits = jnp.any(relative[:, :, None] == window_ids[None, None, :], axis=1).astype(F32)
    hits = jnp.repeat(hits, BLOCK, axis=1).reshape(patch_blocks, 3, rows)
    before, fresh, behind = (hits[:, i][:, None, :] for i in range(3))
    odd = place % 2 == 1
    even_mask, odd_mask = jnp.where(odd, before, behind), jnp.where(odd, behind, before)
    at_end = (place == 0) | (place == last)
    to_inner = [(0, 1), (last, last - 1)]
    to_end = [(1, 0), (last - 1, last)]
    inner_flag = jnp.where(at_end, 0, 1).astype(jnp.int32).reshape(1)
    host_flag = ((place == 1) | (place == last - 1)).astype(jnp.int32).reshape(1)

    inner = range(1, last)
    pairs = [(i, i + 1) for i in range(last)] + [(i + 1, i) for i in range(last)]
    even_pairs = [(a, b) for a, b in pairs if min(a, b) % 2 == 0 and b in inner]
    odd_pairs = [(a, b) for a, b in pairs if min(a, b) % 2 == 1 and b in inner]
    stale, even, other = [None] * units, [None] * units, [None] * units

    def send_even(unit, *held):
        even[unit] = lax.ppermute(after(stale[unit], *held), "patch", even_pairs)

    def send_other(unit, *held):
        other[unit] = lax.ppermute(after(stale[unit], *held), "patch", odd_pairs)

    def qkv_relay(group, *held):
        source = after(w_qkv, *held) if held else w_qkv
        at = (rank * depth, group_first[group] * width)
        own = lax.dynamic_slice(source, at, (depth, group_heads[group] * width))
        if group == 1:
            own = jnp.concatenate([own, own_out.reshape(depth, out_cols)], axis=1)
        return Relay(own, count, reps)

    def columns(owner, part):
        return lax.dynamic_slice_in_dim(ready, owner * shard_rows + part * depth, depth, 1)

    def term_of(owner, part, piece):
        return columns(owner, part), piece

    def add_terms(acc, terms):
        for left, right in terms:
            acc += jnp.dot(left, right, preferred_element_type=F32)
        return acc

    out_shape = (out_depth, w_out.shape[1])
    out_cols = out_depth * w_out.shape[1] // depth
    small_cols = group_heads[1] * width
    large = qkv_relay(0)
    large.step(1)
    inputs = states.astype(F32)
    centered = inputs - jnp.mean(inputs, axis=-1, keepdims=True)
    variance = jnp.mean(centered * centered, axis=-1, keepdims=True)
    normed = centered * lax.rsqrt(variance + 1e-06)
    modulated = (normed * (1.0 + modulation[0, 1]) + modulation[0, 0]).astype(BF16)
    for at in range(units):
        stale[at] = stale_group(stale_kv, at * unit_heads, unit_heads)
    modulated, stale[0] = lax.optimization_barrier((modulated, stale[0]))

    ready = after(modulated, *large.sent(1))
    own_columns = lax.dynamic_slice_in_dim(ready, place * shard_rows, shard_rows, 1)
    accs = [None, None]
    come = [[], []]
    far_mask = lax.ppermute(jnp.where(place == 0, behind, before), "patch", to_inner)
    share = model_width // (tps * secs)
    residual = lax.dynamic_slice_in_dim(states, (tp_index * secs + sec_index) * share, share, 1)
    got_all = []
    for offset in range(1, secs):
        target = (1 + offset) % secs
        sent = lax.dynamic_slice_in_dim(states, (tp_index * secs + target) * share, share, 1)
        got = lax.ppermute(sent, "sec", [(1, target)])
        got_all.append(got)
        residual = jnp.where(sec_index == target, got, residual)

    def swaps(group, at):
        return [piece[0] for _, piece in come[group][at][1][1:]] if 0 <= at < len(come[group]) else []

    def given(*items):
        return [item for item in items if item is not None]

    def at_or_none(items, at):
        return items[at] if at < len(items) else None

    def own_half(group, at):
        owner, parts = come[group][at]
        return [term_of(owner, parts[0][0], parts[0][1][0])]

    def other_half(group, at):
        owner, parts = come[group][at]
        return [term_of(owner, part, piece[0]) for part, piece in parts[1:]]

    come[0].append(large.brought(1))
    send_even(0, *large.sent(1))
    for k in range(2, count):
        held = [modulated, far_mask] + got_all if k == 2 else [accs[0]] + swaps(0, k - 3)
        if k == 3:
            held += [even[0], residual]
        large.step(k, *held)
        come[0].append(large.brought(k))
        if k == 2:
            accs[0] = own_terms(after(own_columns, *large.sent(1)), w_qkv, 0, group_heads[0])
            if units > 1:
                send_even(1, *large.sent(2))
                send_other(0, *large.sent(2))
        elif k == 3:
            accs[0] = add_terms(accs[0], own_half(0, 0) + other_half(0, 0))

    own_out = lax.dynamic_slice_in_dim(after(w_out, *large.sent(1)), rank * out_depth, out_depth, 0)
    small = qkv_relay(1, *large.sent(min(2, last)))
    small.step(
        1, *large.sent(last), accs[0], *swaps(0, last - 2), *given(at_or_none(even, 1), at_or_none(other, 0))
    )
    come[1].append(small.brought(1, small_cols if last == 1 else None))
    for at in range(2, last - 1):
        accs[0] = add_terms(accs[0], own_half(0, at) + other_half(0, at - 1))
    accs[1] = own_terms(after(own_columns, *large.sent(last)), w_qkv, group_first[1], group_heads[1])
    final_terms = own_half(0, last - 1) + other_half(0, last - 1)
    if last > 1:
        final_terms = other_half(0, last - 2) + final_terms
    if last > 2:
        final_terms = own_half(0, 1) + final_terms
    queries_0 = finish(accs[0], final_terms)
    far_queries_0 = lax.ppermute(queries_0[0], "patch", to_inner)
    queries_1 = None

    def near_part(group, at, fresh_too, sides, flags, prior):
        queries, keys, values = (queries_0, queries_1)[group]
        here = (at * unit_heads, unit_heads)
        return windows(flags, queries, here, [(keys, values, fresh)] if fresh_too else [], sides, prior)

    def sides_of(unit_at):
        late = unit_at > 0
        stale_at = (unit_at - 1) * unit_heads if late else 0
        return [(even[unit_at], even_mask, 0), (other[1 if late else 0], odd_mask, stale_at)]

    all_even = [(a, b) for a, b in pairs if min(a, b) % 2 == 0]
    late_stale = stale_group(after(stale_kv, *large.sent(last)), unit_heads, heads - unit_heads)

    def late_exchanges(held):
        for at in group_units[1]:
            even[at] = lax.ppermute(after(stale[at], *held, *swaps(1, 0)), "patch", all_even)
        for at in group_units[0]:
            if even[at] is None:
                send_even(at, *held)
        other[1] = lax.ppermute(after(late_stale, *held), "patch", odd_pairs)

    first_large = group_units[0]
    inner_flags = jnp.concatenate([inner_flag, inner_flag])
    near = [None] * units
    near[0] = near_part(0, 0, True, sides_of(0), inner_flags, ())
    for k in range(2, count):
        if k == 2:
            held = [accs[1]]
        elif k == 3:
            held = [*queries_0, near[0][0]]
        else:
            held = swaps(1, k - 4)
        small.step(k, *held)
        come[1].append(small.brought(k, small_cols if k == last else None))
        if k == 2:
            late_exchanges(small.sent(2))
    if other[1] is None:
        late_exchanges(small.sent(last))

    stale_full = stale_group(after(stale_kv, *small.sent(1)), 0, group_heads[0])
    far_num, far_tot = foreign_part(host_flag, far_queries_0, 0, group_heads[0], stale_full, far_mask)
    come_last = come[1][-1][1][0][1]
    exchanged = [even[at] for at in group_units[1]] + [other[1]]
    back_tot = lax.ppermute(after(far_tot, *small.sent(last)), "patch", to_end)
    back_num = lax.ppermute(
        after(far_num, *small.sent(last), *come_last, *exchanged, *swaps(1, last - 2), back_tot), "patch", to_end
    )
    for at, unit_at in enumerate(first_large):
        if unit_at:
            part = near_part(0, at, True, sides_of(unit_at)[:1], inner_flag, ())
            near[unit_at] = near_part(0, at, False, sides_of(unit_at)[1:], inner_flag, tuple(part))

    early = []
    for at in range(last - 2):
        early += own_half(1, at) + other_half(1, at)
    if early:
        accs[1] = add_terms(accs[1], [(left, right[:, :small_cols]) for left, right in early])
    final_terms = []
    for at in range(max(last - 2, 0), last):
        final_terms += own_half(1, at) + other_half(1, at)
    fenced = lax.optimization_barrier((accs[1], near[first_large[-1]][0]))
    queries_1 = finish(fenced[0], final_terms)
    always = jnp.concatenate([jnp.ones((1,), jnp.int32), inner_flag])
    for at, unit_at in enumerate(group_units[1]):
        near[unit_at] = near_part(1, at, True, sides_of(unit_at), always, ())
    done = normalise([near[at] for at in group_units[0]], (back_num, back_tot))

    out_mine, out_others, out_owns, owners = [own_out], [[] for _ in range(reps - 1)], [], [place]
    for owner, parts in come[1]:
        owners.append(owner)
        for at, (_, piece) in enumerate(parts):
            rows_out = (piece[0][:, small_cols:] if len(piece) == 1 else piece[1]).reshape(out_shape)
            if at == 0:
                out_mine.append(rows_out)
            else:
                out_others[at - 1].append(rows_out)
    out_mine = jnp.stack(out_mine)
    out_others = [jnp.stack(items) for items in out_others]
    for offset in range(1, reps):
        out_owns.append(lax.dynamic_slice_in_dim(w_out, (rank - offset) % reps * out_depth, out_depth, 0))

    per = count // (tps * secs)
    order = [
        (block * secs + (sec_index + offset) % secs) * per + at
        for offset in list(range(1, secs)) + [0]
        for block in range(tps)
        for at in range(per)
    ]
    turns = [sum(jnp.where(owners[t] == column, t, 0) for t in range(count)) for column in order]
    where = jnp.stack(turns + [jnp.maximum(turn - 1, 0) for turn in turns] + order + [rank]).astype(jnp.int32)
    gate_blocks = gate.reshape(count, 1, w_out.shape[1])
    keeps = tps * per
    results = []
    start = 0
    for share_rows in ROW_CHUNKS:
        chunk = rows * share_rows // sum(ROW_CHUNKS)
        sends, keep = branch(
            where, out_mine, out_owns, out_others, gate_blocks, done,
            [near[unit_at] for unit_at in group_units[1]], start, chunk, keeps,
        )
        got = [keep]
        for offset in range(1, secs):
            sent = sends[(offset - 1) * keeps : offset * keeps]
            got.append(lax.ppermute(sent, "sec", [(i, (i + offset) % secs) for i in range(secs)]))

        def block_of(index):
            return sum(lax.dynamic_slice_in_dim(part, index * per, per, 0).astype(F32) for part in got)

        others = []
        for offset in range(1, tps):
            sent = block_of((tp_index + offset) % tps).astype(BF16)
            others.append(lax.ppermute(sent, "tp", [(i, (i + offset) % tps) for i in range(tps)]))
        others = [after(part, *results) for part in others] if results else others
        result = block_of(tp_index) + sum(part.astype(F32) for part in others)
        result = jnp.moveaxis(result, 0, 1).reshape(chunk, share)
        results.append((result + residual[start : start + chunk].astype(F32)).astype(BF16))
        start += chunk
    return jnp.concatenate(results, axis=0)


def solution(mesh):
    return jax.shard_map(
        body,
        mesh=mesh,
        in_specs=(
            P("sec", ("rep", "patch"), None),
            P("sec", None, None),
            P("sec", None),
            P("sec", "patch", "tp"),
            P("sec", ("rep", "patch"), "tp"),
            P("sec", "tp", "patch"),
            P(("rep", "patch"), None),
        ),
        out_specs=P(("rep", "patch"), ("tp", "sec")),
        check_vma=False,
    )
```

```python
import functools
import math

import jax
import jax.numpy as jnp
from jax import lax
from jax.experimental import pallas as pl
from jax.experimental.pallas import tpu as pltpu
from jax.sharding import PartitionSpec as P

HEAD_DIM = 128
BLOCK = 128
QUERY_TILE = 512
ROW_CHUNKS = (1, 1)
ROW_TILE = 512
COST_SCALE = 0.1
VMEM_LIMIT = 28 * 1024 * 1024
F32 = jnp.float32
BF16 = jnp.bfloat16


def after(value, *others):
    return lax.optimization_barrier((value,) + others)[0]


def params():
    return pltpu.CompilerParams(vmem_limit_bytes=VMEM_LIMIT)


def cost(flops, moved, exps=0):
    scale = COST_SCALE
    return pl.CostEstimate(flops=int(flops * scale), bytes_accessed=int(moved * scale), transcendentals=int(exps * scale))


def unit(value):
    return value * lax.rsqrt(jnp.mean(value * value, axis=-1, keepdims=True) + 1e-06)


def stale_kernel(in_ref, out_ref):
    out_ref[:, :HEAD_DIM] = unit(in_ref[:, :HEAD_DIM].astype(F32)).astype(BF16)
    out_ref[:, HEAD_DIM:] = in_ref[:, HEAD_DIM:]


def stale_group(stale, first, heads):
    rows = stale.shape[0]
    return pl.pallas_call(
        stale_kernel,
        grid=(heads,),
        in_specs=[pl.BlockSpec((rows, 2 * HEAD_DIM), lambda h: (0, first + h))],
        out_specs=pl.BlockSpec((rows, 2 * HEAD_DIM), lambda h: (0, h)),
        out_shape=jax.ShapeDtypeStruct((rows, heads * 2 * HEAD_DIM), BF16),
        compiler_params=params(),
        cost_estimate=cost(rows * heads * 512, rows * heads * 1024),
    )(stale)


def own_kernel(left_ref, right_ref, out_ref):
    out_ref[...] = jnp.dot(left_ref[...], right_ref[...], preferred_element_type=F32)


def own_terms(left, right, first, heads):
    rows, depth = left.shape
    width = 3 * HEAD_DIM
    return pl.pallas_call(
        own_kernel,
        grid=(heads,),
        in_specs=[
            pl.BlockSpec((rows, depth), lambda h: (0, 0)),
            pl.BlockSpec((depth, width), lambda h: (0, first + h)),
        ],
        out_specs=pl.BlockSpec((rows, width), lambda h: (0, h)),
        out_shape=jax.ShapeDtypeStruct((rows, heads * width), F32),
        compiler_params=params(),
        cost_estimate=cost(2 * rows * depth * heads * width, rows * heads * width * 4 + depth * (rows + heads * width) * 2),
    )(left, right)


def finish_kernel(terms, *refs):
    total = refs[2 * terms][...]
    for at in range(terms):
        total += jnp.dot(refs[at][...], refs[terms + at][...], preferred_element_type=F32)
    q_ref, k_ref, v_ref = refs[2 * terms + 1 :]
    q_ref[...] = unit(total[:, :HEAD_DIM]).astype(BF16)
    k_ref[...] = unit(total[:, HEAD_DIM : 2 * HEAD_DIM]).astype(BF16)
    v_ref[...] = total[:, 2 * HEAD_DIM :].astype(BF16)


def finish(acc, terms):
    lefts, rights = [left for left, _ in terms], [right for _, right in terms]
    width, rows = 3 * HEAD_DIM, acc.shape[0]
    heads, tile = acc.shape[1] // width, rows
    depth = sum(left.shape[1] for left in lefts)
    out = pl.BlockSpec((tile, HEAD_DIM), lambda h, i: (i, h))
    return pl.pallas_call(
        functools.partial(finish_kernel, len(terms)),
        grid=(heads, rows // tile),
        in_specs=[pl.BlockSpec((tile, left.shape[1]), lambda h, i: (i, 0)) for left in lefts]
        + [pl.BlockSpec((right.shape[0], width), lambda h, i: (0, h)) for right in rights]
        + [pl.BlockSpec((tile, width), lambda h, i: (i, h))],
        out_specs=[out] * 3,
        out_shape=[jax.ShapeDtypeStruct((rows, heads * HEAD_DIM), BF16)] * 3,
        compiler_params=params(),
        cost_estimate=cost(2 * rows * depth * heads * width, rows * heads * width * 6),
    )(*lefts, *rights, acc)


def weigh(query, key, mask):
    tile, keys = query.shape[0], key.shape[0]
    scores = lax.dot_general(query, key, (((1,), (1,)), ((), ())), preferred_element_type=F32)
    exponents = jnp.exp(scores * (1.0 / math.sqrt(HEAD_DIM)))
    exponents = exponents.reshape(tile // BLOCK, BLOCK, keys) * mask
    return exponents.reshape(tile, keys).astype(BF16)


def with_ones(value):
    return jnp.concatenate([value, jnp.ones(value.shape, value.dtype)], axis=1)


def window_kernel(fresh, sides, prior, flag_ref, q_ref, *refs):
    num_ref, tot_ref = refs[-2:]
    query = q_ref[...]
    shape = (query.shape[0], 2 * HEAD_DIM)

    def terms(first, windows):
        both = jnp.zeros(shape, F32)
        for at in range(first, first + windows):
            k_ref, v_ref, m_ref = refs[3 * at : 3 * at + 3]
            weights = weigh(query, k_ref[...], m_ref[...])
            both += jnp.dot(weights, with_ones(v_ref[...]), preferred_element_type=F32)
        return both[:, :HEAD_DIM], both[:, HEAD_DIM:]

    if prior:
        num, tot = refs[3 * (fresh + sides)][...], refs[3 * (fresh + sides) + 1][...]
    if fresh:
        num, tot = terms(0, fresh)
    num_ref[...] = num
    tot_ref[...] = tot
    for side in range(sides):

        @pl.when(flag_ref[side] == 1)
        def _(side=side):
            more, more_tot = terms(fresh + side, 1)
            num_ref[...] += more
            tot_ref[...] += more_tot


def windows(flag, queries, here, fresh, sides, prior):
    first, heads = here
    rows, cols = queries.shape[0], heads * HEAD_DIM
    query = pl.BlockSpec((QUERY_TILE, HEAD_DIM), lambda h, i, f: (i, first + h))
    tile = pl.BlockSpec((QUERY_TILE, HEAD_DIM), lambda h, i, f: (i, h))
    specs, values = [], []
    for keys, vals, mask in fresh:
        block = pl.BlockSpec((keys.shape[0], HEAD_DIM), lambda h, i, f: (0, first + h))
        specs += [block, block]
        values += [keys, vals, mask]
        specs.append(pl.BlockSpec((QUERY_TILE // BLOCK, 1, keys.shape[0]), lambda h, i, f: (i, 0, 0)))
    for stale, mask, at in sides:
        specs.append(pl.BlockSpec((stale.shape[0], HEAD_DIM), lambda h, i, f, at=at: (0, 2 * (at + h))))
        specs.append(pl.BlockSpec((stale.shape[0], HEAD_DIM), lambda h, i, f, at=at: (0, 2 * (at + h) + 1)))
        specs.append(pl.BlockSpec((QUERY_TILE // BLOCK, 1, stale.shape[0]), lambda h, i, f: (i, 0, 0)))
        values += [stale, stale, mask]
    count = len(fresh) + len(sides)
    return pl.pallas_call(
        functools.partial(window_kernel, len(fresh), len(sides), len(prior)),
        grid_spec=pltpu.PrefetchScalarGridSpec(
            num_scalar_prefetch=1,
            grid=(heads, rows // QUERY_TILE),
            in_specs=[query] + specs + [tile] * len(prior),
            out_specs=[tile, tile],
        ),
        out_shape=[jax.ShapeDtypeStruct((rows, cols), F32)] * 2,
        compiler_params=params(),
        cost_estimate=cost(6 * count * rows * rows * cols, rows * cols * 14 * count, count * rows * rows * heads),
    )(flag, queries, *values, *prior)


def foreign_kernel(flag_ref, q_ref, k_ref, v_ref, mask_ref, num_ref, tot_ref):
    head = pl.program_id(1)

    @pl.when(head == 0)
    def _():
        tot_ref[...] = jnp.zeros_like(tot_ref)

    @pl.when(flag_ref[0] == 1)
    def _():
        value = v_ref[...]
        weights = weigh(q_ref[...], k_ref[...], mask_ref[...])
        num_ref[...] = jnp.dot(weights, value, preferred_element_type=F32).astype(BF16)
        sums = lax.dot_general(
            jnp.ones((8, weights.shape[1]), BF16), weights, (((1,), (1,)), ((), ())), preferred_element_type=F32
        )
        row = lax.broadcasted_iota(jnp.int32, sums.shape, 0)
        tot_ref[...] = jnp.where(row == head, sums, tot_ref[...])

    @pl.when(flag_ref[0] != 1)
    def _():
        num_ref[...] = jnp.zeros_like(num_ref)


def foreign_part(flag, queries, first, heads, stale, mask):
    rows, cols, window = queries.shape[0], heads * HEAD_DIM, stale.shape[0]
    query = pl.BlockSpec((QUERY_TILE, HEAD_DIM), lambda i, h, f: (i, h))
    tile = pl.BlockSpec((QUERY_TILE, HEAD_DIM), lambda i, h, f: (i, h))
    return pl.pallas_call(
        foreign_kernel,
        grid_spec=pltpu.PrefetchScalarGridSpec(
            num_scalar_prefetch=1,
            grid=(rows // QUERY_TILE, heads),
            in_specs=[
                query,
                pl.BlockSpec((window, HEAD_DIM), lambda i, h, f: (0, 2 * (first + h))),
                pl.BlockSpec((window, HEAD_DIM), lambda i, h, f: (0, 2 * (first + h) + 1)),
                pl.BlockSpec((QUERY_TILE // BLOCK, 1, window), lambda i, h, f: (i, 0, 0)),
            ],
            out_specs=[tile, pl.BlockSpec((8, QUERY_TILE), lambda i, h, f: (0, i))],
        ),
        out_shape=[jax.ShapeDtypeStruct((rows, cols), BF16), jax.ShapeDtypeStruct((8, rows), F32)],
        compiler_params=params(),
        cost_estimate=cost(4 * rows * window * cols, rows * cols * 8, rows * window * heads),
    )(flag, queries, stale, stale, mask)


def normalise_into(att_ref, column, near_refs, num_ref=None, tot_ref=None):
    totals = None if tot_ref is None else jnp.transpose(tot_ref[...])
    at = 0
    for n_ref, t_ref in near_refs:
        for head in range(n_ref.shape[1] // HEAD_DIM):
            cols = slice(head * HEAD_DIM, (head + 1) * HEAD_DIM)
            num, tot = n_ref[:, cols], t_ref[:, cols]
            if num_ref is not None:
                num += num_ref[:, at * HEAD_DIM : (at + 1) * HEAD_DIM].astype(F32)
                tot += totals[:, at : at + 1]
            att_ref[:, (column + at) * HEAD_DIM : (column + at + 1) * HEAD_DIM] = (num / tot).astype(BF16)
            at += 1


def normalise_kernel(*refs):
    near_refs = [(refs[2 * at], refs[2 * at + 1]) for at in range((len(refs) - 3) // 2)]
    normalise_into(refs[-1], 0, near_refs, refs[-3], refs[-2])


def normalise(near, far):
    num, tot = far
    rows, cols = num.shape
    tile = 512
    specs, values = [], []
    for pair in near:
        specs += [pl.BlockSpec((tile, pair[0].shape[1]), lambda i: (i, 0))] * 2
        values += list(pair)
    return pl.pallas_call(
        normalise_kernel,
        grid=(rows // tile,),
        in_specs=specs + [pl.BlockSpec((tile, cols), lambda i: (i, 0)), pl.BlockSpec((8, tile), lambda i: (0, i))],
        out_specs=pl.BlockSpec((tile, cols), lambda i: (i, 0)),
        out_shape=jax.ShapeDtypeStruct((rows, cols), BF16),
        compiler_params=params(),
        cost_estimate=cost(rows * cols * 4, rows * cols * 12),
    )(*values, num, tot)


def branch_kernel(near, keeps, parts, where_ref, *refs):
    step, steps = pl.program_id(0), pl.num_programs(0)
    mine_ref, own_refs, other_refs = refs[0], refs[1:parts], refs[parts : 2 * parts - 1]
    g_ref, done_ref = refs[2 * parts - 1 : 2 * parts + 1]
    rest = refs[2 * parts + 1 :]
    send_ref, keep_ref, att_ref, lefts_ref = rest[-4:]
    lefts_ref = lefts_ref.at[pl.program_id(1)]
    rank, depth = where_ref[3 * steps], mine_ref.shape[1]

    @pl.when(step == 0)
    def _():
        att_ref[:, : done_ref.shape[1]] = done_ref[...]
        near_refs = [(rest[2 * at], rest[2 * at + 1]) for at in range(near)]
        normalise_into(att_ref, done_ref.shape[1] // HEAD_DIM, near_refs)
        for offset in range(parts):
            part = lax.rem(rank + parts - offset, parts)
            left = att_ref[:, :depth]
            for other in range(1, parts):
                left = jnp.where(part == other, att_ref[:, other * depth : (other + 1) * depth], left)
            lefts_ref[offset] = left

    is_own = where_ref[step] == 0
    term = jnp.dot(lefts_ref[0], mine_ref[0], preferred_element_type=F32)
    for offset in range(1, parts):
        right = jnp.where(is_own, own_refs[offset - 1][...], other_refs[offset - 1][0])
        term += jnp.dot(lefts_ref[offset], right, preferred_element_type=F32)
    result = (term * g_ref[0]).astype(BF16)
    stays = step >= steps - keeps

    @pl.when(stays)
    def _():
        keep_ref[0] = result

    @pl.when(jnp.logical_not(stays))
    def _():
        send_ref[0] = result


def branch(where, mine, owns, others, gate, done, near, first, count, keeps):
    total, depth, width = mine.shape
    tile = ROW_TILE if count % ROW_TILE == 0 and first % ROW_TILE == 0 else BLOCK
    start, tiles = first // tile, count // tile
    sends = total - keeps

    def row_tile(g, i, w):
        return start + jnp.where(g == 0, i, tiles - 1), 0

    specs, values = [pl.BlockSpec((tile, done.shape[1]), row_tile)], [done]
    for num, tot in near:
        spec = pl.BlockSpec((tile, num.shape[1]), row_tile)
        specs += [spec, spec]
        values += [num, tot]
    parts = len(others) + 1
    held = depth * parts
    return pl.pallas_call(
        functools.partial(branch_kernel, len(near), keeps, parts),
        grid_spec=pltpu.PrefetchScalarGridSpec(
            num_scalar_prefetch=1,
            grid=(total, tiles),
            in_specs=[pl.BlockSpec((1, depth, width), lambda g, i, w: (w[g], 0, 0))]
            + [pl.BlockSpec((depth, width), lambda g, i, w: (0, 0))] * len(owns)
            + [pl.BlockSpec((1, depth, width), lambda g, i, w: (w[total + g], 0, 0))] * len(others)
            + [pl.BlockSpec((1, 1, width), lambda g, i, w: (w[2 * total + g], 0, 0))]
            + specs,
            out_specs=[
                pl.BlockSpec((1, tile, width), lambda g, i, w: (jnp.minimum(g, sends - 1), jnp.where(g < sends, i, tiles - 1), 0)),
                pl.BlockSpec((1, tile, width), lambda g, i, w: (jnp.maximum(g - sends, 0), jnp.where(g < sends, 0, i), 0)),
            ],
            scratch_shapes=[pltpu.VMEM((tile, held), BF16), pltpu.VMEM((tiles, parts, tile, depth), BF16)],
        ),
        out_shape=[
            jax.ShapeDtypeStruct((sends, count, width), BF16),
            jax.ShapeDtypeStruct((keeps, count, width), BF16),
        ],
        compiler_params=params(),
        cost_estimate=cost(2 * count * held * total * width, held * total * width * 2 + count * total * width * 2),
    )(where, mine, *owns, *others, gate, *values)


def chosen(place, values, names):
    out = values[0]
    for at in range(1, len(values)):
        if names[at] != names[0]:
            out = jnp.where(place == at, values[at], out)
    return out


class Relay:
    def __init__(self, own, count, reps):
        self.count, self.reps = count, reps
        self.place, self.rank = lax.axis_index("patch"), lax.axis_index("rep")
        self.ahead, self.back = {0: own}, {0: own}

    def step(self, k, *held):
        count = self.count
        ahead, back = self.ahead[k - 1], self.back[k - 1]
        if held:
            ahead, back = after(ahead, *held), after(back, *held)
        self.ahead[k] = lax.ppermute(ahead, "patch", [(i, i + 1) for i in range(k - 1, count - 1)])
        self.back[k] = lax.ppermute(back, "patch", [(i + 1, i) for i in range(count - k)])

    def sent(self, k):
        return self.ahead[k], self.back[k]

    def brought(self, t, cut=None):
        values, owners = [], []
        for at in range(self.count):
            comes = sorted([(k, 0) for k in range(1, at + 1)] + [(k, 1) for k in range(1, self.count - at)])
            k, side = comes[t - 1]
            values.append(self.back[k] if side else self.ahead[k])
            owners.append(at + k if side else at - k)
        owner = sum(jnp.where(self.place == at, owners[at], 0) for at in range(self.count))
        candidates = []
        for value in values:
            if not any(value is other for other in candidates):
                candidates.append(value)
        fenced = lax.optimization_barrier(tuple(candidates))
        at_of = [[value is other for other in candidates].index(True) for value in values]
        cuts = [(0, values[0].shape[1])] if cut is None else [(0, cut), (cut, values[0].shape[1])]
        chosen_cuts = [chosen(self.place, [fenced[at][:, low:high] for at in at_of], at_of) for low, high in cuts]
        parts = [(self.rank, chosen_cuts)]
        for offset in range(1, self.reps):
            pairs = [(a, (a + offset) % self.reps) for a in range(self.reps)]
            swapped, held = [], ()
            for piece in chosen_cuts:
                swapped.append(lax.ppermute(after(piece, *held) if held else piece, "rep", pairs))
                held = (swapped[-1],)
            parts.append(((self.rank - offset) % self.reps, swapped))
        return owner, parts


def body(hidden, modulation, gate, w_qkv, stale_kv, w_out, key_lists):
    count, reps = lax.axis_size("patch"), lax.axis_size("rep")
    tps, secs = lax.axis_size("tp"), lax.axis_size("sec")
    place, rank = lax.axis_index("patch"), lax.axis_index("rep")
    tp_index, sec_index = lax.axis_index("tp"), lax.axis_index("sec")
    rows, model_width = hidden.shape[1], hidden.shape[2]
    heads = w_out.shape[1] // HEAD_DIM
    patch_blocks = rows // BLOCK
    unit_heads = heads // 3 if heads % 3 == 0 else 1
    units = heads // unit_heads
    small_units = max(1, units // 3)
    group_units = [list(range(units - small_units)), list(range(units - small_units, units))]
    group_heads = [len(members) * unit_heads for members in group_units]
    group_first = [0, group_heads[0]]
    states = hidden[0]
    w_qkv, stale_kv, w_out = w_qkv[0], stale_kv[0], w_out[0]
    last = count - 1
    shard_rows = w_qkv.shape[0]
    depth, out_depth = shard_rows // reps, w_out.shape[0] // reps
    width = 3 * HEAD_DIM

    relative = jnp.where(key_lists >= 0, key_lists - (place - 1) * patch_blocks, -1)
    window_ids = jnp.arange(3 * patch_blocks, dtype=jnp.int32)
    hits = jnp.any(relative[:, :, None] == window_ids[None, None, :], axis=1).astype(F32)
    hits = jnp.repeat(hits, BLOCK, axis=1).reshape(patch_blocks, 3, rows)
    before, fresh, behind = (hits[:, i][:, None, :] for i in range(3))
    odd = place % 2 == 1
    even_mask, odd_mask = jnp.where(odd, before, behind), jnp.where(odd, behind, before)
    at_end = (place == 0) | (place == last)
    to_inner = [(0, 1), (last, last - 1)]
    to_end = [(1, 0), (last - 1, last)]
    inner_flag = jnp.where(at_end, 0, 1).astype(jnp.int32).reshape(1)
    host_flag = ((place == 1) | (place == last - 1)).astype(jnp.int32).reshape(1)

    inner = range(1, last)
    pairs = [(i, i + 1) for i in range(last)] + [(i + 1, i) for i in range(last)]
    even_pairs = [(a, b) for a, b in pairs if min(a, b) % 2 == 0 and b in inner]
    odd_pairs = [(a, b) for a, b in pairs if min(a, b) % 2 == 1 and b in inner]
    stale, even, other = [None] * units, [None] * units, [None] * units

    def send_even(unit, *held):
        even[unit] = lax.ppermute(after(stale[unit], *held), "patch", even_pairs)

    def send_other(unit, *held):
        other[unit] = lax.ppermute(after(stale[unit], *held), "patch", odd_pairs)

    def qkv_relay(group, *held):
        source = after(w_qkv, *held) if held else w_qkv
        at = (rank * depth, group_first[group] * width)
        own = lax.dynamic_slice(source, at, (depth, group_heads[group] * width))
        if group == 1:
            own = jnp.concatenate([own, own_out.reshape(depth, out_cols)], axis=1)
        return Relay(own, count, reps)

    def columns(owner, part):
        return lax.dynamic_slice_in_dim(ready, owner * shard_rows + part * depth, depth, 1)

    def term_of(owner, part, piece):
        return columns(owner, part), piece

    def add_terms(acc, terms):
        for left, right in terms:
            acc += jnp.dot(left, right, preferred_element_type=F32)
        return acc

    out_shape = (out_depth, w_out.shape[1])
    out_cols = out_depth * w_out.shape[1] // depth
    small_cols = group_heads[1] * width
    large = qkv_relay(0)
    large.step(1)
    inputs = states.astype(F32)
    centered = inputs - jnp.mean(inputs, axis=-1, keepdims=True)
    variance = jnp.mean(centered * centered, axis=-1, keepdims=True)
    normed = centered * lax.rsqrt(variance + 1e-06)
    modulated = (normed * (1.0 + modulation[0, 1]) + modulation[0, 0]).astype(BF16)
    for at in range(units):
        stale[at] = stale_group(stale_kv, at * unit_heads, unit_heads)
    modulated, stale[0] = lax.optimization_barrier((modulated, stale[0]))

    ready = after(modulated, *large.sent(1))
    own_columns = lax.dynamic_slice_in_dim(ready, place * shard_rows, shard_rows, 1)
    accs = [None, None]
    come = [[], []]
    far_mask = lax.ppermute(jnp.where(place == 0, behind, before), "patch", to_inner)
    share = model_width // (tps * secs)
    residual = lax.dynamic_slice_in_dim(states, (tp_index * secs + sec_index) * share, share, 1)
    got_all = []
    for offset in range(1, secs):
        target = (1 + offset) % secs
        sent = lax.dynamic_slice_in_dim(states, (tp_index * secs + target) * share, share, 1)
        got = lax.ppermute(sent, "sec", [(1, target)])
        got_all.append(got)
        residual = jnp.where(sec_index == target, got, residual)

    def swaps(group, at):
        return [piece[0] for _, piece in come[group][at][1][1:]] if 0 <= at < len(come[group]) else []

    def given(*items):
        return [item for item in items if item is not None]

    def at_or_none(items, at):
        return items[at] if at < len(items) else None

    def own_half(group, at):
        owner, parts = come[group][at]
        return [term_of(owner, parts[0][0], parts[0][1][0])]

    def other_half(group, at):
        owner, parts = come[group][at]
        return [term_of(owner, part, piece[0]) for part, piece in parts[1:]]

    come[0].append(large.brought(1))
    send_even(0, *large.sent(1))
    for k in range(2, count):
        held = [modulated, far_mask] + got_all if k == 2 else [accs[0]] + swaps(0, k - 3)
        if k == 3:
            held += [even[0], residual]
        large.step(k, *held)
        come[0].append(large.brought(k))
        if k == 2:
            accs[0] = own_terms(after(own_columns, *large.sent(1)), w_qkv, 0, group_heads[0])
            if units > 1:
                send_even(1, *large.sent(2))
                send_other(0, *large.sent(2))
        elif k == 3:
            accs[0] = add_terms(accs[0], own_half(0, 0) + own_half(0, 1) + other_half(0, 0))

    own_out = lax.dynamic_slice_in_dim(after(w_out, *large.sent(1)), rank * out_depth, out_depth, 0)
    small = qkv_relay(1, *large.sent(min(2, last)))
    small.step(
        1, *large.sent(last), accs[0], *swaps(0, last - 2), *given(at_or_none(even, 1), at_or_none(other, 0))
    )
    come[1].append(small.brought(1, small_cols if last == 1 else None))
    for at in range(2, last - 1):
        accs[0] = add_terms(accs[0], own_half(0, at) + other_half(0, at - 1))
    accs[1] = own_terms(after(own_columns, *large.sent(last)), w_qkv, group_first[1], group_heads[1])
    final_terms = own_half(0, last - 1) + other_half(0, last - 1)
    if last > 1:
        final_terms = other_half(0, last - 2) + final_terms
    queries_0 = finish(accs[0], final_terms)
    far_queries_0 = lax.ppermute(queries_0[0], "patch", to_inner)
    queries_1 = None

    def near_part(group, at, fresh_too, sides, flags, prior):
        queries, keys, values = (queries_0, queries_1)[group]
        here = (at * unit_heads, unit_heads)
        return windows(flags, queries, here, [(keys, values, fresh)] if fresh_too else [], sides, prior)

    def sides_of(unit_at):
        late = unit_at > 0
        stale_at = (unit_at - 1) * unit_heads if late else 0
        return [(even[unit_at], even_mask, 0), (other[1 if late else 0], odd_mask, stale_at)]

    all_even = [(a, b) for a, b in pairs if min(a, b) % 2 == 0]
    late_stale = stale_group(after(stale_kv, *large.sent(last)), unit_heads, heads - unit_heads)

    def late_exchanges(held):
        for at in group_units[1]:
            even[at] = lax.ppermute(after(stale[at], *held, *swaps(1, 0)), "patch", all_even)
        for at in group_units[0]:
            if even[at] is None:
                send_even(at, *held)
        other[1] = lax.ppermute(after(late_stale, *held), "patch", odd_pairs)

    first_large = group_units[0]
    inner_flags = jnp.concatenate([inner_flag, inner_flag])
    near = [None] * units
    near[0] = near_part(0, 0, True, sides_of(0), inner_flags, ())
    for k in range(2, count):
        if k == 2:
            held = [accs[1]]
        elif k == 3:
            held = [*queries_0, near[0][0]]
        else:
            held = swaps(1, k - 4)
        small.step(k, *held)
        come[1].append(small.brought(k, small_cols if k == last else None))
        if k == 2:
            late_exchanges(small.sent(2))
    if other[1] is None:
        late_exchanges(small.sent(last))

    stale_full = stale_group(after(stale_kv, *small.sent(1)), 0, group_heads[0])
    far_num, far_tot = foreign_part(host_flag, far_queries_0, 0, group_heads[0], stale_full, far_mask)
    come_last = come[1][-1][1][0][1]
    exchanged = [even[at] for at in group_units[1]] + [other[1]]
    back_tot = lax.ppermute(after(far_tot, *small.sent(last)), "patch", to_end)
    back_num = lax.ppermute(
        after(far_num, *small.sent(last), *come_last, *exchanged, *swaps(1, last - 2), back_tot), "patch", to_end
    )
    for at, unit_at in enumerate(first_large):
        if unit_at:
            part = near_part(0, at, True, sides_of(unit_at)[:1], inner_flag, ())
            near[unit_at] = near_part(0, at, False, sides_of(unit_at)[1:], inner_flag, tuple(part))

    early = []
    for at in range(last - 2):
        early += own_half(1, at) + other_half(1, at)
    if early:
        accs[1] = add_terms(accs[1], [(left, right[:, :small_cols]) for left, right in early])
    final_terms = []
    for at in range(max(last - 2, 0), last):
        final_terms += own_half(1, at) + other_half(1, at)
    fenced = lax.optimization_barrier((accs[1], near[first_large[-1]][0]))
    queries_1 = finish(fenced[0], final_terms)
    always = jnp.concatenate([jnp.ones((1,), jnp.int32), inner_flag])
    for at, unit_at in enumerate(group_units[1]):
        near[unit_at] = near_part(1, at, True, sides_of(unit_at), always, ())
    done = normalise([near[at] for at in group_units[0]], (back_num, back_tot))

    out_mine, out_others, out_owns, owners = [own_out], [[] for _ in range(reps - 1)], [], [place]
    for owner, parts in come[1]:
        owners.append(owner)
        for at, (_, piece) in enumerate(parts):
            rows_out = (piece[0][:, small_cols:] if len(piece) == 1 else piece[1]).reshape(out_shape)
            if at == 0:
                out_mine.append(rows_out)
            else:
                out_others[at - 1].append(rows_out)
    out_mine = jnp.stack(out_mine)
    out_others = [jnp.stack(items) for items in out_others]
    for offset in range(1, reps):
        out_owns.append(lax.dynamic_slice_in_dim(w_out, (rank - offset) % reps * out_depth, out_depth, 0))

    per = count // (tps * secs)
    order = [
        (block * secs + (sec_index + offset) % secs) * per + at
        for offset in list(range(1, secs)) + [0]
        for block in range(tps)
        for at in range(per)
    ]
    turns = [sum(jnp.where(owners[t] == column, t, 0) for t in range(count)) for column in order]
    where = jnp.stack(turns + [jnp.maximum(turn - 1, 0) for turn in turns] + order + [rank]).astype(jnp.int32)
    gate_blocks = gate.reshape(count, 1, w_out.shape[1])
    keeps = tps * per
    results = []
    start = 0
    for share_rows in ROW_CHUNKS:
        chunk = rows * share_rows // sum(ROW_CHUNKS)
        sends, keep = branch(
            where, out_mine, out_owns, out_others, gate_blocks, done,
            [near[unit_at] for unit_at in group_units[1]], start, chunk, keeps,
        )
        got = [keep]
        for offset in range(1, secs):
            sent = sends[(offset - 1) * keeps : offset * keeps]
            got.append(lax.ppermute(sent, "sec", [(i, (i + offset) % secs) for i in range(secs)]))

        def block_of(index):
            return sum(lax.dynamic_slice_in_dim(part, index * per, per, 0).astype(F32) for part in got)

        others = []
        for offset in range(1, tps):
            sent = block_of((tp_index + offset) % tps).astype(BF16)
            others.append(lax.ppermute(sent, "tp", [(i, (i + offset) % tps) for i in range(tps)]))
        others = [after(part, *results) for part in others] if results else others
        result = block_of(tp_index) + sum(part.astype(F32) for part in others)
        result = jnp.moveaxis(result, 0, 1).reshape(chunk, share)
        results.append((result + residual[start : start + chunk].astype(F32)).astype(BF16))
        start += chunk
    return jnp.concatenate(results, axis=0)


def solution(mesh):
    return jax.shard_map(
        body,
        mesh=mesh,
        in_specs=(
            P("sec", ("rep", "patch"), None),
            P("sec", None, None),
            P("sec", None),
            P("sec", "patch", "tp"),
            P("sec", ("rep", "patch"), "tp"),
            P("sec", "tp", "patch"),
            P(("rep", "patch"), None),
        ),
        out_specs=P(("rep", "patch"), ("tp", "sec")),
        check_vma=False,
    )
```
